32 devices in a mesh: dp: 4 (over y, core), rows: 8 (over z, x).
Axes of the slice: x: 2, y: 2, z: 4, core: 2. Of those that a mesh axis runs over, the one named last changes fastest.
Arguments:
- item_table: float32 [16384, 256], P('rows'), may hold values from -0.5 to 0.5
- row_accum: float32 [16384], P('rows'), may hold values from 0.1 to 10
- owner_map: int32 [4, 8, 512, 1], P('dp', 'rows'), may hold values from 0 to 7; in each aligned block of 512 rows (0 to 511, 512 to 1023, ..., all dimensions but the last counted through in order) at most 192 rows name the same one
- row_index: int32 [4, 8, 512], P('dp', 'rows'), may hold values from 0 to 2047
- bag_index: int32 [4, 8, 512], P('dp', 'rows'), may hold values from 0 to 3, never falling along the last dimension, each value on 1 to 256 neighbouring positions
- prev_owner: int32 [4, 8, 512, 1], P('dp', 'rows'), may hold values from 0 to 7; in each aligned block of 512 rows (0 to 511, 512 to 1023, ..., all dimensions but the last counted through in order) at most 192 rows name the same one
- prev_row: int32 [4, 8, 512], P('dp', 'rows'), may hold values from 0 to 2047
- prev_bag: int32 [4, 8, 512], P('dp', 'rows'), may hold values from 0 to 3, never falling along the last dimension, each value on 1 to 256 neighbouring positions
- grad_pooled: float32 [4, 8, 4, 256], P('dp', 'rows'), may hold values from -6 to 6
Outputs:
- pooled: float32 [4, 8, 4, 256], P('dp', 'rows')
- new_table: float32 [16384, 256], P('rows')
- new_accum: float32 [16384], P('rows')
The draws below stay inside these ranges and needn't reach their ends.
Inputs may be any that keep to these rules, and one draw needn't show every extreme that they name: `owner_map`: among the positions of one device no owner is named more than 192 times, a bound that some block reaches. `prev_owner`: among the positions of one device no owner is named more than 192 times, a bound that some block reaches. `bag_index`: never falls along a device's positions; every bag has 1 to 256 positions, one exactly 256. `prev_bag`: never falls along a device's positions; every bag has 1 to 256 positions, one exactly 256.
All inputs are finite; a program needn't handle non-finite values.
Results may differ from the reference program's by a relative error of at most 0.0003.
Values sent between devices are 32-bit elements; how exact they have to be, the bound alone decides.
No kernel may reach another device: no remote copies, remote signals or barrier semaphores. Data moves between devices by JAX's collectives and lax.ppermute only.
A program may use at most 64 MiB of HBM per device.

```python
import math
import jax
import jax.numpy as jnp
import numpy as np
from jax import lax

E = 256
ROWS_DEV = 2048
BAGS = 4
BAG_MEAN = 128
P_SIZE = 512
BAG_MAX = 256
GROUPS = 4
OWNERS = 8
SLAB = 16384
CAP = 192


def plant(values, rng, least, top_value):
    spot = [jax.random.randint(jax.random.fold_in(rng, axis), (), 0, length) for axis, length in enumerate(values.shape)]
    longest = values.shape.index(max(values.shape))
    beside = spot[:longest] + [(spot[longest] + 1) % values.shape[longest]] + spot[longest + 1:]
    return values.at[tuple(spot)].set(least).at[tuple(beside)].set(top_value)


def block_scale(key, extent, split, low, largest):
    factor_of, own = 1.0, jax.random.fold_in(key, 6)
    for position, shards_of in split:
        heights = jnp.exp(jax.random.uniform(jax.random.fold_in(own, position), (shards_of,), jnp.float32, low / len(split), largest / len(split)))
        factor_of = factor_of * jnp.repeat(heights, extent[position] // shards_of).reshape([-1 if axis == position else 1 for axis in range(len(extent))])
    return factor_of


def profile(amount, total, reach, lean):
    weights = [(1 << 20) // math.isqrt(grade ** lean) + 1 for grade in range(2, amount + 1)]
    surplus, given = total - reach - (amount - 1), [1] * (amount - 1)
    while surplus > 0:
        free = [i for i in range(amount - 1) if given[i] < reach]
        whole, remaining = sum([weights[i] for i in free]), surplus
        for i in free:
            extra = min(reach - given[i], max(1, remaining * weights[i] // whole), surplus)
            given[i] = given[i] + extra
            surplus = surplus - extra
    return np.array([reach] + given)


def uneven_parts(key, count, total, limit, slope):
    if count == 2:
        one = jax.random.randint(key, (), max(1, total - limit), min(limit, total - 1) + 1)
        return jnp.stack([one, total - one])
    sizes = jnp.asarray(profile(count, total, limit, slope), jnp.int32)
    couples = (count - 1) // 2
    donor, receiver = sizes[1:1 + 2 * couples:2], sizes[2:2 + 2 * couples:2]
    slack = jnp.minimum(donor - 1, limit - receiver)
    passed = jax.random.randint(jax.random.fold_in(key, 1), (couples,), 0, 1 << 20) % (slack + 1)
    sizes = sizes.at[1:1 + 2 * couples:2].set(donor - passed).at[2:2 + 2 * couples:2].set(receiver + passed)
    return sizes[jax.random.permutation(jax.random.fold_in(key, 2), count)]


def assign_block(own_key, own, number, rows, amount, top, reach, skew):
    order = jax.random.permutation(own_key, amount)
    packed, ordinary = load_shares(amount, rows * top, reach, skew, True), load_shares(amount, rows * top, reach, skew, False)
    places = jnp.arange(amount)

    def named(lengths, rotation):
        used = int((lengths > 0).sum())
        fixed = max(1, used // 4)
        passed = fixed + (places - fixed + rotation * (used - fixed)) % max(1, amount - fixed)
        return jnp.zeros((amount,), jnp.int32).at[order[jnp.where(places < fixed, places, passed)]].set(jnp.asarray(lengths, jnp.int32))

    lengths = jnp.where(number % 4 == 0, named(packed, number // 4), named(ordinary, number - number // 4 - 1))
    mixed = jax.random.permutation(jax.random.fold_in(own, 3), amount)
    giver, taker = mixed[0:amount // 2 * 2:2], mixed[1:amount // 2 * 2:2]
    slack = jnp.minimum(lengths[giver] - 1, reach - lengths[taker]) // 2
    slack = jnp.where((giver == order[0]) | (taker == order[0]) | (lengths[taker] == 0), 0, jnp.maximum(slack, 0))
    passed = jax.random.randint(jax.random.fold_in(own, 4), (amount // 2,), 0, 1 << 20) % (slack + 1)
    lengths = lengths.at[giver].add(-passed).at[taker].add(passed)
    members = jnp.searchsorted(jnp.cumsum(lengths), jnp.arange(rows * top), side="right").astype(jnp.int32)
    listing = members.reshape(top, rows).T
    listing = listing[jax.random.permutation(jax.random.fold_in(own, 1), rows)]
    rotation = jax.random.randint(jax.random.fold_in(own, 2), (rows, 1), 0, top)
    return jnp.take_along_axis(listing, (jnp.arange(top)[None, :] + rotation) % top, axis=1)


def load_shares(amount, total, bound, lean, full):
    weights = [(1 << 20) // math.isqrt(grade ** lean) + 1 for grade in range(1, amount + 1)]
    largest = bound if full else min(bound, max(-(-total // amount), total * weights[0] // sum(weights)))
    least = 1 if total - largest >= amount - 1 else 0
    counts, surplus = [largest] + [least] * (amount - 1), total - largest - least * (amount - 1)
    while surplus > 0:
        candidates = [i for i in range(1, amount) if counts[i] < largest] or [i for i in range(1, amount) if counts[i] < bound]
        mass, left = sum([weights[i] for i in candidates]), surplus
        for i in candidates:
            addition = min(bound - counts[i], max(1, left * weights[i] // mass), surplus)
            counts[i] = counts[i] + addition
            surplus = surplus - addition
    return np.array(counts)


def scatter_about(own_key, shape, width, limit, shards=(), dtype=jnp.bfloat16):
    entries = jax.random.normal(own_key, shape, jnp.float32) * width
    if len(shards) > 0:
        entries = block_scale(own_key, shape, shards, -0.22, 0.18) * entries
    return jnp.clip(entries, min=-limit, max=limit).astype(dtype)


def setup_inputs(seed: int = 0) -> dict:
    splits = jax.random.split(jax.random.key(seed), 10)
    item_table = scatter_about(splits[0], (SLAB, E), BAG_MEAN ** -0.5, 0.5, ((0, 8),), jnp.float32)
    row_accum = jnp.clip(jnp.exp(math.log(10.0) - 4.6051702 * jax.random.uniform(splits[1], (SLAB,), jnp.float32) ** block_scale(splits[1], (SLAB,), ((0, 8),), -0.2, 0.2)), 0.1, 10.0)
    owner_map_keys = jax.random.split(jax.random.fold_in(splits[2], 1), GROUPS * OWNERS * P_SIZE // P_SIZE)
    owner_map_turns = jax.random.permutation(jax.random.fold_in(splits[2], 3), GROUPS * OWNERS * P_SIZE // P_SIZE)
    owner_map = jax.vmap(lambda own, number: assign_block(jax.random.fold_in(splits[2], 2), own, number, P_SIZE, OWNERS, 1, CAP, 2))(owner_map_keys, owner_map_turns).reshape((GROUPS, OWNERS, P_SIZE, 1))
    row_index = plant(jax.random.randint(splits[3], (GROUPS, OWNERS, P_SIZE), 0, ROWS_DEV), jax.random.fold_in(splits[3], 1), 0, ROWS_DEV - 1).astype(jnp.int32)
    bag_index = jax.vmap(lambda own: jnp.searchsorted(jnp.cumsum(uneven_parts(own, BAGS, P_SIZE, BAG_MAX, 2)), jnp.arange(P_SIZE), side="right"))(jax.random.split(splits[4], GROUPS * OWNERS)).reshape((GROUPS, OWNERS, P_SIZE)).astype(jnp.int32)
    prev_owner_keys = jax.random.split(jax.random.fold_in(splits[5], 1), GROUPS * OWNERS * P_SIZE // P_SIZE)
    prev_owner_turns = jax.random.permutation(jax.random.fold_in(splits[5], 3), GROUPS * OWNERS * P_SIZE // P_SIZE)
    prev_owner = jax.vmap(lambda own, number: assign_block(jax.random.fold_in(splits[5], 2), own, number, P_SIZE, OWNERS, 1, CAP, 2))(prev_owner_keys, prev_owner_turns).reshape((GROUPS, OWNERS, P_SIZE, 1))
    prev_row = plant(jax.random.randint(splits[6], (GROUPS, OWNERS, P_SIZE), 0, ROWS_DEV), jax.random.fold_in(splits[6], 1), 0, ROWS_DEV - 1).astype(jnp.int32)
    prev_bag = jax.vmap(lambda own: jnp.searchsorted(jnp.cumsum(uneven_parts(own, BAGS, P_SIZE, BAG_MAX, 2)), jnp.arange(P_SIZE), side="right"))(jax.random.split(splits[7], GROUPS * OWNERS)).reshape((GROUPS, OWNERS, P_SIZE)).astype(jnp.int32)
    grad_pooled = scatter_about(splits[8], (GROUPS, OWNERS, BAGS, E), 1.0, 6.0, ((0, 4), (1, 8)), jnp.float32)
    return {"item_table": item_table, "row_accum": row_accum, "owner_map": owner_map, "row_index": row_index, "bag_index": bag_index, "prev_owner": prev_owner, "prev_row": prev_row, "prev_bag": prev_bag, "grad_pooled": grad_pooled}


learn_rate = 0.1

def reference(item_table, row_accum, owner_map, row_index, bag_index, prev_owner, prev_row, prev_bag, grad_pooled):
    owner_range = jnp.arange(OWNERS).astype(jnp.int32)

    def pool_group(operands):
        owners_now, rows_now, bags_now = operands
        slab_index = (owners_now[..., 0] * ROWS_DEV + rows_now).astype(jnp.int32)
        looked = item_table[slab_index.reshape(-1)]
        segment = (bags_now + BAGS * owner_range[:, None]).astype(jnp.int32).reshape(-1)
        summed = jax.ops.segment_sum(looked, segment, num_segments=OWNERS * BAGS)
        return summed.reshape(OWNERS, BAGS, E)
    pooled = lax.map(pool_group, (owner_map, row_index, bag_index))

    def add_group(running, operands):
        owners_old, rows_old, bags_old, grad_group = operands
        slab_index = (owners_old[..., 0] * ROWS_DEV + rows_old).astype(jnp.int32).reshape(-1)
        grad_each = grad_group[owner_range[:, None], bags_old].reshape(-1, E)
        return (running + jax.ops.segment_sum(grad_each, slab_index, num_segments=SLAB), None)
    grad_rows, _ = lax.scan(add_group, jnp.zeros((SLAB, E), jnp.float32), (prev_owner, prev_row, prev_bag, grad_pooled))
    new_accum = row_accum + lax.optimization_barrier(jnp.mean(grad_rows * grad_rows, axis=1))
    new_table = item_table - learn_rate * grad_rows / jnp.sqrt(new_accum)[:, None]
    return (pooled, new_table, new_accum)
```

```python
import functools

import jax
import jax.numpy as jnp
from jax import lax
from jax.experimental import pallas as pl
from jax.experimental.pallas import tpu as pltpu
from jax.sharding import PartitionSpec as P

learn_rate = 0.1
LANES = 128
PREV_BOUNDS = 64


def bound_block(bags, bag_count, first):
    lane = lax.broadcasted_iota(jnp.int32, (1, LANES), 1)
    block = jnp.zeros((1, LANES), jnp.float32)
    for j in range(1, bag_count):
        start = jnp.sum((bags < j).astype(jnp.float32), axis=1, keepdims=True)
        block = jnp.where(lane == first + j - 1, start, block)
    return block


def pack_kernel(rows_dev, owner, row, bag, prev_owner, prev_row, prev_bag, grad, out):
    copies = out.shape[0]
    positions = row.shape[1]
    bag_count, width = grad.shape

    def put(start, value):
        shape = (copies, 1, value.shape[1])
        out[:, :, start:start + value.shape[1]] = jnp.broadcast_to(value[None], shape)

    put(0, (owner[...] * rows_dev + row[...]).astype(jnp.float32))
    put(positions, (prev_owner[...] * rows_dev + prev_row[...]).astype(jnp.float32))
    put(
        2 * positions,
        bound_block(bag[...], bag_count, 0)
        + bound_block(prev_bag[...], bag_count, PREV_BOUNDS),
    )
    for j in range(bag_count):
        put(2 * positions + LANES + j * width, grad[j:j + 1, :])


def split_two(x):
    high = x.astype(jnp.bfloat16)
    return high, (x - high.astype(jnp.float32)).astype(jnp.bfloat16)


def codes(ids, bounds, first, bag_count, base):
    rel = ids.astype(jnp.int32) - base
    place = lax.broadcasted_iota(jnp.int32, ids.shape, 1).astype(jnp.float32)
    bag = jnp.zeros(ids.shape, jnp.int32)
    for j in range(1, bag_count):
        start = bounds[:, first + j - 1:first + j]
        bag = bag + (place >= start).astype(jnp.int32)
    code = lax.shift_right_arithmetic(rel, 7) * bag_count + bag
    return code.astype(jnp.float32), (rel & (LANES - 1)).astype(jnp.float32)


def count_into(counts, code_ref, lane_ref, devices, bag_count):
    blocks = counts.shape[0]
    positions = code_ref.shape[1]
    code_range = lax.broadcasted_iota(
        jnp.int32, (blocks * bag_count, positions), 0).astype(jnp.bfloat16)
    lane_range = lax.broadcasted_iota(
        jnp.int32, (LANES, positions), 0).astype(jnp.bfloat16)
    for d in range(devices):
        code = code_ref[d:d + 1, :].astype(jnp.bfloat16)
        lane = lane_ref[d:d + 1, :].astype(jnp.bfloat16)
        one, none = jnp.ones((), jnp.bfloat16), jnp.zeros((), jnp.bfloat16)
        left = jnp.where(code_range == code, one, none)
        right = jnp.where(lane_range == lane, one, none)
        hits = lax.dot_general(
            left, right, (((1,), (1,)), ((), ())), preferred_element_type=jnp.float32)
        counts[:, d * bag_count:(d + 1) * bag_count, :] = hits.reshape(
            blocks, bag_count, LANES)


def pool_kernel(bag_count, positions, msg, table, out, code_ref, lane_ref, counts):
    rows_dev = table.shape[0]
    devices = out.shape[0]
    group = lax.axis_index("dp") * devices
    base = lax.axis_index("rows") * rows_dev
    ids = msg[pl.ds(group, devices), 0, 0:positions]
    bounds = msg[pl.ds(group, devices), 0, 2 * positions:2 * positions + LANES]
    code_ref[...], lane_ref[...] = codes(ids, bounds, 0, bag_count, base)
    count_into(counts, code_ref, lane_ref, devices, bag_count)
    blocks = rows_dev // LANES
    total = jnp.zeros((devices * bag_count, table.shape[1]), jnp.float32)
    flat = jnp.concatenate(
        [counts[h].astype(jnp.bfloat16) for h in range(blocks)], axis=1)
    for part in split_two(table[...]):
        total += jnp.dot(flat, part, preferred_element_type=jnp.float32)
    out[...] = total.reshape(out.shape)


def update_kernel(
    bag_count, positions, chunk, msg, table, accum, new_table, new_accum,
    code_ref, lane_ref, counts, grads, sums,
):
    devices = msg.shape[0]
    step_rows, width = table.shape
    blocks = counts.shape[0]
    base = lax.axis_index("rows") * (blocks * LANES)
    step = pl.program_id(0)
    offset = 2 * positions + LANES

    def count_chunk(first):
        ids = msg[pl.ds(first, chunk), 0, positions:2 * positions]
        bounds = msg[pl.ds(first, chunk), 0, 2 * positions:2 * positions + LANES]
        code_ref[...], lane_ref[...] = codes(ids, bounds, PREV_BOUNDS, bag_count, base)
        count_into(counts, code_ref, lane_ref, chunk, bag_count)
        for d in range(chunk):
            for j in range(bag_count):
                grads[d * bag_count + j:d * bag_count + j + 1, :] = msg[
                    first + d, :, offset + j * width:offset + (j + 1) * width]

    def block_sum(h, parts):
        hits = counts[h].astype(jnp.bfloat16)
        total = jnp.zeros((LANES, width), jnp.float32)
        for part in parts:
            total += lax.dot_general(
                hits, part, (((0,), (0,)), ((), ())), preferred_element_type=jnp.float32)
        return total

    single = devices == chunk

    @pl.when(step == 0)
    def _():
        if single:
            count_chunk(0)
            return
        sums[...] = jnp.zeros_like(sums)

        @pl.loop(0, devices // chunk)
        def _(c):
            count_chunk(c * chunk)
            parts = split_two(grads[...])

            @pl.loop(0, blocks)
            def _(h):
                sums[h] += block_sum(h, parts)

    diagonal = (
        lax.broadcasted_iota(jnp.int32, (LANES, LANES), 0)
        == lax.broadcasted_iota(jnp.int32, (LANES, LANES), 1))
    if single:
        parts = split_two(grads[...])
    per_step = step_rows // LANES
    for i in range(per_step):
        h = step * per_step + i
        grad = block_sum(h, parts) if single else sums[h]
        here = slice(i * LANES, (i + 1) * LANES)
        squares = grad * grad
        folded = squares[:, 0:LANES]
        for k in range(1, width // LANES):
            folded += squares[:, k * LANES:(k + 1) * LANES]
        old = jnp.where(diagonal, accum[pl.ds(h, 1), :], 0.0)
        fresh = jnp.sum(folded * (1.0 / width) + old, axis=1, keepdims=True)
        new_table[here, :] = table[here, :] - grad * (learn_rate * lax.rsqrt(fresh))
        new_accum[pl.ds(h, 1), :] = jnp.sum(
            jnp.where(diagonal, fresh, 0.0), axis=0, keepdims=True)


def local(
    item_table, row_accum, owner_map, row_index, bag_index,
    prev_owner, prev_row, prev_bag, grad_pooled,
):
    owners = lax.axis_size("rows")
    devices = owners * lax.axis_size("dp")
    rows_dev, width = item_table.shape
    bag_count = grad_pooled.shape[2]
    positions = row_index.shape[2]
    blocks = rows_dev // LANES
    length = 2 * positions + LANES + bag_count * width
    vmem = pl.BlockSpec(memory_space=pltpu.VMEM)
    params = pltpu.CompilerParams(vmem_limit_bytes=48 * 1024 * 1024)

    def line(x):
        return x.reshape(1, positions)

    message = pl.pallas_call(
        functools.partial(pack_kernel, rows_dev),
        out_shape=jax.ShapeDtypeStruct((devices, 1, length), jnp.float32),
        in_specs=[vmem] * 7,
        out_specs=vmem,
        compiler_params=params,
        name="pack",
    )(
        line(owner_map), line(row_index), line(bag_index),
        line(prev_owner), line(prev_row), line(prev_bag), grad_pooled[0, 0],
    )
    gathered = lax.all_to_all(
        message, ("dp", "rows"), split_axis=0, concat_axis=0, tiled=True)

    partial_pooled = pl.pallas_call(
        functools.partial(pool_kernel, bag_count, positions),
        out_shape=jax.ShapeDtypeStruct((owners, bag_count, width), jnp.float32),
        in_specs=[vmem] * 2,
        out_specs=vmem,
        scratch_shapes=[
            pltpu.VMEM((owners, positions), jnp.float32),
            pltpu.VMEM((owners, positions), jnp.float32),
            pltpu.VMEM((blocks, owners * bag_count, LANES), jnp.float32),
        ],
        compiler_params=params,
        cost_estimate=pl.CostEstimate(
            flops=4 * owners * bag_count * rows_dev * width,
            bytes_accessed=rows_dev * width * 4, transcendentals=0),
        name="pool",
    )(gathered, item_table)
    returned = lax.all_to_all(
        partial_pooled, "rows", split_axis=0, concat_axis=0, tiled=True)

    chunk = min(devices, LANES // bag_count)
    steps = 4
    step_rows = rows_dev // steps
    segments = chunk * bag_count
    whole = lambda i: (0, 0)
    new_table, new_accum = pl.pallas_call(
        functools.partial(update_kernel, bag_count, positions, chunk),
        grid=(steps,),
        out_shape=(
            jax.ShapeDtypeStruct((rows_dev, width), jnp.float32),
            jax.ShapeDtypeStruct((blocks, LANES), jnp.float32),
        ),
        in_specs=[
            vmem,
            pl.BlockSpec((step_rows, width), lambda i: (i, 0)),
            pl.BlockSpec((blocks, LANES), whole),
        ],
        out_specs=(
            pl.BlockSpec((step_rows, width), lambda i: (i, 0)),
            pl.BlockSpec((blocks, LANES), whole),
        ),
        scratch_shapes=[
            pltpu.VMEM((chunk, positions), jnp.float32),
            pltpu.VMEM((chunk, positions), jnp.float32),
            pltpu.VMEM((blocks, segments, LANES), jnp.float32),
            pltpu.VMEM((segments, width), jnp.float32),
            pltpu.VMEM((blocks, LANES, width) if devices > chunk else (1, 8, LANES), jnp.float32),
        ],
        compiler_params=params,
        cost_estimate=pl.CostEstimate(
            flops=8 * devices * bag_count * rows_dev * width,
            bytes_accessed=3 * rows_dev * width * 4, transcendentals=0),
        name="update",
    )(gathered, item_table, row_accum.reshape(blocks, LANES))

    pooled = jnp.sum(returned, axis=0)
    return (pooled[None, None], new_table, new_accum.reshape(rows_dev))


def solution(mesh):
    placed = (
        P("rows", None),
        P("rows"),
        P("dp", "rows", None, None),
        P("dp", "rows", None),
        P("dp", "rows", None),
        P("dp", "rows", None, None),
        P("dp", "rows", None),
        P("dp", "rows", None),
        P("dp", "rows", None, None),
    )
    return jax.shard_map(
        local,
        mesh=mesh,
        in_specs=placed,
        out_specs=(P("dp", "rows", None, None), P("rows", None), P("rows")),
        check_vma=False,
    )
```

```python
import functools

import jax
import jax.numpy as jnp
from jax import lax
from jax.experimental import pallas as pl
from jax.experimental.pallas import tpu as pltpu
from jax.sharding import PartitionSpec as P

learn_rate = 0.1
LANES = 128


def bound_block(bags, bag_count):
    lane = lax.broadcasted_iota(jnp.int32, (1, LANES), 1)
    block = jnp.zeros((1, LANES), jnp.float32)
    for j in range(1, bag_count):
        start = jnp.sum((bags < j).astype(jnp.float32), axis=1, keepdims=True)
        block = jnp.where(lane == j - 1, start, block)
    return block


def pack_kernel(rows_dev, *refs):
    sources, out, held, sems = refs[:7], refs[7], refs[8:15], refs[15]
    copies = [
        pltpu.make_async_copy(source, place, sems.at[i])
        for i, (source, place) in enumerate(zip(sources, held))
    ]
    for copy in copies:
        copy.start()
    for copy in copies:
        copy.wait()
    owner, row, bag, prev_owner, prev_row, prev_bag, grad = held
    positions = row.shape[1]
    bag_count, width = grad.shape

    def put(start, value):
        out[:, start:start + value.shape[1]] = value

    put(0, (owner[...] * rows_dev + row[...]).astype(jnp.float32))
    put(positions, bound_block(bag[...], bag_count))
    start = positions + LANES
    put(start, (prev_owner[...] * rows_dev + prev_row[...]).astype(jnp.float32))
    put(start + positions, bound_block(prev_bag[...], bag_count))
    start = start + positions + LANES
    for j in range(bag_count):
        put(start + j * width, grad[j:j + 1, :])


def split_two(x):
    high = x.astype(jnp.bfloat16)
    return high, (x - high.astype(jnp.float32)).astype(jnp.bfloat16)


def codes(ids, bounds, bag_count, base):
    rel = ids.astype(jnp.int32) - base
    place = lax.broadcasted_iota(jnp.int32, ids.shape, 1).astype(jnp.float32)
    bag = jnp.zeros(ids.shape, jnp.int32)
    for j in range(1, bag_count):
        start = bounds[:, j - 1:j]
        bag = bag + (place >= start).astype(jnp.int32)
    code = lax.shift_right_arithmetic(rel, 7) * bag_count + bag
    return code.astype(jnp.float32), (rel & (LANES - 1)).astype(jnp.float32)


def count_into(counts, code_ref, lane_ref, devices, bag_count):
    blocks = counts.shape[0]
    positions = code_ref.shape[1]
    code_range = lax.broadcasted_iota(
        jnp.int32, (blocks * bag_count, positions), 0).astype(jnp.bfloat16)
    lane_range = lax.broadcasted_iota(
        jnp.int32, (LANES, positions), 0).astype(jnp.bfloat16)
    for d in range(devices):
        code = code_ref[d:d + 1, :].astype(jnp.bfloat16)
        lane = lane_ref[d:d + 1, :].astype(jnp.bfloat16)
        one, none = jnp.ones((), jnp.bfloat16), jnp.zeros((), jnp.bfloat16)
        left = jnp.where(code_range == code, one, none)
        right = jnp.where(lane_range == lane, one, none)
        hits = lax.dot_general(
            left, right, (((1,), (1,)), ((), ())), preferred_element_type=jnp.float32)
        counts[:, d * bag_count:(d + 1) * bag_count, :] = hits.reshape(
            blocks, bag_count, LANES)


def join_kernel(start, *refs):
    sources, out = refs[:-1], refs[-1]
    for i, source in enumerate(sources):
        out[i] = source[:, start:]


def pool_kernel(bag_count, positions, owners, *refs):
    sources, table = refs[:owners], refs[owners]
    outs = refs[owners + 1:2 * owners + 1]
    ids_ref, bounds_ref, code_ref, lane_ref, counts, held, sem = refs[2 * owners + 1:]
    copy = pltpu.make_async_copy(table, held, sem)
    copy.start()
    rows_dev, width = table.shape
    base = lax.axis_index("rows") * rows_dev
    for i, source in enumerate(sources):
        ids_ref[i:i + 1, :] = source[:, 0:positions]
        bounds_ref[i:i + 1, :] = source[:, positions:positions + LANES]
    code_ref[...], lane_ref[...] = codes(ids_ref[...], bounds_ref[...], bag_count, base)
    count_into(counts, code_ref, lane_ref, owners, bag_count)
    blocks = rows_dev // LANES
    flat = jnp.concatenate(
        [counts[h].astype(jnp.bfloat16) for h in range(blocks)], axis=1)
    copy.wait()
    total = jnp.zeros((owners * bag_count, width), jnp.float32)
    for part in split_two(held[...]):
        total += jnp.dot(flat, part, preferred_element_type=jnp.float32)
    for i, out in enumerate(outs):
        out[...] = total[i * bag_count:(i + 1) * bag_count, :]


def update_kernel(bag_count, positions, groups, chunk, *refs):
    sources, (table, accum, new_table, new_accum) = refs[:groups], refs[groups:groups + 4]
    msg, code_ref, lane_ref, counts, grads, sums = refs[groups + 4:]
    devices = msg.shape[0]
    owners = devices // groups
    step_rows, width = table.shape
    blocks = counts.shape[0]
    base = lax.axis_index("rows") * (blocks * LANES)
    step = pl.program_id(0)
    offset = positions + LANES

    def count_chunk(first):
        ids = msg[pl.ds(first, chunk), 0, 0:positions]
        bounds = msg[pl.ds(first, chunk), 0, positions:positions + LANES]
        code_ref[...], lane_ref[...] = codes(ids, bounds, bag_count, base)
        count_into(counts, code_ref, lane_ref, chunk, bag_count)
        for d in range(chunk):
            for j in range(bag_count):
                grads[d * bag_count + j:d * bag_count + j + 1, :] = msg[
                    first + d, :, offset + j * width:offset + (j + 1) * width]

    def block_sum(h, parts):
        hits = counts[h].astype(jnp.bfloat16)
        total = jnp.zeros((LANES, width), jnp.float32)
        for part in parts:
            total += lax.dot_general(
                hits, part, (((0,), (0,)), ((), ())), preferred_element_type=jnp.float32)
        return total

    single = devices == chunk

    @pl.when(step == 0)
    def _():
        for i, source in enumerate(sources):
            msg[i * owners:(i + 1) * owners] = source[...]
        if single:
            count_chunk(0)
            return
        sums[...] = jnp.zeros_like(sums)

        @pl.loop(0, devices // chunk)
        def _(c):
            count_chunk(c * chunk)
            parts = split_two(grads[...])

            @pl.loop(0, blocks)
            def _(h):
                sums[h] += block_sum(h, parts)

    diagonal = (
        lax.broadcasted_iota(jnp.int32, (LANES, LANES), 0)
        == lax.broadcasted_iota(jnp.int32, (LANES, LANES), 1))
    if single:
        parts = split_two(grads[...])
    per_step = step_rows // LANES
    for i in range(per_step):
        h = step * per_step + i
        grad = block_sum(h, parts) if single else sums[h]
        here = slice(i * LANES, (i + 1) * LANES)
        squares = grad * grad
        folded = squares[:, 0:LANES]
        for k in range(1, width // LANES):
            folded += squares[:, k * LANES:(k + 1) * LANES]
        old = jnp.where(diagonal, accum[pl.ds(h, 1), :], 0.0)
        fresh = jnp.sum(folded * (1.0 / width) + old, axis=1, keepdims=True)
        new_table[here, :] = table[here, :] - grad * (learn_rate * lax.rsqrt(fresh))
        new_accum[pl.ds(h, 1), :] = jnp.sum(
            jnp.where(diagonal, fresh, 0.0), axis=0, keepdims=True)


def shift(x, axis, step):
    size = lax.axis_size(axis)
    return lax.ppermute(x, axis, [(i, (i + step) % size) for i in range(size)])


def local(
    item_table, row_accum, owner_map, row_index, bag_index,
    prev_owner, prev_row, prev_bag, grad_pooled,
):
    owners, groups = lax.axis_size("rows"), lax.axis_size("dp")
    devices = owners * groups
    rows_dev, width = item_table.shape
    bag_count = grad_pooled.shape[2]
    positions = row_index.shape[2]
    blocks = rows_dev // LANES
    now_length = positions + LANES
    prev_length = now_length + bag_count * width
    vmem = pl.BlockSpec(memory_space=pltpu.VMEM)
    hbm = pl.BlockSpec(memory_space=pltpu.HBM)
    params = pltpu.CompilerParams(vmem_limit_bytes=48 * 1024 * 1024)
    greedy = pltpu.CompilerParams(vmem_limit_bytes=64 * 1024 * 1024)

    def line(x):
        return x.reshape(1, positions)

    message = pl.pallas_call(
        functools.partial(pack_kernel, rows_dev),
        out_shape=jax.ShapeDtypeStruct((1, now_length + prev_length), jnp.float32),
        in_specs=[hbm] * 7,
        out_specs=vmem,
        scratch_shapes=[pltpu.VMEM((1, positions), jnp.int32)] * 6
        + [pltpu.VMEM((bag_count, width), jnp.float32), pltpu.SemaphoreType.DMA((7,))],
        compiler_params=greedy,
        name="pack",
    )(
        line(owner_map), line(row_index), line(bag_index),
        line(prev_owner), line(prev_row), line(prev_bag), grad_pooled[0, 0],
    )
    messages = [message] + [shift(message, "rows", k) for k in range(1, owners)]

    joined = pl.pallas_call(
        functools.partial(join_kernel, now_length),
        out_shape=jax.ShapeDtypeStruct((owners, 1, prev_length), jnp.float32),
        in_specs=[vmem] * owners,
        out_specs=vmem,
        compiler_params=params,
        name="join",
    )(*messages)
    all_groups = [joined] + [shift(joined, "dp", k) for k in range(1, groups)]

    partials = pl.pallas_call(
        functools.partial(pool_kernel, bag_count, positions, owners),
        out_shape=[jax.ShapeDtypeStruct((bag_count, width), jnp.float32)] * owners,
        in_specs=[vmem] * owners + [hbm],
        out_specs=[vmem] * owners,
        scratch_shapes=[
            pltpu.VMEM((owners, positions), jnp.float32),
            pltpu.VMEM((owners, LANES), jnp.float32),
            pltpu.VMEM((owners, positions), jnp.float32),
            pltpu.VMEM((owners, positions), jnp.float32),
            pltpu.VMEM((blocks, owners * bag_count, LANES), jnp.float32),
            pltpu.VMEM((rows_dev, width), jnp.float32),
            pltpu.SemaphoreType.DMA,
        ],
        compiler_params=params,
        cost_estimate=pl.CostEstimate(
            flops=4 * owners * bag_count * rows_dev * width,
            bytes_accessed=rows_dev * width * 4, transcendentals=0),
        name="pool",
    )(*messages, item_table)
    answers = [partials[0]] + [
        shift(partials[k], "rows", owners - k) for k in range(1, owners)]

    chunk = min(devices, LANES // bag_count)
    steps = 4
    step_rows = rows_dev // steps
    segments = chunk * bag_count
    whole = lambda i: (0, 0)
    new_table, new_accum = pl.pallas_call(
        functools.partial(update_kernel, bag_count, positions, groups, chunk),
        grid=(steps,),
        out_shape=(
            jax.ShapeDtypeStruct((rows_dev, width), jnp.float32),
            jax.ShapeDtypeStruct((blocks, LANES), jnp.float32),
        ),
        in_specs=[vmem] * groups + [
            pl.BlockSpec((step_rows, width), lambda i: (i, 0)),
            pl.BlockSpec((blocks, LANES), whole),
        ],
        out_specs=(
            pl.BlockSpec((step_rows, width), lambda i: (i, 0)),
            pl.BlockSpec((blocks, LANES), whole),
        ),
        scratch_shapes=[
            pltpu.VMEM((devices, 1, prev_length), jnp.float32),
            pltpu.VMEM((chunk, positions), jnp.float32),
            pltpu.VMEM((chunk, positions), jnp.float32),
            pltpu.VMEM((blocks, segments, LANES), jnp.float32),
            pltpu.VMEM((segments, width), jnp.float32),
            pltpu.VMEM((blocks, LANES, width) if devices > chunk else (1, 8, LANES), jnp.float32),
        ],
        compiler_params=params,
        cost_estimate=pl.CostEstimate(
            flops=8 * devices * bag_count * rows_dev * width,
            bytes_accessed=3 * rows_dev * width * 4, transcendentals=0),
        name="update",
    )(*all_groups, item_table, row_accum.reshape(blocks, LANES))

    pooled = functools.reduce(lambda x, y: x + y, answers)
    return (pooled[None, None], new_table, new_accum.reshape(rows_dev))


def solution(mesh):
    placed = (
        P("rows", None),
        P("rows"),
        P("dp", "rows", None, None),
        P("dp", "rows", None),
        P("dp", "rows", None),
        P("dp", "rows", None, None),
        P("dp", "rows", None),
        P("dp", "rows", None),
        P("dp", "rows", None, None),
    )
    return jax.shard_map(
        local,
        mesh=mesh,
        in_specs=placed,
        out_specs=(P("dp", "rows", None, None), P("rows", None), P("rows")),
        check_vma=False,
    )
```

```python
import functools

import jax
import jax.numpy as jnp
from jax import lax
from jax.experimental import pallas as pl
from jax.experimental.pallas import tpu as pltpu
from jax.sharding import PartitionSpec as P

learn_rate = 0.1
LANES = 128


def bound_block(bags, bag_count):
    lane = lax.broadcasted_iota(jnp.int32, (1, LANES), 1)
    block = jnp.zeros((1, LANES), jnp.float32)
    for j in range(1, bag_count):
        start = jnp.sum((bags < j).astype(jnp.float32), axis=1, keepdims=True)
        block = jnp.where(lane == j - 1, start, block)
    return block


def pack_kernel(rows_dev, *refs):
    sources, out, held, sems = refs[:7], refs[7], refs[8:15], refs[15]
    copies = [
        pltpu.make_async_copy(source, place, sems.at[i])
        for i, (source, place) in enumerate(zip(sources, held))
    ]
    for copy in copies:
        copy.start()
    for copy in copies:
        copy.wait()
    owner, row, bag, prev_owner, prev_row, prev_bag, grad = held
    positions = row.shape[1]
    bag_count, width = grad.shape

    def put(start, value):
        shape = (out.shape[0], 1, value.shape[1])
        out[:, :, start:start + value.shape[1]] = jnp.broadcast_to(value[None], shape)

    put(0, (owner[...] * rows_dev + row[...]).astype(jnp.float32))
    put(positions, bound_block(bag[...], bag_count))
    start = positions + LANES
    put(start, (prev_owner[...] * rows_dev + prev_row[...]).astype(jnp.float32))
    put(start + positions, bound_block(prev_bag[...], bag_count))
    start = start + positions + LANES
    for j in range(bag_count):
        put(start + j * width, grad[j:j + 1, :])


def split_two(x):
    high = x.astype(jnp.bfloat16)
    return high, (x - high.astype(jnp.float32)).astype(jnp.bfloat16)


def codes(ids, bounds, bag_count, base):
    rel = ids.astype(jnp.int32) - base
    place = lax.broadcasted_iota(jnp.int32, ids.shape, 1).astype(jnp.float32)
    bag = jnp.zeros(ids.shape, jnp.int32)
    for j in range(1, bag_count):
        start = bounds[:, j - 1:j]
        bag = bag + (place >= start).astype(jnp.int32)
    code = lax.shift_right_arithmetic(rel, 7) * bag_count + bag
    return code.astype(jnp.float32), (rel & (LANES - 1)).astype(jnp.float32)


def count_into(counts, code_ref, lane_ref, devices, bag_count):
    blocks = counts.shape[0]
    positions = code_ref.shape[1]
    code_range = lax.broadcasted_iota(
        jnp.int32, (blocks * bag_count, positions), 0).astype(jnp.bfloat16)
    lane_range = lax.broadcasted_iota(
        jnp.int32, (LANES, positions), 0).astype(jnp.bfloat16)
    for d in range(devices):
        code = code_ref[d:d + 1, :].astype(jnp.bfloat16)
        lane = lane_ref[d:d + 1, :].astype(jnp.bfloat16)
        one, none = jnp.ones((), jnp.bfloat16), jnp.zeros((), jnp.bfloat16)
        left = jnp.where(code_range == code, one, none)
        right = jnp.where(lane_range == lane, one, none)
        hits = lax.dot_general(
            left, right, (((1,), (1,)), ((), ())), preferred_element_type=jnp.float32)
        counts[:, d * bag_count:(d + 1) * bag_count, :] = hits.reshape(
            blocks, bag_count, LANES)


def prepare_kernel(table, high, low):
    rows = table.shape[0]
    here = pl.ds(pl.multiple_of(pl.program_id(0) * rows, rows), rows)
    high[here, :], low[here, :] = split_two(table[...])


def pool_kernel(
    bag_count, positions, msg, high, low, out, joined, code_ref, lane_ref, counts,
):
    rows_dev, width = high.shape
    owners = msg.shape[0]
    base = lax.axis_index("rows") * rows_dev
    ids = msg[:, 0, 0:positions]
    bounds = msg[:, 0, positions:positions + LANES]
    code_ref[...], lane_ref[...] = codes(ids, bounds, bag_count, base)
    count_into(counts, code_ref, lane_ref, owners, bag_count)
    blocks = rows_dev // LANES
    flat = jnp.concatenate(
        [counts[h].astype(jnp.bfloat16) for h in range(blocks)], axis=1)
    total = jnp.zeros((owners * bag_count, width), jnp.float32)
    for part in (high, low):
        total += jnp.dot(flat, part[...], preferred_element_type=jnp.float32)
    out[...] = total.reshape(out.shape)
    joined[...] = msg[:, :, positions + LANES:]


def update_kernel(bag_count, positions, groups, chunk, *refs):
    sources, (table, accum, new_table, new_accum) = refs[:groups], refs[groups:groups + 4]
    msg, code_ref, lane_ref, counts, grads, sums = refs[groups + 4:]
    devices = msg.shape[0]
    owners = devices // groups
    step_rows, width = table.shape
    blocks = counts.shape[0]
    base = lax.axis_index("rows") * (blocks * LANES)
    step = pl.program_id(0)
    offset = positions + LANES

    def count_chunk(first):
        ids = msg[pl.ds(first, chunk), 0, 0:positions]
        bounds = msg[pl.ds(first, chunk), 0, positions:positions + LANES]
        code_ref[...], lane_ref[...] = codes(ids, bounds, bag_count, base)
        count_into(counts, code_ref, lane_ref, chunk, bag_count)
        for d in range(chunk):
            for j in range(bag_count):
                grads[d * bag_count + j:d * bag_count + j + 1, :] = msg[
                    first + d, :, offset + j * width:offset + (j + 1) * width]

    def block_sum(h, parts):
        hits = counts[h].astype(jnp.bfloat16)
        total = jnp.zeros((LANES, width), jnp.float32)
        for part in parts:
            total += lax.dot_general(
                hits, part, (((0,), (0,)), ((), ())), preferred_element_type=jnp.float32)
        return total

    single = devices == chunk

    @pl.when(step == 0)
    def _():
        for i, source in enumerate(sources):
            msg[i * owners:(i + 1) * owners] = source[...]
        if single:
            count_chunk(0)
            return
        sums[...] = jnp.zeros_like(sums)

        @pl.loop(0, devices // chunk)
        def _(c):
            count_chunk(c * chunk)
            parts = split_two(grads[...])

            @pl.loop(0, blocks)
            def _(h):
                sums[h] += block_sum(h, parts)

    diagonal = (
        lax.broadcasted_iota(jnp.int32, (LANES, LANES), 0)
        == lax.broadcasted_iota(jnp.int32, (LANES, LANES), 1))
    if single:
        parts = split_two(grads[...])
    per_step = step_rows // LANES
    for i in range(per_step):
        h = step * per_step + i
        grad = block_sum(h, parts) if single else sums[h]
        here = slice(i * LANES, (i + 1) * LANES)
        squares = grad * grad
        folded = squares[:, 0:LANES]
        for k in range(1, width // LANES):
            folded += squares[:, k * LANES:(k + 1) * LANES]
        old = jnp.where(diagonal, accum[pl.ds(h, 1), :], 0.0)
        fresh = jnp.sum(folded * (1.0 / width) + old, axis=1, keepdims=True)
        new_table[here, :] = table[here, :] - grad * (learn_rate * lax.rsqrt(fresh))
        new_accum[pl.ds(h, 1), :] = jnp.sum(
            jnp.where(diagonal, fresh, 0.0), axis=0, keepdims=True)


def shift(x, axis, step):
    size = lax.axis_size(axis)
    return lax.ppermute(x, axis, [(i, (i + step) % size) for i in range(size)])


def local(
    item_table, row_accum, owner_map, row_index, bag_index,
    prev_owner, prev_row, prev_bag, grad_pooled,
):
    owners, groups = lax.axis_size("rows"), lax.axis_size("dp")
    devices = owners * groups
    rows_dev, width = item_table.shape
    bag_count = grad_pooled.shape[2]
    positions = row_index.shape[2]
    blocks = rows_dev // LANES
    now_length = positions + LANES
    prev_length = now_length + bag_count * width
    vmem = pl.BlockSpec(memory_space=pltpu.VMEM)
    hbm = pl.BlockSpec(memory_space=pltpu.HBM)
    params = pltpu.CompilerParams(vmem_limit_bytes=48 * 1024 * 1024)

    def line(x):
        return x.reshape(1, positions)

    def stay(x):
        return pltpu.with_memory_space_constraint(x, pltpu.HBM)

    message = pl.pallas_call(
        functools.partial(pack_kernel, rows_dev),
        out_shape=jax.ShapeDtypeStruct((owners, 1, now_length + prev_length), jnp.float32),
        in_specs=[hbm] * 7,
        out_specs=vmem,
        scratch_shapes=[pltpu.VMEM((1, positions), jnp.int32)] * 6
        + [pltpu.VMEM((bag_count, width), jnp.float32), pltpu.SemaphoreType.DMA((7,))],
        compiler_params=params,
        name="pack",
    )(*[stay(x) for x in (
        line(owner_map), line(row_index), line(bag_index),
        line(prev_owner), line(prev_row), line(prev_bag), grad_pooled[0, 0],
    )])
    gathered = lax.all_to_all(message, "rows", split_axis=0, concat_axis=0, tiled=True)

    steps = 4
    step_rows = rows_dev // steps
    high, low = pl.pallas_call(
        prepare_kernel,
        grid=(steps,),
        out_shape=[jax.ShapeDtypeStruct((rows_dev, width), jnp.bfloat16)] * 2,
        in_specs=[pl.BlockSpec((step_rows, width), lambda i: (i, 0))],
        out_specs=[vmem] * 2,
        compiler_params=params,
        cost_estimate=pl.CostEstimate(
            flops=4 * rows_dev * width, bytes_accessed=2 * rows_dev * width * 4,
            transcendentals=0),
        name="prepare",
    )(stay(item_table))

    partial_pooled, joined = pl.pallas_call(
        functools.partial(pool_kernel, bag_count, positions),
        out_shape=(
            jax.ShapeDtypeStruct((owners, bag_count, width), jnp.float32),
            jax.ShapeDtypeStruct((owners, 1, prev_length), jnp.float32),
        ),
        in_specs=[vmem] * 3,
        out_specs=[vmem] * 2,
        scratch_shapes=[
            pltpu.VMEM((owners, positions), jnp.float32),
            pltpu.VMEM((owners, positions), jnp.float32),
            pltpu.VMEM((blocks, owners * bag_count, LANES), jnp.float32),
        ],
        compiler_params=params,
        cost_estimate=pl.CostEstimate(
            flops=4 * owners * bag_count * rows_dev * width,
            bytes_accessed=rows_dev * width * 4, transcendentals=0),
        name="pool",
    )(gathered, high, low)
    returned = lax.all_to_all(
        partial_pooled, "rows", split_axis=0, concat_axis=0, tiled=True)
    all_groups = [joined] + [shift(joined, "dp", k) for k in range(1, groups)]

    chunk = min(devices, LANES // bag_count)
    segments = chunk * bag_count
    whole = lambda i: (0, 0)
    new_table, new_accum = pl.pallas_call(
        functools.partial(update_kernel, bag_count, positions, groups, chunk),
        grid=(steps,),
        out_shape=(
            jax.ShapeDtypeStruct((rows_dev, width), jnp.float32),
            jax.ShapeDtypeStruct((blocks, LANES), jnp.float32),
        ),
        in_specs=[vmem] * groups + [
            pl.BlockSpec((step_rows, width), lambda i: (i, 0)),
            pl.BlockSpec((blocks, LANES), whole),
        ],
        out_specs=(
            pl.BlockSpec((step_rows, width), lambda i: (i, 0)),
            pl.BlockSpec((blocks, LANES), whole),
        ),
        scratch_shapes=[
            pltpu.VMEM((devices, 1, prev_length), jnp.float32),
            pltpu.VMEM((chunk, positions), jnp.float32),
            pltpu.VMEM((chunk, positions), jnp.float32),
            pltpu.VMEM((blocks, segments, LANES), jnp.float32),
            pltpu.VMEM((segments, width), jnp.float32),
            pltpu.VMEM((blocks, LANES, width) if devices > chunk else (1, 8, LANES), jnp.float32),
        ],
        compiler_params=params,
        cost_estimate=pl.CostEstimate(
            flops=8 * devices * bag_count * rows_dev * width,
            bytes_accessed=3 * rows_dev * width * 4, transcendentals=0),
        name="update",
    )(*all_groups, stay(item_table), row_accum.reshape(blocks, LANES))

    pooled = jnp.sum(returned, axis=0)
    return (pooled[None, None], new_table, new_accum.reshape(rows_dev))


def solution(mesh):
    placed = (
        P("rows", None),
        P("rows"),
        P("dp", "rows", None, None),
        P("dp", "rows", None),
        P("dp", "rows", None),
        P("dp", "rows", None, None),
        P("dp", "rows", None),
        P("dp", "rows", None),
        P("dp", "rows", None, None),
    )
    return jax.shard_map(
        local,
        mesh=mesh,
        in_specs=placed,
        out_specs=(P("dp", "rows", None, None), P("rows", None), P("rows")),
        check_vma=False,
    )
```

```python
import functools

import jax
import jax.numpy as jnp
from jax import lax
from jax.experimental import pallas as pl
from jax.experimental.pallas import tpu as pltpu
from jax.sharding import PartitionSpec as P

learn_rate = 0.1
LANES = 128


def pack_kernel(rows_dev, *refs):
    sources, out, held, sems = refs[:7], refs[7], refs[8:15], refs[15]
    copies = [
        pltpu.make_async_copy(source, place, sems.at[i])
        for i, (source, place) in enumerate(zip(sources, held))
    ]
    for copy in copies:
        copy.start()
    for copy in copies:
        copy.wait()
    owner, row, bag, prev_owner, prev_row, prev_bag, grad = held
    lines = row.shape[0]
    bag_count, width = grad.shape

    def put(start, value):
        shape = (out.shape[0],) + value.shape
        out[:, start:start + value.shape[0], :] = jnp.broadcast_to(value[None], shape)

    put(0, (owner[...] * rows_dev + row[...]).astype(jnp.float32))
    put(lines, bag[...].astype(jnp.float32))
    put(2 * lines, (prev_owner[...] * rows_dev + prev_row[...]).astype(jnp.float32))
    put(3 * lines, prev_bag[...].astype(jnp.float32))
    for k in range(width // LANES):
        put(4 * lines + k * bag_count, grad[:, k * LANES:(k + 1) * LANES])


def split_two(x):
    high = x.astype(jnp.bfloat16)
    return high, (x - high.astype(jnp.float32)).astype(jnp.bfloat16)


def prepare_kernel(table, high, low, kept):
    rows = table.shape[0]
    here = pl.ds(pl.multiple_of(pl.program_id(0) * rows, rows), rows)
    values = table[...]
    kept[here, :] = values
    high[here, :], low[here, :] = split_two(values)


def codes(ids, bags, bag_count, base):
    rel = ids.astype(jnp.int32) - base
    code = lax.shift_right_arithmetic(rel, 7) * bag_count + bags.astype(jnp.int32)
    return code.astype(jnp.float32), (rel & (LANES - 1)).astype(jnp.float32)


def count_into(counts, code_ref, lane_ref, devices, bag_count):
    blocks = counts.shape[0]
    lines = code_ref.shape[1]
    one, none = jnp.ones((), jnp.bfloat16), jnp.zeros((), jnp.bfloat16)

    def one_hot(ref, d, size):
        numbers = lax.broadcasted_iota(jnp.int32, (size, LANES), 0).astype(jnp.bfloat16)
        parts = []
        for k in range(lines):
            row = jnp.broadcast_to(ref[d, k:k + 1, :], (size, LANES)).astype(jnp.bfloat16)
            parts.append(jnp.where(numbers == row, one, none))
        return jnp.concatenate(parts, axis=1)

    for d in range(devices):
        hits = lax.dot_general(
            one_hot(code_ref, d, blocks * bag_count), one_hot(lane_ref, d, LANES),
            (((1,), (1,)), ((), ())), preferred_element_type=jnp.float32)
        counts[:, d * bag_count:(d + 1) * bag_count, :] = hits.reshape(
            blocks, bag_count, LANES)


def pool_kernel(bag_count, lines, msg, high, low, out, joined, code_ref, lane_ref, counts):
    rows_dev, width = high.shape
    owners = msg.shape[0]
    base = lax.axis_index("rows") * rows_dev
    code_ref[...], lane_ref[...] = codes(
        msg[:, 0:lines, :], msg[:, lines:2 * lines, :], bag_count, base)
    joined[...] = msg[:, 2 * lines:, :]
    count_into(counts, code_ref, lane_ref, owners, bag_count)
    blocks = rows_dev // LANES
    flat = jnp.concatenate(
        [counts[h].astype(jnp.bfloat16) for h in range(blocks)], axis=1)
    total = jnp.zeros((owners * bag_count, width), jnp.float32)
    for part in (high, low):
        total += jnp.dot(flat, part[...], preferred_element_type=jnp.float32)
    out[...] = total.reshape(out.shape)


def update_kernel(bag_count, lines, groups, chunk, *refs):
    sources, (table, accum, new_table, new_accum) = refs[:groups], refs[groups:groups + 4]
    msg, code_ref, lane_ref, counts, grads, sums, fresh_table, sems = refs[groups + 4:]
    rows_dev, width = table.shape
    devices = msg.shape[0]
    owners = devices // groups
    blocks = counts.shape[0]
    base = lax.axis_index("rows") * rows_dev
    single = devices == chunk

    def count_chunk(first):
        here = pl.ds(first, chunk)
        code_ref[...], lane_ref[...] = codes(
            msg[here, 0:lines, :], msg[here, lines:2 * lines, :], bag_count, base)
        count_into(counts, code_ref, lane_ref, chunk, bag_count)
        for k in range(width // LANES):
            start = 2 * lines + k * bag_count
            grads[:, k * LANES:(k + 1) * LANES] = msg[
                here, start:start + bag_count, :].reshape(chunk * bag_count, LANES)
        return split_two(grads[...])

    def block_sum(h, parts):
        hits = counts[h].astype(jnp.bfloat16)
        total = jnp.zeros((LANES, width), jnp.float32)
        for part in parts:
            total += lax.dot_general(
                hits, part, (((0,), (0,)), ((), ())), preferred_element_type=jnp.float32)
        return total

    for i, source in enumerate(sources):
        msg[i * owners:(i + 1) * owners] = source[...]
    if single:
        parts = count_chunk(0)
    else:
        sums[...] = jnp.zeros_like(sums)

        @pl.loop(0, devices // chunk)
        def _(c):
            parts = count_chunk(c * chunk)

            @pl.loop(0, blocks)
            def _(h):
                sums[h] += block_sum(h, parts)

    diagonal = (
        lax.broadcasted_iota(jnp.int32, (LANES, LANES), 0)
        == lax.broadcasted_iota(jnp.int32, (LANES, LANES), 1))
    pieces = sems.shape[0]
    per_piece = blocks // pieces
    copies = []
    for h in range(blocks):
        grad = block_sum(h, parts) if single else sums[h]
        here = slice(h * LANES, (h + 1) * LANES)
        squares = grad * grad
        folded = squares[:, 0:LANES]
        for k in range(1, width // LANES):
            folded += squares[:, k * LANES:(k + 1) * LANES]
        old = jnp.where(diagonal, accum[h:h + 1, :], 0.0)
        fresh = jnp.sum(folded * (1.0 / width) + old, axis=1, keepdims=True)
        fresh_table[here, :] = table[here, :] - grad * (learn_rate * lax.rsqrt(fresh))
        new_accum[h:h + 1, :] = jnp.sum(
            jnp.where(diagonal, fresh, 0.0), axis=0, keepdims=True)
        if (h + 1) % per_piece == 0:
            i = h // per_piece
            piece = pl.ds(i * per_piece * LANES, per_piece * LANES)
            copies.append(pltpu.make_async_copy(
                fresh_table.at[piece, :], new_table.at[piece, :], sems.at[i]))
            copies[-1].start()
    for copy in copies:
        copy.wait()


def shift(x, axis, step):
    size = lax.axis_size(axis)
    return lax.ppermute(x, axis, [(i, (i + step) % size) for i in range(size)])


def local(
    item_table, row_accum, owner_map, row_index, bag_index,
    prev_owner, prev_row, prev_bag, grad_pooled,
):
    owners, groups = lax.axis_size("rows"), lax.axis_size("dp")
    devices = owners * groups
    rows_dev, width = item_table.shape
    bag_count = grad_pooled.shape[2]
    lines = row_index.shape[2] // LANES
    blocks = rows_dev // LANES
    prev_length = 2 * lines + bag_count * width // LANES
    vmem = pl.BlockSpec(memory_space=pltpu.VMEM)
    hbm = pl.BlockSpec(memory_space=pltpu.HBM)
    params = pltpu.CompilerParams(vmem_limit_bytes=48 * 1024 * 1024)

    def stay(x):
        return pltpu.with_memory_space_constraint(x, pltpu.HBM)

    def line(x):
        return x.reshape(lines, LANES)

    message = pl.pallas_call(
        functools.partial(pack_kernel, rows_dev),
        out_shape=jax.ShapeDtypeStruct((owners, 2 * lines + prev_length, LANES), jnp.float32),
        in_specs=[hbm] * 7,
        out_specs=vmem,
        scratch_shapes=[pltpu.VMEM((lines, LANES), jnp.int32)] * 6
        + [pltpu.VMEM((bag_count, width), jnp.float32), pltpu.SemaphoreType.DMA((7,))],
        compiler_params=params,
        name="pack",
    )(*[stay(x) for x in (
        line(owner_map), line(row_index), line(bag_index),
        line(prev_owner), line(prev_row), line(prev_bag), grad_pooled[0, 0],
    )])
    gathered = lax.all_to_all(message, "rows", split_axis=0, concat_axis=0, tiled=True)

    steps = 4
    step_rows = rows_dev // steps
    high, low, kept = pl.pallas_call(
        prepare_kernel,
        grid=(steps,),
        out_shape=[
            jax.ShapeDtypeStruct((rows_dev, width), jnp.bfloat16),
            jax.ShapeDtypeStruct((rows_dev, width), jnp.bfloat16),
            jax.ShapeDtypeStruct((rows_dev, width), jnp.float32),
        ],
        in_specs=[pl.BlockSpec((step_rows, width), lambda i: (i, 0))],
        out_specs=[vmem] * 3,
        compiler_params=params,
        cost_estimate=pl.CostEstimate(
            flops=4 * rows_dev * width, bytes_accessed=3 * rows_dev * width * 4,
            transcendentals=0),
        name="prepare",
    )(stay(item_table))

    partial_pooled, joined = pl.pallas_call(
        functools.partial(pool_kernel, bag_count, lines),
        out_shape=(
            jax.ShapeDtypeStruct((owners, bag_count, width), jnp.float32),
            jax.ShapeDtypeStruct((owners, prev_length, LANES), jnp.float32),
        ),
        in_specs=[vmem] * 3,
        out_specs=[vmem] * 2,
        scratch_shapes=[
            pltpu.VMEM((owners, lines, LANES), jnp.float32),
            pltpu.VMEM((owners, lines, LANES), jnp.float32),
            pltpu.VMEM((blocks, owners * bag_count, LANES), jnp.float32),
        ],
        compiler_params=params,
        cost_estimate=pl.CostEstimate(
            flops=4 * owners * bag_count * rows_dev * width,
            bytes_accessed=rows_dev * width * 4, transcendentals=0),
        name="pool",
    )(gathered, high, low)
    returned = lax.all_to_all(
        partial_pooled, "rows", split_axis=0, concat_axis=0, tiled=True)
    all_groups = [joined] + [shift(joined, "dp", k) for k in range(1, groups)]

    chunk = min(devices, LANES // bag_count)
    segments = chunk * bag_count
    pieces = 4
    new_table, new_accum = pl.pallas_call(
        functools.partial(update_kernel, bag_count, lines, groups, chunk),
        out_shape=(
            jax.ShapeDtypeStruct((rows_dev, width), jnp.float32),
            jax.ShapeDtypeStruct((blocks, LANES), jnp.float32),
        ),
        in_specs=[vmem] * (groups + 2),
        out_specs=(hbm, vmem),
        scratch_shapes=[
            pltpu.VMEM((devices, prev_length, LANES), jnp.float32),
            pltpu.VMEM((chunk, lines, LANES), jnp.float32),
            pltpu.VMEM((chunk, lines, LANES), jnp.float32),
            pltpu.VMEM((blocks, segments, LANES), jnp.float32),
            pltpu.VMEM((segments, width), jnp.float32),
            pltpu.VMEM((blocks, LANES, width) if devices > chunk else (1, 8, LANES), jnp.float32),
            pltpu.VMEM((rows_dev, width), jnp.float32),
            pltpu.SemaphoreType.DMA((pieces,)),
        ],
        compiler_params=params,
        cost_estimate=pl.CostEstimate(flops=1, bytes_accessed=1024, transcendentals=0),
        name="update",
    )(*all_groups, kept, row_accum.reshape(blocks, LANES))

    pooled = jnp.sum(returned, axis=0)
    return (pooled[None, None], new_table, new_accum.reshape(rows_dev))


def solution(mesh):
    placed = (
        P("rows", None),
        P("rows"),
        P("dp", "rows", None, None),
        P("dp", "rows", None),
        P("dp", "rows", None),
        P("dp", "rows", None, None),
        P("dp", "rows", None),
        P("dp", "rows", None),
        P("dp", "rows", None, None),
    )
    return jax.shard_map(
        local,
        mesh=mesh,
        in_specs=placed,
        out_specs=(P("dp", "rows", None, None), P("rows", None), P("rows")),
        check_vma=False,
    )
```

```python
import functools

import jax
import jax.numpy as jnp
from jax import lax
from jax.experimental import pallas as pl
from jax.experimental.pallas import tpu as pltpu
from jax.sharding import PartitionSpec as P

learn_rate = 0.1
LANES = 128


def pack_kernel(rows_dev, *refs):
    sources, out, held, sems = refs[:7], refs[7], refs[8:15], refs[15]
    copies = [
        pltpu.make_async_copy(source, place, sems.at[i])
        for i, (source, place) in enumerate(zip(sources, held))
    ]
    for copy in copies:
        copy.start()
    for copy in copies:
        copy.wait()
    owner, row, bag, prev_owner, prev_row, prev_bag, grad = held
    lines = row.shape[0]
    bag_count, width = grad.shape

    def put(start, value):
        shape = (out.shape[0],) + value.shape
        out[:, start:start + value.shape[0], :] = jnp.broadcast_to(value[None], shape)

    put(0, (owner[...] * rows_dev + row[...]).astype(jnp.float32))
    put(lines, bag[...].astype(jnp.float32))
    put(2 * lines, (prev_owner[...] * rows_dev + prev_row[...]).astype(jnp.float32))
    put(3 * lines, prev_bag[...].astype(jnp.float32))
    for k in range(width // LANES):
        put(4 * lines + k * bag_count, grad[:, k * LANES:(k + 1) * LANES])


def split_two(x):
    high = x.astype(jnp.bfloat16)
    return high, (x - high.astype(jnp.float32)).astype(jnp.bfloat16)


def prepare_kernel(table, high, low, kept):
    rows = table.shape[0]
    here = pl.ds(pl.multiple_of(pl.program_id(0) * rows, rows), rows)
    values = table[...]
    kept[here, :] = values
    high[here, :], low[here, :] = split_two(values)


def codes(ids, bags, bag_count, base):
    rel = ids.astype(jnp.int32) - base
    code = lax.shift_right_arithmetic(rel, 7) * bag_count + bags.astype(jnp.int32)
    return code.astype(jnp.float32), (rel & (LANES - 1)).astype(jnp.float32)


def count_into(counts, code_ref, lane_ref, devices, bag_count):
    blocks = counts.shape[0]
    lines = code_ref.shape[1]
    one, none = jnp.ones((), jnp.bfloat16), jnp.zeros((), jnp.bfloat16)

    def one_hot(ref, d, size):
        numbers = lax.broadcasted_iota(jnp.int32, (size, LANES), 0).astype(jnp.bfloat16)
        parts = []
        for k in range(lines):
            row = jnp.broadcast_to(ref[d, k:k + 1, :], (size, LANES)).astype(jnp.bfloat16)
            parts.append(jnp.where(numbers == row, one, none))
        return jnp.concatenate(parts, axis=1)

    for d in range(devices):
        hits = lax.dot_general(
            one_hot(code_ref, d, blocks * bag_count), one_hot(lane_ref, d, LANES),
            (((1,), (1,)), ((), ())), preferred_element_type=jnp.float32)
        counts[:, d * bag_count:(d + 1) * bag_count, :] = hits.reshape(
            blocks, bag_count, LANES)


def pool_kernel(bag_count, lines, msg, high, low, out, joined, code_ref, lane_ref, counts):
    rows_dev, width = high.shape
    owners = msg.shape[0]
    base = lax.axis_index("rows") * rows_dev
    code_ref[...], lane_ref[...] = codes(
        msg[:, 0:lines, :], msg[:, lines:2 * lines, :], bag_count, base)
    joined[...] = msg[:, 2 * lines:, :]
    count_into(counts, code_ref, lane_ref, owners, bag_count)
    blocks = rows_dev // LANES
    flat = jnp.concatenate(
        [counts[h].astype(jnp.bfloat16) for h in range(blocks)], axis=1)
    total = jnp.zeros((owners * bag_count, width), jnp.float32)
    for part in (high, low):
        total += jnp.dot(flat, part[...], preferred_element_type=jnp.float32)
    out[...] = total.reshape(out.shape)


def update_kernel(bag_count, lines, groups, chunk, *refs):
    sources, (table, accum, new_table, new_accum) = refs[:groups], refs[groups:groups + 4]
    msg, code_ref, lane_ref, counts, grads, sums, fresh_table, sems = refs[groups + 4:]
    rows_dev, width = table.shape
    devices = msg.shape[0]
    owners = devices // groups
    blocks = counts.shape[0]
    base = lax.axis_index("rows") * rows_dev
    single = devices == chunk

    def count_chunk(first):
        here = pl.ds(first, chunk)
        code_ref[...], lane_ref[...] = codes(
            msg[here, 0:lines, :], msg[here, lines:2 * lines, :], bag_count, base)
        count_into(counts, code_ref, lane_ref, chunk, bag_count)
        for k in range(width // LANES):
            start = 2 * lines + k * bag_count
            grads[:, k * LANES:(k + 1) * LANES] = msg[
                here, start:start + bag_count, :].reshape(chunk * bag_count, LANES)
        return split_two(grads[...])

    def block_sum(h, parts):
        hits = counts[h].astype(jnp.bfloat16)
        total = jnp.zeros((LANES, width), jnp.float32)
        for part in parts:
            total += lax.dot_general(
                hits, part, (((0,), (0,)), ((), ())), preferred_element_type=jnp.float32)
        return total

    for i, source in enumerate(sources):
        msg[i * owners:(i + 1) * owners] = source[...]
    if single:
        parts = count_chunk(0)
    else:
        sums[...] = jnp.zeros_like(sums)

        @pl.loop(0, devices // chunk)
        def _(c):
            parts = count_chunk(c * chunk)

            @pl.loop(0, blocks)
            def _(h):
                sums[h] += block_sum(h, parts)

    diagonal = (
        lax.broadcasted_iota(jnp.int32, (LANES, LANES), 0)
        == lax.broadcasted_iota(jnp.int32, (LANES, LANES), 1))
    pieces = sems.shape[0]
    per_piece = blocks // pieces
    copies = []
    for h in range(blocks):
        grad = block_sum(h, parts) if single else sums[h]
        here = slice(h * LANES, (h + 1) * LANES)
        squares = grad * grad
        folded = squares[:, 0:LANES]
        for k in range(1, width // LANES):
            folded += squares[:, k * LANES:(k + 1) * LANES]
        old = jnp.where(diagonal, accum[h:h + 1, :], 0.0)
        fresh = jnp.sum(folded * (1.0 / width) + old, axis=1, keepdims=True)
        fresh_table[here, :] = table[here, :] - grad * (learn_rate * lax.rsqrt(fresh))
        new_accum[h:h + 1, :] = jnp.sum(
            jnp.where(diagonal, fresh, 0.0), axis=0, keepdims=True)
        if (h + 1) % per_piece == 0:
            i = h // per_piece
            piece = pl.ds(i * per_piece * LANES, per_piece * LANES)
            copies.append(pltpu.make_async_copy(
                fresh_table.at[piece, :], new_table.at[piece, :], sems.at[i]))
            copies[-1].start()
    for copy in copies:
        copy.wait()


def finish_kernel(returned, accum, pooled, new_accum):
    total = returned[0]
    for i in range(1, returned.shape[0]):
        total += returned[i]
    pooled[...] = total
    new_accum[...] = accum[...]


def shift(x, axis, step):
    size = lax.axis_size(axis)
    return lax.ppermute(x, axis, [(i, (i + step) % size) for i in range(size)])


def local(
    item_table, row_accum, owner_map, row_index, bag_index,
    prev_owner, prev_row, prev_bag, grad_pooled,
):
    owners, groups = lax.axis_size("rows"), lax.axis_size("dp")
    devices = owners * groups
    rows_dev, width = item_table.shape
    bag_count = grad_pooled.shape[2]
    lines = row_index.shape[2] // LANES
    blocks = rows_dev // LANES
    prev_length = 2 * lines + bag_count * width // LANES
    vmem = pl.BlockSpec(memory_space=pltpu.VMEM)
    hbm = pl.BlockSpec(memory_space=pltpu.HBM)
    params = pltpu.CompilerParams(vmem_limit_bytes=16 * 1024 * 1024)
    chunk = min(devices, LANES // bag_count)

    def stay(x):
        return pltpu.with_memory_space_constraint(x, pltpu.HBM)

    def line(x):
        return x.reshape(lines, LANES)

    message = pl.pallas_call(
        functools.partial(pack_kernel, rows_dev),
        out_shape=jax.ShapeDtypeStruct((owners, 2 * lines + prev_length, LANES), jnp.float32),
        in_specs=[hbm] * 7,
        out_specs=vmem,
        scratch_shapes=[pltpu.VMEM((lines, LANES), jnp.int32)] * 6
        + [pltpu.VMEM((bag_count, width), jnp.float32), pltpu.SemaphoreType.DMA((7,))],
        compiler_params=params,
        name="pack",
    )(*[stay(x) for x in (
        line(owner_map), line(row_index), line(bag_index),
        line(prev_owner), line(prev_row), line(prev_bag), grad_pooled[0, 0],
    )])
    gathered = lax.all_to_all(message, "rows", split_axis=0, concat_axis=0, tiled=True)

    steps = 4
    step_rows = rows_dev // steps
    high, low, kept = pl.pallas_call(
        prepare_kernel,
        grid=(steps,),
        out_shape=[
            pltpu.VMEM((rows_dev, width), jnp.bfloat16),
            pltpu.VMEM((rows_dev, width), jnp.bfloat16),
            pltpu.VMEM((rows_dev, width), jnp.float32),
        ],
        in_specs=[pl.BlockSpec((step_rows, width), lambda i: (i, 0))],
        out_specs=[vmem] * 3,
        compiler_params=params,
        cost_estimate=pl.CostEstimate(
            flops=4 * rows_dev * width, bytes_accessed=3 * rows_dev * width * 4,
            transcendentals=0),
        name="prepare",
    )(stay(item_table))

    partial_pooled, joined = pl.pallas_call(
        functools.partial(pool_kernel, bag_count, lines),
        out_shape=(
            jax.ShapeDtypeStruct((owners, bag_count, width), jnp.float32),
            jax.ShapeDtypeStruct((owners, prev_length, LANES), jnp.float32),
        ),
        in_specs=[vmem] * 3,
        out_specs=[vmem] * 2,
        scratch_shapes=[
            pltpu.VMEM((owners, lines, LANES), jnp.float32),
            pltpu.VMEM((owners, lines, LANES), jnp.float32),
            pltpu.VMEM((blocks, owners * bag_count, LANES), jnp.float32),
        ],
        compiler_params=params,
        cost_estimate=pl.CostEstimate(
            flops=4 * owners * bag_count * rows_dev * width,
            bytes_accessed=rows_dev * width * 4, transcendentals=0),
        name="pool",
    )(gathered, high, low)
    returned = lax.all_to_all(
        partial_pooled, "rows", split_axis=0, concat_axis=0, tiled=True)
    all_groups = [joined] + [shift(joined, "dp", k) for k in range(1, groups)]

    segments = chunk * bag_count
    pieces = 4
    new_table, new_accum = pl.pallas_call(
        functools.partial(update_kernel, bag_count, lines, groups, chunk),
        out_shape=(
            jax.ShapeDtypeStruct((rows_dev, width), jnp.float32),
            pltpu.VMEM((blocks, LANES), jnp.float32),
        ),
        in_specs=[vmem] * (groups + 2),
        out_specs=(hbm, vmem),
        scratch_shapes=[
            pltpu.VMEM((devices, prev_length, LANES), jnp.float32),
            pltpu.VMEM((chunk, lines, LANES), jnp.float32),
            pltpu.VMEM((chunk, lines, LANES), jnp.float32),
            pltpu.VMEM((blocks, segments, LANES), jnp.float32),
            pltpu.VMEM((segments, width), jnp.float32),
            pltpu.VMEM((blocks, LANES, width) if devices > chunk else (1, 8, LANES), jnp.float32),
            pltpu.VMEM((rows_dev, width), jnp.float32),
            pltpu.SemaphoreType.DMA((pieces,)),
        ],
        compiler_params=params if devices == chunk else pltpu.CompilerParams(
            vmem_limit_bytes=40 * 1024 * 1024),
        cost_estimate=pl.CostEstimate(flops=1, bytes_accessed=1 << 20, transcendentals=0),
        name="update",
    )(*all_groups, kept, row_accum.reshape(blocks, LANES))

    pooled, new_accum = pl.pallas_call(
        finish_kernel,
        out_shape=(
            jax.ShapeDtypeStruct((bag_count, width), jnp.float32),
            jax.ShapeDtypeStruct((blocks, LANES), jnp.float32),
        ),
        in_specs=[vmem] * 2,
        out_specs=[vmem] * 2,
        compiler_params=params,
        name="finish",
    )(returned, new_accum)
    return (pooled[None, None], new_table, new_accum.reshape(rows_dev))


def solution(mesh):
    placed = (
        P("rows", None),
        P("rows"),
        P("dp", "rows", None, None),
        P("dp", "rows", None),
        P("dp", "rows", None),
        P("dp", "rows", None, None),
        P("dp", "rows", None),
        P("dp", "rows", None),
        P("dp", "rows", None, None),
    )
    return jax.shard_map(
        local,
        mesh=mesh,
        in_specs=placed,
        out_specs=(P("dp", "rows", None, None), P("rows", None), P("rows")),
        check_vma=False,
    )
```

```python
import functools

import jax
import jax.numpy as jnp
from jax import lax
from jax.experimental import pallas as pl
from jax.experimental.pallas import tpu as pltpu
from jax.sharding import PartitionSpec as P

learn_rate = 0.1
LANES = 128


def pack_kernel(rows_dev, *refs):
    sources, out, held, sems = refs[:7], refs[7], refs[8:15], refs[15]
    copies = [
        pltpu.make_async_copy(source, place, sems.at[i])
        for i, (source, place) in enumerate(zip(sources, held))
    ]
    for copy in copies:
        copy.start()
    for copy in copies:
        copy.wait()
    owner, row, bag, prev_owner, prev_row, prev_bag, grad = held
    lines = row.shape[0]
    bag_count, width = grad.shape

    def put(start, value):
        shape = (out.shape[0],) + value.shape
        out[:, start:start + value.shape[0], :] = jnp.broadcast_to(value[None], shape)

    put(0, (owner[...] * rows_dev + row[...]).astype(jnp.float32))
    put(lines, bag[...].astype(jnp.float32))
    put(2 * lines, (prev_owner[...] * rows_dev + prev_row[...]).astype(jnp.float32))
    put(3 * lines, prev_bag[...].astype(jnp.float32))
    for k in range(width // LANES):
        put(4 * lines + k * bag_count, grad[:, k * LANES:(k + 1) * LANES])


def split_two(x):
    high = x.astype(jnp.bfloat16)
    return high, (x - high.astype(jnp.float32)).astype(jnp.bfloat16)


def prepare_kernel(table, high, low):
    rows = table.shape[0]
    here = pl.ds(pl.multiple_of(pl.program_id(0) * rows, rows), rows)
    high[here, :], low[here, :] = split_two(table[...])


def codes(ids, bags, bag_count, base):
    rel = ids.astype(jnp.int32) - base
    code = lax.shift_right_arithmetic(rel, 7) * bag_count + bags.astype(jnp.int32)
    return code.astype(jnp.float32), (rel & (LANES - 1)).astype(jnp.float32)


def count_into(counts, code_ref, lane_ref, devices, bag_count):
    blocks = counts.shape[0]
    lines = code_ref.shape[1]
    one, none = jnp.ones((), jnp.bfloat16), jnp.zeros((), jnp.bfloat16)

    def one_hot(ref, d, size):
        numbers = lax.broadcasted_iota(jnp.int32, (size, LANES), 0).astype(jnp.bfloat16)
        parts = []
        for k in range(lines):
            row = jnp.broadcast_to(ref[d, k:k + 1, :], (size, LANES)).astype(jnp.bfloat16)
            parts.append(jnp.where(numbers == row, one, none))
        return jnp.concatenate(parts, axis=1)

    for d in range(devices):
        hits = lax.dot_general(
            one_hot(code_ref, d, blocks * bag_count), one_hot(lane_ref, d, LANES),
            (((1,), (1,)), ((), ())), preferred_element_type=jnp.float32)
        counts[:, d * bag_count:(d + 1) * bag_count, :] = hits.reshape(
            blocks, bag_count, LANES)


def pool_kernel(bag_count, lines, msg, high, low, out, joined, code_ref, lane_ref, counts):
    rows_dev, width = high.shape
    owners = msg.shape[0]
    base = lax.axis_index("rows") * rows_dev
    code_ref[...], lane_ref[...] = codes(
        msg[:, 0:lines, :], msg[:, lines:2 * lines, :], bag_count, base)
    joined[...] = msg[:, 2 * lines:, :]
    count_into(counts, code_ref, lane_ref, owners, bag_count)
    blocks = rows_dev // LANES
    flat = jnp.concatenate(
        [counts[h].astype(jnp.bfloat16) for h in range(blocks)], axis=1)
    total = jnp.zeros((owners * bag_count, width), jnp.float32)
    for part in (high, low):
        total += jnp.dot(flat, part[...], preferred_element_type=jnp.float32)
    out[...] = total.reshape(out.shape)


def update_kernel(bag_count, lines, groups, chunk, *refs):
    sources, (table, accum, new_table, new_accum) = refs[:groups], refs[groups:groups + 4]
    msg, code_ref, lane_ref, counts, grads, sums, held, sems = refs[groups + 4:]
    rows_dev, width = table.shape
    pieces = sems.shape[1]

    def piece(i):
        return pl.ds(i * (rows_dev // pieces), rows_dev // pieces)

    fetches = [
        pltpu.make_async_copy(table.at[piece(i), :], held.at[piece(i), :], sems.at[0, i])
        for i in range(pieces)
    ]
    for fetch in fetches:
        fetch.start()
    devices = msg.shape[0]
    owners = devices // groups
    blocks = counts.shape[0]
    base = lax.axis_index("rows") * rows_dev
    single = devices == chunk

    def count_chunk(first):
        here = pl.ds(first, chunk)
        code_ref[...], lane_ref[...] = codes(
            msg[here, 0:lines, :], msg[here, lines:2 * lines, :], bag_count, base)
        count_into(counts, code_ref, lane_ref, chunk, bag_count)
        for k in range(width // LANES):
            start = 2 * lines + k * bag_count
            grads[:, k * LANES:(k + 1) * LANES] = msg[
                here, start:start + bag_count, :].reshape(chunk * bag_count, LANES)
        return split_two(grads[...])

    def block_sum(h, parts):
        hits = counts[h].astype(jnp.bfloat16)
        total = jnp.zeros((LANES, width), jnp.float32)
        for part in parts:
            total += lax.dot_general(
                hits, part, (((0,), (0,)), ((), ())), preferred_element_type=jnp.float32)
        return total

    for i, source in enumerate(sources):
        msg[i * owners:(i + 1) * owners] = source[...]
    if single:
        parts = count_chunk(0)
    else:
        sums[...] = jnp.zeros_like(sums)

        @pl.loop(0, devices // chunk)
        def _(c):
            parts = count_chunk(c * chunk)

            @pl.loop(0, blocks)
            def _(h):
                sums[h] += block_sum(h, parts)

    diagonal = (
        lax.broadcasted_iota(jnp.int32, (LANES, LANES), 0)
        == lax.broadcasted_iota(jnp.int32, (LANES, LANES), 1))
    per_piece = blocks // pieces
    copies = []
    for h in range(blocks):
        i = h // per_piece
        if h % per_piece == 0:
            fetches[i].wait()
        grad = block_sum(h, parts) if single else sums[h]
        here = slice(h * LANES, (h + 1) * LANES)
        squares = grad * grad
        folded = squares[:, 0:LANES]
        for k in range(1, width // LANES):
            folded += squares[:, k * LANES:(k + 1) * LANES]
        old = jnp.where(diagonal, accum[h:h + 1, :], 0.0)
        fresh = jnp.sum(folded * (1.0 / width) + old, axis=1, keepdims=True)
        held[here, :] = held[here, :] - grad * (learn_rate * lax.rsqrt(fresh))
        new_accum[h:h + 1, :] = jnp.sum(
            jnp.where(diagonal, fresh, 0.0), axis=0, keepdims=True)
        if (h + 1) % per_piece == 0:
            copies.append(pltpu.make_async_copy(
                held.at[piece(i), :], new_table.at[piece(i), :], sems.at[1, i]))
            copies[-1].start()
    for copy in copies:
        copy.wait()


def finish_kernel(returned, accum, pooled, new_accum):
    total = returned[0]
    for i in range(1, returned.shape[0]):
        total += returned[i]
    pooled[...] = total
    new_accum[...] = accum[...]


def shift(x, axis, step):
    size = lax.axis_size(axis)
    return lax.ppermute(x, axis, [(i, (i + step) % size) for i in range(size)])


def local(
    item_table, row_accum, owner_map, row_index, bag_index,
    prev_owner, prev_row, prev_bag, grad_pooled,
):
    owners, groups = lax.axis_size("rows"), lax.axis_size("dp")
    devices = owners * groups
    rows_dev, width = item_table.shape
    bag_count = grad_pooled.shape[2]
    lines = row_index.shape[2] // LANES
    blocks = rows_dev // LANES
    prev_length = 2 * lines + bag_count * width // LANES
    vmem = pl.BlockSpec(memory_space=pltpu.VMEM)
    hbm = pl.BlockSpec(memory_space=pltpu.HBM)
    params = pltpu.CompilerParams(vmem_limit_bytes=16 * 1024 * 1024)
    chunk = min(devices, LANES // bag_count)

    def stay(x):
        return pltpu.with_memory_space_constraint(x, pltpu.HBM)

    def line(x):
        return x.reshape(lines, LANES)

    message = pl.pallas_call(
        functools.partial(pack_kernel, rows_dev),
        out_shape=pltpu.VMEM((owners, 2 * lines + prev_length, LANES), jnp.float32),
        in_specs=[hbm] * 7,
        out_specs=vmem,
        scratch_shapes=[pltpu.VMEM((lines, LANES), jnp.int32)] * 6
        + [pltpu.VMEM((bag_count, width), jnp.float32), pltpu.SemaphoreType.DMA((7,))],
        compiler_params=params,
        name="pack",
    )(*[stay(x) for x in (
        line(owner_map), line(row_index), line(bag_index),
        line(prev_owner), line(prev_row), line(prev_bag), grad_pooled[0, 0],
    )])
    gathered = lax.all_to_all(message, "rows", split_axis=0, concat_axis=0, tiled=True)

    steps = 4
    step_rows = rows_dev // steps
    high, low = pl.pallas_call(
        prepare_kernel,
        grid=(steps,),
        out_shape=[
            pltpu.VMEM((rows_dev, width), jnp.bfloat16),
            pltpu.VMEM((rows_dev, width), jnp.bfloat16),
        ],
        in_specs=[pl.BlockSpec((step_rows, width), lambda i: (i, 0))],
        out_specs=[vmem] * 2,
        compiler_params=params,
        cost_estimate=pl.CostEstimate(
            flops=4 * rows_dev * width, bytes_accessed=2 * rows_dev * width * 4,
            transcendentals=0),
        name="prepare",
    )(stay(item_table))

    partial_pooled, joined = pl.pallas_call(
        functools.partial(pool_kernel, bag_count, lines),
        out_shape=(
            pltpu.VMEM((owners, bag_count, width), jnp.float32),
            pltpu.VMEM((owners, prev_length, LANES), jnp.float32),
        ),
        in_specs=[vmem] * 3,
        out_specs=[vmem] * 2,
        scratch_shapes=[
            pltpu.VMEM((owners, lines, LANES), jnp.float32),
            pltpu.VMEM((owners, lines, LANES), jnp.float32),
            pltpu.VMEM((blocks, owners * bag_count, LANES), jnp.float32),
        ],
        compiler_params=params,
        cost_estimate=pl.CostEstimate(
            flops=4 * owners * bag_count * rows_dev * width,
            bytes_accessed=rows_dev * width * 4, transcendentals=0),
        name="pool",
    )(gathered, high, low)
    returned = lax.all_to_all(
        partial_pooled, "rows", split_axis=0, concat_axis=0, tiled=True)
    all_groups = [joined] + [shift(joined, "dp", k) for k in range(1, groups)]

    segments = chunk * bag_count
    pieces = 4
    new_table, new_accum = pl.pallas_call(
        functools.partial(update_kernel, bag_count, lines, groups, chunk),
        out_shape=(
            jax.ShapeDtypeStruct((rows_dev, width), jnp.float32),
            pltpu.VMEM((blocks, LANES), jnp.float32),
        ),
        in_specs=[vmem] * groups + [hbm, vmem],
        out_specs=(hbm, vmem),
        scratch_shapes=[
            pltpu.VMEM((devices, prev_length, LANES), jnp.float32),
            pltpu.VMEM((chunk, lines, LANES), jnp.float32),
            pltpu.VMEM((chunk, lines, LANES), jnp.float32),
            pltpu.VMEM((blocks, segments, LANES), jnp.float32),
            pltpu.VMEM((segments, width), jnp.float32),
            pltpu.VMEM((blocks, LANES, width) if devices > chunk else (1, 8, LANES), jnp.float32),
            pltpu.VMEM((rows_dev, width), jnp.float32),
            pltpu.SemaphoreType.DMA((2, pieces)),
        ],
        compiler_params=params if devices == chunk else pltpu.CompilerParams(
            vmem_limit_bytes=40 * 1024 * 1024),
        cost_estimate=pl.CostEstimate(flops=1, bytes_accessed=1 << 20, transcendentals=0),
        name="update",
    )(*all_groups, stay(item_table), row_accum.reshape(blocks, LANES))

    pooled, new_accum = pl.pallas_call(
        finish_kernel,
        out_shape=(
            jax.ShapeDtypeStruct((bag_count, width), jnp.float32),
            jax.ShapeDtypeStruct((blocks, LANES), jnp.float32),
        ),
        in_specs=[vmem] * 2,
        out_specs=[vmem] * 2,
        compiler_params=params,
        name="finish",
    )(returned, new_accum)
    return (pooled[None, None], new_table, new_accum.reshape(rows_dev))


def solution(mesh):
    placed = (
        P("rows", None),
        P("rows"),
        P("dp", "rows", None, None),
        P("dp", "rows", None),
        P("dp", "rows", None),
        P("dp", "rows", None, None),
        P("dp", "rows", None),
        P("dp", "rows", None),
        P("dp", "rows", None, None),
    )
    return jax.shard_map(
        local,
        mesh=mesh,
        in_specs=placed,
        out_specs=(P("dp", "rows", None, None), P("rows", None), P("rows")),
        check_vma=False,
    )
```

```python
import functools

import jax
import jax.numpy as jnp
from jax import lax
from jax.experimental import pallas as pl
from jax.experimental.pallas import tpu as pltpu
from jax.sharding import PartitionSpec as P

learn_rate = 0.1
LANES = 128


def pack_kernel(rows_dev, *refs):
    sources, out, held, sems = refs[:7], refs[7], refs[8:15], refs[15]
    copies = [
        pltpu.make_async_copy(source, place, sems.at[i])
        for i, (source, place) in enumerate(zip(sources, held))
    ]
    for copy in copies:
        copy.start()
    for copy in copies:
        copy.wait()
    owner, row, bag, prev_owner, prev_row, prev_bag, grad = held
    lines = row.shape[0]
    bag_count, width = grad.shape

    def put(start, value):
        shape = (out.shape[0],) + value.shape
        out[:, start:start + value.shape[0], :] = jnp.broadcast_to(value[None], shape)

    put(0, (owner[...] * rows_dev + row[...]).astype(jnp.float32))
    put(lines, bag[...].astype(jnp.float32))
    put(2 * lines, (prev_owner[...] * rows_dev + prev_row[...]).astype(jnp.float32))
    put(3 * lines, prev_bag[...].astype(jnp.float32))
    for k in range(width // LANES):
        put(4 * lines + k * bag_count, grad[:, k * LANES:(k + 1) * LANES])


def split_two(x):
    high = x.astype(jnp.bfloat16)
    return high, (x - high.astype(jnp.float32)).astype(jnp.bfloat16)


def prepare_kernel(table, high, low):
    rows = table.shape[0]
    here = pl.ds(pl.multiple_of(pl.program_id(0) * rows, rows), rows)
    high[here, :], low[here, :] = split_two(table[...])


def codes(ids, bags, bag_count, base):
    rel = ids.astype(jnp.int32) - base
    code = lax.shift_right_arithmetic(rel, 7) * bag_count + bags.astype(jnp.int32)
    return code.astype(jnp.float32), (rel & (LANES - 1)).astype(jnp.float32)


def count_into(counts, code_ref, lane_ref, devices, bag_count):
    blocks = counts.shape[0]
    lines = code_ref.shape[1]
    one, none = jnp.ones((), jnp.bfloat16), jnp.zeros((), jnp.bfloat16)

    def one_hot(ref, d, size):
        numbers = lax.broadcasted_iota(jnp.int32, (size, LANES), 0).astype(jnp.bfloat16)
        parts = []
        for k in range(lines):
            row = jnp.broadcast_to(ref[d, k:k + 1, :], (size, LANES)).astype(jnp.bfloat16)
            parts.append(jnp.where(numbers == row, one, none))
        return jnp.concatenate(parts, axis=1)

    for d in range(devices):
        hits = lax.dot_general(
            one_hot(code_ref, d, blocks * bag_count), one_hot(lane_ref, d, LANES),
            (((1,), (1,)), ((), ())), preferred_element_type=jnp.float32)
        counts[:, d * bag_count:(d + 1) * bag_count, :] = hits.reshape(
            blocks, bag_count, LANES)


def pool_kernel(
    bag_count, lines, msg, high, low, table, out, joined, kept,
    code_ref, lane_ref, counts, sem,
):
    fetch = pltpu.make_async_copy(table, kept, sem)
    fetch.start()
    rows_dev, width = high.shape
    owners = msg.shape[0]
    base = lax.axis_index("rows") * rows_dev
    code_ref[...], lane_ref[...] = codes(
        msg[:, 0:lines, :], msg[:, lines:2 * lines, :], bag_count, base)
    joined[...] = msg[:, 2 * lines:, :]
    count_into(counts, code_ref, lane_ref, owners, bag_count)
    blocks = rows_dev // LANES
    flat = jnp.concatenate(
        [counts[h].astype(jnp.bfloat16) for h in range(blocks)], axis=1)
    total = jnp.zeros((owners * bag_count, width), jnp.float32)
    for part in (high, low):
        total += jnp.dot(flat, part[...], preferred_element_type=jnp.float32)
    out[...] = total.reshape(out.shape)
    fetch.wait()


def update_kernel(bag_count, lines, groups, chunk, *refs):
    sources, (table, accum, new_table, new_accum) = refs[:groups], refs[groups:groups + 4]
    msg, code_ref, lane_ref, counts, grads, sums, fresh_table, sems = refs[groups + 4:]
    rows_dev, width = table.shape
    pieces = sems.shape[0]
    devices = msg.shape[0]
    owners = devices // groups
    blocks = counts.shape[0]
    base = lax.axis_index("rows") * rows_dev
    single = devices == chunk

    def count_chunk(first):
        here = pl.ds(first, chunk)
        code_ref[...], lane_ref[...] = codes(
            msg[here, 0:lines, :], msg[here, lines:2 * lines, :], bag_count, base)
        count_into(counts, code_ref, lane_ref, chunk, bag_count)
        for k in range(width // LANES):
            start = 2 * lines + k * bag_count
            grads[:, k * LANES:(k + 1) * LANES] = msg[
                here, start:start + bag_count, :].reshape(chunk * bag_count, LANES)
        return split_two(grads[...])

    def block_sum(h, parts):
        hits = counts[h].astype(jnp.bfloat16)
        total = jnp.zeros((LANES, width), jnp.float32)
        for part in parts:
            total += lax.dot_general(
                hits, part, (((0,), (0,)), ((), ())), preferred_element_type=jnp.float32)
        return total

    for i, source in enumerate(sources):
        msg[i * owners:(i + 1) * owners] = source[...]
    if single:
        parts = count_chunk(0)
    else:
        sums[...] = jnp.zeros_like(sums)

        @pl.loop(0, devices // chunk)
        def _(c):
            parts = count_chunk(c * chunk)

            @pl.loop(0, blocks)
            def _(h):
                sums[h] += block_sum(h, parts)

    diagonal = (
        lax.broadcasted_iota(jnp.int32, (LANES, LANES), 0)
        == lax.broadcasted_iota(jnp.int32, (LANES, LANES), 1))
    per_piece = blocks // pieces
    copies = []
    for h in range(blocks):
        i = h // per_piece
        grad = block_sum(h, parts) if single else sums[h]
        here = slice(h * LANES, (h + 1) * LANES)
        squares = grad * grad
        folded = squares[:, 0:LANES]
        for k in range(1, width // LANES):
            folded += squares[:, k * LANES:(k + 1) * LANES]
        old = jnp.where(diagonal, accum[h:h + 1, :], 0.0)
        fresh = jnp.sum(folded * (1.0 / width) + old, axis=1, keepdims=True)
        fresh_table[here, :] = table[here, :] - grad * (learn_rate * lax.rsqrt(fresh))
        new_accum[h:h + 1, :] = jnp.sum(
            jnp.where(diagonal, fresh, 0.0), axis=0, keepdims=True)
        if (h + 1) % per_piece == 0:
            piece = pl.ds(i * per_piece * LANES, per_piece * LANES)
            copies.append(pltpu.make_async_copy(
                fresh_table.at[piece, :], new_table.at[piece, :], sems.at[i]))
            copies[-1].start()
    for copy in copies:
        copy.wait()


def finish_kernel(returned, accum, pooled, new_accum):
    total = returned[0]
    for i in range(1, returned.shape[0]):
        total += returned[i]
    pooled[...] = total
    new_accum[...] = accum[...]


def shift(x, axis, step):
    size = lax.axis_size(axis)
    return lax.ppermute(x, axis, [(i, (i + step) % size) for i in range(size)])


def local(
    item_table, row_accum, owner_map, row_index, bag_index,
    prev_owner, prev_row, prev_bag, grad_pooled,
):
    owners, groups = lax.axis_size("rows"), lax.axis_size("dp")
    devices = owners * groups
    rows_dev, width = item_table.shape
    bag_count = grad_pooled.shape[2]
    lines = row_index.shape[2] // LANES
    blocks = rows_dev // LANES
    prev_length = 2 * lines + bag_count * width // LANES
    vmem = pl.BlockSpec(memory_space=pltpu.VMEM)
    hbm = pl.BlockSpec(memory_space=pltpu.HBM)
    params = pltpu.CompilerParams(vmem_limit_bytes=16 * 1024 * 1024)
    chunk = min(devices, LANES // bag_count)

    def stay(x):
        return pltpu.with_memory_space_constraint(x, pltpu.HBM)

    def line(x):
        return x.reshape(lines, LANES)

    message = pl.pallas_call(
        functools.partial(pack_kernel, rows_dev),
        out_shape=pltpu.VMEM((owners, 2 * lines + prev_length, LANES), jnp.float32),
        in_specs=[hbm] * 7,
        out_specs=vmem,
        scratch_shapes=[pltpu.VMEM((lines, LANES), jnp.int32)] * 6
        + [pltpu.VMEM((bag_count, width), jnp.float32), pltpu.SemaphoreType.DMA((7,))],
        compiler_params=params,
        name="pack",
    )(*[stay(x) for x in (
        line(owner_map), line(row_index), line(bag_index),
        line(prev_owner), line(prev_row), line(prev_bag), grad_pooled[0, 0],
    )])
    gathered = lax.all_to_all(message, "rows", split_axis=0, concat_axis=0, tiled=True)

    steps = 4
    step_rows = rows_dev // steps
    high, low = pl.pallas_call(
        prepare_kernel,
        grid=(steps,),
        out_shape=[
            pltpu.VMEM((rows_dev, width), jnp.bfloat16),
            pltpu.VMEM((rows_dev, width), jnp.bfloat16),
        ],
        in_specs=[pl.BlockSpec((step_rows, width), lambda i: (i, 0))],
        out_specs=[vmem] * 2,
        compiler_params=params,
        cost_estimate=pl.CostEstimate(
            flops=4 * rows_dev * width, bytes_accessed=2 * rows_dev * width * 4,
            transcendentals=0),
        name="prepare",
    )(stay(item_table))

    partial_pooled, joined, kept = pl.pallas_call(
        functools.partial(pool_kernel, bag_count, lines),
        out_shape=(
            pltpu.VMEM((owners, bag_count, width), jnp.float32),
            pltpu.VMEM((owners, prev_length, LANES), jnp.float32),
            pltpu.VMEM((rows_dev, width), jnp.float32),
        ),
        in_specs=[vmem] * 3 + [hbm],
        out_specs=[vmem] * 3,
        scratch_shapes=[
            pltpu.VMEM((owners, lines, LANES), jnp.float32),
            pltpu.VMEM((owners, lines, LANES), jnp.float32),
            pltpu.VMEM((blocks, owners * bag_count, LANES), jnp.float32),
            pltpu.SemaphoreType.DMA,
        ],
        compiler_params=params,
        cost_estimate=pl.CostEstimate(
            flops=4 * owners * bag_count * rows_dev * width,
            bytes_accessed=rows_dev * width * 4, transcendentals=0),
        name="pool",
    )(gathered, high, low, stay(item_table))
    returned = lax.all_to_all(
        partial_pooled, "rows", split_axis=0, concat_axis=0, tiled=True)
    all_groups = [joined] + [shift(joined, "dp", k) for k in range(1, groups)]

    segments = chunk * bag_count
    pieces = 4
    new_table, new_accum = pl.pallas_call(
        functools.partial(update_kernel, bag_count, lines, groups, chunk),
        out_shape=(
            jax.ShapeDtypeStruct((rows_dev, width), jnp.float32),
            pltpu.VMEM((blocks, LANES), jnp.float32),
        ),
        in_specs=[vmem] * (groups + 2),
        out_specs=(hbm, vmem),
        scratch_shapes=[
            pltpu.VMEM((devices, prev_length, LANES), jnp.float32),
            pltpu.VMEM((chunk, lines, LANES), jnp.float32),
            pltpu.VMEM((chunk, lines, LANES), jnp.float32),
            pltpu.VMEM((blocks, segments, LANES), jnp.float32),
            pltpu.VMEM((segments, width), jnp.float32),
            pltpu.VMEM((blocks, LANES, width) if devices > chunk else (1, 8, LANES), jnp.float32),
            pltpu.VMEM((rows_dev, width), jnp.float32),
            pltpu.SemaphoreType.DMA((pieces,)),
        ],
        compiler_params=params if devices == chunk else pltpu.CompilerParams(
            vmem_limit_bytes=40 * 1024 * 1024),
        cost_estimate=pl.CostEstimate(flops=1, bytes_accessed=1 << 20, transcendentals=0),
        name="update",
    )(*all_groups, kept, row_accum.reshape(blocks, LANES))

    pooled, new_accum = pl.pallas_call(
        finish_kernel,
        out_shape=(
            jax.ShapeDtypeStruct((bag_count, width), jnp.float32),
            jax.ShapeDtypeStruct((blocks, LANES), jnp.float32),
        ),
        in_specs=[vmem] * 2,
        out_specs=[vmem] * 2,
        compiler_params=params,
        name="finish",
    )(returned, new_accum)
    return (pooled[None, None], new_table, new_accum.reshape(rows_dev))


def solution(mesh):
    placed = (
        P("rows", None),
        P("rows"),
        P("dp", "rows", None, None),
        P("dp", "rows", None),
        P("dp", "rows", None),
        P("dp", "rows", None, None),
        P("dp", "rows", None),
        P("dp", "rows", None),
        P("dp", "rows", None, None),
    )
    return jax.shard_map(
        local,
        mesh=mesh,
        in_specs=placed,
        out_specs=(P("dp", "rows", None, None), P("rows", None), P("rows")),
        check_vma=False,
    )
```

```python
import functools

import jax
import jax.numpy as jnp
from jax import lax
from jax.experimental import pallas as pl
from jax.experimental.pallas import tpu as pltpu
from jax.sharding import PartitionSpec as P

learn_rate = 0.1
LANES = 128


def pack_kernel(rows_dev, *refs):
    sources, out, held, sems = refs[:7], refs[7], refs[8:15], refs[15]
    copies = [
        pltpu.make_async_copy(source, place, sems.at[i])
        for i, (source, place) in enumerate(zip(sources, held))
    ]
    for copy in copies:
        copy.start()
    for copy in copies:
        copy.wait()
    owner, row, bag, prev_owner, prev_row, prev_bag, grad = held
    lines = row.shape[0]
    bag_count, width = grad.shape

    def put(start, value):
        shape = (out.shape[0],) + value.shape
        out[:, start:start + value.shape[0], :] = jnp.broadcast_to(value[None], shape)

    put(0, (owner[...] * rows_dev + row[...]).astype(jnp.float32))
    put(lines, bag[...].astype(jnp.float32))
    put(2 * lines, (prev_owner[...] * rows_dev + prev_row[...]).astype(jnp.float32))
    put(3 * lines, prev_bag[...].astype(jnp.float32))
    for k in range(width // LANES):
        put(4 * lines + k * bag_count, grad[:, k * LANES:(k + 1) * LANES])


def split_two(x):
    high = x.astype(jnp.bfloat16)
    return high, (x - high.astype(jnp.float32)).astype(jnp.bfloat16)


def prepare_kernel(table, kept, sems):
    pieces = sems.shape[0]
    rows = table.shape[0] // pieces
    copies = [
        pltpu.make_async_copy(
            table.at[pl.ds(i * rows, rows), :], kept.at[pl.ds(i * rows, rows), :], sems.at[i])
        for i in range(pieces)
    ]
    for copy in copies:
        copy.start()
    for copy in copies:
        copy.wait()


def codes(ids, bags, bag_count, base):
    rel = ids.astype(jnp.int32) - base
    code = lax.shift_right_arithmetic(rel, 7) * bag_count + bags.astype(jnp.int32)
    return code.astype(jnp.float32), (rel & (LANES - 1)).astype(jnp.float32)


def count_into(counts, code_ref, lane_ref, devices, bag_count):
    blocks = counts.shape[0]
    lines = code_ref.shape[1]
    one, none = jnp.ones((), jnp.bfloat16), jnp.zeros((), jnp.bfloat16)

    def one_hot(ref, d, size):
        numbers = lax.broadcasted_iota(jnp.int32, (size, LANES), 0).astype(jnp.bfloat16)
        parts = []
        for k in range(lines):
            row = jnp.broadcast_to(ref[d, k:k + 1, :], (size, LANES)).astype(jnp.bfloat16)
            parts.append(jnp.where(numbers == row, one, none))
        return jnp.concatenate(parts, axis=1)

    for d in range(devices):
        hits = lax.dot_general(
            one_hot(code_ref, d, blocks * bag_count), one_hot(lane_ref, d, LANES),
            (((1,), (1,)), ((), ())), preferred_element_type=jnp.float32)
        counts[:, d * bag_count:(d + 1) * bag_count, :] = hits.reshape(
            blocks, bag_count, LANES)


def pool_kernel(bag_count, lines, msg, table, out, joined, code_ref, lane_ref, counts):
    rows_dev, width = table.shape
    owners = msg.shape[0]
    base = lax.axis_index("rows") * rows_dev
    code_ref[...], lane_ref[...] = codes(
        msg[:, 0:lines, :], msg[:, lines:2 * lines, :], bag_count, base)
    joined[...] = msg[:, 2 * lines:, :]
    count_into(counts, code_ref, lane_ref, owners, bag_count)
    blocks = rows_dev // LANES
    flat = jnp.concatenate(
        [counts[h].astype(jnp.bfloat16) for h in range(blocks)], axis=1)
    total = jnp.zeros((owners * bag_count, width), jnp.float32)
    for part in split_two(table[...]):
        total += jnp.dot(flat, part, preferred_element_type=jnp.float32)
    out[...] = total.reshape(out.shape)


def update_kernel(bag_count, lines, groups, chunk, *refs):
    sources, (table, accum, new_table, new_accum) = refs[:groups], refs[groups:groups + 4]
    msg, code_ref, lane_ref, counts, grads, sums, fresh_table, sems = refs[groups + 4:]
    rows_dev, width = table.shape
    pieces = sems.shape[0]
    devices = msg.shape[0]
    owners = devices // groups
    blocks = counts.shape[0]
    base = lax.axis_index("rows") * rows_dev
    single = devices == chunk

    def count_chunk(first):
        here = pl.ds(first, chunk)
        code_ref[...], lane_ref[...] = codes(
            msg[here, 0:lines, :], msg[here, lines:2 * lines, :], bag_count, base)
        count_into(counts, code_ref, lane_ref, chunk, bag_count)
        for k in range(width // LANES):
            start = 2 * lines + k * bag_count
            grads[:, k * LANES:(k + 1) * LANES] = msg[
                here, start:start + bag_count, :].reshape(chunk * bag_count, LANES)
        return split_two(grads[...])

    def block_sum(h, parts):
        hits = counts[h].astype(jnp.bfloat16)
        total = jnp.zeros((LANES, width), jnp.float32)
        for part in parts:
            total += lax.dot_general(
                hits, part, (((0,), (0,)), ((), ())), preferred_element_type=jnp.float32)
        return total

    for i, source in enumerate(sources):
        msg[i * owners:(i + 1) * owners] = source[...]
    if single:
        parts = count_chunk(0)
    else:
        sums[...] = jnp.zeros_like(sums)

        @pl.loop(0, devices // chunk)
        def _(c):
            parts = count_chunk(c * chunk)

            @pl.loop(0, blocks)
            def _(h):
                sums[h] += block_sum(h, parts)

    diagonal = (
        lax.broadcasted_iota(jnp.int32, (LANES, LANES), 0)
        == lax.broadcasted_iota(jnp.int32, (LANES, LANES), 1))
    per_piece = blocks // pieces
    copies = []
    for h in range(blocks):
        i = h // per_piece
        grad = block_sum(h, parts) if single else sums[h]
        here = slice(h * LANES, (h + 1) * LANES)
        squares = grad * grad
        folded = squares[:, 0:LANES]
        for k in range(1, width // LANES):
            folded += squares[:, k * LANES:(k + 1) * LANES]
        old = jnp.where(diagonal, accum[h:h + 1, :], 0.0)
        fresh = jnp.sum(folded * (1.0 / width) + old, axis=1, keepdims=True)
        fresh_table[here, :] = table[here, :] - grad * (learn_rate * lax.rsqrt(fresh))
        new_accum[h:h + 1, :] = jnp.sum(
            jnp.where(diagonal, fresh, 0.0), axis=0, keepdims=True)
        if (h + 1) % per_piece == 0:
            piece = pl.ds(i * per_piece * LANES, per_piece * LANES)
            copies.append(pltpu.make_async_copy(
                fresh_table.at[piece, :], new_table.at[piece, :], sems.at[i]))
            copies[-1].start()
    for copy in copies:
        copy.wait()


def finish_kernel(returned, accum, pooled, new_accum):
    total = returned[0]
    for i in range(1, returned.shape[0]):
        total += returned[i]
    pooled[...] = total
    new_accum[...] = accum[...]


def shift(x, axis, step):
    size = lax.axis_size(axis)
    return lax.ppermute(x, axis, [(i, (i + step) % size) for i in range(size)])


def local(
    item_table, row_accum, owner_map, row_index, bag_index,
    prev_owner, prev_row, prev_bag, grad_pooled,
):
    owners, groups = lax.axis_size("rows"), lax.axis_size("dp")
    devices = owners * groups
    rows_dev, width = item_table.shape
    bag_count = grad_pooled.shape[2]
    lines = row_index.shape[2] // LANES
    blocks = rows_dev // LANES
    prev_length = 2 * lines + bag_count * width // LANES
    vmem = pl.BlockSpec(memory_space=pltpu.VMEM)
    hbm = pl.BlockSpec(memory_space=pltpu.HBM)
    params = pltpu.CompilerParams(vmem_limit_bytes=16 * 1024 * 1024)
    chunk = min(devices, LANES // bag_count)

    def stay(x):
        return pltpu.with_memory_space_constraint(x, pltpu.HBM)

    def line(x):
        return x.reshape(lines, LANES)

    message = pl.pallas_call(
        functools.partial(pack_kernel, rows_dev),
        out_shape=pltpu.VMEM((owners, 2 * lines + prev_length, LANES), jnp.float32),
        in_specs=[hbm] * 7,
        out_specs=vmem,
        scratch_shapes=[pltpu.VMEM((lines, LANES), jnp.int32)] * 6
        + [pltpu.VMEM((bag_count, width), jnp.float32), pltpu.SemaphoreType.DMA((7,))],
        compiler_params=params,
        name="pack",
    )(*[stay(x) for x in (
        line(owner_map), line(row_index), line(bag_index),
        line(prev_owner), line(prev_row), line(prev_bag), grad_pooled[0, 0],
    )])
    gathered = lax.all_to_all(message, "rows", split_axis=0, concat_axis=0, tiled=True)

    pieces = 4
    kept = pl.pallas_call(
        prepare_kernel,
        out_shape=pltpu.VMEM((rows_dev, width), jnp.float32),
        in_specs=[hbm],
        out_specs=vmem,
        scratch_shapes=[pltpu.SemaphoreType.DMA((pieces,))],
        compiler_params=params,
        cost_estimate=pl.CostEstimate(
            flops=0, bytes_accessed=2 * rows_dev * width * 4, transcendentals=0),
        name="prepare",
    )(stay(item_table))

    partial_pooled, joined = pl.pallas_call(
        functools.partial(pool_kernel, bag_count, lines),
        out_shape=(
            pltpu.VMEM((owners, bag_count, width), jnp.float32),
            pltpu.VMEM((owners, prev_length, LANES), jnp.float32),
        ),
        in_specs=[vmem] * 2,
        out_specs=[vmem] * 2,
        scratch_shapes=[
            pltpu.VMEM((owners, lines, LANES), jnp.float32),
            pltpu.VMEM((owners, lines, LANES), jnp.float32),
            pltpu.VMEM((blocks, owners * bag_count, LANES), jnp.float32),
        ],
        compiler_params=params,
        cost_estimate=pl.CostEstimate(
            flops=4 * owners * bag_count * rows_dev * width,
            bytes_accessed=rows_dev * width * 4, transcendentals=0),
        name="pool",
    )(gathered, kept)
    returned = lax.all_to_all(
        partial_pooled, "rows", split_axis=0, concat_axis=0, tiled=True)
    all_groups = [joined] + [shift(joined, "dp", k) for k in range(1, groups)]

    segments = chunk * bag_count
    new_table, new_accum = pl.pallas_call(
        functools.partial(update_kernel, bag_count, lines, groups, chunk),
        out_shape=(
            jax.ShapeDtypeStruct((rows_dev, width), jnp.float32),
            pltpu.VMEM((blocks, LANES), jnp.float32),
        ),
        in_specs=[vmem] * (groups + 2),
        out_specs=(hbm, vmem),
        scratch_shapes=[
            pltpu.VMEM((devices, prev_length, LANES), jnp.float32),
            pltpu.VMEM((chunk, lines, LANES), jnp.float32),
            pltpu.VMEM((chunk, lines, LANES), jnp.float32),
            pltpu.VMEM((blocks, segments, LANES), jnp.float32),
            pltpu.VMEM((segments, width), jnp.float32),
            pltpu.VMEM((blocks, LANES, width) if devices > chunk else (1, 8, LANES), jnp.float32),
            pltpu.VMEM((rows_dev, width), jnp.float32),
            pltpu.SemaphoreType.DMA((pieces,)),
        ],
        compiler_params=params if devices == chunk else pltpu.CompilerParams(
            vmem_limit_bytes=40 * 1024 * 1024),
        cost_estimate=pl.CostEstimate(flops=1, bytes_accessed=1 << 20, transcendentals=0),
        name="update",
    )(*all_groups, kept, row_accum.reshape(blocks, LANES))

    pooled, new_accum = pl.pallas_call(
        finish_kernel,
        out_shape=(
            jax.ShapeDtypeStruct((bag_count, width), jnp.float32),
            jax.ShapeDtypeStruct((blocks, LANES), jnp.float32),
        ),
        in_specs=[vmem] * 2,
        out_specs=[vmem] * 2,
        compiler_params=params,
        name="finish",
    )(returned, new_accum)
    return (pooled[None, None], new_table, new_accum.reshape(rows_dev))


def solution(mesh):
    placed = (
        P("rows", None),
        P("rows"),
        P("dp", "rows", None, None),
        P("dp", "rows", None),
        P("dp", "rows", None),
        P("dp", "rows", None, None),
        P("dp", "rows", None),
        P("dp", "rows", None),
        P("dp", "rows", None, None),
    )
    return jax.shard_map(
        local,
        mesh=mesh,
        in_specs=placed,
        out_specs=(P("dp", "rows", None, None), P("rows", None), P("rows")),
        check_vma=False,
    )
```

```python
import functools

import jax
import jax.numpy as jnp
from jax import lax
from jax.experimental import pallas as pl
from jax.experimental.pallas import tpu as pltpu
from jax.sharding import PartitionSpec as P

learn_rate = 0.1
LANES = 128


def pack_kernel(rows_dev, *refs):
    sources, out, held, sems = refs[:7], refs[7], refs[8:15], refs[15]
    copies = [
        pltpu.make_async_copy(source, place, sems.at[i])
        for i, (source, place) in enumerate(zip(sources, held))
    ]
    for copy in copies:
        copy.start()
    for copy in copies:
        copy.wait()
    owner, row, bag, prev_owner, prev_row, prev_bag, grad = held
    lines = row.shape[0]
    bag_count, width = grad.shape

    def put(start, value):
        shape = (out.shape[0],) + value.shape
        out[:, start:start + value.shape[0], :] = jnp.broadcast_to(value[None], shape)

    put(0, (owner[...] * rows_dev + row[...]).astype(jnp.float32))
    put(lines, bag[...].astype(jnp.float32))
    put(2 * lines, (prev_owner[...] * rows_dev + prev_row[...]).astype(jnp.float32))
    put(3 * lines, prev_bag[...].astype(jnp.float32))
    for k in range(width // LANES):
        put(4 * lines + k * bag_count, grad[:, k * LANES:(k + 1) * LANES])


def split_two(x):
    high = x.astype(jnp.bfloat16)
    return high, (x - high.astype(jnp.float32)).astype(jnp.bfloat16)


def prepare_kernel(table, kept, sems):
    pieces = sems.shape[0]
    rows = table.shape[0] // pieces
    copies = [
        pltpu.make_async_copy(
            table.at[pl.ds(i * rows, rows), :], kept.at[pl.ds(i * rows, rows), :], sems.at[i])
        for i in range(pieces)
    ]
    for copy in copies:
        copy.start()
    for copy in copies:
        copy.wait()


def codes(ids, bags, bag_count, base):
    rel = ids.astype(jnp.int32) - base
    code = lax.shift_right_arithmetic(rel, 7) * bag_count + bags.astype(jnp.int32)
    return code.astype(jnp.float32), (rel & (LANES - 1)).astype(jnp.float32)


def count_into(counts, code_ref, lane_ref, devices, bag_count):
    blocks = counts.shape[0]
    lines = code_ref.shape[1]
    one, none = jnp.ones((), jnp.bfloat16), jnp.zeros((), jnp.bfloat16)

    def one_hot(ref, d, size):
        numbers = lax.broadcasted_iota(jnp.int32, (size, LANES), 0).astype(jnp.bfloat16)
        parts = []
        for k in range(lines):
            row = jnp.broadcast_to(ref[d, k:k + 1, :], (size, LANES)).astype(jnp.bfloat16)
            parts.append(jnp.where(numbers == row, one, none))
        return jnp.concatenate(parts, axis=1)

    for d in range(devices):
        hits = lax.dot_general(
            one_hot(code_ref, d, blocks * bag_count), one_hot(lane_ref, d, LANES),
            (((1,), (1,)), ((), ())), preferred_element_type=jnp.float32)
        counts[:, d * bag_count:(d + 1) * bag_count, :] = hits.reshape(
            blocks, bag_count, LANES)


def pool_kernel(
    bag_count, lines, msg, table, out, joined, go, code_ref, lane_ref, counts,
):
    go[0, 0] = 1
    rows_dev, width = table.shape
    owners = msg.shape[0]
    base = lax.axis_index("rows") * rows_dev
    code_ref[...], lane_ref[...] = codes(
        msg[:, 0:lines, :], msg[:, lines:2 * lines, :], bag_count, base)
    joined[...] = msg[:, 2 * lines:, :]
    count_into(counts, code_ref, lane_ref, owners, bag_count)
    blocks = rows_dev // LANES
    flat = jnp.concatenate(
        [counts[h].astype(jnp.bfloat16) for h in range(blocks)], axis=1)
    total = jnp.zeros((owners * bag_count, width), jnp.float32)
    for part in split_two(table[...]):
        total += jnp.dot(flat, part, preferred_element_type=jnp.float32)
    out[...] = total.reshape(out.shape)


def update_kernel(bag_count, lines, groups, chunk, *refs):
    sources, (table, accum, new_table, new_accum) = refs[:groups], refs[groups:groups + 4]
    msg, code_ref, lane_ref, counts, grads, sums, fresh_table, sems = refs[groups + 4:]
    rows_dev, width = table.shape
    pieces = sems.shape[0]
    devices = msg.shape[0]
    owners = devices // groups
    blocks = counts.shape[0]
    base = lax.axis_index("rows") * rows_dev
    single = devices == chunk

    def count_chunk(first):
        here = pl.ds(first, chunk)
        code_ref[...], lane_ref[...] = codes(
            msg[here, 0:lines, :], msg[here, lines:2 * lines, :], bag_count, base)
        count_into(counts, code_ref, lane_ref, chunk, bag_count)
        for k in range(width // LANES):
            start = 2 * lines + k * bag_count
            grads[:, k * LANES:(k + 1) * LANES] = msg[
                here, start:start + bag_count, :].reshape(chunk * bag_count, LANES)
        return split_two(grads[...])

    def block_sum(h, parts):
        hits = counts[h].astype(jnp.bfloat16)
        total = jnp.zeros((LANES, width), jnp.float32)
        for part in parts:
            total += lax.dot_general(
                hits, part, (((0,), (0,)), ((), ())), preferred_element_type=jnp.float32)
        return total

    for i, source in enumerate(sources):
        msg[i * owners:(i + 1) * owners] = source[...]
    if single:
        parts = count_chunk(0)
    else:
        sums[...] = jnp.zeros_like(sums)

        @pl.loop(0, devices // chunk)
        def _(c):
            parts = count_chunk(c * chunk)

            @pl.loop(0, blocks)
            def _(h):
                sums[h] += block_sum(h, parts)

    diagonal = (
        lax.broadcasted_iota(jnp.int32, (LANES, LANES), 0)
        == lax.broadcasted_iota(jnp.int32, (LANES, LANES), 1))
    per_piece = blocks // pieces
    copies = []
    for h in range(blocks):
        i = h // per_piece
        grad = block_sum(h, parts) if single else sums[h]
        here = slice(h * LANES, (h + 1) * LANES)
        squares = grad * grad
        folded = squares[:, 0:LANES]
        for k in range(1, width // LANES):
            folded += squares[:, k * LANES:(k + 1) * LANES]
        old = jnp.where(diagonal, accum[h:h + 1, :], 0.0)
        fresh = jnp.sum(folded * (1.0 / width) + old, axis=1, keepdims=True)
        fresh_table[here, :] = table[here, :] - grad * (learn_rate * lax.rsqrt(fresh))
        new_accum[h:h + 1, :] = jnp.sum(
            jnp.where(diagonal, fresh, 0.0), axis=0, keepdims=True)
        if (h + 1) % per_piece == 0:
            piece = pl.ds(i * per_piece * LANES, per_piece * LANES)
            copies.append(pltpu.make_async_copy(
                fresh_table.at[piece, :], new_table.at[piece, :], sems.at[i]))
            copies[-1].start()
    for copy in copies:
        copy.wait()


def pass_kernel(table, accum, new_table, new_accum, sem):
    copy = pltpu.make_async_copy(table, new_table, sem)
    copy.start()
    new_accum[...] = accum[...]
    copy.wait()


def finish_kernel(returned, accum, pooled, new_accum):
    total = returned[0]
    for i in range(1, returned.shape[0]):
        total += returned[i]
    pooled[...] = total
    new_accum[...] = accum[...]


def shift(x, axis, step):
    size = lax.axis_size(axis)
    return lax.ppermute(x, axis, [(i, (i + step) % size) for i in range(size)])


def local(
    item_table, row_accum, owner_map, row_index, bag_index,
    prev_owner, prev_row, prev_bag, grad_pooled,
):
    owners, groups = lax.axis_size("rows"), lax.axis_size("dp")
    devices = owners * groups
    rows_dev, width = item_table.shape
    bag_count = grad_pooled.shape[2]
    lines = row_index.shape[2] // LANES
    blocks = rows_dev // LANES
    prev_length = 2 * lines + bag_count * width // LANES
    vmem = pl.BlockSpec(memory_space=pltpu.VMEM)
    hbm = pl.BlockSpec(memory_space=pltpu.HBM)
    params = pltpu.CompilerParams(vmem_limit_bytes=16 * 1024 * 1024)
    chunk = min(devices, LANES // bag_count)

    def stay(x):
        return pltpu.with_memory_space_constraint(x, pltpu.HBM)

    def line(x):
        return x.reshape(lines, LANES)

    message = pl.pallas_call(
        functools.partial(pack_kernel, rows_dev),
        out_shape=pltpu.VMEM((owners, 2 * lines + prev_length, LANES), jnp.float32),
        in_specs=[hbm] * 7,
        out_specs=vmem,
        scratch_shapes=[pltpu.VMEM((lines, LANES), jnp.int32)] * 6
        + [pltpu.VMEM((bag_count, width), jnp.float32), pltpu.SemaphoreType.DMA((7,))],
        compiler_params=params,
        name="pack",
    )(*[stay(x) for x in (
        line(owner_map), line(row_index), line(bag_index),
        line(prev_owner), line(prev_row), line(prev_bag), grad_pooled[0, 0],
    )])
    gathered = lax.all_to_all(message, "rows", split_axis=0, concat_axis=0, tiled=True)

    pieces = 4
    kept = pl.pallas_call(
        prepare_kernel,
        out_shape=pltpu.VMEM((rows_dev, width), jnp.float32),
        in_specs=[hbm],
        out_specs=vmem,
        scratch_shapes=[pltpu.SemaphoreType.DMA((pieces,))],
        compiler_params=params,
        cost_estimate=pl.CostEstimate(
            flops=0, bytes_accessed=2 * rows_dev * width * 4, transcendentals=0),
        name="prepare",
    )(stay(item_table))

    partial_pooled, joined, go = pl.pallas_call(
        functools.partial(pool_kernel, bag_count, lines),
        out_shape=(
            pltpu.VMEM((owners, bag_count, width), jnp.float32),
            pltpu.VMEM((owners, prev_length, LANES), jnp.float32),
            jax.ShapeDtypeStruct((1, 1), jnp.int32),
        ),
        in_specs=[vmem] * 2,
        out_specs=[vmem] * 2 + [pl.BlockSpec(memory_space=pltpu.SMEM)],
        scratch_shapes=[
            pltpu.VMEM((owners, lines, LANES), jnp.float32),
            pltpu.VMEM((owners, lines, LANES), jnp.float32),
            pltpu.VMEM((blocks, owners * bag_count, LANES), jnp.float32),
        ],
        compiler_params=params,
        cost_estimate=pl.CostEstimate(
            flops=4 * owners * bag_count * rows_dev * width,
            bytes_accessed=rows_dev * width * 4, transcendentals=0),
        name="pool",
    )(gathered, kept)
    returned = lax.all_to_all(
        partial_pooled, "rows", split_axis=0, concat_axis=0, tiled=True)
    segments = chunk * bag_count

    def forward_and_update(joined, kept, row_accum):
        all_groups = [joined] + [shift(joined, "dp", k) for k in range(1, groups)]

        return pl.pallas_call(
            functools.partial(update_kernel, bag_count, lines, groups, chunk),
            out_shape=(
                pltpu.HBM((rows_dev, width), jnp.float32),
                pltpu.VMEM((blocks, LANES), jnp.float32),
            ),
            in_specs=[vmem] * (groups + 2),
            out_specs=(hbm, vmem),
            scratch_shapes=[
                pltpu.VMEM((devices, prev_length, LANES), jnp.float32),
                pltpu.VMEM((chunk, lines, LANES), jnp.float32),
                pltpu.VMEM((chunk, lines, LANES), jnp.float32),
                pltpu.VMEM((blocks, segments, LANES), jnp.float32),
                pltpu.VMEM((segments, width), jnp.float32),
                pltpu.VMEM((blocks, LANES, width) if devices > chunk else (1, 8, LANES), jnp.float32),
                pltpu.VMEM((rows_dev, width), jnp.float32),
                pltpu.SemaphoreType.DMA((pieces,)),
            ],
            compiler_params=params if devices == chunk else pltpu.CompilerParams(
                vmem_limit_bytes=40 * 1024 * 1024),
            cost_estimate=pl.CostEstimate(flops=1, bytes_accessed=1 << 20, transcendentals=0),
            name="update",
        )(*all_groups, kept, row_accum)

    def skip(joined, kept, row_accum):
        return pl.pallas_call(
            pass_kernel,
            out_shape=(
                pltpu.HBM((rows_dev, width), jnp.float32),
                pltpu.VMEM((blocks, LANES), jnp.float32),
            ),
            in_specs=[vmem] * 2,
            out_specs=(hbm, vmem),
            scratch_shapes=[pltpu.SemaphoreType.DMA],
            compiler_params=params,
            name="pass",
        )(kept, row_accum)

    new_table, new_accum = lax.cond(
        go[0, 0] > 0, forward_and_update, skip,
        joined, kept, row_accum.reshape(blocks, LANES))

    pooled, new_accum = pl.pallas_call(
        finish_kernel,
        out_shape=(
            jax.ShapeDtypeStruct((bag_count, width), jnp.float32),
            jax.ShapeDtypeStruct((blocks, LANES), jnp.float32),
        ),
        in_specs=[vmem] * 2,
        out_specs=[vmem] * 2,
        compiler_params=params,
        name="finish",
    )(returned, new_accum)
    return (pooled[None, None], new_table, new_accum.reshape(rows_dev))


def solution(mesh):
    placed = (
        P("rows", None),
        P("rows"),
        P("dp", "rows", None, None),
        P("dp", "rows", None),
        P("dp", "rows", None),
        P("dp", "rows", None, None),
        P("dp", "rows", None),
        P("dp", "rows", None),
        P("dp", "rows", None, None),
    )
    return jax.shard_map(
        local,
        mesh=mesh,
        in_specs=placed,
        out_specs=(P("dp", "rows", None, None), P("rows", None), P("rows")),
        check_vma=False,
    )
```

```python
import functools

import jax
import jax.numpy as jnp
from jax import lax
from jax.experimental import pallas as pl
from jax.experimental.pallas import tpu as pltpu
from jax.sharding import PartitionSpec as P

learn_rate = 0.1
LANES = 128


def pack_kernel(rows_dev, *refs):
    sources, out, held, sems = refs[:7], refs[7], refs[8:15], refs[15]
    copies = [
        pltpu.make_async_copy(source, place, sems.at[i])
        for i, (source, place) in enumerate(zip(sources, held))
    ]
    for copy in copies:
        copy.start()
    for copy in copies:
        copy.wait()
    owner, row, bag, prev_owner, prev_row, prev_bag, grad = held
    lines = row.shape[0]
    bag_count, width = grad.shape

    def put(start, value):
        shape = (out.shape[0],) + value.shape
        out[:, start:start + value.shape[0], :] = jnp.broadcast_to(value[None], shape)

    put(0, (owner[...] * rows_dev + row[...]).astype(jnp.float32))
    put(lines, bag[...].astype(jnp.float32))
    put(2 * lines, (prev_owner[...] * rows_dev + prev_row[...]).astype(jnp.float32))
    put(3 * lines, prev_bag[...].astype(jnp.float32))
    for k in range(width // LANES):
        put(4 * lines + k * bag_count, grad[:, k * LANES:(k + 1) * LANES])


def split_two(x):
    high = x.astype(jnp.bfloat16)
    return high, (x - high.astype(jnp.float32)).astype(jnp.bfloat16)


def prepare_kernel(table, kept, sems):
    pieces = sems.shape[0]
    rows = table.shape[0] // pieces
    copies = [
        pltpu.make_async_copy(
            table.at[pl.ds(i * rows, rows), :], kept.at[pl.ds(i * rows, rows), :], sems.at[i])
        for i in range(pieces)
    ]
    for copy in copies:
        copy.start()
    for copy in copies:
        copy.wait()


def codes(ids, bags, bag_count, base):
    rel = ids.astype(jnp.int32) - base
    code = lax.shift_right_arithmetic(rel, 7) * bag_count + bags.astype(jnp.int32)
    return code.astype(jnp.float32), (rel & (LANES - 1)).astype(jnp.float32)


def count_into(counts, code_ref, lane_ref, devices, bag_count):
    blocks = counts.shape[0]
    lines = code_ref.shape[1]
    one, none = jnp.ones((), jnp.bfloat16), jnp.zeros((), jnp.bfloat16)

    def one_hot(ref, d, size):
        numbers = lax.broadcasted_iota(jnp.int32, (size, LANES), 0).astype(jnp.bfloat16)
        parts = []
        for k in range(lines):
            row = jnp.broadcast_to(ref[d, k:k + 1, :], (size, LANES)).astype(jnp.bfloat16)
            parts.append(jnp.where(numbers == row, one, none))
        return jnp.concatenate(parts, axis=1)

    for d in range(devices):
        hits = lax.dot_general(
            one_hot(code_ref, d, blocks * bag_count), one_hot(lane_ref, d, LANES),
            (((1,), (1,)), ((), ())), preferred_element_type=jnp.float32)
        counts[:, d * bag_count:(d + 1) * bag_count, :] = hits.reshape(
            blocks, bag_count, LANES)


def pool_kernel(bag_count, lines, msg, table, out, joined, code_ref, lane_ref, counts):
    rows_dev, width = table.shape
    owners = msg.shape[0]
    base = lax.axis_index("rows") * rows_dev
    code_ref[...], lane_ref[...] = codes(
        msg[:, 0:lines, :], msg[:, lines:2 * lines, :], bag_count, base)
    joined[...] = msg[:, 2 * lines:, :]
    count_into(counts, code_ref, lane_ref, owners, bag_count)
    blocks = rows_dev // LANES
    flat = jnp.concatenate(
        [counts[h].astype(jnp.bfloat16) for h in range(blocks)], axis=1)
    total = jnp.zeros((owners * bag_count, width), jnp.float32)
    for part in split_two(table[...]):
        total += jnp.dot(flat, part, preferred_element_type=jnp.float32)
    out[...] = total.reshape(out.shape)


def update_kernel(bag_count, lines, groups, chunk, *refs):
    sources, (table, accum, new_table, new_accum) = refs[:groups], refs[groups:groups + 4]
    msg, code_ref, lane_ref, counts, grads, sums, fresh_table, sems = refs[groups + 4:]
    rows_dev, width = table.shape
    pieces = sems.shape[0]
    devices = msg.shape[0]
    owners = devices // groups
    blocks = counts.shape[0]
    base = lax.axis_index("rows") * rows_dev
    single = devices == chunk

    def count_chunk(first):
        here = pl.ds(first, chunk)
        code_ref[...], lane_ref[...] = codes(
            msg[here, 0:lines, :], msg[here, lines:2 * lines, :], bag_count, base)
        count_into(counts, code_ref, lane_ref, chunk, bag_count)
        for k in range(width // LANES):
            start = 2 * lines + k * bag_count
            grads[:, k * LANES:(k + 1) * LANES] = msg[
                here, start:start + bag_count, :].reshape(chunk * bag_count, LANES)
        return split_two(grads[...])

    def block_sum(h, parts):
        hits = counts[h].astype(jnp.bfloat16)
        total = jnp.zeros((LANES, width), jnp.float32)
        for part in parts:
            total += lax.dot_general(
                hits, part, (((0,), (0,)), ((), ())), preferred_element_type=jnp.float32)
        return total

    for i, source in enumerate(sources):
        msg[i * owners:(i + 1) * owners] = source[...]
    if single:
        parts = count_chunk(0)
    else:
        sums[...] = jnp.zeros_like(sums)

        @pl.loop(0, devices // chunk)
        def _(c):
            parts = count_chunk(c * chunk)

            @pl.loop(0, blocks)
            def _(h):
                sums[h] += block_sum(h, parts)

    diagonal = (
        lax.broadcasted_iota(jnp.int32, (LANES, LANES), 0)
        == lax.broadcasted_iota(jnp.int32, (LANES, LANES), 1))
    per_piece = blocks // pieces
    copies = []
    for h in range(blocks):
        i = h // per_piece
        grad = block_sum(h, parts) if single else sums[h]
        here = slice(h * LANES, (h + 1) * LANES)
        squares = grad * grad
        folded = squares[:, 0:LANES]
        for k in range(1, width // LANES):
            folded += squares[:, k * LANES:(k + 1) * LANES]
        old = jnp.where(diagonal, accum[h:h + 1, :], 0.0)
        fresh = jnp.sum(folded * (1.0 / width) + old, axis=1, keepdims=True)
        fresh_table[here, :] = table[here, :] - grad * (learn_rate * lax.rsqrt(fresh))
        new_accum[h:h + 1, :] = jnp.sum(
            jnp.where(diagonal, fresh, 0.0), axis=0, keepdims=True)
        if (h + 1) % per_piece == 0:
            piece = pl.ds(i * per_piece * LANES, per_piece * LANES)
            copies.append(pltpu.make_async_copy(
                fresh_table.at[piece, :], new_table.at[piece, :], sems.at[i]))
            copies[-1].start()
    for copy in copies:
        copy.wait()


def finish_kernel(returned, accum, pooled, new_accum):
    total = returned[0]
    for i in range(1, returned.shape[0]):
        total += returned[i]
    pooled[...] = total
    new_accum[...] = accum[...]


def exchange(x, axis):
    size = lax.axis_size(axis)
    order = [(i + size // 2) % size for i in range(size)]
    return lax.all_to_all(
        x, axis, split_axis=0, concat_axis=0, axis_index_groups=[order], tiled=True)


def shift(x, axis, step):
    size = lax.axis_size(axis)
    return lax.ppermute(x, axis, [(i, (i + step) % size) for i in range(size)])


def local(
    item_table, row_accum, owner_map, row_index, bag_index,
    prev_owner, prev_row, prev_bag, grad_pooled,
):
    owners, groups = lax.axis_size("rows"), lax.axis_size("dp")
    devices = owners * groups
    rows_dev, width = item_table.shape
    bag_count = grad_pooled.shape[2]
    lines = row_index.shape[2] // LANES
    blocks = rows_dev // LANES
    prev_length = 2 * lines + bag_count * width // LANES
    vmem = pl.BlockSpec(memory_space=pltpu.VMEM)
    hbm = pl.BlockSpec(memory_space=pltpu.HBM)
    params = pltpu.CompilerParams(vmem_limit_bytes=16 * 1024 * 1024)
    chunk = min(devices, LANES // bag_count)

    def stay(x):
        return pltpu.with_memory_space_constraint(x, pltpu.HBM)

    def line(x):
        return x.reshape(lines, LANES)

    message = pl.pallas_call(
        functools.partial(pack_kernel, rows_dev),
        out_shape=pltpu.VMEM((owners, 2 * lines + prev_length, LANES), jnp.float32),
        in_specs=[hbm] * 7,
        out_specs=vmem,
        scratch_shapes=[pltpu.VMEM((lines, LANES), jnp.int32)] * 6
        + [pltpu.VMEM((bag_count, width), jnp.float32), pltpu.SemaphoreType.DMA((7,))],
        compiler_params=params,
        name="pack",
    )(*[stay(x) for x in (
        line(owner_map), line(row_index), line(bag_index),
        line(prev_owner), line(prev_row), line(prev_bag), grad_pooled[0, 0],
    )])
    gathered = exchange(message, "rows")

    pieces = 4
    kept = pl.pallas_call(
        prepare_kernel,
        out_shape=pltpu.VMEM((rows_dev, width), jnp.float32),
        in_specs=[hbm],
        out_specs=vmem,
        scratch_shapes=[pltpu.SemaphoreType.DMA((pieces,))],
        compiler_params=params,
        cost_estimate=pl.CostEstimate(
            flops=0, bytes_accessed=2 * rows_dev * width * 4, transcendentals=0),
        name="prepare",
    )(stay(item_table))

    partial_pooled, joined = pl.pallas_call(
        functools.partial(pool_kernel, bag_count, lines),
        out_shape=(
            pltpu.VMEM((owners, bag_count, width), jnp.float32),
            pltpu.VMEM((owners, prev_length, LANES), jnp.float32),
        ),
        in_specs=[vmem] * 2,
        out_specs=[vmem] * 2,
        scratch_shapes=[
            pltpu.VMEM((owners, lines, LANES), jnp.float32),
            pltpu.VMEM((owners, lines, LANES), jnp.float32),
            pltpu.VMEM((blocks, owners * bag_count, LANES), jnp.float32),
        ],
        compiler_params=params,
        cost_estimate=pl.CostEstimate(
            flops=4 * owners * bag_count * rows_dev * width,
            bytes_accessed=rows_dev * width * 4, transcendentals=0),
        name="pool",
    )(gathered, kept)
    returned = exchange(partial_pooled, "rows")
    all_groups = [joined] + [shift(joined, "dp", k) for k in range(1, groups)]

    segments = chunk * bag_count
    new_table, new_accum = pl.pallas_call(
        functools.partial(update_kernel, bag_count, lines, groups, chunk),
        out_shape=(
            jax.ShapeDtypeStruct((rows_dev, width), jnp.float32),
            pltpu.VMEM((blocks, LANES), jnp.float32),
        ),
        in_specs=[vmem] * (groups + 2),
        out_specs=(hbm, vmem),
        scratch_shapes=[
            pltpu.VMEM((devices, prev_length, LANES), jnp.float32),
            pltpu.VMEM((chunk, lines, LANES), jnp.float32),
            pltpu.VMEM((chunk, lines, LANES), jnp.float32),
            pltpu.VMEM((blocks, segments, LANES), jnp.float32),
            pltpu.VMEM((segments, width), jnp.float32),
            pltpu.VMEM((blocks, LANES, width) if devices > chunk else (1, 8, LANES), jnp.float32),
            pltpu.VMEM((rows_dev, width), jnp.float32),
            pltpu.SemaphoreType.DMA((pieces,)),
        ],
        compiler_params=params if devices == chunk else pltpu.CompilerParams(
            vmem_limit_bytes=40 * 1024 * 1024),
        cost_estimate=pl.CostEstimate(flops=1, bytes_accessed=1 << 20, transcendentals=0),
        name="update",
    )(*all_groups, kept, row_accum.reshape(blocks, LANES))

    pooled, new_accum = pl.pallas_call(
        finish_kernel,
        out_shape=(
            jax.ShapeDtypeStruct((bag_count, width), jnp.float32),
            jax.ShapeDtypeStruct((blocks, LANES), jnp.float32),
        ),
        in_specs=[vmem] * 2,
        out_specs=[vmem] * 2,
        compiler_params=params,
        name="finish",
    )(returned, new_accum)
    return (pooled[None, None], new_table, new_accum.reshape(rows_dev))


def solution(mesh):
    placed = (
        P("rows", None),
        P("rows"),
        P("dp", "rows", None, None),
        P("dp", "rows", None),
        P("dp", "rows", None),
        P("dp", "rows", None, None),
        P("dp", "rows", None),
        P("dp", "rows", None),
        P("dp", "rows", None, None),
    )
    return jax.shard_map(
        local,
        mesh=mesh,
        in_specs=placed,
        out_specs=(P("dp", "rows", None, None), P("rows", None), P("rows")),
        check_vma=False,
    )
```

```python
import functools

import jax
import jax.numpy as jnp
from jax import lax
from jax.experimental import pallas as pl
from jax.experimental.pallas import tpu as pltpu
from jax.sharding import PartitionSpec as P

learn_rate = 0.1
LANES = 128


def pack_kernel(rows_dev, *refs):
    sources, out, held, sems = refs[:7], refs[7], refs[8:15], refs[15]
    copies = [
        pltpu.make_async_copy(source, place, sems.at[i])
        for i, (source, place) in enumerate(zip(sources, held))
    ]
    for copy in copies:
        copy.start()
    for copy in copies:
        copy.wait()
    owner, row, bag, prev_owner, prev_row, prev_bag, grad = held
    lines = row.shape[0]
    bag_count, width = grad.shape

    def put(start, value):
        shape = (out.shape[0],) + value.shape
        out[:, start:start + value.shape[0], :] = jnp.broadcast_to(value[None], shape)

    put(0, (owner[...] * rows_dev + row[...]).astype(jnp.float32))
    put(lines, bag[...].astype(jnp.float32))
    put(2 * lines, (prev_owner[...] * rows_dev + prev_row[...]).astype(jnp.float32))
    put(3 * lines, prev_bag[...].astype(jnp.float32))
    for k in range(width // LANES):
        put(4 * lines + k * bag_count, grad[:, k * LANES:(k + 1) * LANES])


def split_two(x):
    high = x.astype(jnp.bfloat16)
    return high, (x - high.astype(jnp.float32)).astype(jnp.bfloat16)


def prepare_kernel(table, kept, sems):
    pieces = sems.shape[0]
    rows = table.shape[0] // pieces
    copies = [
        pltpu.make_async_copy(
            table.at[pl.ds(i * rows, rows), :], kept.at[pl.ds(i * rows, rows), :], sems.at[i])
        for i in range(pieces)
    ]
    for copy in copies:
        copy.start()
    for copy in copies:
        copy.wait()


def codes(ids, bags, bag_count, base):
    rel = ids.astype(jnp.int32) - base
    code = lax.shift_right_arithmetic(rel, 7) * bag_count + bags.astype(jnp.int32)
    return code.astype(jnp.float32), (rel & (LANES - 1)).astype(jnp.float32)


def count_into(counts, code_ref, lane_ref, devices, bag_count):
    blocks = counts.shape[0]
    lines = code_ref.shape[1]
    one, none = jnp.ones((), jnp.bfloat16), jnp.zeros((), jnp.bfloat16)

    def one_hot(ref, d, size):
        numbers = lax.broadcasted_iota(jnp.int32, (size, LANES), 0).astype(jnp.bfloat16)
        parts = []
        for k in range(lines):
            row = jnp.broadcast_to(ref[d, k:k + 1, :], (size, LANES)).astype(jnp.bfloat16)
            parts.append(jnp.where(numbers == row, one, none))
        return jnp.concatenate(parts, axis=1)

    for d in range(devices):
        hits = lax.dot_general(
            one_hot(code_ref, d, blocks * bag_count), one_hot(lane_ref, d, LANES),
            (((1,), (1,)), ((), ())), preferred_element_type=jnp.float32)
        counts[:, d * bag_count:(d + 1) * bag_count, :] = hits.reshape(
            blocks, bag_count, LANES)


def pool_kernel(bag_count, lines, msg, table, out, joined, code_ref, lane_ref, counts):
    rows_dev, width = table.shape
    owners = msg.shape[0]
    base = lax.axis_index("rows") * rows_dev
    code_ref[...], lane_ref[...] = codes(
        msg[:, 0:lines, :], msg[:, lines:2 * lines, :], bag_count, base)
    joined[...] = msg[:, 2 * lines:, :]
    count_into(counts, code_ref, lane_ref, owners, bag_count)
    blocks = rows_dev // LANES
    flat = jnp.concatenate(
        [counts[h].astype(jnp.bfloat16) for h in range(blocks)], axis=1)
    total = jnp.zeros((owners * bag_count, width), jnp.float32)
    for part in split_two(table[...]):
        total += jnp.dot(flat, part, preferred_element_type=jnp.float32)
    out[...] = total.reshape(out.shape)


def update_kernel(bag_count, lines, groups, chunk, *refs):
    sources, (table, accum, new_table, new_accum) = refs[:groups], refs[groups:groups + 4]
    msg, code_ref, lane_ref, counts, grads, sums, fresh_table, sems = refs[groups + 4:]
    rows_dev, width = table.shape
    pieces = sems.shape[0]
    devices = msg.shape[0]
    owners = devices // groups
    blocks = counts.shape[0]
    base = lax.axis_index("rows") * rows_dev
    single = devices == chunk

    def count_chunk(first):
        here = pl.ds(first, chunk)
        code_ref[...], lane_ref[...] = codes(
            msg[here, 0:lines, :], msg[here, lines:2 * lines, :], bag_count, base)
        count_into(counts, code_ref, lane_ref, chunk, bag_count)
        for k in range(width // LANES):
            start = 2 * lines + k * bag_count
            grads[:, k * LANES:(k + 1) * LANES] = msg[
                here, start:start + bag_count, :].reshape(chunk * bag_count, LANES)
        return split_two(grads[...])

    def block_sum(h, parts):
        hits = counts[h].astype(jnp.bfloat16)
        total = jnp.zeros((LANES, width), jnp.float32)
        for part in parts:
            total += lax.dot_general(
                hits, part, (((0,), (0,)), ((), ())), preferred_element_type=jnp.float32)
        return total

    for i, source in enumerate(sources):
        msg[i * owners:(i + 1) * owners] = source[...]
    if single:
        parts = count_chunk(0)
    else:
        sums[...] = jnp.zeros_like(sums)

        @pl.loop(0, devices // chunk)
        def _(c):
            parts = count_chunk(c * chunk)

            @pl.loop(0, blocks)
            def _(h):
                sums[h] += block_sum(h, parts)

    diagonal = (
        lax.broadcasted_iota(jnp.int32, (LANES, LANES), 0)
        == lax.broadcasted_iota(jnp.int32, (LANES, LANES), 1))
    per_piece = blocks // pieces
    copies = []
    for h in range(blocks):
        i = h // per_piece
        grad = block_sum(h, parts) if single else sums[h]
        here = slice(h * LANES, (h + 1) * LANES)
        squares = grad * grad
        folded = squares[:, 0:LANES]
        for k in range(1, width // LANES):
            folded += squares[:, k * LANES:(k + 1) * LANES]
        old = jnp.where(diagonal, accum[h:h + 1, :], 0.0)
        fresh = jnp.sum(folded * (1.0 / width) + old, axis=1, keepdims=True)
        fresh_table[here, :] = table[here, :] - grad * (learn_rate * lax.rsqrt(fresh))
        new_accum[h:h + 1, :] = jnp.sum(
            jnp.where(diagonal, fresh, 0.0), axis=0, keepdims=True)
        if (h + 1) % per_piece == 0:
            piece = pl.ds(i * per_piece * LANES, per_piece * LANES)
            copies.append(pltpu.make_async_copy(
                fresh_table.at[piece, :], new_table.at[piece, :], sems.at[i]))
            copies[-1].start()
    for copy in copies:
        copy.wait()


def finish_kernel(returned, accum, pooled, new_accum):
    total = returned[0]
    for i in range(1, returned.shape[0]):
        total += returned[i]
    pooled[...] = total
    new_accum[...] = accum[...]


def exchange(x, axis):
    size = lax.axis_size(axis)
    order = [(i + size // 2 - 1) % size for i in range(size)]
    return lax.all_to_all(
        x, axis, split_axis=0, concat_axis=0, axis_index_groups=[order], tiled=True)


def shift(x, axis, step):
    size = lax.axis_size(axis)
    return lax.ppermute(x, axis, [(i, (i + step) % size) for i in range(size)])


def local(
    item_table, row_accum, owner_map, row_index, bag_index,
    prev_owner, prev_row, prev_bag, grad_pooled,
):
    owners, groups = lax.axis_size("rows"), lax.axis_size("dp")
    devices = owners * groups
    rows_dev, width = item_table.shape
    bag_count = grad_pooled.shape[2]
    lines = row_index.shape[2] // LANES
    blocks = rows_dev // LANES
    prev_length = 2 * lines + bag_count * width // LANES
    vmem = pl.BlockSpec(memory_space=pltpu.VMEM)
    hbm = pl.BlockSpec(memory_space=pltpu.HBM)
    params = pltpu.CompilerParams(vmem_limit_bytes=16 * 1024 * 1024)
    chunk = min(devices, LANES // bag_count)

    def stay(x):
        return pltpu.with_memory_space_constraint(x, pltpu.HBM)

    def line(x):
        return x.reshape(lines, LANES)

    message = pl.pallas_call(
        functools.partial(pack_kernel, rows_dev),
        out_shape=pltpu.VMEM((owners, 2 * lines + prev_length, LANES), jnp.float32),
        in_specs=[hbm] * 7,
        out_specs=vmem,
        scratch_shapes=[pltpu.VMEM((lines, LANES), jnp.int32)] * 6
        + [pltpu.VMEM((bag_count, width), jnp.float32), pltpu.SemaphoreType.DMA((7,))],
        compiler_params=params,
        name="pack",
    )(*[stay(x) for x in (
        line(owner_map), line(row_index), line(bag_index),
        line(prev_owner), line(prev_row), line(prev_bag), grad_pooled[0, 0],
    )])
    gathered = exchange(message, "rows")

    pieces = 4
    kept = pl.pallas_call(
        prepare_kernel,
        out_shape=pltpu.VMEM((rows_dev, width), jnp.float32),
        in_specs=[hbm],
        out_specs=vmem,
        scratch_shapes=[pltpu.SemaphoreType.DMA((pieces,))],
        compiler_params=params,
        cost_estimate=pl.CostEstimate(
            flops=0, bytes_accessed=2 * rows_dev * width * 4, transcendentals=0),
        name="prepare",
    )(stay(item_table))

    partial_pooled, joined = pl.pallas_call(
        functools.partial(pool_kernel, bag_count, lines),
        out_shape=(
            pltpu.VMEM((owners, bag_count, width), jnp.float32),
            pltpu.VMEM((owners, prev_length, LANES), jnp.float32),
        ),
        in_specs=[vmem] * 2,
        out_specs=[vmem] * 2,
        scratch_shapes=[
            pltpu.VMEM((owners, lines, LANES), jnp.float32),
            pltpu.VMEM((owners, lines, LANES), jnp.float32),
            pltpu.VMEM((blocks, owners * bag_count, LANES), jnp.float32),
        ],
        compiler_params=params,
        cost_estimate=pl.CostEstimate(
            flops=4 * owners * bag_count * rows_dev * width,
            bytes_accessed=rows_dev * width * 4, transcendentals=0),
        name="pool",
    )(gathered, kept)
    returned = exchange(partial_pooled, "rows")
    all_groups = [joined] + [shift(joined, "dp", k) for k in range(1, groups)]

    segments = chunk * bag_count
    new_table, new_accum = pl.pallas_call(
        functools.partial(update_kernel, bag_count, lines, groups, chunk),
        out_shape=(
            jax.ShapeDtypeStruct((rows_dev, width), jnp.float32),
            pltpu.VMEM((blocks, LANES), jnp.float32),
        ),
        in_specs=[vmem] * (groups + 2),
        out_specs=(hbm, vmem),
        scratch_shapes=[
            pltpu.VMEM((devices, prev_length, LANES), jnp.float32),
            pltpu.VMEM((chunk, lines, LANES), jnp.float32),
            pltpu.VMEM((chunk, lines, LANES), jnp.float32),
            pltpu.VMEM((blocks, segments, LANES), jnp.float32),
            pltpu.VMEM((segments, width), jnp.float32),
            pltpu.VMEM((blocks, LANES, width) if devices > chunk else (1, 8, LANES), jnp.float32),
            pltpu.VMEM((rows_dev, width), jnp.float32),
            pltpu.SemaphoreType.DMA((pieces,)),
        ],
        compiler_params=params if devices == chunk else pltpu.CompilerParams(
            vmem_limit_bytes=40 * 1024 * 1024),
        cost_estimate=pl.CostEstimate(flops=1, bytes_accessed=1 << 20, transcendentals=0),
        name="update",
    )(*all_groups, kept, row_accum.reshape(blocks, LANES))

    pooled, new_accum = pl.pallas_call(
        finish_kernel,
        out_shape=(
            jax.ShapeDtypeStruct((bag_count, width), jnp.float32),
            jax.ShapeDtypeStruct((blocks, LANES), jnp.float32),
        ),
        in_specs=[vmem] * 2,
        out_specs=[vmem] * 2,
        compiler_params=params,
        name="finish",
    )(returned, new_accum)
    return (pooled[None, None], new_table, new_accum.reshape(rows_dev))


def solution(mesh):
    placed = (
        P("rows", None),
        P("rows"),
        P("dp", "rows", None, None),
        P("dp", "rows", None),
        P("dp", "rows", None),
        P("dp", "rows", None, None),
        P("dp", "rows", None),
        P("dp", "rows", None),
        P("dp", "rows", None, None),
    )
    return jax.shard_map(
        local,
        mesh=mesh,
        in_specs=placed,
        out_specs=(P("dp", "rows", None, None), P("rows", None), P("rows")),
        check_vma=False,
    )
```

```python
import functools

import jax
import jax.numpy as jnp
from jax import lax
from jax.experimental import pallas as pl
from jax.experimental.pallas import tpu as pltpu
from jax.sharding import PartitionSpec as P

learn_rate = 0.1
LANES = 128


def pack_kernel(rows_dev, *refs):
    sources, out, held, sems = refs[:7], refs[7], refs[8:15], refs[15]
    copies = [
        pltpu.make_async_copy(source, place, sems.at[i])
        for i, (source, place) in enumerate(zip(sources, held))
    ]
    for copy in copies:
        copy.start()
    for copy in copies:
        copy.wait()
    owner, row, bag, prev_owner, prev_row, prev_bag, grad = held
    lines = row.shape[0]
    bag_count, width = grad.shape

    def put(start, value):
        shape = (out.shape[0],) + value.shape
        out[:, start:start + value.shape[0], :] = jnp.broadcast_to(value[None], shape)

    put(0, (owner[...] * rows_dev + row[...]).astype(jnp.float32))
    put(lines, bag[...].astype(jnp.float32))
    put(2 * lines, (prev_owner[...] * rows_dev + prev_row[...]).astype(jnp.float32))
    put(3 * lines, prev_bag[...].astype(jnp.float32))
    for k in range(width // LANES):
        put(4 * lines + k * bag_count, grad[:, k * LANES:(k + 1) * LANES])


def split_two(x):
    high = x.astype(jnp.bfloat16)
    return high, (x - high.astype(jnp.float32)).astype(jnp.bfloat16)


def prepare_kernel(table, kept, sems):
    pieces = sems.shape[0]
    rows = table.shape[0] // pieces
    copies = [
        pltpu.make_async_copy(
            table.at[pl.ds(i * rows, rows), :], kept.at[pl.ds(i * rows, rows), :], sems.at[i])
        for i in range(pieces)
    ]
    for copy in copies:
        copy.start()
    for copy in copies:
        copy.wait()


def codes(ids, bags, bag_count, base):
    rel = ids.astype(jnp.int32) - base
    code = lax.shift_right_arithmetic(rel, 7) * bag_count + bags.astype(jnp.int32)
    return code.astype(jnp.float32), (rel & (LANES - 1)).astype(jnp.float32)


def count_into(counts, code_ref, lane_ref, devices, bag_count):
    blocks = counts.shape[0]
    lines = code_ref.shape[1]
    one, none = jnp.ones((), jnp.bfloat16), jnp.zeros((), jnp.bfloat16)

    def one_hot(ref, d, size):
        numbers = lax.broadcasted_iota(jnp.int32, (size, LANES), 0).astype(jnp.bfloat16)
        parts = []
        for k in range(lines):
            row = jnp.broadcast_to(ref[d, k:k + 1, :], (size, LANES)).astype(jnp.bfloat16)
            parts.append(jnp.where(numbers == row, one, none))
        return jnp.concatenate(parts, axis=1)

    for d in range(devices):
        hits = lax.dot_general(
            one_hot(code_ref, d, blocks * bag_count), one_hot(lane_ref, d, LANES),
            (((1,), (1,)), ((), ())), preferred_element_type=jnp.float32)
        counts[:, d * bag_count:(d + 1) * bag_count, :] = hits.reshape(
            blocks, bag_count, LANES)


def pool_kernel(bag_count, lines, turn, msg, table, out, joined, code_ref, lane_ref, counts):
    rows_dev, width = table.shape
    owners = msg.shape[0]
    base = lax.axis_index("rows") * rows_dev
    code_ref[...], lane_ref[...] = codes(
        msg[:, 0:lines, :], msg[:, lines:2 * lines, :], bag_count, base)
    joined[...] = msg[:, 2 * lines:, :]
    count_into(counts, code_ref, lane_ref, owners, bag_count)
    blocks = rows_dev // LANES
    flat = jnp.concatenate(
        [counts[h].astype(jnp.bfloat16) for h in range(blocks)], axis=1)
    total = jnp.zeros((owners * bag_count, width), jnp.float32)
    for part in split_two(table[...]):
        total += jnp.dot(flat, part, preferred_element_type=jnp.float32)
    for i in range(owners):
        seen = (i + turn) % owners
        out[i] = total[seen * bag_count:(seen + 1) * bag_count, :]


def update_kernel(bag_count, lines, groups, chunk, *refs):
    sources, (table, accum, new_table, new_accum) = refs[:groups], refs[groups:groups + 4]
    msg, code_ref, lane_ref, counts, grads, sums, fresh_table, sems = refs[groups + 4:]
    rows_dev, width = table.shape
    pieces = sems.shape[0]
    devices = msg.shape[0]
    owners = devices // groups
    blocks = counts.shape[0]
    base = lax.axis_index("rows") * rows_dev
    single = devices == chunk

    def count_chunk(first):
        here = pl.ds(first, chunk)
        code_ref[...], lane_ref[...] = codes(
            msg[here, 0:lines, :], msg[here, lines:2 * lines, :], bag_count, base)
        count_into(counts, code_ref, lane_ref, chunk, bag_count)
        for k in range(width // LANES):
            start = 2 * lines + k * bag_count
            grads[:, k * LANES:(k + 1) * LANES] = msg[
                here, start:start + bag_count, :].reshape(chunk * bag_count, LANES)
        return split_two(grads[...])

    def block_sum(h, parts):
        hits = counts[h].astype(jnp.bfloat16)
        total = jnp.zeros((LANES, width), jnp.float32)
        for part in parts:
            total += lax.dot_general(
                hits, part, (((0,), (0,)), ((), ())), preferred_element_type=jnp.float32)
        return total

    for i, source in enumerate(sources):
        msg[i * owners:(i + 1) * owners] = source[...]
    if single:
        parts = count_chunk(0)
    else:
        sums[...] = jnp.zeros_like(sums)

        @pl.loop(0, devices // chunk)
        def _(c):
            parts = count_chunk(c * chunk)

            @pl.loop(0, blocks)
            def _(h):
                sums[h] += block_sum(h, parts)

    diagonal = (
        lax.broadcasted_iota(jnp.int32, (LANES, LANES), 0)
        == lax.broadcasted_iota(jnp.int32, (LANES, LANES), 1))
    per_piece = blocks // pieces
    copies = []
    for h in range(blocks):
        i = h // per_piece
        grad = block_sum(h, parts) if single else sums[h]
        here = slice(h * LANES, (h + 1) * LANES)
        squares = grad * grad
        folded = squares[:, 0:LANES]
        for k in range(1, width // LANES):
            folded += squares[:, k * LANES:(k + 1) * LANES]
        old = jnp.where(diagonal, accum[h:h + 1, :], 0.0)
        fresh = jnp.sum(folded * (1.0 / width) + old, axis=1, keepdims=True)
        fresh_table[here, :] = table[here, :] - grad * (learn_rate * lax.rsqrt(fresh))
        new_accum[h:h + 1, :] = jnp.sum(
            jnp.where(diagonal, fresh, 0.0), axis=0, keepdims=True)
        if (h + 1) % per_piece == 0:
            piece = pl.ds(i * per_piece * LANES, per_piece * LANES)
            copies.append(pltpu.make_async_copy(
                fresh_table.at[piece, :], new_table.at[piece, :], sems.at[i]))
            copies[-1].start()
    for copy in copies:
        copy.wait()


def finish_kernel(returned, accum, pooled, new_accum):
    total = returned[0]
    for i in range(1, returned.shape[0]):
        total += returned[i]
    pooled[...] = total
    new_accum[...] = accum[...]


def listing(size, leader):
    return [(i + leader) % size for i in range(size)]


def exchange(x, axis, leader):
    order = listing(lax.axis_size(axis), leader)
    return lax.all_to_all(
        x, axis, split_axis=0, concat_axis=0, axis_index_groups=[order], tiled=True)


def shift(x, axis, step):
    size = lax.axis_size(axis)
    return lax.ppermute(x, axis, [(i, (i + step) % size) for i in range(size)])


def local(
    item_table, row_accum, owner_map, row_index, bag_index,
    prev_owner, prev_row, prev_bag, grad_pooled,
):
    owners, groups = lax.axis_size("rows"), lax.axis_size("dp")
    devices = owners * groups
    out_leader, back_leader = owners // 2 - 1, owners // 2
    rows_dev, width = item_table.shape
    bag_count = grad_pooled.shape[2]
    lines = row_index.shape[2] // LANES
    blocks = rows_dev // LANES
    prev_length = 2 * lines + bag_count * width // LANES
    vmem = pl.BlockSpec(memory_space=pltpu.VMEM)
    hbm = pl.BlockSpec(memory_space=pltpu.HBM)
    params = pltpu.CompilerParams(vmem_limit_bytes=16 * 1024 * 1024)
    chunk = min(devices, LANES // bag_count)

    def stay(x):
        return pltpu.with_memory_space_constraint(x, pltpu.HBM)

    def line(x):
        return x.reshape(lines, LANES)

    message = pl.pallas_call(
        functools.partial(pack_kernel, rows_dev),
        out_shape=pltpu.VMEM((owners, 2 * lines + prev_length, LANES), jnp.float32),
        in_specs=[hbm] * 7,
        out_specs=vmem,
        scratch_shapes=[pltpu.VMEM((lines, LANES), jnp.int32)] * 6
        + [pltpu.VMEM((bag_count, width), jnp.float32), pltpu.SemaphoreType.DMA((7,))],
        compiler_params=params,
        name="pack",
    )(*[stay(x) for x in (
        line(owner_map), line(row_index), line(bag_index),
        line(prev_owner), line(prev_row), line(prev_bag), grad_pooled[0, 0],
    )])
    gathered = exchange(message, "rows", out_leader)

    pieces = 4
    kept = pl.pallas_call(
        prepare_kernel,
        out_shape=pltpu.VMEM((rows_dev, width), jnp.float32),
        in_specs=[hbm],
        out_specs=vmem,
        scratch_shapes=[pltpu.SemaphoreType.DMA((pieces,))],
        compiler_params=params,
        cost_estimate=pl.CostEstimate(
            flops=0, bytes_accessed=2 * rows_dev * width * 4, transcendentals=0),
        name="prepare",
    )(stay(item_table))

    partial_pooled, joined = pl.pallas_call(
        functools.partial(pool_kernel, bag_count, lines, back_leader - out_leader),
        out_shape=(
            pltpu.VMEM((owners, bag_count, width), jnp.float32),
            pltpu.VMEM((owners, prev_length, LANES), jnp.float32),
        ),
        in_specs=[vmem] * 2,
        out_specs=[vmem] * 2,
        scratch_shapes=[
            pltpu.VMEM((owners, lines, LANES), jnp.float32),
            pltpu.VMEM((owners, lines, LANES), jnp.float32),
            pltpu.VMEM((blocks, owners * bag_count, LANES), jnp.float32),
        ],
        compiler_params=params,
        cost_estimate=pl.CostEstimate(
            flops=4 * owners * bag_count * rows_dev * width,
            bytes_accessed=rows_dev * width * 4, transcendentals=0),
        name="pool",
    )(gathered, kept)
    returned = exchange(partial_pooled, "rows", back_leader)
    all_groups = [joined] + [shift(joined, "dp", k) for k in range(1, groups)]

    segments = chunk * bag_count
    new_table, new_accum = pl.pallas_call(
        functools.partial(update_kernel, bag_count, lines, groups, chunk),
        out_shape=(
            jax.ShapeDtypeStruct((rows_dev, width), jnp.float32),
            pltpu.VMEM((blocks, LANES), jnp.float32),
        ),
        in_specs=[vmem] * (groups + 2),
        out_specs=(hbm, vmem),
        scratch_shapes=[
            pltpu.VMEM((devices, prev_length, LANES), jnp.float32),
            pltpu.VMEM((chunk, lines, LANES), jnp.float32),
            pltpu.VMEM((chunk, lines, LANES), jnp.float32),
            pltpu.VMEM((blocks, segments, LANES), jnp.float32),
            pltpu.VMEM((segments, width), jnp.float32),
            pltpu.VMEM((blocks, LANES, width) if devices > chunk else (1, 8, LANES), jnp.float32),
            pltpu.VMEM((rows_dev, width), jnp.float32),
            pltpu.SemaphoreType.DMA((pieces,)),
        ],
        compiler_params=params if devices == chunk else pltpu.CompilerParams(
            vmem_limit_bytes=40 * 1024 * 1024),
        cost_estimate=pl.CostEstimate(flops=1, bytes_accessed=1 << 20, transcendentals=0),
        name="update",
    )(*all_groups, kept, row_accum.reshape(blocks, LANES))

    pooled, new_accum = pl.pallas_call(
        finish_kernel,
        out_shape=(
            jax.ShapeDtypeStruct((bag_count, width), jnp.float32),
            jax.ShapeDtypeStruct((blocks, LANES), jnp.float32),
        ),
        in_specs=[vmem] * 2,
        out_specs=[vmem] * 2,
        compiler_params=params,
        name="finish",
    )(returned, new_accum)
    return (pooled[None, None], new_table, new_accum.reshape(rows_dev))


def solution(mesh):
    placed = (
        P("rows", None),
        P("rows"),
        P("dp", "rows", None, None),
        P("dp", "rows", None),
        P("dp", "rows", None),
        P("dp", "rows", None, None),
        P("dp", "rows", None),
        P("dp", "rows", None),
        P("dp", "rows", None, None),
    )
    return jax.shard_map(
        local,
        mesh=mesh,
        in_specs=placed,
        out_specs=(P("dp", "rows", None, None), P("rows", None), P("rows")),
        check_vma=False,
    )
```

```python
import functools

import jax
import jax.numpy as jnp
from jax import lax
from jax.experimental import pallas as pl
from jax.experimental.pallas import tpu as pltpu
from jax.sharding import PartitionSpec as P

learn_rate = 0.1
LANES = 128


def pack_kernel(rows_dev, *refs):
    sources, out, held, sems = refs[:7], refs[7], refs[8:15], refs[15]
    copies = [
        pltpu.make_async_copy(source, place, sems.at[i])
        for i, (source, place) in enumerate(zip(sources, held))
    ]
    for copy in copies:
        copy.start()
    for copy in copies:
        copy.wait()
    owner, row, bag, prev_owner, prev_row, prev_bag, grad = held
    lines = row.shape[0]
    bag_count, width = grad.shape

    def put(start, value):
        shape = (out.shape[0],) + value.shape
        out[:, start:start + value.shape[0], :] = jnp.broadcast_to(value[None], shape)

    put(0, (owner[...] * rows_dev + row[...]).astype(jnp.float32))
    put(lines, bag[...].astype(jnp.float32))
    put(2 * lines, (prev_owner[...] * rows_dev + prev_row[...]).astype(jnp.float32))
    put(3 * lines, prev_bag[...].astype(jnp.float32))
    for k in range(width // LANES):
        put(4 * lines + k * bag_count, grad[:, k * LANES:(k + 1) * LANES])


def split_two(x):
    high = x.astype(jnp.bfloat16)
    return high, (x - high.astype(jnp.float32)).astype(jnp.bfloat16)


def prepare_kernel(table, kept, sems):
    pieces = sems.shape[0]
    rows = table.shape[0] // pieces
    copies = [
        pltpu.make_async_copy(
            table.at[pl.ds(i * rows, rows), :], kept.at[pl.ds(i * rows, rows), :], sems.at[i])
        for i in range(pieces)
    ]
    for copy in copies:
        copy.start()
    for copy in copies:
        copy.wait()


def codes(ids, bags, bag_count, base):
    rel = ids.astype(jnp.int32) - base
    code = lax.shift_right_arithmetic(rel, 7) * bag_count + bags.astype(jnp.int32)
    return code.astype(jnp.float32), (rel & (LANES - 1)).astype(jnp.float32)


def count_into(counts, code_ref, lane_ref, devices, bag_count):
    blocks = counts.shape[0]
    lines = code_ref.shape[1]
    one, none = jnp.ones((), jnp.bfloat16), jnp.zeros((), jnp.bfloat16)

    def one_hot(ref, d, size):
        numbers = lax.broadcasted_iota(jnp.int32, (size, LANES), 0).astype(jnp.bfloat16)
        parts = []
        for k in range(lines):
            row = jnp.broadcast_to(ref[d, k:k + 1, :], (size, LANES)).astype(jnp.bfloat16)
            parts.append(jnp.where(numbers == row, one, none))
        return jnp.concatenate(parts, axis=1)

    for d in range(devices):
        hits = lax.dot_general(
            one_hot(code_ref, d, blocks * bag_count), one_hot(lane_ref, d, LANES),
            (((1,), (1,)), ((), ())), preferred_element_type=jnp.float32)
        counts[:, d * bag_count:(d + 1) * bag_count, :] = hits.reshape(
            blocks, bag_count, LANES)


def pool_kernel(
    bag_count, lines, turn, msg, table, out, joined, go, code_ref, lane_ref, counts,
):
    go[0, 0] = 1
    rows_dev, width = table.shape
    owners = msg.shape[0]
    base = lax.axis_index("rows") * rows_dev
    code_ref[...], lane_ref[...] = codes(
        msg[:, 0:lines, :], msg[:, lines:2 * lines, :], bag_count, base)
    joined[...] = msg[:, 2 * lines:, :]
    count_into(counts, code_ref, lane_ref, owners, bag_count)
    blocks = rows_dev // LANES
    flat = jnp.concatenate(
        [counts[h].astype(jnp.bfloat16) for h in range(blocks)], axis=1)
    total = jnp.zeros((owners * bag_count, width), jnp.float32)
    for part in split_two(table[...]):
        total += jnp.dot(flat, part, preferred_element_type=jnp.float32)
    for i in range(owners):
        seen = (i + turn) % owners
        out[i] = total[seen * bag_count:(seen + 1) * bag_count, :]


def read_chunk(msg, here, chunk, lines, bag_count, base, code_ref, lane_ref, counts, grads):
    width = grads.shape[1]
    code_ref[...], lane_ref[...] = codes(
        msg[here, 0:lines, :], msg[here, lines:2 * lines, :], bag_count, base)
    count_into(counts, code_ref, lane_ref, chunk, bag_count)
    for k in range(width // LANES):
        start = 2 * lines + k * bag_count
        grads[:, k * LANES:(k + 1) * LANES] = msg[
            here, start:start + bag_count, :].reshape(chunk * bag_count, LANES)


def block_sum(hits, parts):
    total = jnp.zeros((hits.shape[1], parts[0].shape[1]), jnp.float32)
    for part in parts:
        total += lax.dot_general(
            hits, part, (((0,), (0,)), ((), ())), preferred_element_type=jnp.float32)
    return total


def apply_rows(grad_of, table, accum, new_table, new_accum, fresh_table, sems):
    blocks, width = accum.shape[0], table.shape[1]
    diagonal = (
        lax.broadcasted_iota(jnp.int32, (LANES, LANES), 0)
        == lax.broadcasted_iota(jnp.int32, (LANES, LANES), 1))
    per_piece = blocks // sems.shape[0]
    copies = []
    for h in range(blocks):
        grad = grad_of(h)
        here = slice(h * LANES, (h + 1) * LANES)
        squares = grad * grad
        folded = squares[:, 0:LANES]
        for k in range(1, width // LANES):
            folded += squares[:, k * LANES:(k + 1) * LANES]
        old = jnp.where(diagonal, accum[h:h + 1, :], 0.0)
        fresh = jnp.sum(folded * (1.0 / width) + old, axis=1, keepdims=True)
        fresh_table[here, :] = table[here, :] - grad * (learn_rate * lax.rsqrt(fresh))
        new_accum[h:h + 1, :] = jnp.sum(
            jnp.where(diagonal, fresh, 0.0), axis=0, keepdims=True)
        if (h + 1) % per_piece == 0:
            i = h // per_piece
            piece = pl.ds(i * per_piece * LANES, per_piece * LANES)
            copies.append(pltpu.make_async_copy(
                fresh_table.at[piece, :], new_table.at[piece, :], sems.at[i]))
            copies[-1].start()
    for copy in copies:
        copy.wait()


def count_kernel(bag_count, lines, *refs):
    sources, (counts_out, high, low) = refs[:-8], refs[-8:-5]
    msg, code_ref, lane_ref, counts, grads = refs[-5:]
    owners = sources[0].shape[0]
    devices, blocks = msg.shape[0], counts.shape[0]
    base = lax.axis_index("rows") * (blocks * LANES)
    for i, source in enumerate(sources):
        msg[i * owners:(i + 1) * owners] = source[...]
    read_chunk(
        msg, slice(0, devices), devices, lines, bag_count, base,
        code_ref, lane_ref, counts, grads)
    counts_out[...] = counts[...].astype(jnp.bfloat16)
    high[...], low[...] = split_two(grads[...])


def apply_kernel(bag_count, lines, *refs):
    msg, counted, high, low, table, accum, new_table, new_accum = refs[:8]
    code_ref, lane_ref, counts, grads, fresh_table, sems = refs[8:]
    devices, blocks = msg.shape[0], counts.shape[0]
    base = lax.axis_index("rows") * (blocks * LANES)
    read_chunk(
        msg, slice(0, devices), devices, lines, bag_count, base,
        code_ref, lane_ref, counts, grads)
    parts = [
        jnp.concatenate([early[...], late], axis=0)
        for early, late in zip((high, low), split_two(grads[...]))
    ]

    def grad_of(h):
        hits = jnp.concatenate([counted[h], counts[h].astype(jnp.bfloat16)], axis=0)
        return block_sum(hits, parts)

    apply_rows(grad_of, table, accum, new_table, new_accum, fresh_table, sems)


def update_kernel(bag_count, lines, groups, chunk, *refs):
    sources, (table, accum, new_table, new_accum) = refs[:groups], refs[groups:groups + 4]
    msg, code_ref, lane_ref, counts, grads, sums, fresh_table, sems = refs[groups + 4:]
    devices, blocks = msg.shape[0], counts.shape[0]
    owners = devices // groups
    base = lax.axis_index("rows") * (blocks * LANES)
    for i, source in enumerate(sources):
        msg[i * owners:(i + 1) * owners] = source[...]
    sums[...] = jnp.zeros_like(sums)

    @pl.loop(0, devices // chunk)
    def _(c):
        read_chunk(
            msg, pl.ds(c * chunk, chunk), chunk, lines, bag_count, base,
            code_ref, lane_ref, counts, grads)
        parts = split_two(grads[...])

        @pl.loop(0, blocks)
        def _(h):
            sums[h] += block_sum(counts[h].astype(jnp.bfloat16), parts)

    apply_rows(lambda h: sums[h], table, accum, new_table, new_accum, fresh_table, sems)


def pass_kernel(table, accum, new_table, new_accum, sem):
    copy = pltpu.make_async_copy(table, new_table, sem)
    copy.start()
    new_accum[...] = accum[...]
    copy.wait()


def finish_kernel(returned, accum, pooled, new_accum):
    total = returned[0]
    for i in range(1, returned.shape[0]):
        total += returned[i]
    pooled[...] = total
    new_accum[...] = accum[...]


def listing(size, leader):
    return [(i + leader) % size for i in range(size)]


def exchange(x, axis, leader):
    order = listing(lax.axis_size(axis), leader)
    return lax.all_to_all(
        x, axis, split_axis=0, concat_axis=0, axis_index_groups=[order], tiled=True)


def forward(x, axis, step):
    size = lax.axis_size(axis)
    return lax.ppermute(
        x, axis, [(i, ((i // 2 + step) * 2 + 1 - i % 2) % size) for i in range(size)])


def local(
    item_table, row_accum, owner_map, row_index, bag_index,
    prev_owner, prev_row, prev_bag, grad_pooled,
):
    owners, groups = lax.axis_size("rows"), lax.axis_size("dp")
    devices = owners * groups
    out_leader, back_leader = owners // 2 - 1, owners // 2
    rows_dev, width = item_table.shape
    bag_count = grad_pooled.shape[2]
    lines = row_index.shape[2] // LANES
    blocks = rows_dev // LANES
    prev_length = 2 * lines + bag_count * width // LANES
    vmem = pl.BlockSpec(memory_space=pltpu.VMEM)
    hbm = pl.BlockSpec(memory_space=pltpu.HBM)
    params = pltpu.CompilerParams(vmem_limit_bytes=16 * 1024 * 1024)
    chunk = min(devices, LANES // bag_count)

    def stay(x):
        return pltpu.with_memory_space_constraint(x, pltpu.HBM)

    def line(x):
        return x.reshape(lines, LANES)

    message = pl.pallas_call(
        functools.partial(pack_kernel, rows_dev),
        out_shape=pltpu.VMEM((owners, 2 * lines + prev_length, LANES), jnp.float32),
        in_specs=[hbm] * 7,
        out_specs=vmem,
        scratch_shapes=[pltpu.VMEM((lines, LANES), jnp.int32)] * 6
        + [pltpu.VMEM((bag_count, width), jnp.float32), pltpu.SemaphoreType.DMA((7,))],
        compiler_params=params,
        name="pack",
    )(*[stay(x) for x in (
        line(owner_map), line(row_index), line(bag_index),
        line(prev_owner), line(prev_row), line(prev_bag), grad_pooled[0, 0],
    )])
    gathered = exchange(message, "rows", out_leader)

    pieces = 4
    kept = pl.pallas_call(
        prepare_kernel,
        out_shape=pltpu.VMEM((rows_dev, width), jnp.float32),
        in_specs=[hbm],
        out_specs=vmem,
        scratch_shapes=[pltpu.SemaphoreType.DMA((pieces,))],
        compiler_params=params,
        cost_estimate=pl.CostEstimate(
            flops=0, bytes_accessed=2 * rows_dev * width * 4, transcendentals=0),
        name="prepare",
    )(stay(item_table))

    partial_pooled, joined, go = pl.pallas_call(
        functools.partial(pool_kernel, bag_count, lines, back_leader - out_leader),
        out_shape=(
            pltpu.VMEM((owners, bag_count, width), jnp.float32),
            pltpu.VMEM((owners, prev_length, LANES), jnp.float32),
            jax.ShapeDtypeStruct((1, 1), jnp.int32),
        ),
        in_specs=[vmem] * 2,
        out_specs=[vmem] * 2 + [pl.BlockSpec(memory_space=pltpu.SMEM)],
        scratch_shapes=[
            pltpu.VMEM((owners, lines, LANES), jnp.float32),
            pltpu.VMEM((owners, lines, LANES), jnp.float32),
            pltpu.VMEM((blocks, owners * bag_count, LANES), jnp.float32),
        ],
        compiler_params=params,
        cost_estimate=pl.CostEstimate(
            flops=4 * owners * bag_count * rows_dev * width,
            bytes_accessed=rows_dev * width * 4, transcendentals=0),
        name="pool",
    )(gathered, kept)
    returned = exchange(partial_pooled, "rows", back_leader)
    own = [joined, forward(joined, "dp", 0)]
    across = [forward(joined, "dp", step) for step in range(1, groups // 2)]

    segments = chunk * bag_count
    updated = (
        pltpu.HBM((rows_dev, width), jnp.float32),
        pltpu.VMEM((blocks, LANES), jnp.float32),
    )

    def room(count):
        return [
            pltpu.VMEM((count, lines, LANES), jnp.float32),
            pltpu.VMEM((count, lines, LANES), jnp.float32),
            pltpu.VMEM((blocks, count * bag_count, LANES), jnp.float32),
            pltpu.VMEM((count * bag_count, width), jnp.float32),
        ]

    fresh_room = [
        pltpu.VMEM((rows_dev, width), jnp.float32),
        pltpu.SemaphoreType.DMA((pieces,)),
    ]

    def split_update(early, late, kept, row_accum):
        count = len(early) * owners
        counted = pl.pallas_call(
            functools.partial(count_kernel, bag_count, lines),
            out_shape=(
                pltpu.VMEM((blocks, count * bag_count, LANES), jnp.bfloat16),
                pltpu.VMEM((count * bag_count, width), jnp.bfloat16),
                pltpu.VMEM((count * bag_count, width), jnp.bfloat16),
            ),
            in_specs=[vmem] * len(early),
            out_specs=[vmem] * 3,
            scratch_shapes=[pltpu.VMEM((count, prev_length, LANES), jnp.float32)] + room(count),
            compiler_params=params,
            cost_estimate=pl.CostEstimate(
                flops=1 << 28, bytes_accessed=1 << 22, transcendentals=0),
            name="count",
        )(*early)
        return pl.pallas_call(
            functools.partial(apply_kernel, bag_count, lines),
            out_shape=updated,
            in_specs=[vmem] * 6,
            out_specs=(hbm, vmem),
            scratch_shapes=room(owners) + fresh_room,
            compiler_params=params,
            name="apply",
        )(late, *counted, kept, row_accum)

    def whole_update(sources, kept, row_accum):
        return pl.pallas_call(
            functools.partial(update_kernel, bag_count, lines, groups, chunk),
            out_shape=updated,
            in_specs=[vmem] * (groups + 2),
            out_specs=(hbm, vmem),
            scratch_shapes=[pltpu.VMEM((devices, prev_length, LANES), jnp.float32)]
            + room(chunk) + [pltpu.VMEM((blocks, LANES, width), jnp.float32)] + fresh_room,
            compiler_params=pltpu.CompilerParams(vmem_limit_bytes=40 * 1024 * 1024),
            name="update",
        )(*sources, kept, row_accum)

    def hand_over(own, across, kept, row_accum):
        handed = [forward(x, "dp", 0) for x in across]
        if devices == chunk and len(handed) == 1:
            return split_update([*own, *across], handed[0], kept, row_accum)
        return whole_update([*own, *across, *handed], kept, row_accum)

    def skip(own, across, kept, row_accum):
        return pl.pallas_call(
            pass_kernel,
            out_shape=updated,
            in_specs=[vmem] * 2,
            out_specs=(hbm, vmem),
            scratch_shapes=[pltpu.SemaphoreType.DMA],
            compiler_params=params,
            name="pass",
        )(kept, row_accum)

    new_table, new_accum = lax.cond(
        go[0, 0] > 0, hand_over, skip, own, across, kept, row_accum.reshape(blocks, LANES))

    pooled, new_accum = pl.pallas_call(
        finish_kernel,
        out_shape=(
            jax.ShapeDtypeStruct((bag_count, width), jnp.float32),
            jax.ShapeDtypeStruct((blocks, LANES), jnp.float32),
        ),
        in_specs=[vmem] * 2,
        out_specs=[vmem] * 2,
        compiler_params=params,
        name="finish",
    )(returned, new_accum)
    return (pooled[None, None], new_table, new_accum.reshape(rows_dev))


def solution(mesh):
    placed = (
        P("rows", None),
        P("rows"),
        P("dp", "rows", None, None),
        P("dp", "rows", None),
        P("dp", "rows", None),
        P("dp", "rows", None, None),
        P("dp", "rows", None),
        P("dp", "rows", None),
        P("dp", "rows", None, None),
    )
    return jax.shard_map(
        local,
        mesh=mesh,
        in_specs=placed,
        out_specs=(P("dp", "rows", None, None), P("rows", None), P("rows")),
        check_vma=False,
    )
```

```python
import functools

import jax
import jax.numpy as jnp
from jax import lax
from jax.experimental import pallas as pl
from jax.experimental.pallas import tpu as pltpu
from jax.sharding import PartitionSpec as P

learn_rate = 0.1
LANES = 128


def pack_kernel(rows_dev, *refs):
    sources, out, held, sems = refs[:7], refs[7], refs[8:15], refs[15]
    copies = [
        pltpu.make_async_copy(source, place, sems.at[i])
        for i, (source, place) in enumerate(zip(sources, held))
    ]
    for copy in copies:
        copy.start()
    for copy in copies:
        copy.wait()
    owner, row, bag, prev_owner, prev_row, prev_bag, grad = held
    lines = row.shape[0]
    bag_count, width = grad.shape

    def put(start, value):
        shape = (out.shape[0],) + value.shape
        out[:, start:start + value.shape[0], :] = jnp.broadcast_to(value[None], shape)

    put(0, (owner[...] * rows_dev + row[...]).astype(jnp.float32))
    put(lines, bag[...].astype(jnp.float32))
    put(2 * lines, (prev_owner[...] * rows_dev + prev_row[...]).astype(jnp.float32))
    put(3 * lines, prev_bag[...].astype(jnp.float32))
    for k in range(width // LANES):
        put(4 * lines + k * bag_count, grad[:, k * LANES:(k + 1) * LANES])


def split_two(x):
    high = x.astype(jnp.bfloat16)
    return high, (x - high.astype(jnp.float32)).astype(jnp.bfloat16)


def prepare_kernel(table, kept, sems):
    pieces = sems.shape[0]
    rows = table.shape[0] // pieces
    copies = [
        pltpu.make_async_copy(
            table.at[pl.ds(i * rows, rows), :], kept.at[pl.ds(i * rows, rows), :], sems.at[i])
        for i in range(pieces)
    ]
    for copy in copies:
        copy.start()
    for copy in copies:
        copy.wait()


def codes(ids, bags, bag_count, base):
    rel = ids.astype(jnp.int32) - base
    code = lax.shift_right_arithmetic(rel, 7) * bag_count + bags.astype(jnp.int32)
    return code.astype(jnp.float32), (rel & (LANES - 1)).astype(jnp.float32)


def count_into(counts, code_ref, lane_ref, devices, bag_count):
    blocks = counts.shape[0]
    lines = code_ref.shape[1]
    one, none = jnp.ones((), jnp.bfloat16), jnp.zeros((), jnp.bfloat16)

    def one_hot(ref, d, size):
        numbers = lax.broadcasted_iota(jnp.int32, (size, LANES), 0).astype(jnp.bfloat16)
        parts = []
        for k in range(lines):
            row = jnp.broadcast_to(ref[d, k:k + 1, :], (size, LANES)).astype(jnp.bfloat16)
            parts.append(jnp.where(numbers == row, one, none))
        return jnp.concatenate(parts, axis=1)

    for d in range(devices):
        hits = lax.dot_general(
            one_hot(code_ref, d, blocks * bag_count), one_hot(lane_ref, d, LANES),
            (((1,), (1,)), ((), ())), preferred_element_type=jnp.float32)
        counts[:, d * bag_count:(d + 1) * bag_count, :] = hits.reshape(
            blocks, bag_count, LANES)


def pool_kernel(
    bag_count, lines, turn, msg, table, out, joined, go, code_ref, lane_ref, counts,
):
    go[0, 0] = 1
    rows_dev, width = table.shape
    owners = msg.shape[0]
    base = lax.axis_index("rows") * rows_dev
    code_ref[...], lane_ref[...] = codes(
        msg[:, 0:lines, :], msg[:, lines:2 * lines, :], bag_count, base)
    joined[...] = msg[:, 2 * lines:, :]
    count_into(counts, code_ref, lane_ref, owners, bag_count)
    blocks = rows_dev // LANES
    flat = jnp.concatenate(
        [counts[h].astype(jnp.bfloat16) for h in range(blocks)], axis=1)
    total = jnp.zeros((owners * bag_count, width), jnp.float32)
    for part in split_two(table[...]):
        total += jnp.dot(flat, part, preferred_element_type=jnp.float32)
    for i in range(owners):
        seen = (i + turn) % owners
        out[i] = total[seen * bag_count:(seen + 1) * bag_count, :]


def read_chunk(msg, here, chunk, lines, bag_count, base, code_ref, lane_ref, counts, grads):
    width = grads.shape[1]
    code_ref[...], lane_ref[...] = codes(
        msg[here, 0:lines, :], msg[here, lines:2 * lines, :], bag_count, base)
    count_into(counts, code_ref, lane_ref, chunk, bag_count)
    for k in range(width // LANES):
        start = 2 * lines + k * bag_count
        grads[:, k * LANES:(k + 1) * LANES] = msg[
            here, start:start + bag_count, :].reshape(chunk * bag_count, LANES)


def block_sum(hits, parts):
    total = jnp.zeros((hits.shape[1], parts[0].shape[1]), jnp.float32)
    for part in parts:
        total += lax.dot_general(
            hits, part, (((0,), (0,)), ((), ())), preferred_element_type=jnp.float32)
    return total


def apply_rows(grad_of, table, accum, new_table, new_accum, fresh_table, sems):
    blocks, width = accum.shape[0], table.shape[1]
    diagonal = (
        lax.broadcasted_iota(jnp.int32, (LANES, LANES), 0)
        == lax.broadcasted_iota(jnp.int32, (LANES, LANES), 1))
    per_piece = blocks // sems.shape[0]
    copies = []
    for h in range(blocks):
        grad = grad_of(h)
        here = slice(h * LANES, (h + 1) * LANES)
        squares = grad * grad
        folded = squares[:, 0:LANES]
        for k in range(1, width // LANES):
            folded += squares[:, k * LANES:(k + 1) * LANES]
        old = jnp.where(diagonal, accum[h:h + 1, :], 0.0)
        fresh = jnp.sum(folded * (1.0 / width) + old, axis=1, keepdims=True)
        fresh_table[here, :] = table[here, :] - grad * (learn_rate * lax.rsqrt(fresh))
        new_accum[h:h + 1, :] = jnp.sum(
            jnp.where(diagonal, fresh, 0.0), axis=0, keepdims=True)
        if (h + 1) % per_piece == 0:
            i = h // per_piece
            piece = pl.ds(i * per_piece * LANES, per_piece * LANES)
            copies.append(pltpu.make_async_copy(
                fresh_table.at[piece, :], new_table.at[piece, :], sems.at[i]))
            copies[-1].start()
    for copy in copies:
        copy.wait()


def count_kernel(bag_count, lines, *refs):
    sources, (counts_out, high, low) = refs[:-8], refs[-8:-5]
    msg, code_ref, lane_ref, counts, grads = refs[-5:]
    owners = sources[0].shape[0]
    devices, blocks = msg.shape[0], counts.shape[0]
    base = lax.axis_index("rows") * (blocks * LANES)
    for i, source in enumerate(sources):
        msg[i * owners:(i + 1) * owners] = source[...]
    read_chunk(
        msg, slice(0, devices), devices, lines, bag_count, base,
        code_ref, lane_ref, counts, grads)
    counts_out[...] = counts[...].astype(jnp.bfloat16)
    high[...], low[...] = split_two(grads[...])


def apply_kernel(bag_count, lines, late, *refs):
    sources, (counted, high, low, table, accum) = refs[:late], refs[late:late + 5]
    new_table, new_accum, msg, code_ref, lane_ref, counts, grads, fresh_table, sems = refs[late + 5:]
    owners = sources[0].shape[0]
    devices, blocks = msg.shape[0], counts.shape[0]
    base = lax.axis_index("rows") * (blocks * LANES)
    for i, source in enumerate(sources):
        msg[i * owners:(i + 1) * owners] = source[...]
    read_chunk(
        msg, slice(0, devices), devices, lines, bag_count, base,
        code_ref, lane_ref, counts, grads)
    parts = [
        jnp.concatenate([early[...], late], axis=0)
        for early, late in zip((high, low), split_two(grads[...]))
    ]

    def grad_of(h):
        hits = jnp.concatenate([counted[h], counts[h].astype(jnp.bfloat16)], axis=0)
        return block_sum(hits, parts)

    apply_rows(grad_of, table, accum, new_table, new_accum, fresh_table, sems)


def update_kernel(bag_count, lines, groups, chunk, *refs):
    sources, (table, accum, new_table, new_accum) = refs[:groups], refs[groups:groups + 4]
    msg, code_ref, lane_ref, counts, grads, sums, fresh_table, sems = refs[groups + 4:]
    devices, blocks = msg.shape[0], counts.shape[0]
    owners = devices // groups
    base = lax.axis_index("rows") * (blocks * LANES)
    for i, source in enumerate(sources):
        msg[i * owners:(i + 1) * owners] = source[...]
    sums[...] = jnp.zeros_like(sums)

    @pl.loop(0, devices // chunk)
    def _(c):
        read_chunk(
            msg, pl.ds(c * chunk, chunk), chunk, lines, bag_count, base,
            code_ref, lane_ref, counts, grads)
        parts = split_two(grads[...])

        @pl.loop(0, blocks)
        def _(h):
            sums[h] += block_sum(counts[h].astype(jnp.bfloat16), parts)

    apply_rows(lambda h: sums[h], table, accum, new_table, new_accum, fresh_table, sems)


def pass_kernel(table, accum, new_table, new_accum, sem):
    copy = pltpu.make_async_copy(table, new_table, sem)
    copy.start()
    new_accum[...] = accum[...]
    copy.wait()


def finish_kernel(returned, accum, pooled, new_accum):
    total = returned[0]
    for i in range(1, returned.shape[0]):
        total += returned[i]
    pooled[...] = total
    new_accum[...] = accum[...]


def listing(size, leader):
    return [(i + leader) % size for i in range(size)]


def exchange(x, axis, leader):
    order = listing(lax.axis_size(axis), leader)
    return lax.all_to_all(
        x, axis, split_axis=0, concat_axis=0, axis_index_groups=[order], tiled=True)


def forward(x, axis, step):
    size = lax.axis_size(axis)
    return lax.ppermute(
        x, axis, [(i, ((i // 2 + step) * 2 + 1 - i % 2) % size) for i in range(size)])


def local(
    item_table, row_accum, owner_map, row_index, bag_index,
    prev_owner, prev_row, prev_bag, grad_pooled,
):
    owners, groups = lax.axis_size("rows"), lax.axis_size("dp")
    devices = owners * groups
    out_leader, back_leader = owners // 2 - 1, owners // 2
    rows_dev, width = item_table.shape
    bag_count = grad_pooled.shape[2]
    lines = row_index.shape[2] // LANES
    blocks = rows_dev // LANES
    prev_length = 2 * lines + bag_count * width // LANES
    vmem = pl.BlockSpec(memory_space=pltpu.VMEM)
    hbm = pl.BlockSpec(memory_space=pltpu.HBM)
    params = pltpu.CompilerParams(vmem_limit_bytes=16 * 1024 * 1024)
    chunk = min(devices, LANES // bag_count)

    def stay(x):
        return pltpu.with_memory_space_constraint(x, pltpu.HBM)

    def line(x):
        return x.reshape(lines, LANES)

    message = pl.pallas_call(
        functools.partial(pack_kernel, rows_dev),
        out_shape=pltpu.VMEM((owners, 2 * lines + prev_length, LANES), jnp.float32),
        in_specs=[hbm] * 7,
        out_specs=vmem,
        scratch_shapes=[pltpu.VMEM((lines, LANES), jnp.int32)] * 6
        + [pltpu.VMEM((bag_count, width), jnp.float32), pltpu.SemaphoreType.DMA((7,))],
        compiler_params=params,
        name="pack",
    )(*[stay(x) for x in (
        line(owner_map), line(row_index), line(bag_index),
        line(prev_owner), line(prev_row), line(prev_bag), grad_pooled[0, 0],
    )])
    gathered = exchange(message, "rows", out_leader)

    pieces = 4
    kept = pl.pallas_call(
        prepare_kernel,
        out_shape=pltpu.VMEM((rows_dev, width), jnp.float32),
        in_specs=[hbm],
        out_specs=vmem,
        scratch_shapes=[pltpu.SemaphoreType.DMA((pieces,))],
        compiler_params=params,
        cost_estimate=pl.CostEstimate(
            flops=0, bytes_accessed=2 * rows_dev * width * 4, transcendentals=0),
        name="prepare",
    )(stay(item_table))

    partial_pooled, joined, go = pl.pallas_call(
        functools.partial(pool_kernel, bag_count, lines, back_leader - out_leader),
        out_shape=(
            pltpu.VMEM((owners, bag_count, width), jnp.float32),
            pltpu.VMEM((owners, prev_length, LANES), jnp.float32),
            jax.ShapeDtypeStruct((1, 1), jnp.int32),
        ),
        in_specs=[vmem] * 2,
        out_specs=[vmem] * 2 + [pl.BlockSpec(memory_space=pltpu.SMEM)],
        scratch_shapes=[
            pltpu.VMEM((owners, lines, LANES), jnp.float32),
            pltpu.VMEM((owners, lines, LANES), jnp.float32),
            pltpu.VMEM((blocks, owners * bag_count, LANES), jnp.float32),
        ],
        compiler_params=params,
        cost_estimate=pl.CostEstimate(
            flops=4 * owners * bag_count * rows_dev * width,
            bytes_accessed=rows_dev * width * 4, transcendentals=0),
        name="pool",
    )(gathered, kept)
    returned = exchange(partial_pooled, "rows", back_leader)
    there = [joined] + [forward(joined, "dp", step) for step in range(1, groups // 2)]

    segments = chunk * bag_count
    results = 8 if blocks % 8 == 0 else 1
    updated = (
        pltpu.HBM((rows_dev, width), jnp.float32),
        pltpu.VMEM((blocks, LANES), jnp.float32),
    )

    def room(count):
        return [
            pltpu.VMEM((count, lines, LANES), jnp.float32),
            pltpu.VMEM((count, lines, LANES), jnp.float32),
            pltpu.VMEM((blocks, count * bag_count, LANES), jnp.float32),
            pltpu.VMEM((count * bag_count, width), jnp.float32),
        ]

    fresh_room = [
        pltpu.VMEM((rows_dev, width), jnp.float32),
        pltpu.SemaphoreType.DMA((results,)),
    ]

    def split_update(early, late, kept, row_accum):
        count = len(early) * owners
        counted = pl.pallas_call(
            functools.partial(count_kernel, bag_count, lines),
            out_shape=(
                pltpu.VMEM((blocks, count * bag_count, LANES), jnp.bfloat16),
                pltpu.VMEM((count * bag_count, width), jnp.bfloat16),
                pltpu.VMEM((count * bag_count, width), jnp.bfloat16),
            ),
            in_specs=[vmem] * len(early),
            out_specs=[vmem] * 3,
            scratch_shapes=[pltpu.VMEM((count, prev_length, LANES), jnp.float32)] + room(count),
            compiler_params=params,
            cost_estimate=pl.CostEstimate(
                flops=1 << 28, bytes_accessed=1 << 22, transcendentals=0),
            name="count",
        )(*early)
        return pl.pallas_call(
            functools.partial(apply_kernel, bag_count, lines, len(late)),
            out_shape=updated,
            in_specs=[vmem] * (len(late) + 5),
            out_specs=(hbm, vmem),
            scratch_shapes=[pltpu.VMEM((count, prev_length, LANES), jnp.float32)]
            + room(count) + fresh_room,
            compiler_params=params,
            name="apply",
        )(*late, *counted, kept, row_accum)

    def whole_update(sources, kept, row_accum):
        return pl.pallas_call(
            functools.partial(update_kernel, bag_count, lines, groups, chunk),
            out_shape=updated,
            in_specs=[vmem] * (groups + 2),
            out_specs=(hbm, vmem),
            scratch_shapes=[pltpu.VMEM((devices, prev_length, LANES), jnp.float32)]
            + room(chunk) + [pltpu.VMEM((blocks, LANES, width), jnp.float32)] + fresh_room,
            compiler_params=pltpu.CompilerParams(vmem_limit_bytes=40 * 1024 * 1024),
            name="update",
        )(*sources, kept, row_accum)

    def hand_over(there, kept, row_accum):
        handed = [forward(x, "dp", 0) for x in there]
        if devices == chunk:
            return split_update(there, handed, kept, row_accum)
        return whole_update([*there, *handed], kept, row_accum)

    def skip(there, kept, row_accum):
        return pl.pallas_call(
            pass_kernel,
            out_shape=updated,
            in_specs=[vmem] * 2,
            out_specs=(hbm, vmem),
            scratch_shapes=[pltpu.SemaphoreType.DMA],
            compiler_params=params,
            name="pass",
        )(kept, row_accum)

    new_table, new_accum = lax.cond(
        go[0, 0] > 0, hand_over, skip, there, kept, row_accum.reshape(blocks, LANES))

    pooled, new_accum = pl.pallas_call(
        finish_kernel,
        out_shape=(
            jax.ShapeDtypeStruct((bag_count, width), jnp.float32),
            jax.ShapeDtypeStruct((blocks, LANES), jnp.float32),
        ),
        in_specs=[vmem] * 2,
        out_specs=[vmem] * 2,
        compiler_params=params,
        name="finish",
    )(returned, new_accum)
    return (pooled[None, None], new_table, new_accum.reshape(rows_dev))


def solution(mesh):
    placed = (
        P("rows", None),
        P("rows"),
        P("dp", "rows", None, None),
        P("dp", "rows", None),
        P("dp", "rows", None),
        P("dp", "rows", None, None),
        P("dp", "rows", None),
        P("dp", "rows", None),
        P("dp", "rows", None, None),
    )
    return jax.shard_map(
        local,
        mesh=mesh,
        in_specs=placed,
        out_specs=(P("dp", "rows", None, None), P("rows", None), P("rows")),
        check_vma=False,
    )
```

```python
import functools

import jax
import jax.numpy as jnp
from jax import lax
from jax.experimental import pallas as pl
from jax.experimental.pallas import tpu as pltpu
from jax.sharding import PartitionSpec as P

learn_rate = 0.1
LANES = 128


def pack_kernel(rows_dev, *refs):
    sources, out, held, sems = refs[:7], refs[7], refs[8:15], refs[15]
    copies = [
        pltpu.make_async_copy(source, place, sems.at[i])
        for i, (source, place) in enumerate(zip(sources, held))
    ]
    for copy in copies:
        copy.start()
    for copy in copies:
        copy.wait()
    owner, row, bag, prev_owner, prev_row, prev_bag, grad = held
    lines = row.shape[0]
    bag_count, width = grad.shape

    def put(start, value):
        shape = (out.shape[0],) + value.shape
        out[:, start:start + value.shape[0], :] = jnp.broadcast_to(value[None], shape)

    put(0, (owner[...] * rows_dev + row[...]).astype(jnp.float32))
    put(lines, bag[...].astype(jnp.float32))
    put(2 * lines, (prev_owner[...] * rows_dev + prev_row[...]).astype(jnp.float32))
    put(3 * lines, prev_bag[...].astype(jnp.float32))
    for k in range(width // LANES):
        put(4 * lines + k * bag_count, grad[:, k * LANES:(k + 1) * LANES])


def split_two(x):
    high = x.astype(jnp.bfloat16)
    return high, (x - high.astype(jnp.float32)).astype(jnp.bfloat16)


def prepare_kernel(table, kept, sems):
    pieces = sems.shape[0]
    rows = table.shape[0] // pieces
    copies = [
        pltpu.make_async_copy(
            table.at[pl.ds(i * rows, rows), :], kept.at[pl.ds(i * rows, rows), :], sems.at[i])
        for i in range(pieces)
    ]
    for copy in copies:
        copy.start()
    for copy in copies:
        copy.wait()


def codes(ids, bags, bag_count, base):
    rel = ids.astype(jnp.int32) - base
    code = lax.shift_right_arithmetic(rel, 7) * bag_count + bags.astype(jnp.int32)
    return code.astype(jnp.float32), (rel & (LANES - 1)).astype(jnp.float32)


def count_into(counts, code_ref, lane_ref, devices, bag_count):
    blocks = counts.shape[0]
    lines = code_ref.shape[1]
    one, none = jnp.ones((), jnp.bfloat16), jnp.zeros((), jnp.bfloat16)

    def one_hot(ref, d, size):
        numbers = lax.broadcasted_iota(jnp.int32, (size, LANES), 0).astype(jnp.bfloat16)
        parts = []
        for k in range(lines):
            row = jnp.broadcast_to(ref[d, k:k + 1, :], (size, LANES)).astype(jnp.bfloat16)
            parts.append(jnp.where(numbers == row, one, none))
        return jnp.concatenate(parts, axis=1)

    for d in range(devices):
        hits = lax.dot_general(
            one_hot(code_ref, d, blocks * bag_count), one_hot(lane_ref, d, LANES),
            (((1,), (1,)), ((), ())), preferred_element_type=jnp.float32)
        counts[:, d * bag_count:(d + 1) * bag_count, :] = hits.reshape(
            blocks, bag_count, LANES)


def pool_kernel(bag_count, lines, turn, msg, table, out, joined, code_ref, lane_ref, counts):
    rows_dev, width = table.shape
    owners = msg.shape[0]
    base = lax.axis_index("rows") * rows_dev
    code_ref[...], lane_ref[...] = codes(
        msg[:, 0:lines, :], msg[:, lines:2 * lines, :], bag_count, base)
    joined[...] = msg[:, 2 * lines:, :]
    count_into(counts, code_ref, lane_ref, owners, bag_count)
    blocks = rows_dev // LANES
    flat = jnp.concatenate(
        [counts[h].astype(jnp.bfloat16) for h in range(blocks)], axis=1)
    total = jnp.zeros((owners * bag_count, width), jnp.float32)
    for part in split_two(table[...]):
        total += jnp.dot(flat, part, preferred_element_type=jnp.float32)
    for i in range(owners):
        seen = (i + turn) % owners
        out[i] = total[seen * bag_count:(seen + 1) * bag_count, :]


def join_kernel(joined, swapped, both):
    devices, length, _ = joined.shape
    both[0:devices] = joined[...]
    both[devices:] = swapped[:, swapped.shape[1] - length:, :]


def update_kernel(bag_count, lines, pairs, chunk, *refs):
    sources, (table, accum, new_table, new_accum) = refs[:pairs], refs[pairs:pairs + 4]
    msg, code_ref, lane_ref, counts, grads, sums, fresh_table, sems = refs[pairs + 4:]
    rows_dev, width = table.shape
    pieces = sems.shape[0]
    devices = msg.shape[0]
    per_source = devices // pairs
    blocks = counts.shape[0]
    base = lax.axis_index("rows") * rows_dev
    single = devices == chunk

    def count_chunk(first):
        here = pl.ds(first, chunk)
        code_ref[...], lane_ref[...] = codes(
            msg[here, 0:lines, :], msg[here, lines:2 * lines, :], bag_count, base)
        count_into(counts, code_ref, lane_ref, chunk, bag_count)
        for k in range(width // LANES):
            start = 2 * lines + k * bag_count
            grads[:, k * LANES:(k + 1) * LANES] = msg[
                here, start:start + bag_count, :].reshape(chunk * bag_count, LANES)
        return split_two(grads[...])

    def block_sum(h, parts):
        hits = counts[h].astype(jnp.bfloat16)
        total = jnp.zeros((LANES, width), jnp.float32)
        for part in parts:
            total += lax.dot_general(
                hits, part, (((0,), (0,)), ((), ())), preferred_element_type=jnp.float32)
        return total

    for i, source in enumerate(sources):
        msg[i * per_source:(i + 1) * per_source] = source[...]
    if single:
        parts = count_chunk(0)
    else:
        sums[...] = jnp.zeros_like(sums)

        @pl.loop(0, devices // chunk)
        def _(c):
            parts = count_chunk(c * chunk)

            @pl.loop(0, blocks)
            def _(h):
                sums[h] += block_sum(h, parts)

    diagonal = (
        lax.broadcasted_iota(jnp.int32, (LANES, LANES), 0)
        == lax.broadcasted_iota(jnp.int32, (LANES, LANES), 1))
    per_piece = blocks // pieces
    copies = []
    for h in range(blocks):
        i = h // per_piece
        grad = block_sum(h, parts) if single else sums[h]
        here = slice(h * LANES, (h + 1) * LANES)
        squares = grad * grad
        folded = squares[:, 0:LANES]
        for k in range(1, width // LANES):
            folded += squares[:, k * LANES:(k + 1) * LANES]
        old = jnp.where(diagonal, accum[h:h + 1, :], 0.0)
        fresh = jnp.sum(folded * (1.0 / width) + old, axis=1, keepdims=True)
        fresh_table[here, :] = table[here, :] - grad * (learn_rate * lax.rsqrt(fresh))
        new_accum[h:h + 1, :] = jnp.sum(
            jnp.where(diagonal, fresh, 0.0), axis=0, keepdims=True)
        if (h + 1) % per_piece == 0:
            piece = pl.ds(i * per_piece * LANES, per_piece * LANES)
            copies.append(pltpu.make_async_copy(
                fresh_table.at[piece, :], new_table.at[piece, :], sems.at[i]))
            copies[-1].start()
    for copy in copies:
        copy.wait()


def finish_kernel(returned, accum, pooled, new_accum):
    total = returned[0]
    for i in range(1, returned.shape[0]):
        total += returned[i]
    pooled[...] = total
    new_accum[...] = accum[...]


def listing(size, leader):
    return [(i + leader) % size for i in range(size)]


def exchange(x, axis, leader):
    order = listing(lax.axis_size(axis), leader)
    return lax.all_to_all(
        x, axis, split_axis=0, concat_axis=0, axis_index_groups=[order], tiled=True)


def forward(x, axis, step):
    size = lax.axis_size(axis)
    return lax.ppermute(
        x, axis, [(i, ((i // 2 + step) * 2 + 1 - i % 2) % size) for i in range(size)])


def local(
    item_table, row_accum, owner_map, row_index, bag_index,
    prev_owner, prev_row, prev_bag, grad_pooled,
):
    owners, groups = lax.axis_size("rows"), lax.axis_size("dp")
    devices = owners * groups
    out_leader, back_leader = owners // 2 - 1, owners // 2
    rows_dev, width = item_table.shape
    bag_count = grad_pooled.shape[2]
    lines = row_index.shape[2] // LANES
    blocks = rows_dev // LANES
    prev_length = 2 * lines + bag_count * width // LANES
    vmem = pl.BlockSpec(memory_space=pltpu.VMEM)
    hbm = pl.BlockSpec(memory_space=pltpu.HBM)
    params = pltpu.CompilerParams(vmem_limit_bytes=16 * 1024 * 1024)
    chunk = min(devices, LANES // bag_count)

    def stay(x):
        return pltpu.with_memory_space_constraint(x, pltpu.HBM)

    def line(x):
        return x.reshape(lines, LANES)

    message = pl.pallas_call(
        functools.partial(pack_kernel, rows_dev),
        out_shape=pltpu.VMEM((owners, 2 * lines + prev_length, LANES), jnp.float32),
        in_specs=[hbm] * 7,
        out_specs=vmem,
        scratch_shapes=[pltpu.VMEM((lines, LANES), jnp.int32)] * 6
        + [pltpu.VMEM((bag_count, width), jnp.float32), pltpu.SemaphoreType.DMA((7,))],
        compiler_params=params,
        name="pack",
    )(*[stay(x) for x in (
        line(owner_map), line(row_index), line(bag_index),
        line(prev_owner), line(prev_row), line(prev_bag), grad_pooled[0, 0],
    )])
    gathered = exchange(message, "rows", out_leader)

    swapped = forward(gathered, "dp", 0)

    pieces = 4
    kept = pl.pallas_call(
        prepare_kernel,
        out_shape=pltpu.VMEM((rows_dev, width), jnp.float32),
        in_specs=[hbm],
        out_specs=vmem,
        scratch_shapes=[pltpu.SemaphoreType.DMA((pieces,))],
        compiler_params=params,
        cost_estimate=pl.CostEstimate(
            flops=0, bytes_accessed=2 * rows_dev * width * 4, transcendentals=0),
        name="prepare",
    )(stay(item_table))

    partial_pooled, joined = pl.pallas_call(
        functools.partial(pool_kernel, bag_count, lines, back_leader - out_leader),
        out_shape=(
            pltpu.VMEM((owners, bag_count, width), jnp.float32),
            pltpu.VMEM((owners, prev_length, LANES), jnp.float32),
        ),
        in_specs=[vmem] * 2,
        out_specs=[vmem] * 2,
        scratch_shapes=[
            pltpu.VMEM((owners, lines, LANES), jnp.float32),
            pltpu.VMEM((owners, lines, LANES), jnp.float32),
            pltpu.VMEM((blocks, owners * bag_count, LANES), jnp.float32),
        ],
        compiler_params=params,
        cost_estimate=pl.CostEstimate(
            flops=4 * owners * bag_count * rows_dev * width,
            bytes_accessed=rows_dev * width * 4, transcendentals=0),
        name="pool",
    )(gathered, kept)
    returned = exchange(partial_pooled, "rows", back_leader)
    both = pl.pallas_call(
        join_kernel,
        out_shape=pltpu.VMEM((2 * owners, prev_length, LANES), jnp.float32),
        in_specs=[vmem] * 2,
        out_specs=vmem,
        compiler_params=params,
        name="join",
    )(joined, swapped)
    pairs = groups // 2
    sources = [both] + [forward(both, "dp", step) for step in range(1, pairs)]

    segments = chunk * bag_count
    new_table, new_accum = pl.pallas_call(
        functools.partial(update_kernel, bag_count, lines, pairs, chunk),
        out_shape=(
            jax.ShapeDtypeStruct((rows_dev, width), jnp.float32),
            pltpu.VMEM((blocks, LANES), jnp.float32),
        ),
        in_specs=[vmem] * (pairs + 2),
        out_specs=(hbm, vmem),
        scratch_shapes=[
            pltpu.VMEM((devices, prev_length, LANES), jnp.float32),
            pltpu.VMEM((chunk, lines, LANES), jnp.float32),
            pltpu.VMEM((chunk, lines, LANES), jnp.float32),
            pltpu.VMEM((blocks, segments, LANES), jnp.float32),
            pltpu.VMEM((segments, width), jnp.float32),
            pltpu.VMEM((blocks, LANES, width) if devices > chunk else (1, 8, LANES), jnp.float32),
            pltpu.VMEM((rows_dev, width), jnp.float32),
            pltpu.SemaphoreType.DMA((pieces,)),
        ],
        compiler_params=params if devices == chunk else pltpu.CompilerParams(
            vmem_limit_bytes=40 * 1024 * 1024),
        cost_estimate=pl.CostEstimate(flops=1, bytes_accessed=1 << 20, transcendentals=0),
        name="update",
    )(*sources, kept, row_accum.reshape(blocks, LANES))

    pooled, new_accum = pl.pallas_call(
        finish_kernel,
        out_shape=(
            jax.ShapeDtypeStruct((bag_count, width), jnp.float32),
            jax.ShapeDtypeStruct((blocks, LANES), jnp.float32),
        ),
        in_specs=[vmem] * 2,
        out_specs=[vmem] * 2,
        compiler_params=params,
        name="finish",
    )(returned, new_accum)
    return (pooled[None, None], new_table, new_accum.reshape(rows_dev))


def solution(mesh):
    placed = (
        P("rows", None),
        P("rows"),
        P("dp", "rows", None, None),
        P("dp", "rows", None),
        P("dp", "rows", None),
        P("dp", "rows", None, None),
        P("dp", "rows", None),
        P("dp", "rows", None),
        P("dp", "rows", None, None),
    )
    return jax.shard_map(
        local,
        mesh=mesh,
        in_specs=placed,
        out_specs=(P("dp", "rows", None, None), P("rows", None), P("rows")),
        check_vma=False,
    )
```

```python
import functools

import jax
import jax.numpy as jnp
from jax import lax
from jax.experimental import pallas as pl
from jax.experimental.pallas import tpu as pltpu
from jax.sharding import PartitionSpec as P

learn_rate = 0.1
LANES = 128


def pack_kernel(rows_dev, *refs):
    sources, out, held, sems = refs[:7], refs[7], refs[8:15], refs[15]
    copies = [
        pltpu.make_async_copy(source, place, sems.at[i])
        for i, (source, place) in enumerate(zip(sources, held))
    ]
    for copy in copies:
        copy.start()
    for copy in copies:
        copy.wait()
    owner, row, bag, prev_owner, prev_row, prev_bag, grad = held
    lines = row.shape[0]
    bag_count, width = grad.shape

    def put(start, value):
        shape = (out.shape[0],) + value.shape
        out[:, start:start + value.shape[0], :] = jnp.broadcast_to(value[None], shape)

    put(0, (owner[...] * rows_dev + row[...]).astype(jnp.float32))
    put(lines, bag[...].astype(jnp.float32))
    put(2 * lines, (prev_owner[...] * rows_dev + prev_row[...]).astype(jnp.float32))
    put(3 * lines, prev_bag[...].astype(jnp.float32))
    for k in range(width // LANES):
        put(4 * lines + k * bag_count, grad[:, k * LANES:(k + 1) * LANES])


def split_two(x):
    high = x.astype(jnp.bfloat16)
    return high, (x - high.astype(jnp.float32)).astype(jnp.bfloat16)


def codes(ids, bags, bag_count, base):
    rel = ids.astype(jnp.int32) - base
    code = lax.shift_right_arithmetic(rel, 7) * bag_count + bags.astype(jnp.int32)
    return code.astype(jnp.float32), (rel & (LANES - 1)).astype(jnp.float32)


def count_into(counts, code_ref, lane_ref, devices, bag_count):
    blocks = counts.shape[0]
    lines = code_ref.shape[1]
    one, none = jnp.ones((), jnp.bfloat16), jnp.zeros((), jnp.bfloat16)

    def one_hot(ref, d, size):
        numbers = lax.broadcasted_iota(jnp.int32, (size, LANES), 0).astype(jnp.bfloat16)
        parts = []
        for k in range(lines):
            row = jnp.broadcast_to(ref[d, k:k + 1, :], (size, LANES)).astype(jnp.bfloat16)
            parts.append(jnp.where(numbers == row, one, none))
        return jnp.concatenate(parts, axis=1)

    for d in range(devices):
        hits = lax.dot_general(
            one_hot(code_ref, d, blocks * bag_count), one_hot(lane_ref, d, LANES),
            (((1,), (1,)), ((), ())), preferred_element_type=jnp.float32)
        counts[:, d * bag_count:(d + 1) * bag_count, :] = hits.reshape(
            blocks, bag_count, LANES)


def pool_kernel(
    bag_count, lines, turn, msg, table, out, joined, kept, code_ref, lane_ref, counts, sems,
):
    rows_dev, width = table.shape
    rows = rows_dev // sems.shape[0]
    fetches = [
        pltpu.make_async_copy(
            table.at[pl.ds(i * rows, rows), :], kept.at[pl.ds(i * rows, rows), :], sems.at[i])
        for i in range(sems.shape[0])
    ]
    for fetch in fetches:
        fetch.start()
    owners = msg.shape[0]
    base = lax.axis_index("rows") * rows_dev
    code_ref[...], lane_ref[...] = codes(
        msg[:, 0:lines, :], msg[:, lines:2 * lines, :], bag_count, base)
    joined[...] = msg[:, 2 * lines:, :]
    count_into(counts, code_ref, lane_ref, owners, bag_count)
    blocks = rows_dev // LANES
    flat = jnp.concatenate(
        [counts[h].astype(jnp.bfloat16) for h in range(blocks)], axis=1)
    total = jnp.zeros((owners * bag_count, width), jnp.float32)
    for i, fetch in enumerate(fetches):
        fetch.wait()
        here = slice(i * rows, (i + 1) * rows)
        for part in split_two(kept[here, :]):
            total += jnp.dot(flat[:, here], part, preferred_element_type=jnp.float32)
    for i in range(owners):
        seen = (i + turn) % owners
        out[i] = total[seen * bag_count:(seen + 1) * bag_count, :]


def update_kernel(bag_count, lines, groups, chunk, *refs):
    sources, (table, accum, new_table, new_accum) = refs[:groups], refs[groups:groups + 4]
    msg, code_ref, lane_ref, counts, grads, sums, fresh_table, sems = refs[groups + 4:]
    rows_dev, width = table.shape
    pieces = sems.shape[0]
    devices = msg.shape[0]
    owners = devices // groups
    blocks = counts.shape[0]
    base = lax.axis_index("rows") * rows_dev
    single = devices == chunk

    def count_chunk(first):
        here = pl.ds(first, chunk)
        code_ref[...], lane_ref[...] = codes(
            msg[here, 0:lines, :], msg[here, lines:2 * lines, :], bag_count, base)
        count_into(counts, code_ref, lane_ref, chunk, bag_count)
        for k in range(width // LANES):
            start = 2 * lines + k * bag_count
            grads[:, k * LANES:(k + 1) * LANES] = msg[
                here, start:start + bag_count, :].reshape(chunk * bag_count, LANES)
        return split_two(grads[...])

    def block_sum(h, parts):
        hits = counts[h].astype(jnp.bfloat16)
        total = jnp.zeros((LANES, width), jnp.float32)
        for part in parts:
            total += lax.dot_general(
                hits, part, (((0,), (0,)), ((), ())), preferred_element_type=jnp.float32)
        return total

    for i, source in enumerate(sources):
        msg[i * owners:(i + 1) * owners] = source[...]
    if single:
        parts = count_chunk(0)
    else:
        sums[...] = jnp.zeros_like(sums)

        @pl.loop(0, devices // chunk)
        def _(c):
            parts = count_chunk(c * chunk)

            @pl.loop(0, blocks)
            def _(h):
                sums[h] += block_sum(h, parts)

    diagonal = (
        lax.broadcasted_iota(jnp.int32, (LANES, LANES), 0)
        == lax.broadcasted_iota(jnp.int32, (LANES, LANES), 1))
    per_piece = blocks // pieces
    copies = []
    for h in range(blocks):
        i = h // per_piece
        grad = block_sum(h, parts) if single else sums[h]
        here = slice(h * LANES, (h + 1) * LANES)
        squares = grad * grad
        folded = squares[:, 0:LANES]
        for k in range(1, width // LANES):
            folded += squares[:, k * LANES:(k + 1) * LANES]
        old = jnp.where(diagonal, accum[h:h + 1, :], 0.0)
        fresh = jnp.sum(folded * (1.0 / width) + old, axis=1, keepdims=True)
        fresh_table[here, :] = table[here, :] - grad * (learn_rate * lax.rsqrt(fresh))
        new_accum[h:h + 1, :] = jnp.sum(
            jnp.where(diagonal, fresh, 0.0), axis=0, keepdims=True)
        if (h + 1) % per_piece == 0:
            piece = pl.ds(i * per_piece * LANES, per_piece * LANES)
            copies.append(pltpu.make_async_copy(
                fresh_table.at[piece, :], new_table.at[piece, :], sems.at[i]))
            copies[-1].start()
    for copy in copies:
        copy.wait()


def finish_kernel(returned, accum, pooled, new_accum):
    total = returned[0]
    for i in range(1, returned.shape[0]):
        total += returned[i]
    pooled[...] = total
    new_accum[...] = accum[...]


def listing(size, leader):
    return [(i + leader) % size for i in range(size)]


def exchange(x, axis, leader):
    order = listing(lax.axis_size(axis), leader)
    return lax.all_to_all(
        x, axis, split_axis=0, concat_axis=0, axis_index_groups=[order], tiled=True)


def shift(x, axis, step):
    size = lax.axis_size(axis)
    return lax.ppermute(x, axis, [(i, (i + step) % size) for i in range(size)])


def local(
    item_table, row_accum, owner_map, row_index, bag_index,
    prev_owner, prev_row, prev_bag, grad_pooled,
):
    owners, groups = lax.axis_size("rows"), lax.axis_size("dp")
    devices = owners * groups
    out_leader, back_leader = owners // 2 - 1, owners // 2
    rows_dev, width = item_table.shape
    bag_count = grad_pooled.shape[2]
    lines = row_index.shape[2] // LANES
    blocks = rows_dev // LANES
    prev_length = 2 * lines + bag_count * width // LANES
    vmem = pl.BlockSpec(memory_space=pltpu.VMEM)
    hbm = pl.BlockSpec(memory_space=pltpu.HBM)
    params = pltpu.CompilerParams(vmem_limit_bytes=16 * 1024 * 1024)
    chunk = min(devices, LANES // bag_count)

    def stay(x):
        return pltpu.with_memory_space_constraint(x, pltpu.HBM)

    def line(x):
        return x.reshape(lines, LANES)

    message = pl.pallas_call(
        functools.partial(pack_kernel, rows_dev),
        out_shape=pltpu.VMEM((owners, 2 * lines + prev_length, LANES), jnp.float32),
        in_specs=[hbm] * 7,
        out_specs=vmem,
        scratch_shapes=[pltpu.VMEM((lines, LANES), jnp.int32)] * 6
        + [pltpu.VMEM((bag_count, width), jnp.float32), pltpu.SemaphoreType.DMA((7,))],
        compiler_params=params,
        name="pack",
    )(*[stay(x) for x in (
        line(owner_map), line(row_index), line(bag_index),
        line(prev_owner), line(prev_row), line(prev_bag), grad_pooled[0, 0],
    )])
    gathered = exchange(message, "rows", out_leader)

    pieces = 4
    partial_pooled, joined, kept = pl.pallas_call(
        functools.partial(pool_kernel, bag_count, lines, back_leader - out_leader),
        out_shape=(
            pltpu.VMEM((owners, bag_count, width), jnp.float32),
            pltpu.VMEM((owners, prev_length, LANES), jnp.float32),
            pltpu.VMEM((rows_dev, width), jnp.float32),
        ),
        in_specs=[vmem, hbm],
        out_specs=[vmem] * 3,
        scratch_shapes=[
            pltpu.VMEM((owners, lines, LANES), jnp.float32),
            pltpu.VMEM((owners, lines, LANES), jnp.float32),
            pltpu.VMEM((blocks, owners * bag_count, LANES), jnp.float32),
            pltpu.SemaphoreType.DMA((pieces,)),
        ],
        compiler_params=params,
        cost_estimate=pl.CostEstimate(
            flops=4 * owners * bag_count * rows_dev * width,
            bytes_accessed=rows_dev * width * 4, transcendentals=0),
        name="pool",
    )(gathered, stay(item_table))
    returned = exchange(partial_pooled, "rows", back_leader)
    all_groups = [joined] + [shift(joined, "dp", k) for k in range(1, groups)]

    segments = chunk * bag_count
    new_table, new_accum = pl.pallas_call(
        functools.partial(update_kernel, bag_count, lines, groups, chunk),
        out_shape=(
            jax.ShapeDtypeStruct((rows_dev, width), jnp.float32),
            pltpu.VMEM((blocks, LANES), jnp.float32),
        ),
        in_specs=[vmem] * (groups + 2),
        out_specs=(hbm, vmem),
        scratch_shapes=[
            pltpu.VMEM((devices, prev_length, LANES), jnp.float32),
            pltpu.VMEM((chunk, lines, LANES), jnp.float32),
            pltpu.VMEM((chunk, lines, LANES), jnp.float32),
            pltpu.VMEM((blocks, segments, LANES), jnp.float32),
            pltpu.VMEM((segments, width), jnp.float32),
            pltpu.VMEM((blocks, LANES, width) if devices > chunk else (1, 8, LANES), jnp.float32),
            pltpu.VMEM((rows_dev, width), jnp.float32),
            pltpu.SemaphoreType.DMA((pieces,)),
        ],
        compiler_params=params if devices == chunk else pltpu.CompilerParams(
            vmem_limit_bytes=40 * 1024 * 1024),
        cost_estimate=pl.CostEstimate(flops=1, bytes_accessed=1 << 20, transcendentals=0),
        name="update",
    )(*all_groups, kept, row_accum.reshape(blocks, LANES))

    pooled, new_accum = pl.pallas_call(
        finish_kernel,
        out_shape=(
            jax.ShapeDtypeStruct((bag_count, width), jnp.float32),
            jax.ShapeDtypeStruct((blocks, LANES), jnp.float32),
        ),
        in_specs=[vmem] * 2,
        out_specs=[vmem] * 2,
        compiler_params=params,
        name="finish",
    )(returned, new_accum)
    return (pooled[None, None], new_table, new_accum.reshape(rows_dev))


def solution(mesh):
    placed = (
        P("rows", None),
        P("rows"),
        P("dp", "rows", None, None),
        P("dp", "rows", None),
        P("dp", "rows", None),
        P("dp", "rows", None, None),
        P("dp", "rows", None),
        P("dp", "rows", None),
        P("dp", "rows", None, None),
    )
    return jax.shard_map(
        local,
        mesh=mesh,
        in_specs=placed,
        out_specs=(P("dp", "rows", None, None), P("rows", None), P("rows")),
        check_vma=False,
    )
```

```python
import functools

import jax
import jax.numpy as jnp
from jax import lax
from jax.experimental import pallas as pl
from jax.experimental.pallas import tpu as pltpu
from jax.sharding import PartitionSpec as P

learn_rate = 0.1
LANES = 128


def pack_kernel(*refs):
    sources, table, out, part, held, sems = refs[:7], refs[7], refs[8], refs[9], refs[10:17], refs[17]
    rows_dev = table.shape[0]
    copies = [
        pltpu.make_async_copy(source, place, sems.at[i])
        for i, (source, place) in enumerate(zip(sources, held))
    ]
    for copy in copies:
        copy.start()
    fetch = pltpu.make_async_copy(table.at[pl.ds(0, part.shape[0]), :], part, sems.at[7])
    fetch.start()
    for copy in copies:
        copy.wait()
    owner, row, bag, prev_owner, prev_row, prev_bag, grad = held
    lines = row.shape[0]
    bag_count, width = grad.shape

    def put(start, value):
        shape = (out.shape[0],) + value.shape
        out[:, start:start + value.shape[0], :] = jnp.broadcast_to(value[None], shape)

    put(0, (owner[...] * rows_dev + row[...]).astype(jnp.float32))
    put(lines, bag[...].astype(jnp.float32))
    put(2 * lines, (prev_owner[...] * rows_dev + prev_row[...]).astype(jnp.float32))
    put(3 * lines, prev_bag[...].astype(jnp.float32))
    for k in range(width // LANES):
        put(4 * lines + k * bag_count, grad[:, k * LANES:(k + 1) * LANES])
    fetch.wait()


def split_two(x):
    high = x.astype(jnp.bfloat16)
    return high, (x - high.astype(jnp.float32)).astype(jnp.bfloat16)


def codes(ids, bags, bag_count, base):
    rel = ids.astype(jnp.int32) - base
    code = lax.shift_right_arithmetic(rel, 7) * bag_count + bags.astype(jnp.int32)
    return code.astype(jnp.float32), (rel & (LANES - 1)).astype(jnp.float32)


def count_into(counts, code_ref, lane_ref, devices, bag_count):
    blocks = counts.shape[0]
    lines = code_ref.shape[1]
    one, none = jnp.ones((), jnp.bfloat16), jnp.zeros((), jnp.bfloat16)

    def one_hot(ref, d, size):
        numbers = lax.broadcasted_iota(jnp.int32, (size, LANES), 0).astype(jnp.bfloat16)
        parts = []
        for k in range(lines):
            row = jnp.broadcast_to(ref[d, k:k + 1, :], (size, LANES)).astype(jnp.bfloat16)
            parts.append(jnp.where(numbers == row, one, none))
        return jnp.concatenate(parts, axis=1)

    for d in range(devices):
        hits = lax.dot_general(
            one_hot(code_ref, d, blocks * bag_count), one_hot(lane_ref, d, LANES),
            (((1,), (1,)), ((), ())), preferred_element_type=jnp.float32)
        counts[:, d * bag_count:(d + 1) * bag_count, :] = hits.reshape(
            blocks, bag_count, LANES)


def pool_kernel(
    bag_count, lines, turn, msg, first, table, out, joined, second,
    code_ref, lane_ref, counts, sem,
):
    rows_dev, width = table.shape
    half = first.shape[0]
    fetch = pltpu.make_async_copy(table.at[pl.ds(half, rows_dev - half), :], second, sem)
    fetch.start()
    owners = msg.shape[0]
    base = lax.axis_index("rows") * rows_dev
    code_ref[...], lane_ref[...] = codes(
        msg[:, 0:lines, :], msg[:, lines:2 * lines, :], bag_count, base)
    joined[...] = msg[:, 2 * lines:, :]
    count_into(counts, code_ref, lane_ref, owners, bag_count)
    blocks = rows_dev // LANES
    flat = jnp.concatenate(
        [counts[h].astype(jnp.bfloat16) for h in range(blocks)], axis=1)
    total = jnp.zeros((owners * bag_count, width), jnp.float32)
    for part in split_two(first[...]):
        total += jnp.dot(flat[:, :half], part, preferred_element_type=jnp.float32)
    fetch.wait()
    for part in split_two(second[...]):
        total += jnp.dot(flat[:, half:], part, preferred_element_type=jnp.float32)
    for i in range(owners):
        seen = (i + turn) % owners
        out[i] = total[seen * bag_count:(seen + 1) * bag_count, :]


def read_chunk(msg, here, chunk, lines, bag_count, base, code_ref, lane_ref, counts, grads):
    width = grads.shape[1]
    code_ref[...], lane_ref[...] = codes(
        msg[here, 0:lines, :], msg[here, lines:2 * lines, :], bag_count, base)
    count_into(counts, code_ref, lane_ref, chunk, bag_count)
    for k in range(width // LANES):
        start = 2 * lines + k * bag_count
        grads[:, k * LANES:(k + 1) * LANES] = msg[
            here, start:start + bag_count, :].reshape(chunk * bag_count, LANES)


def block_sum(hits, parts):
    total = jnp.zeros((hits.shape[1], parts[0].shape[1]), jnp.float32)
    for part in parts:
        total += lax.dot_general(
            hits, part, (((0,), (0,)), ((), ())), preferred_element_type=jnp.float32)
    return total


def apply_rows(grad_of, tables, accum, new_table, new_accum, fresh_table, sems):
    blocks, width = accum.shape[0], fresh_table.shape[1]
    per_table = blocks // len(tables)
    diagonal = (
        lax.broadcasted_iota(jnp.int32, (LANES, LANES), 0)
        == lax.broadcasted_iota(jnp.int32, (LANES, LANES), 1))
    per_piece = blocks // sems.shape[0]
    copies = []
    for h in range(blocks):
        grad = grad_of(h)
        here = slice(h * LANES, (h + 1) * LANES)
        squares = grad * grad
        folded = squares[:, 0:LANES]
        for k in range(1, width // LANES):
            folded += squares[:, k * LANES:(k + 1) * LANES]
        old = jnp.where(diagonal, accum[h:h + 1, :], 0.0)
        fresh = jnp.sum(folded * (1.0 / width) + old, axis=1, keepdims=True)
        start = h % per_table * LANES
        old_rows = tables[h // per_table][start:start + LANES, :]
        fresh_table[here, :] = old_rows - grad * (learn_rate * lax.rsqrt(fresh))
        new_accum[h:h + 1, :] = jnp.sum(
            jnp.where(diagonal, fresh, 0.0), axis=0, keepdims=True)
        if (h + 1) % per_piece == 0:
            i = h // per_piece
            piece = pl.ds(i * per_piece * LANES, per_piece * LANES)
            copies.append(pltpu.make_async_copy(
                fresh_table.at[piece, :], new_table.at[piece, :], sems.at[i]))
            copies[-1].start()
    for copy in copies:
        copy.wait()


def count_kernel(bag_count, lines, *refs):
    number = (len(refs) - 8) // 2
    sources, passed, (counts_out, high, low) = refs[:number], refs[number:-8], refs[-8:-5]
    msg, code_ref, lane_ref, counts, grads = refs[-5:]
    owners = sources[0].shape[0]
    devices, blocks = msg.shape[0], counts.shape[0]
    base = lax.axis_index("rows") * (blocks * LANES)
    for i, source in enumerate(sources):
        msg[i * owners:(i + 1) * owners] = source[...]
        passed[i][...] = source[...]
    read_chunk(
        msg, slice(0, devices), devices, lines, bag_count, base,
        code_ref, lane_ref, counts, grads)
    counts_out[...] = counts[...].astype(jnp.bfloat16)
    high[...], low[...] = split_two(grads[...])


def apply_kernel(bag_count, lines, late, *refs):
    sources, (counted, high, low, *tables, accum) = refs[:late], refs[late:late + 6]
    new_table, new_accum, msg, code_ref, lane_ref, counts, grads, fresh_table, sems = refs[late + 6:]
    owners = sources[0].shape[0]
    devices, blocks = msg.shape[0], counts.shape[0]
    base = lax.axis_index("rows") * (blocks * LANES)
    for i, source in enumerate(sources):
        msg[i * owners:(i + 1) * owners] = source[...]
    read_chunk(
        msg, slice(0, devices), devices, lines, bag_count, base,
        code_ref, lane_ref, counts, grads)
    parts = [
        jnp.concatenate([early[...], late], axis=0)
        for early, late in zip((high, low), split_two(grads[...]))
    ]

    def grad_of(h):
        hits = jnp.concatenate([counted[h], counts[h].astype(jnp.bfloat16)], axis=0)
        return block_sum(hits, parts)

    apply_rows(grad_of, tables, accum, new_table, new_accum, fresh_table, sems)


def update_kernel(bag_count, lines, groups, chunk, *refs):
    sources, (*tables, accum, new_table, new_accum) = refs[:groups], refs[groups:groups + 5]
    msg, code_ref, lane_ref, counts, grads, sums, fresh_table, sems = refs[groups + 5:]
    devices, blocks = msg.shape[0], counts.shape[0]
    owners = devices // groups
    base = lax.axis_index("rows") * (blocks * LANES)
    for i, source in enumerate(sources):
        msg[i * owners:(i + 1) * owners] = source[...]
    sums[...] = jnp.zeros_like(sums)

    @pl.loop(0, devices // chunk)
    def _(c):
        read_chunk(
            msg, pl.ds(c * chunk, chunk), chunk, lines, bag_count, base,
            code_ref, lane_ref, counts, grads)
        parts = split_two(grads[...])

        @pl.loop(0, blocks)
        def _(h):
            sums[h] += block_sum(counts[h].astype(jnp.bfloat16), parts)

    apply_rows(lambda h: sums[h], tables, accum, new_table, new_accum, fresh_table, sems)


def pass_kernel(first, second, accum, new_table, new_accum, sems):
    half = first.shape[0]
    copies = [
        pltpu.make_async_copy(part, new_table.at[pl.ds(i * half, half), :], sems.at[i])
        for i, part in enumerate((first, second))
    ]
    for copy in copies:
        copy.start()
    new_accum[...] = accum[...]
    for copy in copies:
        copy.wait()


def finish_kernel(returned, accum, pooled, new_accum):
    total = returned[0]
    for i in range(1, returned.shape[0]):
        total += returned[i]
    pooled[...] = total
    new_accum[...] = accum[...]


def listing(size, leader):
    return [(i + leader) % size for i in range(size)]


def exchange(x, axis, leader):
    order = listing(lax.axis_size(axis), leader)
    return lax.all_to_all(
        x, axis, split_axis=0, concat_axis=0, axis_index_groups=[order], tiled=True)


def forward(x, axis, step):
    size = lax.axis_size(axis)
    return lax.ppermute(
        x, axis, [(i, ((i // 2 + step) * 2 + 1 - i % 2) % size) for i in range(size)])


def local(
    item_table, row_accum, owner_map, row_index, bag_index,
    prev_owner, prev_row, prev_bag, grad_pooled,
):
    owners, groups = lax.axis_size("rows"), lax.axis_size("dp")
    devices = owners * groups
    out_leader, back_leader = owners // 2 - 1, owners // 2
    rows_dev, width = item_table.shape
    bag_count = grad_pooled.shape[2]
    lines = row_index.shape[2] // LANES
    blocks = rows_dev // LANES
    prev_length = 2 * lines + bag_count * width // LANES
    vmem = pl.BlockSpec(memory_space=pltpu.VMEM)
    hbm = pl.BlockSpec(memory_space=pltpu.HBM)
    params = pltpu.CompilerParams(vmem_limit_bytes=16 * 1024 * 1024)
    chunk = min(devices, LANES // bag_count)

    def stay(x):
        return pltpu.with_memory_space_constraint(x, pltpu.HBM)

    def line(x):
        return x.reshape(lines, LANES)

    half = rows_dev // 2
    message, first = pl.pallas_call(
        pack_kernel,
        out_shape=(
            pltpu.VMEM((owners, 2 * lines + prev_length, LANES), jnp.float32),
            pltpu.VMEM((half, width), jnp.float32),
        ),
        in_specs=[hbm] * 8,
        out_specs=[vmem] * 2,
        scratch_shapes=[pltpu.VMEM((lines, LANES), jnp.int32)] * 6
        + [pltpu.VMEM((bag_count, width), jnp.float32), pltpu.SemaphoreType.DMA((8,))],
        compiler_params=params,
        name="pack",
    )(*[stay(x) for x in (
        line(owner_map), line(row_index), line(bag_index),
        line(prev_owner), line(prev_row), line(prev_bag), grad_pooled[0, 0], item_table,
    )])
    gathered = exchange(message, "rows", out_leader)

    partial_pooled, joined, second = pl.pallas_call(
        functools.partial(pool_kernel, bag_count, lines, back_leader - out_leader),
        out_shape=(
            pltpu.VMEM((owners, bag_count, width), jnp.float32),
            pltpu.VMEM((owners, prev_length, LANES), jnp.float32),
            pltpu.VMEM((rows_dev - half, width), jnp.float32),
        ),
        in_specs=[vmem, vmem, hbm],
        out_specs=[vmem] * 3,
        scratch_shapes=[
            pltpu.VMEM((owners, lines, LANES), jnp.float32),
            pltpu.VMEM((owners, lines, LANES), jnp.float32),
            pltpu.VMEM((blocks, owners * bag_count, LANES), jnp.float32),
            pltpu.SemaphoreType.DMA,
        ],
        compiler_params=params,
        cost_estimate=pl.CostEstimate(
            flops=4 * owners * bag_count * rows_dev * width,
            bytes_accessed=rows_dev * width * 4, transcendentals=0),
        name="pool",
    )(gathered, first, stay(item_table))
    returned = exchange(partial_pooled, "rows", back_leader)
    there = [joined] + [forward(joined, "dp", step) for step in range(1, groups // 2)]

    segments = chunk * bag_count
    results = 8 if blocks % 8 == 0 else 1
    updated = (
        pltpu.HBM((rows_dev, width), jnp.float32),
        pltpu.VMEM((blocks, LANES), jnp.float32),
    )

    def room(count):
        return [
            pltpu.VMEM((count, lines, LANES), jnp.float32),
            pltpu.VMEM((count, lines, LANES), jnp.float32),
            pltpu.VMEM((blocks, count * bag_count, LANES), jnp.float32),
            pltpu.VMEM((count * bag_count, width), jnp.float32),
        ]

    fresh_room = [
        pltpu.VMEM((rows_dev, width), jnp.float32),
        pltpu.SemaphoreType.DMA((results,)),
    ]

    def hand_over(there, tables, row_accum):
        if devices > chunk:
            handed = [forward(x, "dp", 0) for x in there]
            return pl.pallas_call(
                functools.partial(update_kernel, bag_count, lines, groups, chunk),
                out_shape=updated,
                in_specs=[vmem] * (groups + 3),
                out_specs=(hbm, vmem),
                scratch_shapes=[pltpu.VMEM((devices, prev_length, LANES), jnp.float32)]
                + room(chunk) + [pltpu.VMEM((blocks, LANES, width), jnp.float32)] + fresh_room,
                compiler_params=pltpu.CompilerParams(vmem_limit_bytes=40 * 1024 * 1024),
                name="update",
            )(*there, *handed, *tables, row_accum)
        number = len(there)
        count = number * owners
        *passed, counted, high, low = pl.pallas_call(
            functools.partial(count_kernel, bag_count, lines),
            out_shape=[pltpu.VMEM((owners, prev_length, LANES), jnp.float32)] * number + [
                pltpu.VMEM((blocks, count * bag_count, LANES), jnp.bfloat16),
                pltpu.VMEM((count * bag_count, width), jnp.bfloat16),
                pltpu.VMEM((count * bag_count, width), jnp.bfloat16),
            ],
            in_specs=[vmem] * number,
            out_specs=[vmem] * (number + 3),
            scratch_shapes=[pltpu.VMEM((count, prev_length, LANES), jnp.float32)] + room(count),
            compiler_params=params,
            name="count",
        )(*there)
        handed = [forward(x, "dp", 0) for x in passed]
        return pl.pallas_call(
            functools.partial(apply_kernel, bag_count, lines, number),
            out_shape=updated,
            in_specs=[vmem] * (number + 6),
            out_specs=(hbm, vmem),
            scratch_shapes=[pltpu.VMEM((count, prev_length, LANES), jnp.float32)]
            + room(count) + fresh_room,
            compiler_params=params,
            name="apply",
        )(*handed, counted, high, low, *tables, row_accum)

    def skip(there, tables, row_accum):
        return pl.pallas_call(
            pass_kernel,
            out_shape=updated,
            in_specs=[vmem] * 3,
            out_specs=(hbm, vmem),
            scratch_shapes=[pltpu.SemaphoreType.DMA((2,))],
            compiler_params=params,
            name="pass",
        )(*tables, row_accum)

    inside = lax.axis_index("dp") < groups
    new_table, new_accum = lax.cond(
        inside, hand_over, skip, there, (first, second), row_accum.reshape(blocks, LANES))

    pooled, new_accum = pl.pallas_call(
        finish_kernel,
        out_shape=(
            jax.ShapeDtypeStruct((bag_count, width), jnp.float32),
            jax.ShapeDtypeStruct((blocks, LANES), jnp.float32),
        ),
        in_specs=[vmem] * 2,
        out_specs=[vmem] * 2,
        compiler_params=params,
        name="finish",
    )(returned, new_accum)
    return (pooled[None, None], new_table, new_accum.reshape(rows_dev))


def solution(mesh):
    placed = (
        P("rows", None),
        P("rows"),
        P("dp", "rows", None, None),
        P("dp", "rows", None),
        P("dp", "rows", None),
        P("dp", "rows", None, None),
        P("dp", "rows", None),
        P("dp", "rows", None),
        P("dp", "rows", None, None),
    )
    return jax.shard_map(
        local,
        mesh=mesh,
        in_specs=placed,
        out_specs=(P("dp", "rows", None, None), P("rows", None), P("rows")),
        check_vma=False,
    )
```

```python
import functools

import jax
import jax.numpy as jnp
from jax import lax
from jax.experimental import pallas as pl
from jax.experimental.pallas import tpu as pltpu
from jax.sharding import PartitionSpec as P

learn_rate = 0.1
LANES = 128


def pack_kernel(rows_dev, *refs):
    sources, out, held, sems = refs[:7], refs[7], refs[8:15], refs[15]
    copies = [
        pltpu.make_async_copy(source, place, sems.at[i])
        for i, (source, place) in enumerate(zip(sources, held))
    ]
    for copy in copies:
        copy.start()
    for copy in copies:
        copy.wait()
    owner, row, bag, prev_owner, prev_row, prev_bag, grad = held
    lines = row.shape[0]
    bag_count, width = grad.shape

    def put(start, value):
        shape = (out.shape[0],) + value.shape
        out[:, start:start + value.shape[0], :] = jnp.broadcast_to(value[None], shape)

    put(0, (owner[...] * rows_dev + row[...]).astype(jnp.float32))
    put(lines, bag[...].astype(jnp.float32))
    put(2 * lines, (prev_owner[...] * rows_dev + prev_row[...]).astype(jnp.float32))
    put(3 * lines, prev_bag[...].astype(jnp.float32))
    for k in range(width // LANES):
        put(4 * lines + k * bag_count, grad[:, k * LANES:(k + 1) * LANES])


def split_two(x):
    high = x.astype(jnp.bfloat16)
    return high, (x - high.astype(jnp.float32)).astype(jnp.bfloat16)


def codes(ids, bags, bag_count, base):
    rel = ids.astype(jnp.int32) - base
    code = lax.shift_right_arithmetic(rel, 7) * bag_count + bags.astype(jnp.int32)
    return code.astype(jnp.float32), (rel & (LANES - 1)).astype(jnp.float32)


def count_into(counts, code_ref, lane_ref, devices, bag_count):
    blocks = counts.shape[0]
    lines = code_ref.shape[1]
    one, none = jnp.ones((), jnp.bfloat16), jnp.zeros((), jnp.bfloat16)

    def one_hot(ref, d, size):
        numbers = lax.broadcasted_iota(jnp.int32, (size, LANES), 0).astype(jnp.bfloat16)
        parts = []
        for k in range(lines):
            row = jnp.broadcast_to(ref[d, k:k + 1, :], (size, LANES)).astype(jnp.bfloat16)
            parts.append(jnp.where(numbers == row, one, none))
        return jnp.concatenate(parts, axis=1)

    for d in range(devices):
        hits = lax.dot_general(
            one_hot(code_ref, d, blocks * bag_count), one_hot(lane_ref, d, LANES),
            (((1,), (1,)), ((), ())), preferred_element_type=jnp.float32)
        counts[:, d * bag_count:(d + 1) * bag_count, :] = hits.reshape(
            blocks, bag_count, LANES)


def pool_kernel(
    bag_count, lines, turn, msg, table, out, joined, kept, code_ref, lane_ref, counts, sems,
):
    rows_dev, width = table.shape
    pieces = sems.shape[0]
    rows = rows_dev // pieces
    fetches = [
        pltpu.make_async_copy(
            table.at[pl.ds(i * rows, rows), :], kept.at[pl.ds(i * rows, rows), :], sems.at[i])
        for i in range(pieces)
    ]
    for fetch in fetches:
        fetch.start()
    owners = msg.shape[0]
    base = lax.axis_index("rows") * rows_dev
    code_ref[...], lane_ref[...] = codes(
        msg[:, 0:lines, :], msg[:, lines:2 * lines, :], bag_count, base)
    joined[...] = msg[:, 2 * lines:, :]
    count_into(counts, code_ref, lane_ref, owners, bag_count)
    blocks = rows_dev // LANES
    flat = jnp.concatenate(
        [counts[h].astype(jnp.bfloat16) for h in range(blocks)], axis=1)
    total = jnp.zeros((owners * bag_count, width), jnp.float32)
    for i, fetch in enumerate(fetches):
        fetch.wait()
        here = slice(i * rows, (i + 1) * rows)
        for part in split_two(kept[here, :]):
            total += jnp.dot(flat[:, here], part, preferred_element_type=jnp.float32)
    for i in range(owners):
        seen = (i + turn) % owners
        out[i] = total[seen * bag_count:(seen + 1) * bag_count, :]


def read_chunk(msg, here, chunk, lines, bag_count, base, code_ref, lane_ref, counts, grads):
    width = grads.shape[1]
    code_ref[...], lane_ref[...] = codes(
        msg[here, 0:lines, :], msg[here, lines:2 * lines, :], bag_count, base)
    count_into(counts, code_ref, lane_ref, chunk, bag_count)
    for k in range(width // LANES):
        start = 2 * lines + k * bag_count
        grads[:, k * LANES:(k + 1) * LANES] = msg[
            here, start:start + bag_count, :].reshape(chunk * bag_count, LANES)


def block_sum(hits, parts):
    total = jnp.zeros((hits.shape[1], parts[0].shape[1]), jnp.float32)
    for part in parts:
        total += lax.dot_general(
            hits, part, (((0,), (0,)), ((), ())), preferred_element_type=jnp.float32)
    return total


def apply_rows(grad_of, table, accum, new_table, new_accum, fresh_table, sems):
    blocks, width = accum.shape[0], fresh_table.shape[1]
    diagonal = (
        lax.broadcasted_iota(jnp.int32, (LANES, LANES), 0)
        == lax.broadcasted_iota(jnp.int32, (LANES, LANES), 1))
    per_piece = blocks // sems.shape[0]
    copies = []
    for h in range(blocks):
        grad = grad_of(h)
        here = slice(h * LANES, (h + 1) * LANES)
        squares = grad * grad
        folded = squares[:, 0:LANES]
        for k in range(1, width // LANES):
            folded += squares[:, k * LANES:(k + 1) * LANES]
        old = jnp.where(diagonal, accum[h:h + 1, :], 0.0)
        fresh = jnp.sum(folded * (1.0 / width) + old, axis=1, keepdims=True)
        fresh_table[here, :] = table[here, :] - grad * (learn_rate * lax.rsqrt(fresh))
        new_accum[h:h + 1, :] = jnp.sum(
            jnp.where(diagonal, fresh, 0.0), axis=0, keepdims=True)
        if (h + 1) % per_piece == 0:
            i = h // per_piece
            piece = pl.ds(i * per_piece * LANES, per_piece * LANES)
            copies.append(pltpu.make_async_copy(
                fresh_table.at[piece, :], new_table.at[piece, :], sems.at[i]))
            copies[-1].start()
    for copy in copies:
        copy.wait()


def count_kernel(bag_count, lines, *refs):
    sources, (counts_out, high, low) = refs[:-8], refs[-8:-5]
    msg, code_ref, lane_ref, counts, grads = refs[-5:]
    owners = sources[0].shape[0]
    devices, blocks = msg.shape[0], counts.shape[0]
    base = lax.axis_index("rows") * (blocks * LANES)
    for i, source in enumerate(sources):
        msg[i * owners:(i + 1) * owners] = source[...]
    read_chunk(
        msg, slice(0, devices), devices, lines, bag_count, base,
        code_ref, lane_ref, counts, grads)
    counts_out[...] = counts[...].astype(jnp.bfloat16)
    high[...], low[...] = split_two(grads[...])


def apply_kernel(bag_count, lines, late, *refs):
    sources, (counted, high, low, table, accum) = refs[:late], refs[late:late + 5]
    new_table, new_accum, msg, code_ref, lane_ref, counts, grads, fresh_table, sems = refs[late + 5:]
    owners = sources[0].shape[0]
    devices, blocks = msg.shape[0], counts.shape[0]
    base = lax.axis_index("rows") * (blocks * LANES)
    for i, source in enumerate(sources):
        msg[i * owners:(i + 1) * owners] = source[...]
    read_chunk(
        msg, slice(0, devices), devices, lines, bag_count, base,
        code_ref, lane_ref, counts, grads)
    parts = [
        jnp.concatenate([early[...], late], axis=0)
        for early, late in zip((high, low), split_two(grads[...]))
    ]

    def grad_of(h):
        hits = jnp.concatenate([counted[h], counts[h].astype(jnp.bfloat16)], axis=0)
        return block_sum(hits, parts)

    apply_rows(grad_of, table, accum, new_table, new_accum, fresh_table, sems)


def update_kernel(bag_count, lines, groups, chunk, *refs):
    sources, (table, accum, new_table, new_accum) = refs[:groups], refs[groups:groups + 4]
    msg, code_ref, lane_ref, counts, grads, sums, fresh_table, sems = refs[groups + 4:]
    devices, blocks = msg.shape[0], counts.shape[0]
    owners = devices // groups
    base = lax.axis_index("rows") * (blocks * LANES)
    for i, source in enumerate(sources):
        msg[i * owners:(i + 1) * owners] = source[...]
    sums[...] = jnp.zeros_like(sums)

    @pl.loop(0, devices // chunk)
    def _(c):
        read_chunk(
            msg, pl.ds(c * chunk, chunk), chunk, lines, bag_count, base,
            code_ref, lane_ref, counts, grads)
        parts = split_two(grads[...])

        @pl.loop(0, blocks)
        def _(h):
            sums[h] += block_sum(counts[h].astype(jnp.bfloat16), parts)

    apply_rows(lambda h: sums[h], table, accum, new_table, new_accum, fresh_table, sems)


def pass_kernel(table, accum, new_table, new_accum, sem):
    copy = pltpu.make_async_copy(table, new_table, sem)
    copy.start()
    new_accum[...] = accum[...]
    copy.wait()


def finish_kernel(returned, accum, pooled, new_accum):
    total = returned[0]
    for i in range(1, returned.shape[0]):
        total += returned[i]
    pooled[...] = total
    new_accum[...] = accum[...]


def listing(size, leader):
    return [(i + leader) % size for i in range(size)]


def exchange(x, axis, leader):
    order = listing(lax.axis_size(axis), leader)
    return lax.all_to_all(
        x, axis, split_axis=0, concat_axis=0, axis_index_groups=[order], tiled=True)


def forward(x, axis, step):
    size = lax.axis_size(axis)
    return lax.ppermute(
        x, axis, [(i, ((i // 2 + step) * 2 + 1 - i % 2) % size) for i in range(size)])


def local(
    item_table, row_accum, owner_map, row_index, bag_index,
    prev_owner, prev_row, prev_bag, grad_pooled,
):
    owners, groups = lax.axis_size("rows"), lax.axis_size("dp")
    devices = owners * groups
    out_leader, back_leader = owners // 2 - 1, owners // 2
    rows_dev, width = item_table.shape
    bag_count = grad_pooled.shape[2]
    lines = row_index.shape[2] // LANES
    blocks = rows_dev // LANES
    prev_length = 2 * lines + bag_count * width // LANES
    vmem = pl.BlockSpec(memory_space=pltpu.VMEM)
    hbm = pl.BlockSpec(memory_space=pltpu.HBM)
    params = pltpu.CompilerParams(vmem_limit_bytes=16 * 1024 * 1024)
    chunk = min(devices, LANES // bag_count)

    def stay(x):
        return pltpu.with_memory_space_constraint(x, pltpu.HBM)

    def line(x):
        return x.reshape(lines, LANES)

    message = pl.pallas_call(
        functools.partial(pack_kernel, rows_dev),
        out_shape=pltpu.VMEM((owners, 2 * lines + prev_length, LANES), jnp.float32),
        in_specs=[hbm] * 7,
        out_specs=vmem,
        scratch_shapes=[pltpu.VMEM((lines, LANES), jnp.int32)] * 6
        + [pltpu.VMEM((bag_count, width), jnp.float32), pltpu.SemaphoreType.DMA((7,))],
        compiler_params=params,
        name="pack",
    )(*[stay(x) for x in (
        line(owner_map), line(row_index), line(bag_index),
        line(prev_owner), line(prev_row), line(prev_bag), grad_pooled[0, 0],
    )])
    gathered = exchange(message, "rows", out_leader)

    pieces = 8 if blocks % 8 == 0 else 1
    partial_pooled, joined, kept = pl.pallas_call(
        functools.partial(pool_kernel, bag_count, lines, back_leader - out_leader),
        out_shape=(
            pltpu.VMEM((owners, bag_count, width), jnp.float32),
            pltpu.VMEM((owners, prev_length, LANES), jnp.float32),
            pltpu.VMEM((rows_dev, width), jnp.float32),
        ),
        in_specs=[vmem, hbm],
        out_specs=[vmem] * 3,
        scratch_shapes=[
            pltpu.VMEM((owners, lines, LANES), jnp.float32),
            pltpu.VMEM((owners, lines, LANES), jnp.float32),
            pltpu.VMEM((blocks, owners * bag_count, LANES), jnp.float32),
            pltpu.SemaphoreType.DMA((pieces,)),
        ],
        compiler_params=params,
        cost_estimate=pl.CostEstimate(
            flops=4 * owners * bag_count * rows_dev * width,
            bytes_accessed=rows_dev * width * 4, transcendentals=0),
        name="pool",
    )(gathered, stay(item_table))
    returned = exchange(partial_pooled, "rows", back_leader)
    there = [joined] + [forward(joined, "dp", step) for step in range(1, groups // 2)]

    segments = chunk * bag_count
    updated = (
        pltpu.HBM((rows_dev, width), jnp.float32),
        pltpu.VMEM((blocks, LANES), jnp.float32),
    )

    def room(count):
        return [
            pltpu.VMEM((count, lines, LANES), jnp.float32),
            pltpu.VMEM((count, lines, LANES), jnp.float32),
            pltpu.VMEM((blocks, count * bag_count, LANES), jnp.float32),
            pltpu.VMEM((count * bag_count, width), jnp.float32),
        ]

    fresh_room = [
        pltpu.VMEM((rows_dev, width), jnp.float32),
        pltpu.SemaphoreType.DMA((pieces,)),
    ]

    def hand_over(there, kept, row_accum):
        handed = [forward(x, "dp", 0) for x in there]
        if devices > chunk:
            return pl.pallas_call(
                functools.partial(update_kernel, bag_count, lines, groups, chunk),
                out_shape=updated,
                in_specs=[vmem] * (groups + 2),
                out_specs=(hbm, vmem),
                scratch_shapes=[pltpu.VMEM((devices, prev_length, LANES), jnp.float32)]
                + room(chunk) + [pltpu.VMEM((blocks, LANES, width), jnp.float32)] + fresh_room,
                compiler_params=pltpu.CompilerParams(vmem_limit_bytes=40 * 1024 * 1024),
                name="update",
            )(*there, *handed, kept, row_accum)
        number = len(there)
        count = number * owners
        counted, high, low = pl.pallas_call(
            functools.partial(count_kernel, bag_count, lines),
            out_shape=[
                pltpu.VMEM((blocks, count * bag_count, LANES), jnp.bfloat16),
                pltpu.VMEM((count * bag_count, width), jnp.bfloat16),
                pltpu.VMEM((count * bag_count, width), jnp.bfloat16),
            ],
            in_specs=[vmem] * number,
            out_specs=[vmem] * 3,
            scratch_shapes=[pltpu.VMEM((count, prev_length, LANES), jnp.float32)] + room(count),
            compiler_params=params,
            cost_estimate=pl.CostEstimate(
                flops=1 << 28, bytes_accessed=1 << 22, transcendentals=0),
            name="count",
        )(*there)
        return pl.pallas_call(
            functools.partial(apply_kernel, bag_count, lines, number),
            out_shape=updated,
            in_specs=[vmem] * (number + 5),
            out_specs=(hbm, vmem),
            scratch_shapes=[pltpu.VMEM((count, prev_length, LANES), jnp.float32)]
            + room(count) + fresh_room,
            compiler_params=params,
            name="apply",
        )(*handed, counted, high, low, kept, row_accum)

    def skip(there, kept, row_accum):
        return pl.pallas_call(
            pass_kernel,
            out_shape=updated,
            in_specs=[vmem] * 2,
            out_specs=(hbm, vmem),
            scratch_shapes=[pltpu.SemaphoreType.DMA],
            compiler_params=params,
            name="pass",
        )(kept, row_accum)

    inside = lax.axis_index("dp") < groups
    new_table, new_accum = lax.cond(
        inside, hand_over, skip, there, kept, row_accum.reshape(blocks, LANES))

    pooled, new_accum = pl.pallas_call(
        finish_kernel,
        out_shape=(
            jax.ShapeDtypeStruct((bag_count, width), jnp.float32),
            jax.ShapeDtypeStruct((blocks, LANES), jnp.float32),
        ),
        in_specs=[vmem] * 2,
        out_specs=[vmem] * 2,
        compiler_params=params,
        name="finish",
    )(returned, new_accum)
    return (pooled[None, None], new_table, new_accum.reshape(rows_dev))


def solution(mesh):
    placed = (
        P("rows", None),
        P("rows"),
        P("dp", "rows", None, None),
        P("dp", "rows", None),
        P("dp", "rows", None),
        P("dp", "rows", None, None),
        P("dp", "rows", None),
        P("dp", "rows", None),
        P("dp", "rows", None, None),
    )
    return jax.shard_map(
        local,
        mesh=mesh,
        in_specs=placed,
        out_specs=(P("dp", "rows", None, None), P("rows", None), P("rows")),
        check_vma=False,
    )
```

```python
import functools

import jax
import jax.numpy as jnp
from jax import lax
from jax.experimental import pallas as pl
from jax.experimental.pallas import tpu as pltpu
from jax.sharding import PartitionSpec as P

learn_rate = 0.1
LANES = 128

PREV_BOUNDS = 64


def bound_block(bags, bag_count, first):
    lane = lax.broadcasted_iota(jnp.int32, (1, LANES), 1)
    block = jnp.zeros((1, LANES), jnp.float32)
    for j in range(1, bag_count):
        start = jnp.sum((bags < j).astype(jnp.float32), axis=1, keepdims=True)
        block = jnp.where(lane == first + j - 1, start, block)
    return block


def pack_kernel(rows_dev, *refs):
    sources, out, held, sems = refs[:7], refs[7], refs[8:15], refs[15]
    copies = [
        pltpu.make_async_copy(source, place, sems.at[i])
        for i, (source, place) in enumerate(zip(sources, held))
    ]
    for copy in copies:
        copy.start()
    for copy in copies:
        copy.wait()
    owner, row, bag, prev_owner, prev_row, prev_bag, grad = held
    positions = row.shape[1]
    bag_count, width = grad.shape

    def put(start, value):
        shape = (out.shape[0], 1, value.shape[1])
        out[:, :, start:start + value.shape[1]] = jnp.broadcast_to(value[None], shape)

    put(0, (owner[...] * rows_dev + row[...]).astype(jnp.float32))
    put(positions, (prev_owner[...] * rows_dev + prev_row[...]).astype(jnp.float32))
    put(
        2 * positions,
        bound_block(bag[...], bag_count, 0)
        + bound_block(prev_bag[...], bag_count, PREV_BOUNDS),
    )
    for j in range(bag_count):
        put(2 * positions + LANES + j * width, grad[j:j + 1, :])


def unpack(msg, joined, code_ref, lane_ref, lines, bag_count, width, base):
    devices, positions = msg.shape[0], lines * LANES
    bounds = msg[:, 0, 2 * positions:2 * positions + LANES]
    lane = lax.broadcasted_iota(jnp.int32, (devices, LANES), 1)

    def bags(k, first):
        place = (lane + k * LANES).astype(jnp.float32)
        bag = jnp.zeros((devices, LANES), jnp.float32)
        for j in range(1, bag_count):
            bag += (place >= bounds[:, first + j - 1:first + j]).astype(jnp.float32)
        return bag

    for k in range(lines):
        start = k * LANES
        code_ref[:, k, :], lane_ref[:, k, :] = codes(
            msg[:, 0, start:start + LANES], bags(k, 0), bag_count, base)
        joined[:, k, :] = msg[:, 0, positions + start:positions + start + LANES]
        joined[:, lines + k, :] = bags(k, PREV_BOUNDS)
    for j in range(bag_count):
        for k in range(width // LANES):
            start = 2 * positions + LANES + j * width + k * LANES
            joined[:, 2 * lines + k * bag_count + j, :] = msg[:, 0, start:start + LANES]


def split_two(x):
    high = x.astype(jnp.bfloat16)
    return high, (x - high.astype(jnp.float32)).astype(jnp.bfloat16)


def codes(ids, bags, bag_count, base):
    rel = ids.astype(jnp.int32) - base
    code = lax.shift_right_arithmetic(rel, 7) * bag_count + bags.astype(jnp.int32)
    return code.astype(jnp.float32), (rel & (LANES - 1)).astype(jnp.float32)


def count_into(counts, code_ref, lane_ref, devices, bag_count):
    blocks = counts.shape[0]
    lines = code_ref.shape[1]
    one, none = jnp.ones((), jnp.bfloat16), jnp.zeros((), jnp.bfloat16)

    def one_hot(ref, d, size):
        numbers = lax.broadcasted_iota(jnp.int32, (size, LANES), 0).astype(jnp.bfloat16)
        parts = []
        for k in range(lines):
            row = jnp.broadcast_to(ref[d, k:k + 1, :], (size, LANES)).astype(jnp.bfloat16)
            parts.append(jnp.where(numbers == row, one, none))
        return jnp.concatenate(parts, axis=1)

    for d in range(devices):
        hits = lax.dot_general(
            one_hot(code_ref, d, blocks * bag_count), one_hot(lane_ref, d, LANES),
            (((1,), (1,)), ((), ())), preferred_element_type=jnp.float32)
        counts[:, d * bag_count:(d + 1) * bag_count, :] = hits.reshape(
            blocks, bag_count, LANES)


def pool_kernel(
    bag_count, lines, turn, msg, table, out, joined, kept, code_ref, lane_ref, counts, sems,
):
    rows_dev, width = table.shape
    pieces = sems.shape[0]
    rows = rows_dev // pieces
    fetches = [
        pltpu.make_async_copy(
            table.at[pl.ds(i * rows, rows), :], kept.at[pl.ds(i * rows, rows), :], sems.at[i])
        for i in range(pieces)
    ]
    for fetch in fetches:
        fetch.start()
    owners = msg.shape[0]
    base = lax.axis_index("rows") * rows_dev
    unpack(msg, joined, code_ref, lane_ref, lines, bag_count, width, base)
    count_into(counts, code_ref, lane_ref, owners, bag_count)
    blocks = rows_dev // LANES
    flat = jnp.concatenate(
        [counts[h].astype(jnp.bfloat16) for h in range(blocks)], axis=1)
    total = jnp.zeros((owners * bag_count, width), jnp.float32)
    for i, fetch in enumerate(fetches):
        fetch.wait()
        here = slice(i * rows, (i + 1) * rows)
        for part in split_two(kept[here, :]):
            total += jnp.dot(flat[:, here], part, preferred_element_type=jnp.float32)
    for i in range(owners):
        seen = (i + turn) % owners
        out[i] = total[seen * bag_count:(seen + 1) * bag_count, :]


def read_chunk(msg, here, chunk, lines, bag_count, base, code_ref, lane_ref, counts, grads):
    width = grads.shape[1]
    code_ref[...], lane_ref[...] = codes(
        msg[here, 0:lines, :], msg[here, lines:2 * lines, :], bag_count, base)
    count_into(counts, code_ref, lane_ref, chunk, bag_count)
    for k in range(width // LANES):
        start = 2 * lines + k * bag_count
        grads[:, k * LANES:(k + 1) * LANES] = msg[
            here, start:start + bag_count, :].reshape(chunk * bag_count, LANES)


def block_sum(hits, parts):
    total = jnp.zeros((hits.shape[1], parts[0].shape[1]), jnp.float32)
    for part in parts:
        total += lax.dot_general(
            hits, part, (((0,), (0,)), ((), ())), preferred_element_type=jnp.float32)
    return total


def apply_rows(grad_of, table, accum, new_table, new_accum, fresh_table, sems):
    blocks, width = accum.shape[0], fresh_table.shape[1]
    diagonal = (
        lax.broadcasted_iota(jnp.int32, (LANES, LANES), 0)
        == lax.broadcasted_iota(jnp.int32, (LANES, LANES), 1))
    per_piece = blocks // sems.shape[0]
    copies = []
    for h in range(blocks):
        grad = grad_of(h)
        here = slice(h * LANES, (h + 1) * LANES)
        squares = grad * grad
        folded = squares[:, 0:LANES]
        for k in range(1, width // LANES):
            folded += squares[:, k * LANES:(k + 1) * LANES]
        old = jnp.where(diagonal, accum[h:h + 1, :], 0.0)
        fresh = jnp.sum(folded * (1.0 / width) + old, axis=1, keepdims=True)
        fresh_table[here, :] = table[here, :] - grad * (learn_rate * lax.rsqrt(fresh))
        new_accum[h:h + 1, :] = jnp.sum(
            jnp.where(diagonal, fresh, 0.0), axis=0, keepdims=True)
        if (h + 1) % per_piece == 0:
            i = h // per_piece
            piece = pl.ds(i * per_piece * LANES, per_piece * LANES)
            copies.append(pltpu.make_async_copy(
                fresh_table.at[piece, :], new_table.at[piece, :], sems.at[i]))
            copies[-1].start()
    for copy in copies:
        copy.wait()


def count_kernel(bag_count, lines, *refs):
    sources, (counts_out, high, low) = refs[:-8], refs[-8:-5]
    msg, code_ref, lane_ref, counts, grads = refs[-5:]
    owners = sources[0].shape[0]
    devices, blocks = msg.shape[0], counts.shape[0]
    base = lax.axis_index("rows") * (blocks * LANES)
    for i, source in enumerate(sources):
        msg[i * owners:(i + 1) * owners] = source[...]
    read_chunk(
        msg, slice(0, devices), devices, lines, bag_count, base,
        code_ref, lane_ref, counts, grads)
    counts_out[...] = counts[...].astype(jnp.bfloat16)
    high[...], low[...] = split_two(grads[...])


def apply_kernel(bag_count, lines, late, *refs):
    sources, (counted, high, low, table, accum) = refs[:late], refs[late:late + 5]
    new_table, new_accum, msg, code_ref, lane_ref, counts, grads, fresh_table, sems = refs[late + 5:]
    owners = sources[0].shape[0]
    devices, blocks = msg.shape[0], counts.shape[0]
    base = lax.axis_index("rows") * (blocks * LANES)
    for i, source in enumerate(sources):
        msg[i * owners:(i + 1) * owners] = source[...]
    read_chunk(
        msg, slice(0, devices), devices, lines, bag_count, base,
        code_ref, lane_ref, counts, grads)
    parts = [
        jnp.concatenate([early[...], late], axis=0)
        for early, late in zip((high, low), split_two(grads[...]))
    ]

    def grad_of(h):
        hits = jnp.concatenate([counted[h], counts[h].astype(jnp.bfloat16)], axis=0)
        return block_sum(hits, parts)

    apply_rows(grad_of, table, accum, new_table, new_accum, fresh_table, sems)


def update_kernel(bag_count, lines, groups, chunk, *refs):
    sources, (table, accum, new_table, new_accum) = refs[:groups], refs[groups:groups + 4]
    msg, code_ref, lane_ref, counts, grads, sums, fresh_table, sems = refs[groups + 4:]
    devices, blocks = msg.shape[0], counts.shape[0]
    owners = devices // groups
    base = lax.axis_index("rows") * (blocks * LANES)
    for i, source in enumerate(sources):
        msg[i * owners:(i + 1) * owners] = source[...]
    sums[...] = jnp.zeros_like(sums)

    @pl.loop(0, devices // chunk)
    def _(c):
        read_chunk(
            msg, pl.ds(c * chunk, chunk), chunk, lines, bag_count, base,
            code_ref, lane_ref, counts, grads)
        parts = split_two(grads[...])

        @pl.loop(0, blocks)
        def _(h):
            sums[h] += block_sum(counts[h].astype(jnp.bfloat16), parts)

    apply_rows(lambda h: sums[h], table, accum, new_table, new_accum, fresh_table, sems)


def pass_kernel(table, accum, new_table, new_accum, sem):
    copy = pltpu.make_async_copy(table, new_table, sem)
    copy.start()
    new_accum[...] = accum[...]
    copy.wait()


def finish_kernel(returned, accum, pooled, new_accum):
    total = returned[0]
    for i in range(1, returned.shape[0]):
        total += returned[i]
    pooled[...] = total
    new_accum[...] = accum[...]


def listing(size, leader):
    return [(i + leader) % size for i in range(size)]


def exchange(x, axis, leader):
    order = listing(lax.axis_size(axis), leader)
    return lax.all_to_all(
        x, axis, split_axis=0, concat_axis=0, axis_index_groups=[order], tiled=True)


def forward(x, axis, step):
    size = lax.axis_size(axis)
    return lax.ppermute(
        x, axis, [(i, ((i // 2 + step) * 2 + 1 - i % 2) % size) for i in range(size)])


def local(
    item_table, row_accum, owner_map, row_index, bag_index,
    prev_owner, prev_row, prev_bag, grad_pooled,
):
    owners, groups = lax.axis_size("rows"), lax.axis_size("dp")
    devices = owners * groups
    out_leader, back_leader = owners // 2 - 1, owners // 2
    rows_dev, width = item_table.shape
    bag_count = grad_pooled.shape[2]
    lines = row_index.shape[2] // LANES
    blocks = rows_dev // LANES
    prev_length = 2 * lines + bag_count * width // LANES
    length = (2 * lines + 1) * LANES + bag_count * width
    vmem = pl.BlockSpec(memory_space=pltpu.VMEM)
    hbm = pl.BlockSpec(memory_space=pltpu.HBM)
    params = pltpu.CompilerParams(vmem_limit_bytes=16 * 1024 * 1024)
    chunk = min(devices, LANES // bag_count)

    def stay(x):
        return pltpu.with_memory_space_constraint(x, pltpu.HBM)

    def line(x):
        return x.reshape(1, lines * LANES)

    message = pl.pallas_call(
        functools.partial(pack_kernel, rows_dev),
        out_shape=pltpu.VMEM((owners, 1, length), jnp.float32),
        in_specs=[hbm] * 7,
        out_specs=vmem,
        scratch_shapes=[pltpu.VMEM((1, lines * LANES), jnp.int32)] * 6
        + [pltpu.VMEM((bag_count, width), jnp.float32), pltpu.SemaphoreType.DMA((7,))],
        compiler_params=params,
        name="pack",
    )(*[stay(x) for x in (
        line(owner_map), line(row_index), line(bag_index),
        line(prev_owner), line(prev_row), line(prev_bag), grad_pooled[0, 0],
    )])
    gathered = exchange(message, "rows", out_leader)

    pieces = 4
    partial_pooled, joined, kept = pl.pallas_call(
        functools.partial(pool_kernel, bag_count, lines, back_leader - out_leader),
        out_shape=(
            pltpu.VMEM((owners, bag_count, width), jnp.float32),
            pltpu.VMEM((owners, prev_length, LANES), jnp.float32),
            pltpu.VMEM((rows_dev, width), jnp.float32),
        ),
        in_specs=[vmem, hbm],
        out_specs=[vmem] * 3,
        scratch_shapes=[
            pltpu.VMEM((owners, lines, LANES), jnp.float32),
            pltpu.VMEM((owners, lines, LANES), jnp.float32),
            pltpu.VMEM((blocks, owners * bag_count, LANES), jnp.float32),
            pltpu.SemaphoreType.DMA((pieces,)),
        ],
        compiler_params=params,
        cost_estimate=pl.CostEstimate(
            flops=4 * owners * bag_count * rows_dev * width,
            bytes_accessed=rows_dev * width * 4, transcendentals=0),
        name="pool",
    )(gathered, stay(item_table))
    returned = exchange(partial_pooled, "rows", back_leader)
    there = [joined] + [forward(joined, "dp", step) for step in range(1, groups // 2)]

    segments = chunk * bag_count
    updated = (
        pltpu.HBM((rows_dev, width), jnp.float32),
        pltpu.VMEM((blocks, LANES), jnp.float32),
    )

    def room(count):
        return [
            pltpu.VMEM((count, lines, LANES), jnp.float32),
            pltpu.VMEM((count, lines, LANES), jnp.float32),
            pltpu.VMEM((blocks, count * bag_count, LANES), jnp.float32),
            pltpu.VMEM((count * bag_count, width), jnp.float32),
        ]

    fresh_room = [
        pltpu.VMEM((rows_dev, width), jnp.float32),
        pltpu.SemaphoreType.DMA((pieces,)),
    ]

    def hand_over(there, kept, row_accum):
        handed = [forward(x, "dp", 0) for x in there]
        if devices > chunk:
            return pl.pallas_call(
                functools.partial(update_kernel, bag_count, lines, groups, chunk),
                out_shape=updated,
                in_specs=[vmem] * (groups + 2),
                out_specs=(hbm, vmem),
                scratch_shapes=[pltpu.VMEM((devices, prev_length, LANES), jnp.float32)]
                + room(chunk) + [pltpu.VMEM((blocks, LANES, width), jnp.float32)] + fresh_room,
                compiler_params=pltpu.CompilerParams(vmem_limit_bytes=40 * 1024 * 1024),
                name="update",
            )(*there, *handed, kept, row_accum)
        number = len(there)
        count = number * owners
        counted, high, low = pl.pallas_call(
            functools.partial(count_kernel, bag_count, lines),
            out_shape=[
                pltpu.VMEM((blocks, count * bag_count, LANES), jnp.bfloat16),
                pltpu.VMEM((count * bag_count, width), jnp.bfloat16),
                pltpu.VMEM((count * bag_count, width), jnp.bfloat16),
            ],
            in_specs=[vmem] * number,
            out_specs=[vmem] * 3,
            scratch_shapes=[pltpu.VMEM((count, prev_length, LANES), jnp.float32)] + room(count),
            compiler_params=params,
            cost_estimate=pl.CostEstimate(
                flops=1 << 28, bytes_accessed=1 << 22, transcendentals=0),
            name="count",
        )(*there)
        return pl.pallas_call(
            functools.partial(apply_kernel, bag_count, lines, number),
            out_shape=updated,
            in_specs=[vmem] * (number + 5),
            out_specs=(hbm, vmem),
            scratch_shapes=[pltpu.VMEM((count, prev_length, LANES), jnp.float32)]
            + room(count) + fresh_room,
            compiler_params=params,
            name="apply",
        )(*handed, counted, high, low, kept, row_accum)

    def skip(there, kept, row_accum):
        return pl.pallas_call(
            pass_kernel,
            out_shape=updated,
            in_specs=[vmem] * 2,
            out_specs=(hbm, vmem),
            scratch_shapes=[pltpu.SemaphoreType.DMA],
            compiler_params=params,
            name="pass",
        )(kept, row_accum)

    inside = lax.axis_index("dp") < groups
    new_table, new_accum = lax.cond(
        inside, hand_over, skip, there, kept, row_accum.reshape(blocks, LANES))

    pooled, new_accum = pl.pallas_call(
        finish_kernel,
        out_shape=(
            jax.ShapeDtypeStruct((bag_count, width), jnp.float32),
            jax.ShapeDtypeStruct((blocks, LANES), jnp.float32),
        ),
        in_specs=[vmem] * 2,
        out_specs=[vmem] * 2,
        compiler_params=params,
        name="finish",
    )(returned, new_accum)
    return (pooled[None, None], new_table, new_accum.reshape(rows_dev))


def solution(mesh):
    placed = (
        P("rows", None),
        P("rows"),
        P("dp", "rows", None, None),
        P("dp", "rows", None),
        P("dp", "rows", None),
        P("dp", "rows", None, None),
        P("dp", "rows", None),
        P("dp", "rows", None),
        P("dp", "rows", None, None),
    )
    return jax.shard_map(
        local,
        mesh=mesh,
        in_specs=placed,
        out_specs=(P("dp", "rows", None, None), P("rows", None), P("rows")),
        check_vma=False,
    )
```

```python
import functools

import jax
import jax.numpy as jnp
from jax import lax
from jax.experimental import pallas as pl
from jax.experimental.pallas import tpu as pltpu
from jax.sharding import PartitionSpec as P

learn_rate = 0.1
LANES = 128


def pack_kernel(rows_dev, *refs):
    sources, out, held, sems = refs[:7], refs[7], refs[8:15], refs[15]
    copies = [
        pltpu.make_async_copy(source, place, sems.at[i])
        for i, (source, place) in enumerate(zip(sources, held))
    ]
    for copy in copies:
        copy.start()
    for copy in copies:
        copy.wait()
    owner, row, bag, prev_owner, prev_row, prev_bag, grad = held
    lines = row.shape[0]
    bag_count, width = grad.shape

    def put(start, value):
        shape = (out.shape[0],) + value.shape
        out[:, start:start + value.shape[0], :] = jnp.broadcast_to(value[None], shape)

    put(0, (owner[...] * rows_dev + row[...]).astype(jnp.float32))
    put(lines, bag[...].astype(jnp.float32))
    put(2 * lines, (prev_owner[...] * rows_dev + prev_row[...]).astype(jnp.float32))
    put(3 * lines, prev_bag[...].astype(jnp.float32))
    for k in range(width // LANES):
        put(4 * lines + k * bag_count, grad[:, k * LANES:(k + 1) * LANES])


def split_two(x):
    high = x.astype(jnp.bfloat16)
    return high, (x - high.astype(jnp.float32)).astype(jnp.bfloat16)


def codes(ids, bags, bag_count, base):
    rel = ids.astype(jnp.int32) - base
    code = lax.shift_right_arithmetic(rel, 7) * bag_count + bags.astype(jnp.int32)
    return code.astype(jnp.float32), (rel & (LANES - 1)).astype(jnp.float32)


def count_into(counts, code_ref, lane_ref, devices, bag_count):
    blocks = counts.shape[0]
    lines = code_ref.shape[1]
    one, none = jnp.ones((), jnp.bfloat16), jnp.zeros((), jnp.bfloat16)

    def one_hot(ref, d, size):
        numbers = lax.broadcasted_iota(jnp.int32, (size, LANES), 0).astype(jnp.bfloat16)
        parts = []
        for k in range(lines):
            row = jnp.broadcast_to(ref[d, k:k + 1, :], (size, LANES)).astype(jnp.bfloat16)
            parts.append(jnp.where(numbers == row, one, none))
        return jnp.concatenate(parts, axis=1)

    for d in range(devices):
        hits = lax.dot_general(
            one_hot(code_ref, d, blocks * bag_count), one_hot(lane_ref, d, LANES),
            (((1,), (1,)), ((), ())), preferred_element_type=jnp.float32)
        counts[:, d * bag_count:(d + 1) * bag_count, :] = hits.reshape(
            blocks, bag_count, LANES)


def pool_kernel(
    bag_count, lines, turn, msg, table, out, joined, kept, code_ref, lane_ref, counts, sems,
):
    rows_dev, width = table.shape
    pieces = sems.shape[0]
    rows = rows_dev // pieces
    fetches = [
        pltpu.make_async_copy(
            table.at[pl.ds(i * rows, rows), :], kept.at[pl.ds(i * rows, rows), :], sems.at[i])
        for i in range(pieces)
    ]
    for fetch in fetches:
        fetch.start()
    owners = msg.shape[0]
    base = lax.axis_index("rows") * rows_dev
    code_ref[...], lane_ref[...] = codes(
        msg[:, 0:lines, :], msg[:, lines:2 * lines, :], bag_count, base)
    joined[...] = msg[:, 2 * lines:, :]
    count_into(counts, code_ref, lane_ref, owners, bag_count)
    blocks = rows_dev // LANES
    flat = jnp.concatenate(
        [counts[h].astype(jnp.bfloat16) for h in range(blocks)], axis=1)
    total = jnp.zeros((owners * bag_count, width), jnp.float32)
    for i, fetch in enumerate(fetches):
        fetch.wait()
        here = slice(i * rows, (i + 1) * rows)
        for part in split_two(kept[here, :]):
            total += jnp.dot(flat[:, here], part, preferred_element_type=jnp.float32)
    for i in range(owners):
        seen = (i + turn) % owners
        out[i] = total[seen * bag_count:(seen + 1) * bag_count, :]


def read_chunk(msg, here, chunk, lines, bag_count, base, code_ref, lane_ref, counts, grads):
    width = grads.shape[1]
    code_ref[...], lane_ref[...] = codes(
        msg[here, 0:lines, :], msg[here, lines:2 * lines, :], bag_count, base)
    count_into(counts, code_ref, lane_ref, chunk, bag_count)
    for k in range(width // LANES):
        start = 2 * lines + k * bag_count
        grads[:, k * LANES:(k + 1) * LANES] = msg[
            here, start:start + bag_count, :].reshape(chunk * bag_count, LANES)


def block_sum(hits, parts):
    total = jnp.zeros((hits.shape[1], parts[0].shape[1]), jnp.float32)
    for part in parts:
        total += lax.dot_general(
            hits, part, (((0,), (0,)), ((), ())), preferred_element_type=jnp.float32)
    return total


def apply_rows(grad_of, table, accum, new_table, new_accum, fresh_table, sems):
    blocks, width = accum.shape[0], fresh_table.shape[1]
    diagonal = (
        lax.broadcasted_iota(jnp.int32, (LANES, LANES), 0)
        == lax.broadcasted_iota(jnp.int32, (LANES, LANES), 1))
    per_piece = blocks // sems.shape[0]
    copies = []
    for h in range(blocks):
        grad = grad_of(h)
        here = slice(h * LANES, (h + 1) * LANES)
        squares = grad * grad
        folded = squares[:, 0:LANES]
        for k in range(1, width // LANES):
            folded += squares[:, k * LANES:(k + 1) * LANES]
        old = jnp.where(diagonal, accum[h:h + 1, :], 0.0)
        fresh = jnp.sum(folded * (1.0 / width) + old, axis=1, keepdims=True)
        fresh_table[here, :] = table[here, :] - grad * (learn_rate * lax.rsqrt(fresh))
        new_accum[h:h + 1, :] = jnp.sum(
            jnp.where(diagonal, fresh, 0.0), axis=0, keepdims=True)
        if (h + 1) % per_piece == 0:
            i = h // per_piece
            piece = pl.ds(i * per_piece * LANES, per_piece * LANES)
            copies.append(pltpu.make_async_copy(
                fresh_table.at[piece, :], new_table.at[piece, :], sems.at[i]))
            copies[-1].start()
    for copy in copies:
        copy.wait()


def count_kernel(bag_count, lines, *refs):
    sources, (counts_out, high, low) = refs[:-8], refs[-8:-5]
    msg, code_ref, lane_ref, counts, grads = refs[-5:]
    owners = sources[0].shape[0]
    devices, blocks = msg.shape[0], counts.shape[0]
    base = lax.axis_index("rows") * (blocks * LANES)
    for i, source in enumerate(sources):
        msg[i * owners:(i + 1) * owners] = source[...]
    read_chunk(
        msg, slice(0, devices), devices, lines, bag_count, base,
        code_ref, lane_ref, counts, grads)
    counts_out[...] = counts[...].astype(jnp.bfloat16)
    high[...], low[...] = split_two(grads[...])


def apply_kernel(bag_count, lines, late, *refs):
    sources, (counted, high, low, table, accum) = refs[:late], refs[late:late + 5]
    new_table, new_accum, msg, code_ref, lane_ref, counts, grads, fresh_table, sems = refs[late + 5:]
    owners = sources[0].shape[0]
    devices, blocks = msg.shape[0], counts.shape[0]
    base = lax.axis_index("rows") * (blocks * LANES)
    for i, source in enumerate(sources):
        msg[i * owners:(i + 1) * owners] = source[...]
    read_chunk(
        msg, slice(0, devices), devices, lines, bag_count, base,
        code_ref, lane_ref, counts, grads)
    parts = [
        jnp.concatenate([early[...], late], axis=0)
        for early, late in zip((high, low), split_two(grads[...]))
    ]

    def grad_of(h):
        hits = jnp.concatenate([counted[h], counts[h].astype(jnp.bfloat16)], axis=0)
        return block_sum(hits, parts)

    apply_rows(grad_of, table, accum, new_table, new_accum, fresh_table, sems)


def update_kernel(bag_count, lines, groups, chunk, *refs):
    sources, (table, accum, new_table, new_accum) = refs[:groups], refs[groups:groups + 4]
    msg, code_ref, lane_ref, counts, grads, sums, fresh_table, sems = refs[groups + 4:]
    devices, blocks = msg.shape[0], counts.shape[0]
    owners = devices // groups
    base = lax.axis_index("rows") * (blocks * LANES)
    for i, source in enumerate(sources):
        msg[i * owners:(i + 1) * owners] = source[...]
    sums[...] = jnp.zeros_like(sums)

    @pl.loop(0, devices // chunk)
    def _(c):
        read_chunk(
            msg, pl.ds(c * chunk, chunk), chunk, lines, bag_count, base,
            code_ref, lane_ref, counts, grads)
        parts = split_two(grads[...])

        @pl.loop(0, blocks)
        def _(h):
            sums[h] += block_sum(counts[h].astype(jnp.bfloat16), parts)

    apply_rows(lambda h: sums[h], table, accum, new_table, new_accum, fresh_table, sems)


def pass_kernel(table, accum, new_table, new_accum, sem):
    copy = pltpu.make_async_copy(table, new_table, sem)
    copy.start()
    new_accum[...] = accum[...]
    copy.wait()


def finish_kernel(returned, accum, pooled, new_accum):
    total = returned[0]
    for i in range(1, returned.shape[0]):
        total += returned[i]
    pooled[...] = total
    new_accum[...] = accum[...]


def listing(size, leader):
    return [(i + leader) % size for i in range(size)]


def exchange(x, axis, leader):
    order = listing(lax.axis_size(axis), leader)
    return lax.all_to_all(
        x, axis, split_axis=0, concat_axis=0, axis_index_groups=[order], tiled=True)


def forward(x, axis, step):
    size = lax.axis_size(axis)
    return lax.ppermute(
        x, axis, [(i, ((i // 2 + step) * 2 + 1 - i % 2) % size) for i in range(size)])


def local(
    item_table, row_accum, owner_map, row_index, bag_index,
    prev_owner, prev_row, prev_bag, grad_pooled,
):
    owners, groups = lax.axis_size("rows"), lax.axis_size("dp")
    devices = owners * groups
    out_leader, back_leader = 5 * owners // 8, owners // 4
    rows_dev, width = item_table.shape
    bag_count = grad_pooled.shape[2]
    lines = row_index.shape[2] // LANES
    blocks = rows_dev // LANES
    prev_length = 2 * lines + bag_count * width // LANES
    vmem = pl.BlockSpec(memory_space=pltpu.VMEM)
    hbm = pl.BlockSpec(memory_space=pltpu.HBM)
    params = pltpu.CompilerParams(vmem_limit_bytes=16 * 1024 * 1024)
    chunk = min(devices, LANES // bag_count)

    def stay(x):
        return pltpu.with_memory_space_constraint(x, pltpu.HBM)

    def line(x):
        return x.reshape(lines, LANES)

    message = pl.pallas_call(
        functools.partial(pack_kernel, rows_dev),
        out_shape=pltpu.VMEM((owners, 2 * lines + prev_length, LANES), jnp.float32),
        in_specs=[hbm] * 7,
        out_specs=vmem,
        scratch_shapes=[pltpu.VMEM((lines, LANES), jnp.int32)] * 6
        + [pltpu.VMEM((bag_count, width), jnp.float32), pltpu.SemaphoreType.DMA((7,))],
        compiler_params=params,
        name="pack",
    )(*[stay(x) for x in (
        line(owner_map), line(row_index), line(bag_index),
        line(prev_owner), line(prev_row), line(prev_bag), grad_pooled[0, 0],
    )])
    gathered = exchange(message, "rows", out_leader)

    pieces = 4
    partial_pooled, joined, kept = pl.pallas_call(
        functools.partial(pool_kernel, bag_count, lines, back_leader - out_leader),
        out_shape=(
            pltpu.VMEM((owners, bag_count, width), jnp.float32),
            pltpu.VMEM((owners, prev_length, LANES), jnp.float32),
            pltpu.VMEM((rows_dev, width), jnp.float32),
        ),
        in_specs=[vmem, hbm],
        out_specs=[vmem] * 3,
        scratch_shapes=[
            pltpu.VMEM((owners, lines, LANES), jnp.float32),
            pltpu.VMEM((owners, lines, LANES), jnp.float32),
            pltpu.VMEM((blocks, owners * bag_count, LANES), jnp.float32),
            pltpu.SemaphoreType.DMA((pieces,)),
        ],
        compiler_params=params,
        cost_estimate=pl.CostEstimate(
            flops=4 * owners * bag_count * rows_dev * width,
            bytes_accessed=rows_dev * width * 4, transcendentals=0),
        name="pool",
    )(gathered, stay(item_table))
    returned = exchange(partial_pooled, "rows", back_leader)
    there = [joined] + [forward(joined, "dp", step) for step in range(1, groups // 2)]

    segments = chunk * bag_count
    updated = (
        pltpu.HBM((rows_dev, width), jnp.float32),
        pltpu.VMEM((blocks, LANES), jnp.float32),
    )

    def room(count):
        return [
            pltpu.VMEM((count, lines, LANES), jnp.float32),
            pltpu.VMEM((count, lines, LANES), jnp.float32),
            pltpu.VMEM((blocks, count * bag_count, LANES), jnp.float32),
            pltpu.VMEM((count * bag_count, width), jnp.float32),
        ]

    fresh_room = [
        pltpu.VMEM((rows_dev, width), jnp.float32),
        pltpu.SemaphoreType.DMA((pieces,)),
    ]

    def hand_over(there, kept, row_accum):
        handed = [forward(x, "dp", 0) for x in there]
        if devices > chunk:
            return pl.pallas_call(
                functools.partial(update_kernel, bag_count, lines, groups, chunk),
                out_shape=updated,
                in_specs=[vmem] * (groups + 2),
                out_specs=(hbm, vmem),
                scratch_shapes=[pltpu.VMEM((devices, prev_length, LANES), jnp.float32)]
                + room(chunk) + [pltpu.VMEM((blocks, LANES, width), jnp.float32)] + fresh_room,
                compiler_params=pltpu.CompilerParams(vmem_limit_bytes=40 * 1024 * 1024),
                name="update",
            )(*there, *handed, kept, row_accum)
        number = len(there)
        count = number * owners
        counted, high, low = pl.pallas_call(
            functools.partial(count_kernel, bag_count, lines),
            out_shape=[
                pltpu.VMEM((blocks, count * bag_count, LANES), jnp.bfloat16),
                pltpu.VMEM((count * bag_count, width), jnp.bfloat16),
                pltpu.VMEM((count * bag_count, width), jnp.bfloat16),
            ],
            in_specs=[vmem] * number,
            out_specs=[vmem] * 3,
            scratch_shapes=[pltpu.VMEM((count, prev_length, LANES), jnp.float32)] + room(count),
            compiler_params=params,
            cost_estimate=pl.CostEstimate(
                flops=1 << 28, bytes_accessed=1 << 22, transcendentals=0),
            name="count",
        )(*there)
        return pl.pallas_call(
            functools.partial(apply_kernel, bag_count, lines, number),
            out_shape=updated,
            in_specs=[vmem] * (number + 5),
            out_specs=(hbm, vmem),
            scratch_shapes=[pltpu.VMEM((count, prev_length, LANES), jnp.float32)]
            + room(count) + fresh_room,
            compiler_params=params,
            name="apply",
        )(*handed, counted, high, low, kept, row_accum)

    def skip(there, kept, row_accum):
        return pl.pallas_call(
            pass_kernel,
            out_shape=updated,
            in_specs=[vmem] * 2,
            out_specs=(hbm, vmem),
            scratch_shapes=[pltpu.SemaphoreType.DMA],
            compiler_params=params,
            name="pass",
        )(kept, row_accum)

    inside = lax.axis_index("dp") < groups
    new_table, new_accum = lax.cond(
        inside, hand_over, skip, there, kept, row_accum.reshape(blocks, LANES))

    pooled, new_accum = pl.pallas_call(
        finish_kernel,
        out_shape=(
            jax.ShapeDtypeStruct((bag_count, width), jnp.float32),
            jax.ShapeDtypeStruct((blocks, LANES), jnp.float32),
        ),
        in_specs=[vmem] * 2,
        out_specs=[vmem] * 2,
        compiler_params=params,
        name="finish",
    )(returned, new_accum)
    return (pooled[None, None], new_table, new_accum.reshape(rows_dev))


def solution(mesh):
    placed = (
        P("rows", None),
        P("rows"),
        P("dp", "rows", None, None),
        P("dp", "rows", None),
        P("dp", "rows", None),
        P("dp", "rows", None, None),
        P("dp", "rows", None),
        P("dp", "rows", None),
        P("dp", "rows", None, None),
    )
    return jax.shard_map(
        local,
        mesh=mesh,
        in_specs=placed,
        out_specs=(P("dp", "rows", None, None), P("rows", None), P("rows")),
        check_vma=False,
    )
```

```python
import functools

import jax
import jax.numpy as jnp
from jax import lax
from jax.experimental import pallas as pl
from jax.experimental.pallas import tpu as pltpu
from jax.sharding import PartitionSpec as P

learn_rate = 0.1
LANES = 128


def pack_kernel(rows_dev, *refs):
    sources, out, held, sems = refs[:7], refs[7], refs[8:15], refs[15]
    copies = [
        pltpu.make_async_copy(source, place, sems.at[i])
        for i, (source, place) in enumerate(zip(sources, held))
    ]
    for copy in copies:
        copy.start()
    for copy in copies:
        copy.wait()
    owner, row, bag, prev_owner, prev_row, prev_bag, grad = held
    lines = row.shape[0]
    bag_count, width = grad.shape

    def put(start, value):
        shape = (out.shape[0],) + value.shape
        out[:, start:start + value.shape[0], :] = jnp.broadcast_to(value[None], shape)

    put(0, (owner[...] * rows_dev + row[...]).astype(jnp.float32))
    put(lines, bag[...].astype(jnp.float32))
    put(2 * lines, (prev_owner[...] * rows_dev + prev_row[...]).astype(jnp.float32))
    put(3 * lines, prev_bag[...].astype(jnp.float32))
    for k in range(width // LANES):
        put(4 * lines + k * bag_count, grad[:, k * LANES:(k + 1) * LANES])


def split_two(x):
    high = x.astype(jnp.bfloat16)
    return high, (x - high.astype(jnp.float32)).astype(jnp.bfloat16)


def codes(ids, bags, bag_count, base):
    rel = ids.astype(jnp.int32) - base
    code = lax.shift_right_arithmetic(rel, 7) * bag_count + bags.astype(jnp.int32)
    return code.astype(jnp.float32), (rel & (LANES - 1)).astype(jnp.float32)


def count_into(counts, code_ref, lane_ref, devices, bag_count):
    blocks = counts.shape[0]
    lines = code_ref.shape[1]
    one, none = jnp.ones((), jnp.bfloat16), jnp.zeros((), jnp.bfloat16)

    def one_hot(ref, d, size):
        numbers = lax.broadcasted_iota(jnp.int32, (size, LANES), 0).astype(jnp.bfloat16)
        parts = []
        for k in range(lines):
            row = jnp.broadcast_to(ref[d, k:k + 1, :], (size, LANES)).astype(jnp.bfloat16)
            parts.append(jnp.where(numbers == row, one, none))
        return jnp.concatenate(parts, axis=1)

    for d in range(devices):
        hits = lax.dot_general(
            one_hot(code_ref, d, blocks * bag_count), one_hot(lane_ref, d, LANES),
            (((1,), (1,)), ((), ())), preferred_element_type=jnp.float32)
        counts[:, d * bag_count:(d + 1) * bag_count, :] = hits.reshape(
            blocks, bag_count, LANES)


def pool_kernel(
    bag_count, lines, turn, msg, table, out, joined, kept, code_ref, lane_ref, counts, sems,
):
    rows_dev, width = table.shape
    pieces = sems.shape[0]
    rows = rows_dev // pieces
    fetches = [
        pltpu.make_async_copy(
            table.at[pl.ds(i * rows, rows), :], kept.at[pl.ds(i * rows, rows), :], sems.at[i])
        for i in range(pieces)
    ]
    for fetch in fetches:
        fetch.start()
    owners = msg.shape[0]
    base = lax.axis_index("rows") * rows_dev
    code_ref[...], lane_ref[...] = codes(
        msg[:, 0:lines, :], msg[:, lines:2 * lines, :], bag_count, base)
    joined[...] = msg[:, 2 * lines:, :]
    count_into(counts, code_ref, lane_ref, owners, bag_count)
    blocks = rows_dev // LANES
    flat = jnp.concatenate(
        [counts[h].astype(jnp.bfloat16) for h in range(blocks)], axis=1)
    total = jnp.zeros((owners * bag_count, width), jnp.float32)
    for i, fetch in enumerate(fetches):
        fetch.wait()
        here = slice(i * rows, (i + 1) * rows)
        for part in split_two(kept[here, :]):
            total += jnp.dot(flat[:, here], part, preferred_element_type=jnp.float32)
    for i in range(owners):
        seen = (i + turn) % owners
        out[i] = total[seen * bag_count:(seen + 1) * bag_count, :]


def read_chunk(msg, here, chunk, lines, bag_count, base, code_ref, lane_ref, counts, grads):
    width = grads.shape[1]
    code_ref[...], lane_ref[...] = codes(
        msg[here, 0:lines, :], msg[here, lines:2 * lines, :], bag_count, base)
    count_into(counts, code_ref, lane_ref, chunk, bag_count)
    for k in range(width // LANES):
        start = 2 * lines + k * bag_count
        grads[:, k * LANES:(k + 1) * LANES] = msg[
            here, start:start + bag_count, :].reshape(chunk * bag_count, LANES)


def block_sum(hits, parts):
    total = jnp.zeros((hits.shape[1], parts[0].shape[1]), jnp.float32)
    for part in parts:
        total += lax.dot_general(
            hits, part, (((0,), (0,)), ((), ())), preferred_element_type=jnp.float32)
    return total


def apply_rows(grad_of, table, accum, new_table, new_accum, fresh_table, sems):
    blocks, width = accum.shape[0], fresh_table.shape[1]
    diagonal = (
        lax.broadcasted_iota(jnp.int32, (LANES, LANES), 0)
        == lax.broadcasted_iota(jnp.int32, (LANES, LANES), 1))
    per_piece = blocks // sems.shape[0]
    copies = []
    for h in range(blocks):
        grad = grad_of(h)
        here = slice(h * LANES, (h + 1) * LANES)
        squares = grad * grad
        folded = squares[:, 0:LANES]
        for k in range(1, width // LANES):
            folded += squares[:, k * LANES:(k + 1) * LANES]
        old = jnp.where(diagonal, accum[h:h + 1, :], 0.0)
        fresh = jnp.sum(folded * (1.0 / width) + old, axis=1, keepdims=True)
        fresh_table[here, :] = table[here, :] - grad * (learn_rate * lax.rsqrt(fresh))
        new_accum[h:h + 1, :] = jnp.sum(
            jnp.where(diagonal, fresh, 0.0), axis=0, keepdims=True)
        if (h + 1) % per_piece == 0:
            i = h // per_piece
            piece = pl.ds(i * per_piece * LANES, per_piece * LANES)
            copies.append(pltpu.make_async_copy(
                fresh_table.at[piece, :], new_table.at[piece, :], sems.at[i]))
            copies[-1].start()
    for copy in copies:
        copy.wait()


def count_kernel(bag_count, lines, *refs):
    sources, (counts_out, high, low) = refs[:-8], refs[-8:-5]
    msg, code_ref, lane_ref, counts, grads = refs[-5:]
    owners = sources[0].shape[0]
    devices, blocks = msg.shape[0], counts.shape[0]
    base = lax.axis_index("rows") * (blocks * LANES)
    for i, source in enumerate(sources):
        msg[i * owners:(i + 1) * owners] = source[...]
    read_chunk(
        msg, slice(0, devices), devices, lines, bag_count, base,
        code_ref, lane_ref, counts, grads)
    counts_out[...] = counts[...].astype(jnp.bfloat16)
    high[...], low[...] = split_two(grads[...])


def apply_kernel(bag_count, lines, late, *refs):
    swapped, met, handed = refs[0], refs[1:late], refs[late:2 * late - 1]
    counted, high, low, table, accum, new_table, new_accum, *room = refs[2 * late - 1:]
    msg, code_ref, lane_ref, counts, grads, fresh_table, sems = room
    owners = swapped.shape[0]
    devices, blocks = msg.shape[0], counts.shape[0]
    base = lax.axis_index("rows") * (blocks * LANES)
    msg[0:owners] = swapped[...]
    for i, (one, other) in enumerate(zip(met, handed)):
        msg[(i + 1) * owners:(i + 2) * owners] = one[...] + other[...]
    read_chunk(
        msg, slice(0, devices), devices, lines, bag_count, base,
        code_ref, lane_ref, counts, grads)
    parts = [
        jnp.concatenate([early[...], late], axis=0)
        for early, late in zip((high, low), split_two(grads[...]))
    ]

    def grad_of(h):
        hits = jnp.concatenate([counted[h], counts[h].astype(jnp.bfloat16)], axis=0)
        return block_sum(hits, parts)

    apply_rows(grad_of, table, accum, new_table, new_accum, fresh_table, sems)


def update_kernel(bag_count, lines, groups, chunk, *refs):
    sources, (table, accum, new_table, new_accum) = refs[:groups], refs[groups:groups + 4]
    msg, code_ref, lane_ref, counts, grads, sums, fresh_table, sems = refs[groups + 4:]
    devices, blocks = msg.shape[0], counts.shape[0]
    owners = devices // groups
    base = lax.axis_index("rows") * (blocks * LANES)
    for i, source in enumerate(sources):
        msg[i * owners:(i + 1) * owners] = source[...]
    sums[...] = jnp.zeros_like(sums)

    @pl.loop(0, devices // chunk)
    def _(c):
        read_chunk(
            msg, pl.ds(c * chunk, chunk), chunk, lines, bag_count, base,
            code_ref, lane_ref, counts, grads)
        parts = split_two(grads[...])

        @pl.loop(0, blocks)
        def _(h):
            sums[h] += block_sum(counts[h].astype(jnp.bfloat16), parts)

    apply_rows(lambda h: sums[h], table, accum, new_table, new_accum, fresh_table, sems)


def pass_kernel(table, accum, new_table, new_accum, sem):
    copy = pltpu.make_async_copy(table, new_table, sem)
    copy.start()
    new_accum[...] = accum[...]
    copy.wait()


def finish_kernel(returned, accum, pooled, new_accum):
    total = returned[0]
    for i in range(1, returned.shape[0]):
        total += returned[i]
    pooled[...] = total
    new_accum[...] = accum[...]


def listing(size, leader):
    return [(i + leader) % size for i in range(size)]


def exchange(x, axis, leader):
    order = listing(lax.axis_size(axis), leader)
    return lax.all_to_all(
        x, axis, split_axis=0, concat_axis=0, axis_index_groups=[order], tiled=True)


def hop(x, axis, step, source, target):
    pairs = lax.axis_size(axis) // 2
    return lax.ppermute(
        x, axis, [(2 * m + source, 2 * ((m + step) % pairs) + target) for m in range(pairs)])


def swap(x, axis):
    return lax.ppermute(x, axis, [(i, i + 1 - i % 2 * 2) for i in range(lax.axis_size(axis))])


def local(
    item_table, row_accum, owner_map, row_index, bag_index,
    prev_owner, prev_row, prev_bag, grad_pooled,
):
    owners, groups = lax.axis_size("rows"), lax.axis_size("dp")
    devices = owners * groups
    out_leader, back_leader = 5 * owners // 8, owners // 2 - 1
    rows_dev, width = item_table.shape
    bag_count = grad_pooled.shape[2]
    lines = row_index.shape[2] // LANES
    blocks = rows_dev // LANES
    prev_length = 2 * lines + bag_count * width // LANES
    vmem = pl.BlockSpec(memory_space=pltpu.VMEM)
    hbm = pl.BlockSpec(memory_space=pltpu.HBM)
    params = pltpu.CompilerParams(vmem_limit_bytes=16 * 1024 * 1024)
    chunk = min(devices, LANES // bag_count)

    def stay(x):
        return pltpu.with_memory_space_constraint(x, pltpu.HBM)

    def line(x):
        return x.reshape(lines, LANES)

    message = pl.pallas_call(
        functools.partial(pack_kernel, rows_dev),
        out_shape=pltpu.VMEM((owners, 2 * lines + prev_length, LANES), jnp.float32),
        in_specs=[hbm] * 7,
        out_specs=vmem,
        scratch_shapes=[pltpu.VMEM((lines, LANES), jnp.int32)] * 6
        + [pltpu.VMEM((bag_count, width), jnp.float32), pltpu.SemaphoreType.DMA((7,))],
        compiler_params=params,
        name="pack",
    )(*[stay(x) for x in (
        line(owner_map), line(row_index), line(bag_index),
        line(prev_owner), line(prev_row), line(prev_bag), grad_pooled[0, 0],
    )])
    gathered = exchange(message, "rows", out_leader)

    pieces = 4
    partial_pooled, joined, kept = pl.pallas_call(
        functools.partial(pool_kernel, bag_count, lines, back_leader - out_leader),
        out_shape=(
            pltpu.VMEM((owners, bag_count, width), jnp.float32),
            pltpu.VMEM((owners, prev_length, LANES), jnp.float32),
            pltpu.VMEM((rows_dev, width), jnp.float32),
        ),
        in_specs=[vmem, hbm],
        out_specs=[vmem] * 3,
        scratch_shapes=[
            pltpu.VMEM((owners, lines, LANES), jnp.float32),
            pltpu.VMEM((owners, lines, LANES), jnp.float32),
            pltpu.VMEM((blocks, owners * bag_count, LANES), jnp.float32),
            pltpu.SemaphoreType.DMA((pieces,)),
        ],
        compiler_params=params,
        cost_estimate=pl.CostEstimate(
            flops=4 * owners * bag_count * rows_dev * width,
            bytes_accessed=rows_dev * width * 4, transcendentals=0),
        name="pool",
    )(gathered, stay(item_table))
    returned = exchange(partial_pooled, "rows", back_leader)
    steps = range(1, groups // 2)
    met = [hop(joined, "dp", step, 0, 1) for step in steps]
    met = met + [hop(joined, "dp", step, 1, 1) for step in steps]

    segments = chunk * bag_count
    updated = (
        pltpu.HBM((rows_dev, width), jnp.float32),
        pltpu.VMEM((blocks, LANES), jnp.float32),
    )

    def room(count):
        return [
            pltpu.VMEM((count, lines, LANES), jnp.float32),
            pltpu.VMEM((count, lines, LANES), jnp.float32),
            pltpu.VMEM((blocks, count * bag_count, LANES), jnp.float32),
            pltpu.VMEM((count * bag_count, width), jnp.float32),
        ]

    fresh_room = [
        pltpu.VMEM((rows_dev, width), jnp.float32),
        pltpu.SemaphoreType.DMA((8 if blocks % 8 == 0 else 1,)),
    ]

    def hand_over(joined, met, kept, row_accum):
        swapped = swap(joined, "dp")
        handed = [hop(x, "dp", 0, 1, 0) for x in met]
        if devices > chunk:
            rest = [x + y for x, y in zip(met, handed)]
            return pl.pallas_call(
                functools.partial(update_kernel, bag_count, lines, groups, chunk),
                out_shape=updated,
                in_specs=[vmem] * (groups + 2),
                out_specs=(hbm, vmem),
                scratch_shapes=[pltpu.VMEM((devices, prev_length, LANES), jnp.float32)]
                + room(chunk) + [pltpu.VMEM((blocks, LANES, width), jnp.float32)] + fresh_room,
                compiler_params=pltpu.CompilerParams(vmem_limit_bytes=40 * 1024 * 1024),
                name="update",
            )(joined, swapped, *rest, kept, row_accum)
        counted, high, low = pl.pallas_call(
            functools.partial(count_kernel, bag_count, lines),
            out_shape=[
                pltpu.VMEM((blocks, owners * bag_count, LANES), jnp.bfloat16),
                pltpu.VMEM((owners * bag_count, width), jnp.bfloat16),
                pltpu.VMEM((owners * bag_count, width), jnp.bfloat16),
            ],
            in_specs=[vmem],
            out_specs=[vmem] * 3,
            scratch_shapes=[pltpu.VMEM((owners, prev_length, LANES), jnp.float32)] + room(owners),
            compiler_params=params,
            cost_estimate=pl.CostEstimate(
                flops=1 << 28, bytes_accessed=1 << 22, transcendentals=0),
            name="count",
        )(joined)
        late = 1 + len(met)
        return pl.pallas_call(
            functools.partial(apply_kernel, bag_count, lines, late),
            out_shape=updated,
            in_specs=[vmem] * (2 * late + 4),
            out_specs=(hbm, vmem),
            scratch_shapes=[pltpu.VMEM((late * owners, prev_length, LANES), jnp.float32)]
            + room(late * owners) + fresh_room,
            compiler_params=params,
            name="apply",
        )(swapped, *met, *handed, counted, high, low, kept, row_accum)

    def skip(joined, met, kept, row_accum):
        return pl.pallas_call(
            pass_kernel,
            out_shape=updated,
            in_specs=[vmem] * 2,
            out_specs=(hbm, vmem),
            scratch_shapes=[pltpu.SemaphoreType.DMA],
            compiler_params=params,
            name="pass",
        )(kept, row_accum)

    inside = lax.axis_index("dp") < groups
    new_table, new_accum = lax.cond(
        inside, hand_over, skip, joined, met, kept, row_accum.reshape(blocks, LANES))

    pooled, new_accum = pl.pallas_call(
        finish_kernel,
        out_shape=(
            jax.ShapeDtypeStruct((bag_count, width), jnp.float32),
            jax.ShapeDtypeStruct((blocks, LANES), jnp.float32),
        ),
        in_specs=[vmem] * 2,
        out_specs=[vmem] * 2,
        compiler_params=params,
        name="finish",
    )(returned, new_accum)
    return (pooled[None, None], new_table, new_accum.reshape(rows_dev))


def solution(mesh):
    placed = (
        P("rows", None),
        P("rows"),
        P("dp", "rows", None, None),
        P("dp", "rows", None),
        P("dp", "rows", None),
        P("dp", "rows", None, None),
        P("dp", "rows", None),
        P("dp", "rows", None),
        P("dp", "rows", None, None),
    )
    return jax.shard_map(
        local,
        mesh=mesh,
        in_specs=placed,
        out_specs=(P("dp", "rows", None, None), P("rows", None), P("rows")),
        check_vma=False,
    )
```

```python
import functools

import jax
import jax.numpy as jnp
from jax import lax
from jax.experimental import pallas as pl
from jax.experimental.pallas import tpu as pltpu
from jax.sharding import PartitionSpec as P

learn_rate = 0.1
LANES = 128


def pack_kernel(rows_dev, *refs):
    sources, out, held, sems = refs[:7], refs[7], refs[8:15], refs[15]
    copies = [
        pltpu.make_async_copy(source, place, sems.at[i])
        for i, (source, place) in enumerate(zip(sources, held))
    ]
    for copy in copies:
        copy.start()
    for copy in copies:
        copy.wait()
    owner, row, bag, prev_owner, prev_row, prev_bag, grad = held
    lines = row.shape[0]
    bag_count, width = grad.shape

    def put(start, value):
        shape = (out.shape[0],) + value.shape
        out[:, start:start + value.shape[0], :] = jnp.broadcast_to(value[None], shape)

    put(0, (owner[...] * rows_dev + row[...]).astype(jnp.float32))
    put(lines, bag[...].astype(jnp.float32))
    put(2 * lines, (prev_owner[...] * rows_dev + prev_row[...]).astype(jnp.float32))
    put(3 * lines, prev_bag[...].astype(jnp.float32))
    for k in range(width // LANES):
        put(4 * lines + k * bag_count, grad[:, k * LANES:(k + 1) * LANES])


def split_two(x):
    high = x.astype(jnp.bfloat16)
    return high, (x - high.astype(jnp.float32)).astype(jnp.bfloat16)


def codes(ids, bags, bag_count, base):
    rel = ids.astype(jnp.int32) - base
    code = lax.shift_right_arithmetic(rel, 7) * bag_count + bags.astype(jnp.int32)
    return code.astype(jnp.float32), (rel & (LANES - 1)).astype(jnp.float32)


def count_into(counts, code_ref, lane_ref, devices, bag_count):
    blocks = counts.shape[0]
    lines = code_ref.shape[1]
    one, none = jnp.ones((), jnp.bfloat16), jnp.zeros((), jnp.bfloat16)

    def one_hot(ref, d, size):
        numbers = lax.broadcasted_iota(jnp.int32, (size, LANES), 0).astype(jnp.bfloat16)
        parts = []
        for k in range(lines):
            row = jnp.broadcast_to(ref[d, k:k + 1, :], (size, LANES)).astype(jnp.bfloat16)
            parts.append(jnp.where(numbers == row, one, none))
        return jnp.concatenate(parts, axis=1)

    for d in range(devices):
        hits = lax.dot_general(
            one_hot(code_ref, d, blocks * bag_count), one_hot(lane_ref, d, LANES),
            (((1,), (1,)), ((), ())), preferred_element_type=jnp.float32)
        counts[:, d * bag_count:(d + 1) * bag_count, :] = hits.reshape(
            blocks, bag_count, LANES)


def pool_kernel(
    bag_count, lines, turn, msg, table, out, joined, code_ref, lane_ref, counts,
):
    rows_dev, width = table.shape
    owners = msg.shape[0]
    base = lax.axis_index("rows") * rows_dev
    code_ref[...], lane_ref[...] = codes(
        msg[:, 0:lines, :], msg[:, lines:2 * lines, :], bag_count, base)
    joined[...] = msg[:, 2 * lines:, :]
    count_into(counts, code_ref, lane_ref, owners, bag_count)
    blocks = rows_dev // LANES
    flat = jnp.concatenate(
        [counts[h].astype(jnp.bfloat16) for h in range(blocks)], axis=1)
    total = jnp.zeros((owners * bag_count, width), jnp.float32)
    for part in split_two(table[...]):
        total += jnp.dot(flat, part, preferred_element_type=jnp.float32)
    for i in range(owners):
        seen = (i + turn) % owners
        out[i] = total[seen * bag_count:(seen + 1) * bag_count, :]


def read_chunk(msg, here, chunk, lines, bag_count, base, code_ref, lane_ref, counts, grads):
    width = grads.shape[1]
    code_ref[...], lane_ref[...] = codes(
        msg[here, 0:lines, :], msg[here, lines:2 * lines, :], bag_count, base)
    count_into(counts, code_ref, lane_ref, chunk, bag_count)
    for k in range(width // LANES):
        start = 2 * lines + k * bag_count
        grads[:, k * LANES:(k + 1) * LANES] = msg[
            here, start:start + bag_count, :].reshape(chunk * bag_count, LANES)


def block_sum(hits, parts):
    total = jnp.zeros((hits.shape[1], parts[0].shape[1]), jnp.float32)
    for part in parts:
        total += lax.dot_general(
            hits, part, (((0,), (0,)), ((), ())), preferred_element_type=jnp.float32)
    return total


def apply_rows(grad_of, table, accum, new_table, new_accum, fresh_table, sems):
    blocks, width = accum.shape[0], fresh_table.shape[1]
    diagonal = (
        lax.broadcasted_iota(jnp.int32, (LANES, LANES), 0)
        == lax.broadcasted_iota(jnp.int32, (LANES, LANES), 1))
    per_piece = blocks // sems.shape[0]
    copies = []
    for h in range(blocks):
        grad = grad_of(h)
        here = slice(h * LANES, (h + 1) * LANES)
        squares = grad * grad
        folded = squares[:, 0:LANES]
        for k in range(1, width // LANES):
            folded += squares[:, k * LANES:(k + 1) * LANES]
        old = jnp.where(diagonal, accum[h:h + 1, :], 0.0)
        fresh = jnp.sum(folded * (1.0 / width) + old, axis=1, keepdims=True)
        fresh_table[here, :] = table[here, :] - grad * (learn_rate * lax.rsqrt(fresh))
        new_accum[h:h + 1, :] = jnp.sum(
            jnp.where(diagonal, fresh, 0.0), axis=0, keepdims=True)
        if (h + 1) % per_piece == 0:
            i = h // per_piece
            piece = pl.ds(i * per_piece * LANES, per_piece * LANES)
            copies.append(pltpu.make_async_copy(
                fresh_table.at[piece, :], new_table.at[piece, :], sems.at[i]))
            copies[-1].start()
    for copy in copies:
        copy.wait()


def count_kernel(bag_count, lines, *refs):
    sources, (counts_out, high, low) = refs[:-8], refs[-8:-5]
    msg, code_ref, lane_ref, counts, grads = refs[-5:]
    owners = sources[0].shape[0]
    devices, blocks = msg.shape[0], counts.shape[0]
    base = lax.axis_index("rows") * (blocks * LANES)
    for i, source in enumerate(sources):
        msg[i * owners:(i + 1) * owners] = source[...]
    read_chunk(
        msg, slice(0, devices), devices, lines, bag_count, base,
        code_ref, lane_ref, counts, grads)
    counts_out[...] = counts[...].astype(jnp.bfloat16)
    high[...], low[...] = split_two(grads[...])


def apply_kernel(bag_count, lines, late, *refs):
    sources, (counted, high, low, table, accum) = refs[:late], refs[late:late + 5]
    new_table, new_accum, msg, code_ref, lane_ref, counts, grads, fresh_table, sems = refs[late + 5:]
    owners = sources[0].shape[0]
    devices, blocks = msg.shape[0], counts.shape[0]
    base = lax.axis_index("rows") * (blocks * LANES)
    for i, source in enumerate(sources):
        msg[i * owners:(i + 1) * owners] = source[...]
    read_chunk(
        msg, slice(0, devices), devices, lines, bag_count, base,
        code_ref, lane_ref, counts, grads)
    parts = [
        jnp.concatenate([early[...], late], axis=0)
        for early, late in zip((high, low), split_two(grads[...]))
    ]

    def grad_of(h):
        hits = jnp.concatenate([counted[h], counts[h].astype(jnp.bfloat16)], axis=0)
        return block_sum(hits, parts)

    apply_rows(grad_of, table, accum, new_table, new_accum, fresh_table, sems)


def update_kernel(bag_count, lines, groups, chunk, *refs):
    sources, (table, accum, new_table, new_accum) = refs[:groups], refs[groups:groups + 4]
    msg, code_ref, lane_ref, counts, grads, sums, fresh_table, sems = refs[groups + 4:]
    devices, blocks = msg.shape[0], counts.shape[0]
    owners = devices // groups
    base = lax.axis_index("rows") * (blocks * LANES)
    for i, source in enumerate(sources):
        msg[i * owners:(i + 1) * owners] = source[...]
    sums[...] = jnp.zeros_like(sums)

    @pl.loop(0, devices // chunk)
    def _(c):
        read_chunk(
            msg, pl.ds(c * chunk, chunk), chunk, lines, bag_count, base,
            code_ref, lane_ref, counts, grads)
        parts = split_two(grads[...])

        @pl.loop(0, blocks)
        def _(h):
            sums[h] += block_sum(counts[h].astype(jnp.bfloat16), parts)

    apply_rows(lambda h: sums[h], table, accum, new_table, new_accum, fresh_table, sems)


def pass_kernel(table, accum, new_table, new_accum, sem):
    copy = pltpu.make_async_copy(table, new_table, sem)
    copy.start()
    new_accum[...] = accum[...]
    copy.wait()


def finish_kernel(returned, accum, pooled, new_accum):
    total = returned[0]
    for i in range(1, returned.shape[0]):
        total += returned[i]
    pooled[...] = total
    new_accum[...] = accum[...]


def listing(size, leader):
    return [(i + leader) % size for i in range(size)]


def exchange(x, axis, leader):
    order = listing(lax.axis_size(axis), leader)
    return lax.all_to_all(
        x, axis, split_axis=0, concat_axis=0, axis_index_groups=[order], tiled=True)


def forward(x, axis, step):
    size = lax.axis_size(axis)
    return lax.ppermute(
        x, axis, [(i, ((i // 2 + step) * 2 + 1 - i % 2) % size) for i in range(size)])


def local(
    item_table, row_accum, owner_map, row_index, bag_index,
    prev_owner, prev_row, prev_bag, grad_pooled,
):
    owners, groups = lax.axis_size("rows"), lax.axis_size("dp")
    devices = owners * groups
    out_leader, back_leader = 5 * owners // 8, owners // 4
    rows_dev, width = item_table.shape
    bag_count = grad_pooled.shape[2]
    lines = row_index.shape[2] // LANES
    blocks = rows_dev // LANES
    prev_length = 2 * lines + bag_count * width // LANES
    vmem = pl.BlockSpec(memory_space=pltpu.VMEM)
    hbm = pl.BlockSpec(memory_space=pltpu.HBM)
    params = pltpu.CompilerParams(vmem_limit_bytes=16 * 1024 * 1024)
    chunk = min(devices, LANES // bag_count)

    def stay(x):
        return pltpu.with_memory_space_constraint(x, pltpu.HBM)

    def line(x):
        return x.reshape(lines, LANES)

    message = pl.pallas_call(
        functools.partial(pack_kernel, rows_dev),
        out_shape=pltpu.VMEM((owners, 2 * lines + prev_length, LANES), jnp.float32),
        in_specs=[hbm] * 7,
        out_specs=vmem,
        scratch_shapes=[pltpu.VMEM((lines, LANES), jnp.int32)] * 6
        + [pltpu.VMEM((bag_count, width), jnp.float32), pltpu.SemaphoreType.DMA((7,))],
        compiler_params=params,
        cost_estimate=pl.CostEstimate(
            flops=1 << 33, bytes_accessed=1 << 20, transcendentals=0),
        name="pack",
    )(*[stay(x) for x in (
        line(owner_map), line(row_index), line(bag_index),
        line(prev_owner), line(prev_row), line(prev_bag), grad_pooled[0, 0],
    )])
    gathered = exchange(message, "rows", out_leader)

    pieces = 8 if blocks % 8 == 0 else 1
    partial_pooled, joined = pl.pallas_call(
        functools.partial(pool_kernel, bag_count, lines, back_leader - out_leader),
        out_shape=(
            pltpu.VMEM((owners, bag_count, width), jnp.float32),
            pltpu.VMEM((owners, prev_length, LANES), jnp.float32),
        ),
        in_specs=[vmem] * 2,
        out_specs=[vmem] * 2,
        scratch_shapes=[
            pltpu.VMEM((owners, lines, LANES), jnp.float32),
            pltpu.VMEM((owners, lines, LANES), jnp.float32),
            pltpu.VMEM((blocks, owners * bag_count, LANES), jnp.float32),
        ],
        compiler_params=params,
        cost_estimate=pl.CostEstimate(
            flops=4 * owners * bag_count * rows_dev * width,
            bytes_accessed=rows_dev * width * 4, transcendentals=0),
        name="pool",
    )(gathered, item_table)
    returned = exchange(partial_pooled, "rows", back_leader)
    there = [joined] + [forward(joined, "dp", step) for step in range(1, groups // 2)]

    segments = chunk * bag_count
    updated = (
        pltpu.HBM((rows_dev, width), jnp.float32),
        pltpu.VMEM((blocks, LANES), jnp.float32),
    )

    def room(count):
        return [
            pltpu.VMEM((count, lines, LANES), jnp.float32),
            pltpu.VMEM((count, lines, LANES), jnp.float32),
            pltpu.VMEM((blocks, count * bag_count, LANES), jnp.float32),
            pltpu.VMEM((count * bag_count, width), jnp.float32),
        ]

    fresh_room = [
        pltpu.VMEM((rows_dev, width), jnp.float32),
        pltpu.SemaphoreType.DMA((pieces,)),
    ]

    def hand_over(there, kept, row_accum):
        handed = [forward(x, "dp", 0) for x in there]
        if devices > chunk:
            return pl.pallas_call(
                functools.partial(update_kernel, bag_count, lines, groups, chunk),
                out_shape=updated,
                in_specs=[vmem] * (groups + 2),
                out_specs=(hbm, vmem),
                scratch_shapes=[pltpu.VMEM((devices, prev_length, LANES), jnp.float32)]
                + room(chunk) + [pltpu.VMEM((blocks, LANES, width), jnp.float32)] + fresh_room,
                compiler_params=pltpu.CompilerParams(vmem_limit_bytes=40 * 1024 * 1024),
                name="update",
            )(*there, *handed, kept, row_accum)
        number = len(there)
        count = number * owners
        counted, high, low = pl.pallas_call(
            functools.partial(count_kernel, bag_count, lines),
            out_shape=[
                pltpu.VMEM((blocks, count * bag_count, LANES), jnp.bfloat16),
                pltpu.VMEM((count * bag_count, width), jnp.bfloat16),
                pltpu.VMEM((count * bag_count, width), jnp.bfloat16),
            ],
            in_specs=[vmem] * number,
            out_specs=[vmem] * 3,
            scratch_shapes=[pltpu.VMEM((count, prev_length, LANES), jnp.float32)] + room(count),
            compiler_params=params,
            cost_estimate=pl.CostEstimate(
                flops=1 << 28, bytes_accessed=1 << 22, transcendentals=0),
            name="count",
        )(*there)
        return pl.pallas_call(
            functools.partial(apply_kernel, bag_count, lines, number),
            out_shape=updated,
            in_specs=[vmem] * (number + 5),
            out_specs=(hbm, vmem),
            scratch_shapes=[pltpu.VMEM((count, prev_length, LANES), jnp.float32)]
            + room(count) + fresh_room,
            compiler_params=params,
            name="apply",
        )(*handed, counted, high, low, kept, row_accum)

    def skip(there, kept, row_accum):
        return pl.pallas_call(
            pass_kernel,
            out_shape=updated,
            in_specs=[vmem] * 2,
            out_specs=(hbm, vmem),
            scratch_shapes=[pltpu.SemaphoreType.DMA],
            compiler_params=params,
            name="pass",
        )(kept, row_accum)

    inside = lax.axis_index("dp") < groups
    new_table, new_accum = lax.cond(
        inside, hand_over, skip, there, item_table, row_accum.reshape(blocks, LANES))

    pooled, new_accum = pl.pallas_call(
        finish_kernel,
        out_shape=(
            jax.ShapeDtypeStruct((bag_count, width), jnp.float32),
            jax.ShapeDtypeStruct((blocks, LANES), jnp.float32),
        ),
        in_specs=[vmem] * 2,
        out_specs=[vmem] * 2,
        compiler_params=params,
        name="finish",
    )(returned, new_accum)
    return (pooled[None, None], new_table, new_accum.reshape(rows_dev))


def solution(mesh):
    placed = (
        P("rows", None),
        P("rows"),
        P("dp", "rows", None, None),
        P("dp", "rows", None),
        P("dp", "rows", None),
        P("dp", "rows", None, None),
        P("dp", "rows", None),
        P("dp", "rows", None),
        P("dp", "rows", None, None),
    )
    return jax.shard_map(
        local,
        mesh=mesh,
        in_specs=placed,
        out_specs=(P("dp", "rows", None, None), P("rows", None), P("rows")),
        check_vma=False,
    )
```

```python
import functools

import jax
import jax.numpy as jnp
from jax import lax
from jax.experimental import pallas as pl
from jax.experimental.pallas import tpu as pltpu
from jax.sharding import PartitionSpec as P

learn_rate = 0.1
LANES = 128


def pack_kernel(rows_dev, *refs):
    sources, out, held, sems = refs[:7], refs[7], refs[8:15], refs[15]
    copies = [
        pltpu.make_async_copy(source, place, sems.at[i])
        for i, (source, place) in enumerate(zip(sources, held))
    ]
    for copy in copies:
        copy.start()
    for copy in copies:
        copy.wait()
    owner, row, bag, prev_owner, prev_row, prev_bag, grad = held
    lines = row.shape[0]
    bag_count, width = grad.shape

    def put(start, value):
        shape = (out.shape[0],) + value.shape
        out[:, start:start + value.shape[0], :] = jnp.broadcast_to(value[None], shape)

    put(0, (owner[...] * rows_dev + row[...]).astype(jnp.float32))
    put(lines, bag[...].astype(jnp.float32))
    put(2 * lines, (prev_owner[...] * rows_dev + prev_row[...]).astype(jnp.float32))
    put(3 * lines, prev_bag[...].astype(jnp.float32))
    for k in range(width // LANES):
        put(4 * lines + k * bag_count, grad[:, k * LANES:(k + 1) * LANES])


def split_two(x):
    high = x.astype(jnp.bfloat16)
    return high, (x - high.astype(jnp.float32)).astype(jnp.bfloat16)


def codes(ids, bags, bag_count, base):
    rel = ids.astype(jnp.int32) - base
    code = lax.shift_right_arithmetic(rel, 7) * bag_count + bags.astype(jnp.int32)
    return code.astype(jnp.float32), (rel & (LANES - 1)).astype(jnp.float32)


def count_into(counts, code_ref, lane_ref, devices, bag_count):
    blocks = counts.shape[0]
    lines = code_ref.shape[1]
    one, none = jnp.ones((), jnp.bfloat16), jnp.zeros((), jnp.bfloat16)

    def one_hot(ref, d, size):
        numbers = lax.broadcasted_iota(jnp.int32, (size, LANES), 0).astype(jnp.bfloat16)
        parts = []
        for k in range(lines):
            row = jnp.broadcast_to(ref[d, k:k + 1, :], (size, LANES)).astype(jnp.bfloat16)
            parts.append(jnp.where(numbers == row, one, none))
        return jnp.concatenate(parts, axis=1)

    for d in range(devices):
        hits = lax.dot_general(
            one_hot(code_ref, d, blocks * bag_count), one_hot(lane_ref, d, LANES),
            (((1,), (1,)), ((), ())), preferred_element_type=jnp.float32)
        counts[:, d * bag_count:(d + 1) * bag_count, :] = hits.reshape(
            blocks, bag_count, LANES)


def pool_kernel(
    bag_count, lines, turn, msg, table, out, joined, code_ref, lane_ref, counts,
):
    rows_dev, width = table.shape
    owners = msg.shape[0]
    base = lax.axis_index("rows") * rows_dev
    code_ref[...], lane_ref[...] = codes(
        msg[:, 0:lines, :], msg[:, lines:2 * lines, :], bag_count, base)
    joined[...] = msg[:, 2 * lines:, :]
    count_into(counts, code_ref, lane_ref, owners, bag_count)
    blocks = rows_dev // LANES
    flat = jnp.concatenate(
        [counts[h].astype(jnp.bfloat16) for h in range(blocks)], axis=1)
    total = jnp.zeros((owners * bag_count, width), jnp.float32)
    for part in split_two(table[...]):
        total += jnp.dot(flat, part, preferred_element_type=jnp.float32)
    for i in range(owners):
        seen = (i + turn) % owners
        out[i] = total[seen * bag_count:(seen + 1) * bag_count, :]


def read_chunk(msg, here, chunk, lines, bag_count, base, code_ref, lane_ref, counts, grads):
    width = grads.shape[1]
    code_ref[...], lane_ref[...] = codes(
        msg[here, 0:lines, :], msg[here, lines:2 * lines, :], bag_count, base)
    count_into(counts, code_ref, lane_ref, chunk, bag_count)
    for k in range(width // LANES):
        start = 2 * lines + k * bag_count
        grads[:, k * LANES:(k + 1) * LANES] = msg[
            here, start:start + bag_count, :].reshape(chunk * bag_count, LANES)


def block_sum(hits, parts):
    width = parts.shape[1] // 2
    both = lax.dot_general(
        hits, parts, (((0,), (0,)), ((), ())), preferred_element_type=jnp.float32)
    return both[:, :width] + both[:, width:]


def apply_rows(grad_of, table, accum, new_table, new_accum, fresh_table, sems):
    blocks, width = accum.shape[0], fresh_table.shape[1]
    diagonal = (
        lax.broadcasted_iota(jnp.int32, (LANES, LANES), 0)
        == lax.broadcasted_iota(jnp.int32, (LANES, LANES), 1))
    per_piece = blocks // sems.shape[0]
    copies = []
    for h in range(blocks):
        grad = grad_of(h)
        here = slice(h * LANES, (h + 1) * LANES)
        squares = grad * grad
        folded = squares[:, 0:LANES]
        for k in range(1, width // LANES):
            folded += squares[:, k * LANES:(k + 1) * LANES]
        old = jnp.where(diagonal, accum[h:h + 1, :], 0.0)
        fresh = jnp.sum(folded * (1.0 / width) + old, axis=1, keepdims=True)
        fresh_table[here, :] = table[here, :] - grad * (learn_rate * lax.rsqrt(fresh))
        new_accum[h:h + 1, :] = jnp.sum(
            jnp.where(diagonal, fresh, 0.0), axis=0, keepdims=True)
        if (h + 1) % per_piece == 0:
            i = h // per_piece
            piece = pl.ds(i * per_piece * LANES, per_piece * LANES)
            copies.append(pltpu.make_async_copy(
                fresh_table.at[piece, :], new_table.at[piece, :], sems.at[i]))
            copies[-1].start()
    for copy in copies:
        copy.wait()


def count_kernel(bag_count, lines, *refs):
    sources, (counts_out, high, low) = refs[:-8], refs[-8:-5]
    msg, code_ref, lane_ref, counts, grads = refs[-5:]
    owners = sources[0].shape[0]
    devices, blocks = msg.shape[0], counts.shape[0]
    base = lax.axis_index("rows") * (blocks * LANES)
    for i, source in enumerate(sources):
        msg[i * owners:(i + 1) * owners] = source[...]
    read_chunk(
        msg, slice(0, devices), devices, lines, bag_count, base,
        code_ref, lane_ref, counts, grads)
    counts_out[...] = counts[...].astype(jnp.bfloat16)
    high[...], low[...] = split_two(grads[...])


def apply_kernel(bag_count, lines, late, *refs):
    sources, (counted, high, low, table, accum) = refs[:late], refs[late:late + 5]
    new_table, new_accum, msg, code_ref, lane_ref, counts, grads, fresh_table, sems = refs[late + 5:]
    owners = sources[0].shape[0]
    devices, blocks = msg.shape[0], counts.shape[0]
    base = lax.axis_index("rows") * (blocks * LANES)
    for i, source in enumerate(sources):
        msg[i * owners:(i + 1) * owners] = source[...]
    read_chunk(
        msg, slice(0, devices), devices, lines, bag_count, base,
        code_ref, lane_ref, counts, grads)
    parts = jnp.concatenate([
        jnp.concatenate([early[...], last], axis=0)
        for early, last in zip((high, low), split_two(grads[...]))
    ], axis=1)

    def grad_of(h):
        hits = jnp.concatenate([counted[h], counts[h].astype(jnp.bfloat16)], axis=0)
        return block_sum(hits, parts)

    apply_rows(grad_of, table, accum, new_table, new_accum, fresh_table, sems)


def update_kernel(bag_count, lines, groups, chunk, *refs):
    sources, (table, accum, new_table, new_accum) = refs[:groups], refs[groups:groups + 4]
    msg, code_ref, lane_ref, counts, grads, sums, fresh_table, sems = refs[groups + 4:]
    devices, blocks = msg.shape[0], counts.shape[0]
    owners = devices // groups
    base = lax.axis_index("rows") * (blocks * LANES)
    for i, source in enumerate(sources):
        msg[i * owners:(i + 1) * owners] = source[...]
    sums[...] = jnp.zeros_like(sums)

    @pl.loop(0, devices // chunk)
    def _(c):
        read_chunk(
            msg, pl.ds(c * chunk, chunk), chunk, lines, bag_count, base,
            code_ref, lane_ref, counts, grads)
        parts = jnp.concatenate(split_two(grads[...]), axis=1)

        @pl.loop(0, blocks)
        def _(h):
            sums[h] += block_sum(counts[h].astype(jnp.bfloat16), parts)

    apply_rows(lambda h: sums[h], table, accum, new_table, new_accum, fresh_table, sems)


def pass_kernel(table, accum, new_table, new_accum, sem):
    copy = pltpu.make_async_copy(table, new_table, sem)
    copy.start()
    new_accum[...] = accum[...]
    copy.wait()


def finish_kernel(returned, accum, pooled, new_accum):
    total = returned[0]
    for i in range(1, returned.shape[0]):
        total += returned[i]
    pooled[...] = total
    new_accum[...] = accum[...]


def listing(size, leader):
    return [(i + leader) % size for i in range(size)]


def exchange(x, axis, leader):
    order = listing(lax.axis_size(axis), leader)
    return lax.all_to_all(
        x, axis, split_axis=0, concat_axis=0, axis_index_groups=[order], tiled=True)


def forward(x, axis, step):
    size = lax.axis_size(axis)
    return lax.ppermute(
        x, axis, [(i, ((i // 2 + step) * 2 + 1 - i % 2) % size) for i in range(size)])


def local(
    item_table, row_accum, owner_map, row_index, bag_index,
    prev_owner, prev_row, prev_bag, grad_pooled,
):
    owners, groups = lax.axis_size("rows"), lax.axis_size("dp")
    devices = owners * groups
    out_leader, back_leader = 5 * owners // 8, owners // 4
    rows_dev, width = item_table.shape
    bag_count = grad_pooled.shape[2]
    lines = row_index.shape[2] // LANES
    blocks = rows_dev // LANES
    prev_length = 2 * lines + bag_count * width // LANES
    vmem = pl.BlockSpec(memory_space=pltpu.VMEM)
    hbm = pl.BlockSpec(memory_space=pltpu.HBM)
    params = pltpu.CompilerParams(vmem_limit_bytes=16 * 1024 * 1024)
    chunk = min(devices, LANES // bag_count)

    def stay(x):
        return pltpu.with_memory_space_constraint(x, pltpu.HBM)

    def line(x):
        return x.reshape(lines, LANES)

    message = pl.pallas_call(
        functools.partial(pack_kernel, rows_dev),
        out_shape=pltpu.VMEM((owners, 2 * lines + prev_length, LANES), jnp.float32),
        in_specs=[hbm] * 7,
        out_specs=vmem,
        scratch_shapes=[pltpu.VMEM((lines, LANES), jnp.int32)] * 6
        + [pltpu.VMEM((bag_count, width), jnp.float32), pltpu.SemaphoreType.DMA((7,))],
        compiler_params=params,
        cost_estimate=pl.CostEstimate(
            flops=1 << 33, bytes_accessed=1 << 20, transcendentals=0),
        name="pack",
    )(*[stay(x) for x in (
        line(owner_map), line(row_index), line(bag_index),
        line(prev_owner), line(prev_row), line(prev_bag), grad_pooled[0, 0],
    )])
    gathered = exchange(message, "rows", out_leader)

    pieces = 8 if blocks % 8 == 0 else 1
    partial_pooled, joined = pl.pallas_call(
        functools.partial(pool_kernel, bag_count, lines, back_leader - out_leader),
        out_shape=(
            pltpu.VMEM((owners, bag_count, width), jnp.float32),
            pltpu.VMEM((owners, prev_length, LANES), jnp.float32),
        ),
        in_specs=[vmem] * 2,
        out_specs=[vmem] * 2,
        scratch_shapes=[
            pltpu.VMEM((owners, lines, LANES), jnp.float32),
            pltpu.VMEM((owners, lines, LANES), jnp.float32),
            pltpu.VMEM((blocks, owners * bag_count, LANES), jnp.float32),
        ],
        compiler_params=params,
        cost_estimate=pl.CostEstimate(
            flops=4 * owners * bag_count * rows_dev * width,
            bytes_accessed=rows_dev * width * 4, transcendentals=0),
        name="pool",
    )(gathered, item_table)
    returned = exchange(partial_pooled, "rows", back_leader)
    there = [joined] + [forward(joined, "dp", step) for step in range(1, groups // 2)]

    segments = chunk * bag_count
    updated = (
        pltpu.HBM((rows_dev, width), jnp.float32),
        pltpu.VMEM((blocks, LANES), jnp.float32),
    )

    def room(count):
        return [
            pltpu.VMEM((count, lines, LANES), jnp.float32),
            pltpu.VMEM((count, lines, LANES), jnp.float32),
            pltpu.VMEM((blocks, count * bag_count, LANES), jnp.float32),
            pltpu.VMEM((count * bag_count, width), jnp.float32),
        ]

    fresh_room = [
        pltpu.VMEM((rows_dev, width), jnp.float32),
        pltpu.SemaphoreType.DMA((pieces,)),
    ]

    def hand_over(there, kept, row_accum):
        handed = [forward(x, "dp", 0) for x in there]
        if devices > chunk:
            return pl.pallas_call(
                functools.partial(update_kernel, bag_count, lines, groups, chunk),
                out_shape=updated,
                in_specs=[vmem] * (groups + 2),
                out_specs=(hbm, vmem),
                scratch_shapes=[pltpu.VMEM((devices, prev_length, LANES), jnp.float32)]
                + room(chunk) + [pltpu.VMEM((blocks, LANES, width), jnp.float32)] + fresh_room,
                compiler_params=pltpu.CompilerParams(vmem_limit_bytes=40 * 1024 * 1024),
                name="update",
            )(*there, *handed, kept, row_accum)
        number = len(there)
        count = number * owners
        counted, high, low = pl.pallas_call(
            functools.partial(count_kernel, bag_count, lines),
            out_shape=[
                pltpu.VMEM((blocks, count * bag_count, LANES), jnp.bfloat16),
                pltpu.VMEM((count * bag_count, width), jnp.bfloat16),
                pltpu.VMEM((count * bag_count, width), jnp.bfloat16),
            ],
            in_specs=[vmem] * number,
            out_specs=[vmem] * 3,
            scratch_shapes=[pltpu.VMEM((count, prev_length, LANES), jnp.float32)] + room(count),
            compiler_params=params,
            cost_estimate=pl.CostEstimate(
                flops=1 << 28, bytes_accessed=1 << 22, transcendentals=0),
            name="count",
        )(*there)
        return pl.pallas_call(
            functools.partial(apply_kernel, bag_count, lines, number),
            out_shape=updated,
            in_specs=[vmem] * (number + 5),
            out_specs=(hbm, vmem),
            scratch_shapes=[pltpu.VMEM((count, prev_length, LANES), jnp.float32)]
            + room(count) + fresh_room,
            compiler_params=params,
            name="apply",
        )(*handed, counted, high, low, kept, row_accum)

    def skip(there, kept, row_accum):
        return pl.pallas_call(
            pass_kernel,
            out_shape=updated,
            in_specs=[vmem] * 2,
            out_specs=(hbm, vmem),
            scratch_shapes=[pltpu.SemaphoreType.DMA],
            compiler_params=params,
            name="pass",
        )(kept, row_accum)

    inside = lax.axis_index("dp") < groups
    new_table, new_accum = lax.cond(
        inside, hand_over, skip, there, item_table, row_accum.reshape(blocks, LANES))

    pooled, new_accum = pl.pallas_call(
        finish_kernel,
        out_shape=(
            jax.ShapeDtypeStruct((bag_count, width), jnp.float32),
            jax.ShapeDtypeStruct((blocks, LANES), jnp.float32),
        ),
        in_specs=[vmem] * 2,
        out_specs=[vmem] * 2,
        compiler_params=params,
        name="finish",
    )(returned, new_accum)
    return (pooled[None, None], new_table, new_accum.reshape(rows_dev))


def solution(mesh):
    placed = (
        P("rows", None),
        P("rows"),
        P("dp", "rows", None, None),
        P("dp", "rows", None),
        P("dp", "rows", None),
        P("dp", "rows", None, None),
        P("dp", "rows", None),
        P("dp", "rows", None),
        P("dp", "rows", None, None),
    )
    return jax.shard_map(
        local,
        mesh=mesh,
        in_specs=placed,
        out_specs=(P("dp", "rows", None, None), P("rows", None), P("rows")),
        check_vma=False,
    )
```

```python
import functools

import jax
import jax.numpy as jnp
from jax import lax
from jax.experimental import pallas as pl
from jax.experimental.pallas import tpu as pltpu
from jax.sharding import PartitionSpec as P

learn_rate = 0.1
LANES = 128


def pack_kernel(rows_dev, *refs):
    sources, out, held, sems = refs[:7], refs[7], refs[8:15], refs[15]
    copies = [
        pltpu.make_async_copy(source, place, sems.at[i])
        for i, (source, place) in enumerate(zip(sources, held))
    ]
    for copy in copies:
        copy.start()
    for copy in copies:
        copy.wait()
    owner, row, bag, prev_owner, prev_row, prev_bag, grad = held
    lines = row.shape[0]
    bag_count, width = grad.shape

    def put(start, value):
        shape = (out.shape[0],) + value.shape
        out[:, start:start + value.shape[0], :] = jnp.broadcast_to(value[None], shape)

    put(0, (owner[...] * rows_dev + row[...]).astype(jnp.float32))
    put(lines, bag[...].astype(jnp.float32))
    put(2 * lines, (prev_owner[...] * rows_dev + prev_row[...]).astype(jnp.float32))
    put(3 * lines, prev_bag[...].astype(jnp.float32))
    for k in range(width // LANES):
        put(4 * lines + k * bag_count, grad[:, k * LANES:(k + 1) * LANES])


def split_two(x):
    high = x.astype(jnp.bfloat16)
    return high, (x - high.astype(jnp.float32)).astype(jnp.bfloat16)


def codes(ids, bags, bag_count, base):
    rel = ids.astype(jnp.int32) - base
    code = lax.shift_right_arithmetic(rel, 7) * bag_count + bags.astype(jnp.int32)
    return code.astype(jnp.float32), (rel & (LANES - 1)).astype(jnp.float32)


def count_into(counts, code_ref, lane_ref, devices, bag_count):
    blocks = counts.shape[0]
    lines = code_ref.shape[1]
    one, none = jnp.ones((), jnp.bfloat16), jnp.zeros((), jnp.bfloat16)

    def one_hot(ref, d, size):
        numbers = lax.broadcasted_iota(jnp.int32, (size, LANES), 0).astype(jnp.bfloat16)
        parts = []
        for k in range(lines):
            row = jnp.broadcast_to(ref[d, k:k + 1, :], (size, LANES)).astype(jnp.bfloat16)
            parts.append(jnp.where(numbers == row, one, none))
        return jnp.concatenate(parts, axis=1)

    for d in range(devices):
        hits = lax.dot_general(
            one_hot(code_ref, d, blocks * bag_count), one_hot(lane_ref, d, LANES),
            (((1,), (1,)), ((), ())), preferred_element_type=jnp.float32)
        counts[:, d * bag_count:(d + 1) * bag_count, :] = hits.reshape(
            blocks, bag_count, LANES)


def pool_kernel(
    bag_count, lines, turn, msg, table, out, joined, code_ref, lane_ref, counts,
):
    rows_dev, width = table.shape
    owners = msg.shape[0]
    base = lax.axis_index("rows") * rows_dev
    code_ref[...], lane_ref[...] = codes(
        msg[:, 0:lines, :], msg[:, lines:2 * lines, :], bag_count, base)
    joined[...] = msg[:, 2 * lines:, :]
    count_into(counts, code_ref, lane_ref, owners, bag_count)
    blocks = rows_dev // LANES
    flat = jnp.concatenate(
        [counts[h].astype(jnp.bfloat16) for h in range(blocks)], axis=1)
    parts = jnp.concatenate(split_two(table[...]), axis=1)
    both = jnp.dot(flat, parts, preferred_element_type=jnp.float32)
    total = both[:, :width] + both[:, width:]
    for i in range(owners):
        seen = (i + turn) % owners
        out[i] = total[seen * bag_count:(seen + 1) * bag_count, :]


def read_chunk(msg, here, chunk, lines, bag_count, base, code_ref, lane_ref, counts, grads):
    width = grads.shape[1]
    code_ref[...], lane_ref[...] = codes(
        msg[here, 0:lines, :], msg[here, lines:2 * lines, :], bag_count, base)
    count_into(counts, code_ref, lane_ref, chunk, bag_count)
    for k in range(width // LANES):
        start = 2 * lines + k * bag_count
        grads[:, k * LANES:(k + 1) * LANES] = msg[
            here, start:start + bag_count, :].reshape(chunk * bag_count, LANES)


def block_sum(hits, parts):
    width = parts.shape[1] // 2
    both = lax.dot_general(
        hits, parts, (((0,), (0,)), ((), ())), preferred_element_type=jnp.float32)
    return both[:, :width] + both[:, width:]


def apply_rows(grad_of, table, accum, new_table, new_accum, fresh_table, sems):
    blocks, width = accum.shape[0], fresh_table.shape[1]
    diagonal = (
        lax.broadcasted_iota(jnp.int32, (LANES, LANES), 0)
        == lax.broadcasted_iota(jnp.int32, (LANES, LANES), 1))
    per_piece = blocks // sems.shape[0]
    copies = []
    for h in range(blocks):
        grad = grad_of(h)
        here = slice(h * LANES, (h + 1) * LANES)
        squares = grad * grad
        folded = squares[:, 0:LANES]
        for k in range(1, width // LANES):
            folded += squares[:, k * LANES:(k + 1) * LANES]
        old = jnp.where(diagonal, accum[h:h + 1, :], 0.0)
        fresh = jnp.sum(folded * (1.0 / width) + old, axis=1, keepdims=True)
        fresh_table[here, :] = table[here, :] - grad * (learn_rate * lax.rsqrt(fresh))
        new_accum[h:h + 1, :] = jnp.sum(
            jnp.where(diagonal, fresh, 0.0), axis=0, keepdims=True)
        if (h + 1) % per_piece == 0:
            i = h // per_piece
            piece = pl.ds(i * per_piece * LANES, per_piece * LANES)
            copies.append(pltpu.make_async_copy(
                fresh_table.at[piece, :], new_table.at[piece, :], sems.at[i]))
            copies[-1].start()
    for copy in copies:
        copy.wait()


def count_kernel(bag_count, lines, *refs):
    sources, (counts_out, high, low) = refs[:-8], refs[-8:-5]
    msg, code_ref, lane_ref, counts, grads = refs[-5:]
    owners = sources[0].shape[0]
    devices, blocks = msg.shape[0], counts.shape[0]
    base = lax.axis_index("rows") * (blocks * LANES)
    for i, source in enumerate(sources):
        msg[i * owners:(i + 1) * owners] = source[...]
    read_chunk(
        msg, slice(0, devices), devices, lines, bag_count, base,
        code_ref, lane_ref, counts, grads)
    counts_out[...] = counts[...].astype(jnp.bfloat16)
    high[...], low[...] = split_two(grads[...])


def apply_kernel(bag_count, lines, late, *refs):
    sources, (counted, high, low, table, accum) = refs[:late], refs[late:late + 5]
    new_table, new_accum, msg, code_ref, lane_ref, counts, grads, fresh_table, sems = refs[late + 5:]
    owners = sources[0].shape[0]
    devices, blocks = msg.shape[0], counts.shape[0]
    base = lax.axis_index("rows") * (blocks * LANES)
    for i, source in enumerate(sources):
        msg[i * owners:(i + 1) * owners] = source[...]
    read_chunk(
        msg, slice(0, devices), devices, lines, bag_count, base,
        code_ref, lane_ref, counts, grads)
    parts = jnp.concatenate([
        jnp.concatenate([early[...], last], axis=0)
        for early, last in zip((high, low), split_two(grads[...]))
    ], axis=1)

    def grad_of(h):
        hits = jnp.concatenate([counted[h], counts[h].astype(jnp.bfloat16)], axis=0)
        return block_sum(hits, parts)

    apply_rows(grad_of, table, accum, new_table, new_accum, fresh_table, sems)


def update_kernel(bag_count, lines, groups, chunk, *refs):
    sources, (table, accum, new_table, new_accum) = refs[:groups], refs[groups:groups + 4]
    msg, code_ref, lane_ref, counts, grads, sums, fresh_table, sems = refs[groups + 4:]
    devices, blocks = msg.shape[0], counts.shape[0]
    owners = devices // groups
    base = lax.axis_index("rows") * (blocks * LANES)
    for i, source in enumerate(sources):
        msg[i * owners:(i + 1) * owners] = source[...]
    sums[...] = jnp.zeros_like(sums)

    @pl.loop(0, devices // chunk)
    def _(c):
        read_chunk(
            msg, pl.ds(c * chunk, chunk), chunk, lines, bag_count, base,
            code_ref, lane_ref, counts, grads)
        parts = jnp.concatenate(split_two(grads[...]), axis=1)

        @pl.loop(0, blocks)
        def _(h):
            sums[h] += block_sum(counts[h].astype(jnp.bfloat16), parts)

    apply_rows(lambda h: sums[h], table, accum, new_table, new_accum, fresh_table, sems)


def pass_kernel(table, accum, new_table, new_accum, sem):
    copy = pltpu.make_async_copy(table, new_table, sem)
    copy.start()
    new_accum[...] = accum[...]
    copy.wait()


def finish_kernel(returned, accum, pooled, new_accum):
    total = returned[0]
    for i in range(1, returned.shape[0]):
        total += returned[i]
    pooled[...] = total
    new_accum[...] = accum[...]


def listing(size, leader):
    return [(i + leader) % size for i in range(size)]


def exchange(x, axis, leader):
    order = listing(lax.axis_size(axis), leader)
    return lax.all_to_all(
        x, axis, split_axis=0, concat_axis=0, axis_index_groups=[order], tiled=True)


def forward(x, axis, step):
    size = lax.axis_size(axis)
    return lax.ppermute(
        x, axis, [(i, ((i // 2 + step) * 2 + 1 - i % 2) % size) for i in range(size)])


def local(
    item_table, row_accum, owner_map, row_index, bag_index,
    prev_owner, prev_row, prev_bag, grad_pooled,
):
    owners, groups = lax.axis_size("rows"), lax.axis_size("dp")
    devices = owners * groups
    out_leader, back_leader = 5 * owners // 8, owners // 4
    rows_dev, width = item_table.shape
    bag_count = grad_pooled.shape[2]
    lines = row_index.shape[2] // LANES
    blocks = rows_dev // LANES
    prev_length = 2 * lines + bag_count * width // LANES
    vmem = pl.BlockSpec(memory_space=pltpu.VMEM)
    hbm = pl.BlockSpec(memory_space=pltpu.HBM)
    params = pltpu.CompilerParams(vmem_limit_bytes=16 * 1024 * 1024)
    chunk = min(devices, LANES // bag_count)

    def stay(x):
        return pltpu.with_memory_space_constraint(x, pltpu.HBM)

    def line(x):
        return x.reshape(lines, LANES)

    message = pl.pallas_call(
        functools.partial(pack_kernel, rows_dev),
        out_shape=pltpu.VMEM((owners, 2 * lines + prev_length, LANES), jnp.float32),
        in_specs=[hbm] * 7,
        out_specs=vmem,
        scratch_shapes=[pltpu.VMEM((lines, LANES), jnp.int32)] * 6
        + [pltpu.VMEM((bag_count, width), jnp.float32), pltpu.SemaphoreType.DMA((7,))],
        compiler_params=params,
        cost_estimate=pl.CostEstimate(
            flops=1 << 33, bytes_accessed=1 << 20, transcendentals=0),
        name="pack",
    )(*[stay(x) for x in (
        line(owner_map), line(row_index), line(bag_index),
        line(prev_owner), line(prev_row), line(prev_bag), grad_pooled[0, 0],
    )])
    gathered = exchange(message, "rows", out_leader)

    pieces = 8 if blocks % 8 == 0 else 1
    partial_pooled, joined = pl.pallas_call(
        functools.partial(pool_kernel, bag_count, lines, back_leader - out_leader),
        out_shape=(
            pltpu.VMEM((owners, bag_count, width), jnp.float32),
            pltpu.VMEM((owners, prev_length, LANES), jnp.float32),
        ),
        in_specs=[vmem] * 2,
        out_specs=[vmem] * 2,
        scratch_shapes=[
            pltpu.VMEM((owners, lines, LANES), jnp.float32),
            pltpu.VMEM((owners, lines, LANES), jnp.float32),
            pltpu.VMEM((blocks, owners * bag_count, LANES), jnp.float32),
        ],
        compiler_params=params,
        cost_estimate=pl.CostEstimate(
            flops=4 * owners * bag_count * rows_dev * width,
            bytes_accessed=rows_dev * width * 4, transcendentals=0),
        name="pool",
    )(gathered, item_table)
    returned = exchange(partial_pooled, "rows", back_leader)
    there = [joined] + [forward(joined, "dp", step) for step in range(1, groups // 2)]

    segments = chunk * bag_count
    updated = (
        pltpu.HBM((rows_dev, width), jnp.float32),
        pltpu.VMEM((blocks, LANES), jnp.float32),
    )

    def room(count):
        return [
            pltpu.VMEM((count, lines, LANES), jnp.float32),
            pltpu.VMEM((count, lines, LANES), jnp.float32),
            pltpu.VMEM((blocks, count * bag_count, LANES), jnp.float32),
            pltpu.VMEM((count * bag_count, width), jnp.float32),
        ]

    fresh_room = [
        pltpu.VMEM((rows_dev, width), jnp.float32),
        pltpu.SemaphoreType.DMA((pieces,)),
    ]

    def hand_over(there, kept, row_accum):
        handed = [forward(x, "dp", 0) for x in there]
        if devices > chunk:
            return pl.pallas_call(
                functools.partial(update_kernel, bag_count, lines, groups, chunk),
                out_shape=updated,
                in_specs=[vmem] * (groups + 2),
                out_specs=(hbm, vmem),
                scratch_shapes=[pltpu.VMEM((devices, prev_length, LANES), jnp.float32)]
                + room(chunk) + [pltpu.VMEM((blocks, LANES, width), jnp.float32)] + fresh_room,
                compiler_params=pltpu.CompilerParams(vmem_limit_bytes=40 * 1024 * 1024),
                name="update",
            )(*there, *handed, kept, row_accum)
        number = len(there)
        count = number * owners
        counted, high, low = pl.pallas_call(
            functools.partial(count_kernel, bag_count, lines),
            out_shape=[
                pltpu.VMEM((blocks, count * bag_count, LANES), jnp.bfloat16),
                pltpu.VMEM((count * bag_count, width), jnp.bfloat16),
                pltpu.VMEM((count * bag_count, width), jnp.bfloat16),
            ],
            in_specs=[vmem] * number,
            out_specs=[vmem] * 3,
            scratch_shapes=[pltpu.VMEM((count, prev_length, LANES), jnp.float32)] + room(count),
            compiler_params=params,
            cost_estimate=pl.CostEstimate(
                flops=1 << 28, bytes_accessed=1 << 22, transcendentals=0),
            name="count",
        )(*there)
        return pl.pallas_call(
            functools.partial(apply_kernel, bag_count, lines, number),
            out_shape=updated,
            in_specs=[vmem] * (number + 5),
            out_specs=(hbm, vmem),
            scratch_shapes=[pltpu.VMEM((count, prev_length, LANES), jnp.float32)]
            + room(count) + fresh_room,
            compiler_params=params,
            name="apply",
        )(*handed, counted, high, low, kept, row_accum)

    def skip(there, kept, row_accum):
        return pl.pallas_call(
            pass_kernel,
            out_shape=updated,
            in_specs=[vmem] * 2,
            out_specs=(hbm, vmem),
            scratch_shapes=[pltpu.SemaphoreType.DMA],
            compiler_params=params,
            name="pass",
        )(kept, row_accum)

    inside = lax.axis_index("dp") < groups
    new_table, new_accum = lax.cond(
        inside, hand_over, skip, there, item_table, row_accum.reshape(blocks, LANES))

    pooled, new_accum = pl.pallas_call(
        finish_kernel,
        out_shape=(
            jax.ShapeDtypeStruct((bag_count, width), jnp.float32),
            jax.ShapeDtypeStruct((blocks, LANES), jnp.float32),
        ),
        in_specs=[vmem] * 2,
        out_specs=[vmem] * 2,
        compiler_params=params,
        name="finish",
    )(returned, new_accum)
    return (pooled[None, None], new_table, new_accum.reshape(rows_dev))


def solution(mesh):
    placed = (
        P("rows", None),
        P("rows"),
        P("dp", "rows", None, None),
        P("dp", "rows", None),
        P("dp", "rows", None),
        P("dp", "rows", None, None),
        P("dp", "rows", None),
        P("dp", "rows", None),
        P("dp", "rows", None, None),
    )
    return jax.shard_map(
        local,
        mesh=mesh,
        in_specs=placed,
        out_specs=(P("dp", "rows", None, None), P("rows", None), P("rows")),
        check_vma=False,
    )
```

```python
import functools

import jax
import jax.numpy as jnp
from jax import lax
from jax.experimental import pallas as pl
from jax.experimental.pallas import tpu as pltpu
from jax.sharding import PartitionSpec as P

learn_rate = 0.1
LANES = 128


def pack_kernel(rows_dev, *refs):
    sources, out, held, sems = refs[:7], refs[7], refs[8:15], refs[15]
    copies = [
        pltpu.make_async_copy(source, place, sems.at[i])
        for i, (source, place) in enumerate(zip(sources, held))
    ]
    for copy in copies:
        copy.start()
    for copy in copies:
        copy.wait()
    owner, row, bag, prev_owner, prev_row, prev_bag, grad = held
    lines = row.shape[0]
    bag_count, width = grad.shape

    def put(start, value):
        shape = (out.shape[0],) + value.shape
        out[:, start:start + value.shape[0], :] = jnp.broadcast_to(value[None], shape)

    put(0, (owner[...] * rows_dev + row[...]).astype(jnp.float32))
    put(lines, bag[...].astype(jnp.float32))
    put(2 * lines, (prev_owner[...] * rows_dev + prev_row[...]).astype(jnp.float32))
    put(3 * lines, prev_bag[...].astype(jnp.float32))
    for k in range(width // LANES):
        put(4 * lines + k * bag_count, grad[:, k * LANES:(k + 1) * LANES])


def split_two(x):
    high = x.astype(jnp.bfloat16)
    return high, (x - high.astype(jnp.float32)).astype(jnp.bfloat16)


def codes(ids, bags, bag_count, base):
    rel = ids.astype(jnp.int32) - base
    code = lax.shift_right_arithmetic(rel, 7) * bag_count + bags.astype(jnp.int32)
    return code.astype(jnp.float32), (rel & (LANES - 1)).astype(jnp.float32)


def count_into(counts, code_ref, lane_ref, devices, bag_count):
    blocks = counts.shape[0]
    lines = code_ref.shape[1]
    one, none = jnp.ones((), jnp.bfloat16), jnp.zeros((), jnp.bfloat16)

    def one_hot(ref, d, size):
        numbers = lax.broadcasted_iota(jnp.int32, (size, LANES), 0).astype(jnp.bfloat16)
        numbers = numbers.reshape(size // 16, 16, LANES)
        parts = []
        for k in range(lines):
            row = jnp.broadcast_to(ref[d, k:k + 1, :], (16, LANES)).astype(jnp.bfloat16)
            hot = jnp.where(numbers == row[None], one, none)
            parts.append(hot.reshape(size, LANES))
        return jnp.concatenate(parts, axis=1)

    for d in range(devices):
        hits = lax.dot_general(
            one_hot(code_ref, d, blocks * bag_count), one_hot(lane_ref, d, LANES),
            (((1,), (1,)), ((), ())), preferred_element_type=jnp.float32)
        counts[:, d * bag_count:(d + 1) * bag_count, :] = hits.reshape(
            blocks, bag_count, LANES)


def pool_kernel(
    bag_count, lines, turn, msg, table, out, joined, code_ref, lane_ref, counts,
):
    rows_dev, width = table.shape
    owners = msg.shape[0]
    base = lax.axis_index("rows") * rows_dev
    code_ref[...], lane_ref[...] = codes(
        msg[:, 0:lines, :], msg[:, lines:2 * lines, :], bag_count, base)
    joined[...] = msg[:, 2 * lines:, :]
    count_into(counts, code_ref, lane_ref, owners, bag_count)
    blocks = rows_dev // LANES
    flat = jnp.concatenate(
        [counts[h].astype(jnp.bfloat16) for h in range(blocks)], axis=1)
    parts = jnp.concatenate(split_two(table[...]), axis=1)
    both = jnp.dot(flat, parts, preferred_element_type=jnp.float32)
    total = both[:, :width] + both[:, width:]
    for i in range(owners):
        seen = (i + turn) % owners
        out[i] = total[seen * bag_count:(seen + 1) * bag_count, :]


def read_chunk(msg, here, chunk, lines, bag_count, base, code_ref, lane_ref, counts, grads):
    width = grads.shape[1]
    code_ref[...], lane_ref[...] = codes(
        msg[here, 0:lines, :], msg[here, lines:2 * lines, :], bag_count, base)
    count_into(counts, code_ref, lane_ref, chunk, bag_count)
    for k in range(width // LANES):
        start = 2 * lines + k * bag_count
        grads[:, k * LANES:(k + 1) * LANES] = msg[
            here, start:start + bag_count, :].reshape(chunk * bag_count, LANES)


def block_sum(hits, parts):
    width = parts.shape[1] // 2
    both = lax.dot_general(
        hits, parts, (((0,), (0,)), ((), ())), preferred_element_type=jnp.float32)
    return both[:, :width] + both[:, width:]


def apply_rows(grad_of, table, accum, new_table, new_accum, fresh_table, sems):
    blocks, width = accum.shape[0], fresh_table.shape[1]
    diagonal = (
        lax.broadcasted_iota(jnp.int32, (LANES, LANES), 0)
        == lax.broadcasted_iota(jnp.int32, (LANES, LANES), 1))
    per_piece = blocks // sems.shape[0]
    copies = []
    for h in range(blocks):
        grad = grad_of(h)
        here = slice(h * LANES, (h + 1) * LANES)
        squares = grad * grad
        folded = squares[:, 0:LANES]
        for k in range(1, width // LANES):
            folded += squares[:, k * LANES:(k + 1) * LANES]
        old = jnp.where(diagonal, accum[h:h + 1, :], 0.0)
        fresh = jnp.sum(folded * (1.0 / width) + old, axis=1, keepdims=True)
        fresh_table[here, :] = table[here, :] - grad * (learn_rate * lax.rsqrt(fresh))
        new_accum[h:h + 1, :] = jnp.sum(
            jnp.where(diagonal, fresh, 0.0), axis=0, keepdims=True)
        if (h + 1) % per_piece == 0:
            i = h // per_piece
            piece = pl.ds(i * per_piece * LANES, per_piece * LANES)
            copies.append(pltpu.make_async_copy(
                fresh_table.at[piece, :], new_table.at[piece, :], sems.at[i]))
            copies[-1].start()
    for copy in copies:
        copy.wait()


def count_kernel(bag_count, lines, *refs):
    sources, (counts_out, high, low) = refs[:-8], refs[-8:-5]
    msg, code_ref, lane_ref, counts, grads = refs[-5:]
    owners = sources[0].shape[0]
    devices, blocks = msg.shape[0], counts.shape[0]
    base = lax.axis_index("rows") * (blocks * LANES)
    for i, source in enumerate(sources):
        msg[i * owners:(i + 1) * owners] = source[...]
    read_chunk(
        msg, slice(0, devices), devices, lines, bag_count, base,
        code_ref, lane_ref, counts, grads)
    counts_out[...] = counts[...].astype(jnp.bfloat16)
    high[...], low[...] = split_two(grads[...])


def apply_kernel(bag_count, lines, late, *refs):
    sources, (counted, high, low, table, accum) = refs[:late], refs[late:late + 5]
    new_table, new_accum, msg, code_ref, lane_ref, counts, grads, fresh_table, sems = refs[late + 5:]
    owners = sources[0].shape[0]
    devices, blocks = msg.shape[0], counts.shape[0]
    base = lax.axis_index("rows") * (blocks * LANES)
    for i, source in enumerate(sources):
        msg[i * owners:(i + 1) * owners] = source[...]
    read_chunk(
        msg, slice(0, devices), devices, lines, bag_count, base,
        code_ref, lane_ref, counts, grads)
    parts = jnp.concatenate([
        jnp.concatenate([early[...], last], axis=0)
        for early, last in zip((high, low), split_two(grads[...]))
    ], axis=1)

    def grad_of(h):
        hits = jnp.concatenate([counted[h], counts[h].astype(jnp.bfloat16)], axis=0)
        return block_sum(hits, parts)

    apply_rows(grad_of, table, accum, new_table, new_accum, fresh_table, sems)


def update_kernel(bag_count, lines, groups, chunk, *refs):
    sources, (table, accum, new_table, new_accum) = refs[:groups], refs[groups:groups + 4]
    msg, code_ref, lane_ref, counts, grads, sums, fresh_table, sems = refs[groups + 4:]
    devices, blocks = msg.shape[0], counts.shape[0]
    owners = devices // groups
    base = lax.axis_index("rows") * (blocks * LANES)
    for i, source in enumerate(sources):
        msg[i * owners:(i + 1) * owners] = source[...]
    sums[...] = jnp.zeros_like(sums)

    @pl.loop(0, devices // chunk)
    def _(c):
        read_chunk(
            msg, pl.ds(c * chunk, chunk), chunk, lines, bag_count, base,
            code_ref, lane_ref, counts, grads)
        parts = jnp.concatenate(split_two(grads[...]), axis=1)

        @pl.loop(0, blocks)
        def _(h):
            sums[h] += block_sum(counts[h].astype(jnp.bfloat16), parts)

    apply_rows(lambda h: sums[h], table, accum, new_table, new_accum, fresh_table, sems)


def pass_kernel(table, accum, new_table, new_accum, sem):
    copy = pltpu.make_async_copy(table, new_table, sem)
    copy.start()
    new_accum[...] = accum[...]
    copy.wait()


def finish_kernel(returned, accum, pooled, new_accum):
    total = returned[0]
    for i in range(1, returned.shape[0]):
        total += returned[i]
    pooled[...] = total
    new_accum[...] = accum[...]


def listing(size, leader):
    return [(i + leader) % size for i in range(size)]


def exchange(x, axis, leader):
    order = listing(lax.axis_size(axis), leader)
    return lax.all_to_all(
        x, axis, split_axis=0, concat_axis=0, axis_index_groups=[order], tiled=True)


def forward(x, axis, step):
    size = lax.axis_size(axis)
    return lax.ppermute(
        x, axis, [(i, ((i // 2 + step) * 2 + 1 - i % 2) % size) for i in range(size)])


def local(
    item_table, row_accum, owner_map, row_index, bag_index,
    prev_owner, prev_row, prev_bag, grad_pooled,
):
    owners, groups = lax.axis_size("rows"), lax.axis_size("dp")
    devices = owners * groups
    out_leader, back_leader = 5 * owners // 8, owners // 4
    rows_dev, width = item_table.shape
    bag_count = grad_pooled.shape[2]
    lines = row_index.shape[2] // LANES
    blocks = rows_dev // LANES
    prev_length = 2 * lines + bag_count * width // LANES
    vmem = pl.BlockSpec(memory_space=pltpu.VMEM)
    hbm = pl.BlockSpec(memory_space=pltpu.HBM)
    params = pltpu.CompilerParams(vmem_limit_bytes=16 * 1024 * 1024)
    chunk = min(devices, LANES // bag_count)

    def stay(x):
        return pltpu.with_memory_space_constraint(x, pltpu.HBM)

    def line(x):
        return x.reshape(lines, LANES)

    message = pl.pallas_call(
        functools.partial(pack_kernel, rows_dev),
        out_shape=pltpu.VMEM((owners, 2 * lines + prev_length, LANES), jnp.float32),
        in_specs=[hbm] * 7,
        out_specs=vmem,
        scratch_shapes=[pltpu.VMEM((lines, LANES), jnp.int32)] * 6
        + [pltpu.VMEM((bag_count, width), jnp.float32), pltpu.SemaphoreType.DMA((7,))],
        compiler_params=params,
        cost_estimate=pl.CostEstimate(
            flops=1 << 33, bytes_accessed=1 << 20, transcendentals=0),
        name="pack",
    )(*[stay(x) for x in (
        line(owner_map), line(row_index), line(bag_index),
        line(prev_owner), line(prev_row), line(prev_bag), grad_pooled[0, 0],
    )])
    gathered = exchange(message, "rows", out_leader)

    pieces = 8 if blocks % 8 == 0 else 1
    partial_pooled, joined = pl.pallas_call(
        functools.partial(pool_kernel, bag_count, lines, back_leader - out_leader),
        out_shape=(
            pltpu.VMEM((owners, bag_count, width), jnp.float32),
            pltpu.VMEM((owners, prev_length, LANES), jnp.float32),
        ),
        in_specs=[vmem] * 2,
        out_specs=[vmem] * 2,
        scratch_shapes=[
            pltpu.VMEM((owners, lines, LANES), jnp.float32),
            pltpu.VMEM((owners, lines, LANES), jnp.float32),
            pltpu.VMEM((blocks, owners * bag_count, LANES), jnp.float32),
        ],
        compiler_params=params,
        cost_estimate=pl.CostEstimate(
            flops=4 * owners * bag_count * rows_dev * width,
            bytes_accessed=rows_dev * width * 4, transcendentals=0),
        name="pool",
    )(gathered, item_table)
    returned = exchange(partial_pooled, "rows", back_leader)
    there = [joined] + [forward(joined, "dp", step) for step in range(1, groups // 2)]

    segments = chunk * bag_count
    updated = (
        pltpu.HBM((rows_dev, width), jnp.float32),
        pltpu.VMEM((blocks, LANES), jnp.float32),
    )

    def room(count):
        return [
            pltpu.VMEM((count, lines, LANES), jnp.float32),
            pltpu.VMEM((count, lines, LANES), jnp.float32),
            pltpu.VMEM((blocks, count * bag_count, LANES), jnp.float32),
            pltpu.VMEM((count * bag_count, width), jnp.float32),
        ]

    fresh_room = [
        pltpu.VMEM((rows_dev, width), jnp.float32),
        pltpu.SemaphoreType.DMA((pieces,)),
    ]

    def hand_over(there, kept, row_accum):
        handed = [forward(x, "dp", 0) for x in there]
        if devices > chunk:
            return pl.pallas_call(
                functools.partial(update_kernel, bag_count, lines, groups, chunk),
                out_shape=updated,
                in_specs=[vmem] * (groups + 2),
                out_specs=(hbm, vmem),
                scratch_shapes=[pltpu.VMEM((devices, prev_length, LANES), jnp.float32)]
                + room(chunk) + [pltpu.VMEM((blocks, LANES, width), jnp.float32)] + fresh_room,
                compiler_params=pltpu.CompilerParams(vmem_limit_bytes=40 * 1024 * 1024),
                name="update",
            )(*there, *handed, kept, row_accum)
        number = len(there)
        count = number * owners
        counted, high, low = pl.pallas_call(
            functools.partial(count_kernel, bag_count, lines),
            out_shape=[
                pltpu.VMEM((blocks, count * bag_count, LANES), jnp.bfloat16),
                pltpu.VMEM((count * bag_count, width), jnp.bfloat16),
                pltpu.VMEM((count * bag_count, width), jnp.bfloat16),
            ],
            in_specs=[vmem] * number,
            out_specs=[vmem] * 3,
            scratch_shapes=[pltpu.VMEM((count, prev_length, LANES), jnp.float32)] + room(count),
            compiler_params=params,
            cost_estimate=pl.CostEstimate(
                flops=1 << 28, bytes_accessed=1 << 22, transcendentals=0),
            name="count",
        )(*there)
        return pl.pallas_call(
            functools.partial(apply_kernel, bag_count, lines, number),
            out_shape=updated,
            in_specs=[vmem] * (number + 5),
            out_specs=(hbm, vmem),
            scratch_shapes=[pltpu.VMEM((count, prev_length, LANES), jnp.float32)]
            + room(count) + fresh_room,
            compiler_params=params,
            name="apply",
        )(*handed, counted, high, low, kept, row_accum)

    def skip(there, kept, row_accum):
        return pl.pallas_call(
            pass_kernel,
            out_shape=updated,
            in_specs=[vmem] * 2,
            out_specs=(hbm, vmem),
            scratch_shapes=[pltpu.SemaphoreType.DMA],
            compiler_params=params,
            name="pass",
        )(kept, row_accum)

    inside = lax.axis_index("dp") < groups
    new_table, new_accum = lax.cond(
        inside, hand_over, skip, there, item_table, row_accum.reshape(blocks, LANES))

    pooled, new_accum = pl.pallas_call(
        finish_kernel,
        out_shape=(
            jax.ShapeDtypeStruct((bag_count, width), jnp.float32),
            jax.ShapeDtypeStruct((blocks, LANES), jnp.float32),
        ),
        in_specs=[vmem] * 2,
        out_specs=[vmem] * 2,
        compiler_params=params,
        name="finish",
    )(returned, new_accum)
    return (pooled[None, None], new_table, new_accum.reshape(rows_dev))


def solution(mesh):
    placed = (
        P("rows", None),
        P("rows"),
        P("dp", "rows", None, None),
        P("dp", "rows", None),
        P("dp", "rows", None),
        P("dp", "rows", None, None),
        P("dp", "rows", None),
        P("dp", "rows", None),
        P("dp", "rows", None, None),
    )
    return jax.shard_map(
        local,
        mesh=mesh,
        in_specs=placed,
        out_specs=(P("dp", "rows", None, None), P("rows", None), P("rows")),
        check_vma=False,
    )
```

```python
import functools

import jax
import jax.numpy as jnp
from jax import lax
from jax.experimental import pallas as pl
from jax.experimental.pallas import tpu as pltpu
from jax.sharding import PartitionSpec as P

learn_rate = 0.1
LANES = 128


def pack_kernel(rows_dev, *refs):
    sources, out, held, sems = refs[:7], refs[7], refs[8:15], refs[15]
    copies = [
        pltpu.make_async_copy(source, place, sems.at[i])
        for i, (source, place) in enumerate(zip(sources, held))
    ]
    for copy in copies:
        copy.start()
    for copy in copies:
        copy.wait()
    owner, row, bag, prev_owner, prev_row, prev_bag, grad = held
    lines = row.shape[0]
    bag_count, width = grad.shape

    def put(start, value):
        shape = (out.shape[0],) + value.shape
        out[:, start:start + value.shape[0], :] = jnp.broadcast_to(value[None], shape)

    put(0, (owner[...] * rows_dev + row[...]).astype(jnp.float32))
    put(lines, bag[...].astype(jnp.float32))
    put(2 * lines, (prev_owner[...] * rows_dev + prev_row[...]).astype(jnp.float32))
    put(3 * lines, prev_bag[...].astype(jnp.float32))
    for k in range(width // LANES):
        put(4 * lines + k * bag_count, grad[:, k * LANES:(k + 1) * LANES])


def split_two(x):
    high = x.astype(jnp.bfloat16)
    return high, (x - high.astype(jnp.float32)).astype(jnp.bfloat16)


def codes(ids, bags, bag_count, base):
    rel = ids.astype(jnp.int32) - base
    code = lax.shift_right_arithmetic(rel, 7) * bag_count + bags.astype(jnp.int32)
    return code.astype(jnp.float32), (rel & (LANES - 1)).astype(jnp.float32)


def count_into(counts, code_ref, lane_ref, devices, bag_count):
    blocks = counts.shape[0]
    lines = code_ref.shape[1]
    one, none = jnp.ones((), jnp.bfloat16), jnp.zeros((), jnp.bfloat16)

    def one_hot(ref, d, size):
        numbers = lax.broadcasted_iota(jnp.int32, (size, LANES), 0).astype(jnp.bfloat16)
        numbers = numbers.reshape(size // 16, 16, LANES)
        parts = []
        for k in range(lines):
            row = jnp.broadcast_to(ref[d, k:k + 1, :], (16, LANES)).astype(jnp.bfloat16)
            hot = jnp.where(numbers == row[None], one, none)
            parts.append(hot.reshape(size, LANES))
        return jnp.concatenate(parts, axis=1)

    for d in range(devices):
        hits = lax.dot_general(
            one_hot(code_ref, d, blocks * bag_count), one_hot(lane_ref, d, LANES),
            (((1,), (1,)), ((), ())), preferred_element_type=jnp.float32)
        counts[:, d * bag_count:(d + 1) * bag_count, :] = hits.reshape(
            blocks, bag_count, LANES)


def pool_kernel(
    bag_count, lines, turn, msg, table, out, joined, code_ref, lane_ref, counts,
):
    rows_dev, width = table.shape
    owners = msg.shape[0]
    base = lax.axis_index("rows") * rows_dev
    code_ref[...], lane_ref[...] = codes(
        msg[:, 0:lines, :], msg[:, lines:2 * lines, :], bag_count, base)
    joined[...] = msg[:, 2 * lines:, :]
    count_into(counts, code_ref, lane_ref, owners, bag_count)
    blocks = rows_dev // LANES
    flat = jnp.concatenate(
        [counts[h].astype(jnp.bfloat16) for h in range(blocks)], axis=1)
    parts = jnp.concatenate(split_two(table[...]), axis=1)
    both = jnp.dot(flat, parts, preferred_element_type=jnp.float32)
    total = both[:, :width] + both[:, width:]
    for i in range(owners):
        seen = (i + turn) % owners
        out[i] = total[seen * bag_count:(seen + 1) * bag_count, :]


def read_chunk(msg, here, chunk, lines, bag_count, base, code_ref, lane_ref, counts, grads):
    width = grads.shape[1]
    code_ref[...], lane_ref[...] = codes(
        msg[here, 0:lines, :], msg[here, lines:2 * lines, :], bag_count, base)
    count_into(counts, code_ref, lane_ref, chunk, bag_count)
    for k in range(width // LANES):
        start = 2 * lines + k * bag_count
        grads[:, k * LANES:(k + 1) * LANES] = msg[
            here, start:start + bag_count, :].reshape(chunk * bag_count, LANES)


def block_sum(hits, parts):
    width = parts.shape[1] // 2
    both = lax.dot_general(
        hits, parts, (((0,), (0,)), ((), ())), preferred_element_type=jnp.float32)
    return both[:, :width] + both[:, width:]


def apply_rows(grad_of, table, accum, new_table, new_accum, fresh_table, sems):
    blocks, width = accum.shape[0], fresh_table.shape[1]
    diagonal = (
        lax.broadcasted_iota(jnp.int32, (LANES, LANES), 0)
        == lax.broadcasted_iota(jnp.int32, (LANES, LANES), 1))
    per_piece = blocks // sems.shape[0]
    copies = []
    for h in range(blocks):
        grad = grad_of(h)
        here = slice(h * LANES, (h + 1) * LANES)
        squares = grad * grad
        folded = squares[:, 0:LANES]
        for k in range(1, width // LANES):
            folded += squares[:, k * LANES:(k + 1) * LANES]
        old = jnp.where(diagonal, accum[h:h + 1, :], 0.0)
        fresh = jnp.sum(folded * (1.0 / width) + old, axis=1, keepdims=True)
        fresh_table[here, :] = table[here, :] - grad * (learn_rate * lax.rsqrt(fresh))
        new_accum[h:h + 1, :] = jnp.sum(
            jnp.where(diagonal, fresh, 0.0), axis=0, keepdims=True)
        if (h + 1) % per_piece == 0:
            i = h // per_piece
            piece = pl.ds(i * per_piece * LANES, per_piece * LANES)
            copies.append(pltpu.make_async_copy(
                fresh_table.at[piece, :], new_table.at[piece, :], sems.at[i]))
            copies[-1].start()
    for copy in copies:
        copy.wait()


def count_kernel(bag_count, lines, *refs):
    sources, (counts_out, high, low) = refs[:-8], refs[-8:-5]
    msg, code_ref, lane_ref, counts, grads = refs[-5:]
    owners = sources[0].shape[0]
    devices, blocks = msg.shape[0], counts.shape[0]
    base = lax.axis_index("rows") * (blocks * LANES)
    for i, source in enumerate(sources):
        msg[i * owners:(i + 1) * owners] = source[...]
    read_chunk(
        msg, slice(0, devices), devices, lines, bag_count, base,
        code_ref, lane_ref, counts, grads)
    counts_out[...] = counts[...].astype(jnp.bfloat16)
    high[...], low[...] = split_two(grads[...])


def apply_kernel(bag_count, lines, late, *refs):
    sources, (counted, high, low, table, accum) = refs[:late], refs[late:late + 5]
    new_table, new_accum, msg, code_ref, lane_ref, counts, grads, fresh_table, sems = refs[late + 5:]
    owners = sources[0].shape[0]
    devices, blocks = msg.shape[0], counts.shape[0]
    base = lax.axis_index("rows") * (blocks * LANES)
    for i, source in enumerate(sources):
        msg[i * owners:(i + 1) * owners] = source[...]
    read_chunk(
        msg, slice(0, devices), devices, lines, bag_count, base,
        code_ref, lane_ref, counts, grads)
    parts = jnp.concatenate([
        jnp.concatenate([early[...], last], axis=0)
        for early, last in zip((high, low), split_two(grads[...]))
    ], axis=1)

    def grad_of(h):
        hits = jnp.concatenate([counted[h], counts[h].astype(jnp.bfloat16)], axis=0)
        return block_sum(hits, parts)

    apply_rows(grad_of, table, accum, new_table, new_accum, fresh_table, sems)


def update_kernel(bag_count, lines, groups, chunk, *refs):
    sources, (table, accum, new_table, new_accum) = refs[:groups], refs[groups:groups + 4]
    msg, code_ref, lane_ref, counts, grads, sums, fresh_table, sems = refs[groups + 4:]
    devices, blocks = msg.shape[0], counts.shape[0]
    owners = devices // groups
    base = lax.axis_index("rows") * (blocks * LANES)
    for i, source in enumerate(sources):
        msg[i * owners:(i + 1) * owners] = source[...]
    sums[...] = jnp.zeros_like(sums)

    @pl.loop(0, devices // chunk)
    def _(c):
        read_chunk(
            msg, pl.ds(c * chunk, chunk), chunk, lines, bag_count, base,
            code_ref, lane_ref, counts, grads)
        parts = jnp.concatenate(split_two(grads[...]), axis=1)

        @pl.loop(0, blocks)
        def _(h):
            sums[h] += block_sum(counts[h].astype(jnp.bfloat16), parts)

    apply_rows(lambda h: sums[h], table, accum, new_table, new_accum, fresh_table, sems)


def pass_kernel(table, accum, new_table, new_accum, sem):
    copy = pltpu.make_async_copy(table, new_table, sem)
    copy.start()
    new_accum[...] = accum[...]
    copy.wait()


def finish_kernel(returned, accum, pooled, new_accum):
    total = returned[0]
    for i in range(1, returned.shape[0]):
        total += returned[i]
    pooled[...] = total
    new_accum[...] = accum[...]


def listing(size, leader):
    return [(i + leader) % size for i in range(size)]


def exchange(x, axis, leader):
    order = listing(lax.axis_size(axis), leader)
    return lax.all_to_all(
        x, axis, split_axis=0, concat_axis=0, axis_index_groups=[order], tiled=True)


def forward(x, axis, step):
    size = lax.axis_size(axis)
    return lax.ppermute(
        x, axis, [(i, ((i // 2 + step) * 2 + 1 - i % 2) % size) for i in range(size)])


def local(
    item_table, row_accum, owner_map, row_index, bag_index,
    prev_owner, prev_row, prev_bag, grad_pooled,
):
    owners, groups = lax.axis_size("rows"), lax.axis_size("dp")
    devices = owners * groups
    out_leader, back_leader = 5 * owners // 8, owners // 2
    rows_dev, width = item_table.shape
    bag_count = grad_pooled.shape[2]
    lines = row_index.shape[2] // LANES
    blocks = rows_dev // LANES
    prev_length = 2 * lines + bag_count * width // LANES
    vmem = pl.BlockSpec(memory_space=pltpu.VMEM)
    hbm = pl.BlockSpec(memory_space=pltpu.HBM)
    params = pltpu.CompilerParams(vmem_limit_bytes=16 * 1024 * 1024)
    chunk = min(devices, LANES // bag_count)

    def stay(x):
        return pltpu.with_memory_space_constraint(x, pltpu.HBM)

    def line(x):
        return x.reshape(lines, LANES)

    message = pl.pallas_call(
        functools.partial(pack_kernel, rows_dev),
        out_shape=pltpu.VMEM((owners, 2 * lines + prev_length, LANES), jnp.float32),
        in_specs=[hbm] * 7,
        out_specs=vmem,
        scratch_shapes=[pltpu.VMEM((lines, LANES), jnp.int32)] * 6
        + [pltpu.VMEM((bag_count, width), jnp.float32), pltpu.SemaphoreType.DMA((7,))],
        compiler_params=params,
        cost_estimate=pl.CostEstimate(
            flops=1 << 33, bytes_accessed=1 << 20, transcendentals=0),
        name="pack",
    )(*[stay(x) for x in (
        line(owner_map), line(row_index), line(bag_index),
        line(prev_owner), line(prev_row), line(prev_bag), grad_pooled[0, 0],
    )])
    gathered = exchange(message, "rows", out_leader)

    pieces = 8 if blocks % 8 == 0 else 1
    partial_pooled, joined = pl.pallas_call(
        functools.partial(pool_kernel, bag_count, lines, back_leader - out_leader),
        out_shape=(
            pltpu.VMEM((owners, bag_count, width), jnp.float32),
            pltpu.VMEM((owners, prev_length, LANES), jnp.float32),
        ),
        in_specs=[vmem] * 2,
        out_specs=[vmem] * 2,
        scratch_shapes=[
            pltpu.VMEM((owners, lines, LANES), jnp.float32),
            pltpu.VMEM((owners, lines, LANES), jnp.float32),
            pltpu.VMEM((blocks, owners * bag_count, LANES), jnp.float32),
        ],
        compiler_params=params,
        cost_estimate=pl.CostEstimate(
            flops=4 * owners * bag_count * rows_dev * width,
            bytes_accessed=rows_dev * width * 4, transcendentals=0),
        name="pool",
    )(gathered, item_table)
    returned = exchange(partial_pooled, "rows", back_leader)
    there = [joined] + [forward(joined, "dp", step) for step in range(1, groups // 2)]

    segments = chunk * bag_count
    updated = (
        pltpu.HBM((rows_dev, width), jnp.float32),
        pltpu.VMEM((blocks, LANES), jnp.float32),
    )

    def room(count):
        return [
            pltpu.VMEM((count, lines, LANES), jnp.float32),
            pltpu.VMEM((count, lines, LANES), jnp.float32),
            pltpu.VMEM((blocks, count * bag_count, LANES), jnp.float32),
            pltpu.VMEM((count * bag_count, width), jnp.float32),
        ]

    fresh_room = [
        pltpu.VMEM((rows_dev, width), jnp.float32),
        pltpu.SemaphoreType.DMA((pieces,)),
    ]

    def hand_over(there, kept, row_accum):
        handed = [forward(x, "dp", 0) for x in there]
        if devices > chunk:
            return pl.pallas_call(
                functools.partial(update_kernel, bag_count, lines, groups, chunk),
                out_shape=updated,
                in_specs=[vmem] * (groups + 2),
                out_specs=(hbm, vmem),
                scratch_shapes=[pltpu.VMEM((devices, prev_length, LANES), jnp.float32)]
                + room(chunk) + [pltpu.VMEM((blocks, LANES, width), jnp.float32)] + fresh_room,
                compiler_params=pltpu.CompilerParams(vmem_limit_bytes=40 * 1024 * 1024),
                name="update",
            )(*there, *handed, kept, row_accum)
        number = len(there)
        count = number * owners
        counted, high, low = pl.pallas_call(
            functools.partial(count_kernel, bag_count, lines),
            out_shape=[
                pltpu.VMEM((blocks, count * bag_count, LANES), jnp.bfloat16),
                pltpu.VMEM((count * bag_count, width), jnp.bfloat16),
                pltpu.VMEM((count * bag_count, width), jnp.bfloat16),
            ],
            in_specs=[vmem] * number,
            out_specs=[vmem] * 3,
            scratch_shapes=[pltpu.VMEM((count, prev_length, LANES), jnp.float32)] + room(count),
            compiler_params=params,
            cost_estimate=pl.CostEstimate(
                flops=1 << 28, bytes_accessed=1 << 22, transcendentals=0),
            name="count",
        )(*there)
        return pl.pallas_call(
            functools.partial(apply_kernel, bag_count, lines, number),
            out_shape=updated,
            in_specs=[vmem] * (number + 5),
            out_specs=(hbm, vmem),
            scratch_shapes=[pltpu.VMEM((count, prev_length, LANES), jnp.float32)]
            + room(count) + fresh_room,
            compiler_params=params,
            name="apply",
        )(*handed, counted, high, low, kept, row_accum)

    def skip(there, kept, row_accum):
        return pl.pallas_call(
            pass_kernel,
            out_shape=updated,
            in_specs=[vmem] * 2,
            out_specs=(hbm, vmem),
            scratch_shapes=[pltpu.SemaphoreType.DMA],
            compiler_params=params,
            name="pass",
        )(kept, row_accum)

    inside = lax.axis_index("dp") < groups
    new_table, new_accum = lax.cond(
        inside, hand_over, skip, there, item_table, row_accum.reshape(blocks, LANES))

    pooled, new_accum = pl.pallas_call(
        finish_kernel,
        out_shape=(
            jax.ShapeDtypeStruct((bag_count, width), jnp.float32),
            jax.ShapeDtypeStruct((blocks, LANES), jnp.float32),
        ),
        in_specs=[vmem] * 2,
        out_specs=[vmem] * 2,
        compiler_params=params,
        name="finish",
    )(returned, new_accum)
    return (pooled[None, None], new_table, new_accum.reshape(rows_dev))


def solution(mesh):
    placed = (
        P("rows", None),
        P("rows"),
        P("dp", "rows", None, None),
        P("dp", "rows", None),
        P("dp", "rows", None),
        P("dp", "rows", None, None),
        P("dp", "rows", None),
        P("dp", "rows", None),
        P("dp", "rows", None, None),
    )
    return jax.shard_map(
        local,
        mesh=mesh,
        in_specs=placed,
        out_specs=(P("dp", "rows", None, None), P("rows", None), P("rows")),
        check_vma=False,
    )
```

```python
import functools

import jax
import jax.numpy as jnp
from jax import lax
from jax.experimental import pallas as pl
from jax.experimental.pallas import tpu as pltpu
from jax.sharding import PartitionSpec as P

learn_rate = 0.1
LANES = 128


def pack_kernel(rows_dev, *refs):
    sources, out, held, sems = refs[:7], refs[7], refs[8:15], refs[15]
    copies = [
        pltpu.make_async_copy(source, place, sems.at[i])
        for i, (source, place) in enumerate(zip(sources, held))
    ]
    for copy in copies:
        copy.start()
    for copy in copies:
        copy.wait()
    owner, row, bag, prev_owner, prev_row, prev_bag, grad = held
    lines = row.shape[0]
    bag_count, width = grad.shape

    def put(start, value):
        shape = (out.shape[0],) + value.shape
        out[:, start:start + value.shape[0], :] = jnp.broadcast_to(value[None], shape)

    put(0, (owner[...] * rows_dev + row[...]).astype(jnp.float32))
    put(lines, bag[...].astype(jnp.float32))
    put(2 * lines, (prev_owner[...] * rows_dev + prev_row[...]).astype(jnp.float32))
    put(3 * lines, prev_bag[...].astype(jnp.float32))
    for k in range(width // LANES):
        put(4 * lines + k * bag_count, grad[:, k * LANES:(k + 1) * LANES])


def split_two(x):
    high = x.astype(jnp.bfloat16)
    return high, (x - high.astype(jnp.float32)).astype(jnp.bfloat16)


def codes(ids, bags, bag_count, base):
    rel = ids.astype(jnp.int32) - base
    code = lax.shift_right_arithmetic(rel, 7) * bag_count + bags.astype(jnp.int32)
    return code.astype(jnp.float32), (rel & (LANES - 1)).astype(jnp.float32)


def count_into(counts, code_ref, lane_ref, devices, bag_count):
    blocks = counts.shape[0]
    lines = code_ref.shape[1]
    one, none = jnp.ones((), jnp.bfloat16), jnp.zeros((), jnp.bfloat16)

    def one_hot(ref, d, size):
        numbers = lax.broadcasted_iota(jnp.int32, (size, LANES), 0).astype(jnp.bfloat16)
        numbers = numbers.reshape(size // 16, 16, LANES)
        parts = []
        for k in range(lines):
            row = jnp.broadcast_to(ref[d, k:k + 1, :], (16, LANES)).astype(jnp.bfloat16)
            hot = jnp.where(numbers == row[None], one, none)
            parts.append(hot.reshape(size, LANES))
        return jnp.concatenate(parts, axis=1)

    for d in range(devices):
        hits = lax.dot_general(
            one_hot(code_ref, d, blocks * bag_count), one_hot(lane_ref, d, LANES),
            (((1,), (1,)), ((), ())), preferred_element_type=jnp.float32)
        counts[:, d * bag_count:(d + 1) * bag_count, :] = hits.reshape(
            blocks, bag_count, LANES)


def pool_kernel(
    bag_count, lines, turn, msg, table, out, joined, code_ref, lane_ref, counts,
):
    rows_dev, width = table.shape
    owners = msg.shape[0]
    base = lax.axis_index("rows") * rows_dev
    code_ref[...], lane_ref[...] = codes(
        msg[:, 0:lines, :], msg[:, lines:2 * lines, :], bag_count, base)
    joined[...] = msg[:, 2 * lines:, :]
    count_into(counts, code_ref, lane_ref, owners, bag_count)
    blocks = rows_dev // LANES
    flat = jnp.concatenate(
        [counts[h].astype(jnp.bfloat16) for h in range(blocks)], axis=1)
    parts = jnp.concatenate(split_two(table[...]), axis=1)
    both = jnp.dot(flat, parts, preferred_element_type=jnp.float32)
    total = both[:, :width] + both[:, width:]
    for i in range(owners):
        seen = (i + turn) % owners
        out[i] = total[seen * bag_count:(seen + 1) * bag_count, :]


def read_chunk(msg, here, chunk, lines, bag_count, base, code_ref, lane_ref, counts, grads):
    width = grads.shape[1]
    code_ref[...], lane_ref[...] = codes(
        msg[here, 0:lines, :], msg[here, lines:2 * lines, :], bag_count, base)
    count_into(counts, code_ref, lane_ref, chunk, bag_count)
    for k in range(width // LANES):
        start = 2 * lines + k * bag_count
        grads[:, k * LANES:(k + 1) * LANES] = msg[
            here, start:start + bag_count, :].reshape(chunk * bag_count, LANES)


def block_sum(hits, parts):
    width = parts.shape[1] // 2
    both = lax.dot_general(
        hits, parts, (((0,), (0,)), ((), ())), preferred_element_type=jnp.float32)
    return both[:, :width] + both[:, width:]


def apply_rows(grad_of, table, accum, new_table, new_accum, fresh_table, sems):
    blocks, width = accum.shape[0], fresh_table.shape[1]
    diagonal = (
        lax.broadcasted_iota(jnp.int32, (LANES, LANES), 0)
        == lax.broadcasted_iota(jnp.int32, (LANES, LANES), 1))
    per_piece = blocks // sems.shape[0]
    copies = []
    for h in range(blocks):
        grad = grad_of(h)
        here = slice(h * LANES, (h + 1) * LANES)
        squares = grad * grad
        folded = squares[:, 0:LANES]
        for k in range(1, width // LANES):
            folded += squares[:, k * LANES:(k + 1) * LANES]
        old = jnp.where(diagonal, accum[h:h + 1, :], 0.0)
        fresh = jnp.sum(folded * (1.0 / width) + old, axis=1, keepdims=True)
        fresh_table[here, :] = table[here, :] - grad * (learn_rate * lax.rsqrt(fresh))
        new_accum[h:h + 1, :] = jnp.sum(
            jnp.where(diagonal, fresh, 0.0), axis=0, keepdims=True)
        if (h + 1) % per_piece == 0:
            i = h // per_piece
            piece = pl.ds(i * per_piece * LANES, per_piece * LANES)
            copies.append(pltpu.make_async_copy(
                fresh_table.at[piece, :], new_table.at[piece, :], sems.at[i]))
            copies[-1].start()
    for copy in copies:
        copy.wait()


def count_kernel(bag_count, lines, *refs):
    sources, (counts_out, high, low) = refs[:-8], refs[-8:-5]
    msg, code_ref, lane_ref, counts, grads = refs[-5:]
    owners = sources[0].shape[0]
    devices, blocks = msg.shape[0], counts.shape[0]
    base = lax.axis_index("rows") * (blocks * LANES)
    for i, source in enumerate(sources):
        msg[i * owners:(i + 1) * owners] = source[...]
    read_chunk(
        msg, slice(0, devices), devices, lines, bag_count, base,
        code_ref, lane_ref, counts, grads)
    counts_out[...] = counts[...].astype(jnp.bfloat16)
    high[...], low[...] = split_two(grads[...])


def apply_kernel(bag_count, lines, late, *refs):
    sources, (counted, high, low, table, accum) = refs[:late], refs[late:late + 5]
    new_table, new_accum, msg, code_ref, lane_ref, counts, grads, fresh_table, sems = refs[late + 5:]
    owners = sources[0].shape[0]
    devices, blocks = msg.shape[0], counts.shape[0]
    base = lax.axis_index("rows") * (blocks * LANES)
    for i, source in enumerate(sources):
        msg[i * owners:(i + 1) * owners] = source[...]
    read_chunk(
        msg, slice(0, devices), devices, lines, bag_count, base,
        code_ref, lane_ref, counts, grads)
    parts = jnp.concatenate([
        jnp.concatenate([early[...], last], axis=0)
        for early, last in zip((high, low), split_two(grads[...]))
    ], axis=1)

    def grad_of(h):
        hits = jnp.concatenate([counted[h], counts[h].astype(jnp.bfloat16)], axis=0)
        return block_sum(hits, parts)

    apply_rows(grad_of, table, accum, new_table, new_accum, fresh_table, sems)


def update_kernel(bag_count, lines, groups, chunk, *refs):
    sources, (table, accum, new_table, new_accum) = refs[:groups], refs[groups:groups + 4]
    msg, code_ref, lane_ref, counts, grads, sums, fresh_table, sems = refs[groups + 4:]
    devices, blocks = msg.shape[0], counts.shape[0]
    owners = devices // groups
    base = lax.axis_index("rows") * (blocks * LANES)
    for i, source in enumerate(sources):
        msg[i * owners:(i + 1) * owners] = source[...]
    sums[...] = jnp.zeros_like(sums)

    @pl.loop(0, devices // chunk)
    def _(c):
        read_chunk(
            msg, pl.ds(c * chunk, chunk), chunk, lines, bag_count, base,
            code_ref, lane_ref, counts, grads)
        parts = jnp.concatenate(split_two(grads[...]), axis=1)

        @pl.loop(0, blocks)
        def _(h):
            sums[h] += block_sum(counts[h].astype(jnp.bfloat16), parts)

    apply_rows(lambda h: sums[h], table, accum, new_table, new_accum, fresh_table, sems)


def pass_kernel(table, accum, new_table, new_accum, sem):
    copy = pltpu.make_async_copy(table, new_table, sem)
    copy.start()
    new_accum[...] = accum[...]
    copy.wait()


def finish_kernel(returned, accum, pooled, new_accum):
    total = returned[0]
    for i in range(1, returned.shape[0]):
        total += returned[i]
    pooled[...] = total
    new_accum[...] = accum[...]


def listing(size, leader):
    return [(i + leader) % size for i in range(size)]


def exchange(x, axis, leader):
    order = listing(lax.axis_size(axis), leader)
    return lax.all_to_all(
        x, axis, split_axis=0, concat_axis=0, axis_index_groups=[order], tiled=True)


def forward(x, axis, step):
    size = lax.axis_size(axis)
    return lax.ppermute(
        x, axis, [(i, ((i // 2 + step) * 2 + 1 - i % 2) % size) for i in range(size)])


def local(
    item_table, row_accum, owner_map, row_index, bag_index,
    prev_owner, prev_row, prev_bag, grad_pooled,
):
    owners, groups = lax.axis_size("rows"), lax.axis_size("dp")
    devices = owners * groups
    out_leader, back_leader = owners // 2, owners // 4
    rows_dev, width = item_table.shape
    bag_count = grad_pooled.shape[2]
    lines = row_index.shape[2] // LANES
    blocks = rows_dev // LANES
    prev_length = 2 * lines + bag_count * width // LANES
    vmem = pl.BlockSpec(memory_space=pltpu.VMEM)
    hbm = pl.BlockSpec(memory_space=pltpu.HBM)
    params = pltpu.CompilerParams(vmem_limit_bytes=16 * 1024 * 1024)
    chunk = min(devices, LANES // bag_count)

    def stay(x):
        return pltpu.with_memory_space_constraint(x, pltpu.HBM)

    def line(x):
        return x.reshape(lines, LANES)

    message = pl.pallas_call(
        functools.partial(pack_kernel, rows_dev),
        out_shape=pltpu.VMEM((owners, 2 * lines + prev_length, LANES), jnp.float32),
        in_specs=[hbm] * 7,
        out_specs=vmem,
        scratch_shapes=[pltpu.VMEM((lines, LANES), jnp.int32)] * 6
        + [pltpu.VMEM((bag_count, width), jnp.float32), pltpu.SemaphoreType.DMA((7,))],
        compiler_params=params,
        cost_estimate=pl.CostEstimate(
            flops=1 << 33, bytes_accessed=1 << 20, transcendentals=0),
        name="pack",
    )(*[stay(x) for x in (
        line(owner_map), line(row_index), line(bag_index),
        line(prev_owner), line(prev_row), line(prev_bag), grad_pooled[0, 0],
    )])
    gathered = exchange(message, "rows", out_leader)

    pieces = 8 if blocks % 8 == 0 else 1
    partial_pooled, joined = pl.pallas_call(
        functools.partial(pool_kernel, bag_count, lines, back_leader - out_leader),
        out_shape=(
            pltpu.VMEM((owners, bag_count, width), jnp.float32),
            pltpu.VMEM((owners, prev_length, LANES), jnp.float32),
        ),
        in_specs=[vmem] * 2,
        out_specs=[vmem] * 2,
        scratch_shapes=[
            pltpu.VMEM((owners, lines, LANES), jnp.float32),
            pltpu.VMEM((owners, lines, LANES), jnp.float32),
            pltpu.VMEM((blocks, owners * bag_count, LANES), jnp.float32),
        ],
        compiler_params=params,
        cost_estimate=pl.CostEstimate(
            flops=4 * owners * bag_count * rows_dev * width,
            bytes_accessed=rows_dev * width * 4, transcendentals=0),
        name="pool",
    )(gathered, item_table)
    returned = exchange(partial_pooled, "rows", back_leader)
    there = [joined] + [forward(joined, "dp", step) for step in range(1, groups // 2)]

    segments = chunk * bag_count
    updated = (
        pltpu.HBM((rows_dev, width), jnp.float32),
        pltpu.VMEM((blocks, LANES), jnp.float32),
    )

    def room(count):
        return [
            pltpu.VMEM((count, lines, LANES), jnp.float32),
            pltpu.VMEM((count, lines, LANES), jnp.float32),
            pltpu.VMEM((blocks, count * bag_count, LANES), jnp.float32),
            pltpu.VMEM((count * bag_count, width), jnp.float32),
        ]

    fresh_room = [
        pltpu.VMEM((rows_dev, width), jnp.float32),
        pltpu.SemaphoreType.DMA((pieces,)),
    ]

    def hand_over(there, kept, row_accum):
        handed = [forward(x, "dp", 0) for x in there]
        if devices > chunk:
            return pl.pallas_call(
                functools.partial(update_kernel, bag_count, lines, groups, chunk),
                out_shape=updated,
                in_specs=[vmem] * (groups + 2),
                out_specs=(hbm, vmem),
                scratch_shapes=[pltpu.VMEM((devices, prev_length, LANES), jnp.float32)]
                + room(chunk) + [pltpu.VMEM((blocks, LANES, width), jnp.float32)] + fresh_room,
                compiler_params=pltpu.CompilerParams(vmem_limit_bytes=40 * 1024 * 1024),
                name="update",
            )(*there, *handed, kept, row_accum)
        number = len(there)
        count = number * owners
        counted, high, low = pl.pallas_call(
            functools.partial(count_kernel, bag_count, lines),
            out_shape=[
                pltpu.VMEM((blocks, count * bag_count, LANES), jnp.bfloat16),
                pltpu.VMEM((count * bag_count, width), jnp.bfloat16),
                pltpu.VMEM((count * bag_count, width), jnp.bfloat16),
            ],
            in_specs=[vmem] * number,
            out_specs=[vmem] * 3,
            scratch_shapes=[pltpu.VMEM((count, prev_length, LANES), jnp.float32)] + room(count),
            compiler_params=params,
            cost_estimate=pl.CostEstimate(
                flops=1 << 28, bytes_accessed=1 << 22, transcendentals=0),
            name="count",
        )(*there)
        return pl.pallas_call(
            functools.partial(apply_kernel, bag_count, lines, number),
            out_shape=updated,
            in_specs=[vmem] * (number + 5),
            out_specs=(hbm, vmem),
            scratch_shapes=[pltpu.VMEM((count, prev_length, LANES), jnp.float32)]
            + room(count) + fresh_room,
            compiler_params=params,
            name="apply",
        )(*handed, counted, high, low, kept, row_accum)

    def skip(there, kept, row_accum):
        return pl.pallas_call(
            pass_kernel,
            out_shape=updated,
            in_specs=[vmem] * 2,
            out_specs=(hbm, vmem),
            scratch_shapes=[pltpu.SemaphoreType.DMA],
            compiler_params=params,
            name="pass",
        )(kept, row_accum)

    inside = lax.axis_index("dp") < groups
    new_table, new_accum = lax.cond(
        inside, hand_over, skip, there, item_table, row_accum.reshape(blocks, LANES))

    pooled, new_accum = pl.pallas_call(
        finish_kernel,
        out_shape=(
            jax.ShapeDtypeStruct((bag_count, width), jnp.float32),
            jax.ShapeDtypeStruct((blocks, LANES), jnp.float32),
        ),
        in_specs=[vmem] * 2,
        out_specs=[vmem] * 2,
        compiler_params=params,
        name="finish",
    )(returned, new_accum)
    return (pooled[None, None], new_table, new_accum.reshape(rows_dev))


def solution(mesh):
    placed = (
        P("rows", None),
        P("rows"),
        P("dp", "rows", None, None),
        P("dp", "rows", None),
        P("dp", "rows", None),
        P("dp", "rows", None, None),
        P("dp", "rows", None),
        P("dp", "rows", None),
        P("dp", "rows", None, None),
    )
    return jax.shard_map(
        local,
        mesh=mesh,
        in_specs=placed,
        out_specs=(P("dp", "rows", None, None), P("rows", None), P("rows")),
        check_vma=False,
    )
```
